128 devices in a mesh: dp: 2 (over core), ctx: 16 (over y, z), tensor: 4 (over x).
Axes of the slice: x: 4, y: 4, z: 4, core: 2. Of those that a mesh axis runs over, the one named last changes fastest.
Arguments:
- inputs: bfloat16 [2, 2, 4096, 2048], P(None, 'dp', 'ctx'), may hold values from -6 to 6
- cotangent: bfloat16 [2, 2, 4096, 2048], P(None, 'dp', 'ctx'), may hold values from -6 to 6
- group_place: int32 [32], replicated, may hold values from 0 to 31, as said below
- attend_gain: bfloat16 [2048], P(('dp', 'ctx')), may hold values from 0.5 to 1.5
- attend_shift: bfloat16 [2048], P(('dp', 'ctx')), may hold values from -2 to 2
- project_weight: bfloat16 [2048, 3, 2048], P(('dp', 'ctx'), None, 'tensor'), may hold values from -0.125 to 0.125
- project_bias: bfloat16 [3, 32, 64], P(None, 'tensor', ('dp', 'ctx')), may hold values from -3 to 3
- output_weight: bfloat16 [2048, 2048], P('tensor', ('dp', 'ctx')), may hold values from -4 to 4
- mixer_gain: bfloat16 [2048], P(('dp', 'ctx')), may hold values from 0.5 to 1.5
- mixer_shift: bfloat16 [2048], P(('dp', 'ctx')), may hold values from -2 to 2
- gate_weight: bfloat16 [2048, 5632], P(('dp', 'ctx'), 'tensor'), may hold values from -0.125 to 0.125
- up_weight: bfloat16 [2048, 5632], P(('dp', 'ctx'), 'tensor'), may hold values from -0.125 to 0.125
- down_weight: bfloat16 [5632, 2048], P('tensor', ('dp', 'ctx')), may hold values from -0.078125 to 0.078125
Outputs:
- outputs: bfloat16 [2, 2, 4096, 2048], P(None, 'dp', 'ctx')
- input_grad: bfloat16 [2, 2, 4096, 2048], P(None, 'dp', 'ctx')
- attend_gain_grad: float32 [2048], P(('dp', 'ctx'))
- attend_shift_grad: float32 [2048], P(('dp', 'ctx'))
- project_weight_grad: float32 [2048, 3, 2048], P(('dp', 'ctx'), None, 'tensor')
- project_bias_grad: float32 [3, 32, 64], P(None, 'tensor', ('dp', 'ctx'))
- output_weight_grad: float32 [2048, 2048], P('tensor', ('dp', 'ctx'))
- mixer_gain_grad: float32 [2048], P(('dp', 'ctx'))
- mixer_shift_grad: float32 [2048], P(('dp', 'ctx'))
- gate_weight_grad: float32 [2048, 5632], P(('dp', 'ctx'), 'tensor')
- up_weight_grad: float32 [2048, 5632], P(('dp', 'ctx'), 'tensor')
- down_weight_grad: float32 [5632, 2048], P('tensor', ('dp', 'ctx'))
The draws below stay inside these ranges and needn't reach their ends.
Inputs may be any that keep to these rules, and one draw needn't show every extreme that they name: `group_place`: stored blocks 2 j and 2 j + 1 of every sequence hold blocks of positions c and 31 - c for some c; every block of positions appears once; each block covers 256/2 consecutive positions.
All inputs are finite; a program needn't handle non-finite values.
Results may differ from the reference program's by a relative error of at most 0.029.
Values may be sent and summed in bfloat16 or wider, within the bound.
A program may use at most 320 MiB of HBM per device.

```python
import jax
import jax.numpy as jnp
from jax import lax

D = 2048
FF = 5632
HEADS = 32
HEAD_DIM = 64
ROT = 16
TOK_DEV = 256
MICRO = 2
BATCH = 2
SEQ = 4096
GROUPS = 32


def draw_group_place(key, part):
    paired = jax.random.permutation(key, GROUPS // 2).astype(jnp.int32)
    mirror = GROUPS - 1 - paired
    return jnp.stack([paired, mirror], axis=1).reshape(GROUPS).astype(jnp.int32)


def block_scale(key, dims, shards, low, top_value):
    def one(axis_at, parts):
        draws = jax.random.uniform(jax.random.fold_in(jax.random.fold_in(key, 6), axis_at), (parts,), jnp.float32, low / len(shards), top_value / len(shards))
        return jnp.repeat(jnp.exp(draws), dims[axis_at] // parts).reshape((-1,) + (1,) * (len(dims) - axis_at - 1))

    gain = one(*shards[0])
    for cut in shards[1:]:
        gain = gain * one(*cut)
    return gain


def bell_draw(own_key, dims, deviation, limit, split=(), kind=jnp.bfloat16):
    values = deviation * jax.random.normal(own_key, dims, jnp.float32)
    if split:
        values = values * block_scale(own_key, dims, split, -0.22, 0.18)
    return jnp.clip(values, -limit, limit).astype(kind)


def setup_inputs(seed: int = 0) -> dict:
    streams_of = jax.random.split(jax.random.key(seed), 14)
    return {
        "inputs": bell_draw(streams_of[0], (MICRO, BATCH, SEQ, D), 1.0, 6.0, ((1, 2), (2, 16))),
        "cotangent": bell_draw(streams_of[1], (MICRO, BATCH, SEQ, D), 1.0, 6.0, ((1, 2), (2, 16))),
        "group_place": draw_group_place(jax.random.fold_in(streams_of[13], 71), 0),
        "attend_gain": jnp.clip(1.0 + 0.1 * jax.random.normal(streams_of[3], (D,), jnp.float32), 0.5, 1.5).astype(jnp.bfloat16),
        "attend_shift": bell_draw(streams_of[4], (D,), 0.3, 2.0, ((0, 32),)),
        "project_weight": bell_draw(streams_of[5], (D, 3, D), D ** -0.5, 0.125, ((0, 32), (2, 4))),
        "project_bias": bell_draw(streams_of[6], (3, HEADS, HEAD_DIM), 0.5, 3.0, ((1, 4), (2, 32))),
        "output_weight": bell_draw(streams_of[7], (D, D), (max(1, 5 * D // SEQ)) ** -0.5, 4.0, ((0, 4), (1, 32))),
        "mixer_gain": jnp.clip(1.0 + 0.1 * jax.random.normal(streams_of[8], (D,), jnp.float32), 0.5, 1.5).astype(jnp.bfloat16),
        "mixer_shift": bell_draw(streams_of[9], (D,), 0.3, 2.0, ((0, 32),)),
        "gate_weight": bell_draw(streams_of[10], (D, FF), D ** -0.5, 0.125, ((0, 32), (1, 4))),
        "up_weight": bell_draw(streams_of[11], (D, FF), D ** -0.5, 0.125, ((0, 32), (1, 4))),
        "down_weight": bell_draw(streams_of[12], (FF, D), FF ** -0.5, 0.078125, ((0, 4), (1, 32))),
    }


@jax.custom_vjp
def low(v):
    return lax.optimization_barrier(v.astype(jnp.bfloat16)).astype(jnp.float32)

@jax.custom_vjp
def low_back(v):
    return v

def low_keep(v):
    return (low(v), None)

def low_pass(kept, grad):
    return (grad,)

def back_keep(v):
    return (v, None)

def back_low(kept, grad):
    return (low(grad),)
low.defvjp(low_keep, low_pass)
low_back.defvjp(back_keep, back_low)
EPSILON = 1e-05
SCORE_SCALE = 0.125
MASKED_SCORE = -1e+30
HIGHEST_PRECISION = lax.Precision.HIGHEST

def layer_norm(values, gain_row, shift_row):
    centre = lax.optimization_barrier(jnp.mean(values, axis=-1, keepdims=True))
    spread = values - centre
    inverse = lax.rsqrt(lax.optimization_barrier(jnp.mean(spread * spread, axis=-1, keepdims=True)) + EPSILON)
    return spread * inverse * gain_row + shift_row

def rotary_tables(places, rot_dims):
    frequency = 10000.0 ** (-jnp.arange(0, rot_dims, 2, dtype=jnp.float32) / rot_dims)
    angles = places.astype(jnp.float32)[:, None] * frequency[None, :]
    cosine_table = jnp.concatenate([jnp.cos(angles), jnp.cos(angles)], axis=-1)
    sine_table = jnp.concatenate([jnp.sin(angles), jnp.sin(angles)], axis=-1)
    return (cosine_table, sine_table)

def rotate(values, cosine_table, sine_table):
    rot_dims = cosine_table.shape[-1]
    halfway = rot_dims // 2
    turned = values[..., :rot_dims]
    swapped = jnp.concatenate([-turned[..., halfway:], turned[..., :halfway]], axis=-1)
    result = turned * cosine_table[:, None, :] + swapped * sine_table[:, None, :]
    return jnp.concatenate([result, values[..., rot_dims:]], axis=-1)

def attend(query_heads, key_heads, value_heads, places):
    block_rows = min(512, SEQ)
    query_blocks = query_heads.reshape(SEQ // block_rows, block_rows, HEADS, HEAD_DIM)
    place_blocks = places.reshape(SEQ // block_rows, block_rows)

    def one_block(pair):
        query_block, place_block = pair
        raw_scores = jnp.einsum('qhe,khe->hqk', query_block, key_heads, precision=HIGHEST_PRECISION)
        raw_scores = low_back(raw_scores)
        allowed = place_block[:, None] >= places[None, :]
        scores = jnp.where(allowed[None], raw_scores * SCORE_SCALE, MASKED_SCORE)
        probs = low(jax.nn.softmax(scores, axis=-1))
        return jnp.einsum('hqk,khe->qhe', probs, value_heads, precision=HIGHEST_PRECISION)
    blocks = lax.map(jax.checkpoint(one_block), (query_blocks, place_blocks))
    return blocks.reshape(SEQ, HEADS, HEAD_DIM)

def layer(residual, params, places, cosine_table, sine_table):
    attend_gain, attend_shift, project_weight, project_bias, output_weight, mixer_gain, mixer_shift, gate_weight, up_weight, down_weight = params
    first_low = low(layer_norm(residual, attend_gain, attend_shift))
    project = jnp.einsum('sd,dtf->stf', first_low, project_weight, precision=HIGHEST_PRECISION)
    project = low_back(project + project_bias.reshape(3, D)).reshape(SEQ, 3, HEADS, HEAD_DIM)
    query_heads = low(rotate(project[:, 0], cosine_table, sine_table))
    key_heads = low(rotate(project[:, 1], cosine_table, sine_table))
    value_heads = low(project[:, 2])
    attended = attend(query_heads, key_heads, value_heads, places)
    attended = low_back(low(attended)).reshape(SEQ, D)
    branch = low_back(jnp.dot(attended, output_weight, precision=HIGHEST_PRECISION))
    hidden = residual + branch
    second_low = low(layer_norm(hidden, mixer_gain, mixer_shift))
    gate_value = low_back(jnp.dot(second_low, gate_weight, precision=HIGHEST_PRECISION))
    up_value = low_back(jnp.dot(second_low, up_weight, precision=HIGHEST_PRECISION))
    mixed = low(jax.nn.silu(gate_value) * up_value)
    return hidden + jnp.dot(mixed, down_weight, precision=HIGHEST_PRECISION)

def reference(inputs, cotangent, group_place, attend_gain, attend_shift, project_weight, project_bias, output_weight, mixer_gain, mixer_shift, gate_weight, up_weight, down_weight):
    half_rows = TOK_DEV // 2
    row_index = jnp.arange(SEQ, dtype=jnp.int32)
    places = group_place[row_index // half_rows].astype(jnp.int32) * half_rows + row_index % half_rows
    cosine_table, sine_table = rotary_tables(places, ROT)
    params = tuple((weight_item.astype(jnp.float32) for weight_item in (attend_gain, attend_shift, project_weight, project_bias, output_weight, mixer_gain, mixer_shift, gate_weight, up_weight, down_weight)))
    flat_inputs = inputs.reshape(MICRO * BATCH, SEQ, D).astype(jnp.float32)
    flat_cotangent = cotangent.reshape(MICRO * BATCH, SEQ, D).astype(jnp.float32)

    def one_sequence(totals, pair):
        residual, upstream = pair
        result, pullback = jax.vjp(lambda rows_in, weights_in: layer(rows_in, weights_in, places, cosine_table, sine_table), residual, params)
        grad_input, grad_params = pullback(upstream)
        totals = jax.tree.map(lambda left_sum, right_sum: left_sum + right_sum, totals, grad_params)
        return (totals, (result, grad_input))
    zeros_start = jax.tree.map(jnp.zeros_like, params)
    totals, (results, grads) = lax.scan(one_sequence, zeros_start, (flat_inputs, flat_cotangent))
    shape_out = (MICRO, BATCH, SEQ, D)
    return (results.reshape(shape_out).astype(jnp.bfloat16), grads.reshape(shape_out).astype(jnp.bfloat16), totals[0], totals[1], totals[2], totals[3], totals[4], totals[5], totals[6], totals[7], totals[8], totals[9])
```

```python
import functools

import jax
import jax.numpy as jnp
from jax import lax
from jax.experimental import pallas as pl
from jax.experimental.pallas import tpu as pltpu
from jax.sharding import PartitionSpec as P

MESH = pl.DeviceIdType.MESH
D = 2048
UNITS = 1408
HEAD_DIM = 64
ROT = 16
EPSILON = 1e-05
LOG2E = 1.4426950408889634
LOW = -1e30
TILE = 512
VMEM_LIMIT = 58 * 2**20
STEPS = (1, 3, 2)
BF = jnp.bfloat16
F32 = jnp.float32


def here():
    ctx = lax.axis_index("ctx")
    return (lax.axis_index("dp"), ctx // 4, lax.rem(ctx, 4), lax.axis_index("tensor"))


def at(c, y, z, x):
    return (c, lax.rem(y, 4) * 4 + lax.rem(z, 4), lax.rem(x, 4))


def up(i, d):
    return lax.rem(i + d, 4)


def down(i, d):
    return lax.rem(i + 4 - d, 4)


class Net:
    def __init__(self, send_sems, recv_sems):
        self.send_sems, self.recv_sems = send_sems, recv_sems
        self.sent = []

    def send(self, src, dst, device):
        n = len(self.sent)
        copy = pltpu.make_async_remote_copy(
            src_ref=src,
            dst_ref=dst,
            send_sem=self.send_sems.at[n],
            recv_sem=self.recv_sems.at[n],
            device_id=device,
            device_id_type=MESH,
        )
        copy.start()
        self.sent.append(copy)
        return copy

    def finish(self):
        for copy in self.sent:
            copy.wait_send()


class Local:
    def __init__(self, sems):
        self.sems, self.n = sems, 0

    def copy(self, src, dst):
        copy = pltpu.make_async_copy(src, dst, self.sems.at[self.n])
        copy.start()
        self.n += 1
        return copy


def greet(peers):
    barrier = pltpu.get_barrier_semaphore()
    for peer in peers:
        pl.semaphore_signal(barrier, inc=1, device_id=peer, device_id_type=MESH)
    pl.semaphore_wait(barrier, len(peers))


def y_peers(c, y, z, x):
    return [at(c, y + d, z, x) for d in (1, 2, 3)]


def z_peers(c, y, z, x):
    return [at(c, y, z + d, x) for d in (1, 2, 3)]


def x_peers(c, y, z, x):
    return [at(c, y, z, x + d) for d in (1, 2, 3)]


def core_peer(c, y, z, x):
    return [at(1 - c, y, z, x)]


FIRST, SECOND = pl.ds(0, 32), pl.ds(32, 32)


class Gather:
    def __init__(self, net, local, src, out, me):
        self.net, self.local, self.src, self.out, self.me = net, local, src, out, me
        self.one, self.two, self.core = {}, {}, []

    def start(self):
        net, src, out = self.net, self.src, self.out
        c, y, z, x = self.me
        self.own = self.local.copy(src, out.at[c, y, z])
        for d in STEPS:
            self.one["a", d] = net.send(
                src.at[FIRST], out.at[c, y, z, FIRST], at(c, y + d, z, x)
            )
            self.one["b", d] = net.send(
                src.at[SECOND], out.at[c, y, z, SECOND], at(c, y, z + d, x)
            )
        self.core.append(net.send(src, out.at[c, y, z], at(1 - c, y, z, x)))
        for e in STEPS:
            self.two["a", 0, e] = net.send(
                src.at[FIRST], out.at[c, y, z, FIRST], at(c, y, z + e, x)
            )
            self.two["b", 0, e] = net.send(
                src.at[SECOND], out.at[c, y, z, SECOND], at(c, y + e, z, x)
            )

    def hand_over(self, piece):
        c, y, z, x = self.me
        self.core.append(self.net.send(piece, piece, at(1 - c, y, z, x)))

    def second(self):
        net, out = self.net, self.out
        c, y, z, x = self.me
        for d in STEPS:
            self.one["a", d].wait_recv()
            piece = out.at[c, down(y, d), z, FIRST]
            for e in STEPS:
                self.two["a", d, e] = net.send(piece, piece, at(c, y, z + e, x))
            self.hand_over(piece)
            self.one["b", d].wait_recv()
            piece = out.at[c, y, down(z, d), SECOND]
            for e in STEPS:
                self.two["b", d, e] = net.send(piece, piece, at(c, y + e, z, x))
            self.hand_over(piece)

    def third(self):
        c, y, z, x = self.me
        for d in (0,) + STEPS:
            for e in STEPS:
                self.two["a", d, e].wait_recv()
                self.hand_over(self.out.at[c, down(y, d), down(z, e), FIRST])
                self.two["b", d, e].wait_recv()
                self.hand_over(self.out.at[c, down(y, e), down(z, d), SECOND])

    def finish(self):
        for copy in self.core:
            copy.wait_recv()
        self.own.wait()


GATHER_COPIES = 6 + 6 + 1 + 18 + 6 + 24


def scatter_scratch(width):
    return [
        pltpu.VMEM((4, 4, 64, width), BF),
        pltpu.VMEM((4, 4, 64, width), BF),
        pltpu.VMEM((3, 4, 32, width), BF),
        pltpu.VMEM((3, 4, 32, width), BF),
        pltpu.VMEM((4, 32, width), BF),
        pltpu.VMEM((4, 32, width), BF),
        pltpu.VMEM((3, 32, width), BF),
        pltpu.VMEM((3, 32, width), BF),
    ]


SCATTER_COPIES = 1 + 6 + 6


class Scatter:
    def __init__(self, net, local, grads, out, scratch, me):
        self.net, self.local, self.grads, self.out, self.me = net, local, grads, out, me
        (self.held, self.other, self.one_a, self.one_b, self.sum_a, self.sum_b, self.two_a, self.two_b) = scratch
        self.width = grads.shape[-1]

    def start(self):
        c, y, z, x = self.me
        self.own = self.local.copy(self.grads.at[c], self.held)
        self.zero = self.net.send(self.grads.at[1 - c], self.other, at(1 - c, y, z, x))

    def first(self):
        c, y, z, x = self.me
        self.own.wait()
        self.zero.wait_recv()
        held, other = self.held, self.other

        def add(i, carry):
            for q in range(4):
                rows = pl.ds(q * 16, 16)
                held[i // 4, lax.rem(i, 4), rows, :] = (
                    held[i // 4, lax.rem(i, 4), rows, :].astype(F32)
                    + other[i // 4, lax.rem(i, 4), rows, :].astype(F32)
                ).astype(BF)
            return carry

        lax.fori_loop(0, 16, add, 0)
        self.to_a, self.to_b = {}, {}
        for e in STEPS:
            self.to_a[e] = self.net.send(
                held.at[:, up(z, e), FIRST, :], self.one_a.at[e - 1], at(c, y, z + e, x)
            )
            self.to_b[e] = self.net.send(
                held.at[up(y, e), :, SECOND, :], self.one_b.at[e - 1], at(c, y + e, z, x)
            )

    def second(self):
        c, y, z, x = self.me
        held, one_a, one_b = self.held, self.one_a, self.one_b
        for e in STEPS:
            self.to_a[e].wait_recv()

        def add_a(i, carry):
            for q in range(2):
                rows = pl.ds(q * 16, 16)
                total = held[i, z, rows, :].astype(F32)
                for n in range(3):
                    total += one_a[n, i, rows, :].astype(F32)
                self.sum_a[i, rows, :] = total.astype(BF)
            return carry

        lax.fori_loop(0, 4, add_a, 0)
        self.last_a, self.last_b = {}, {}
        for d in STEPS:
            self.last_a[d] = self.net.send(
                self.sum_a.at[up(y, d)], self.two_a.at[d - 1], at(c, y + d, z, x)
            )
        for e in STEPS:
            self.to_b[e].wait_recv()

        def add_b(i, carry):
            for q in range(2):
                rows = pl.ds(q * 16, 16)
                far = pl.ds(32 + q * 16, 16)
                total = held[y, i, far, :].astype(F32)
                for n in range(3):
                    total += one_b[n, i, rows, :].astype(F32)
                self.sum_b[i, rows, :] = total.astype(BF)
            return carry

        lax.fori_loop(0, 4, add_b, 0)
        for d in STEPS:
            self.last_b[d] = self.net.send(
                self.sum_b.at[up(z, d)], self.two_b.at[d - 1], at(c, y, z + d, x)
            )

    def third(self):
        c, y, z, x = self.me
        for d in STEPS:
            self.last_a[d].wait_recv()
            self.last_b[d].wait_recv()
        for q in range(2):
            rows = pl.ds(q * 16, 16)
            total = self.sum_a[y, rows, :].astype(F32)
            for n in range(3):
                total += self.two_a[n, rows, :].astype(F32)
            self.out[rows, :] = total
            total = self.sum_b[z, rows, :].astype(F32)
            for n in range(3):
                total += self.two_b[n, rows, :].astype(F32)
            self.out[pl.ds(32 + q * 16, 16), :] = total


class SumX:
    def __init__(self, net, local, parts, held, me):
        self.net, self.local, self.parts, self.held, self.me = net, local, parts, held, me

    def start(self):
        c, y, z, x = self.me
        self.own = self.local.copy(self.parts.at[x], self.held.at[3])
        self.copies = [
            self.net.send(self.parts.at[up(x, d)], self.held.at[d - 1], at(c, y, z, x + d))
            for d in STEPS
        ]

    def arrive(self):
        self.own.wait()
        for copy in self.copies:
            copy.wait_recv()

    def total(self, rows):
        value = self.held[3, rows, :].astype(F32)
        for n in range(3):
            value += self.held[n, rows, :].astype(F32)
        return value

    def gather(self, block, out):
        c, y, z, x = self.me
        self.mine = self.local.copy(block, out.at[x])
        self.backs = [self.net.send(block, out.at[x], at(c, y, z, x + d)) for d in STEPS]

    def finish(self):
        self.mine.wait()
        for copy in self.backs:
            copy.wait_recv()


def row_chunks(step):
    def loop(i, carry):
        step(pl.ds(pl.multiple_of(i * 16, 16), 16))
        return carry

    lax.fori_loop(0, 8, loop, 0)


def normed(values):
    centre = jnp.mean(values, axis=-1, keepdims=True)
    spread = values - centre
    inverse = lax.rsqrt(jnp.mean(spread * spread, axis=-1, keepdims=True) + EPSILON)
    return spread * inverse, inverse


def norm_pullback(upstream, norm, inverse, gain):
    scaled = upstream * gain
    first = jnp.mean(scaled, axis=-1, keepdims=True)
    second = jnp.mean(scaled * norm, axis=-1, keepdims=True)
    return inverse * (scaled - first - norm * second)


ANY = pl.BlockSpec(memory_space=pl.ANY)
IN_VMEM = pl.BlockSpec(memory_space=pltpu.VMEM)


def remote_call(body, name, cid, ins, outs, scratch, copies, locals_):
    return pl.pallas_call(
        body,
        name=name,
        in_specs=ins,
        out_specs=[spec for _, _, spec in outs],
        out_shape=[jax.ShapeDtypeStruct(shape, dtype) for shape, dtype, _ in outs],
        scratch_shapes=scratch
        + [
            pltpu.SemaphoreType.DMA((copies,)),
            pltpu.SemaphoreType.DMA((copies,)),
            pltpu.SemaphoreType.DMA((locals_,)),
        ],
        compiler_params=pltpu.CompilerParams(
            collective_id=cid, has_side_effects=True, vmem_limit_bytes=VMEM_LIMIT
        ),
    )


def gather_front(shard):
    def kernel(src, out, ss, rs, ls):
        me = here()
        greet(y_peers(*me) + z_peers(*me) + core_peer(*me))
        net, local = Net(ss, rs), Local(ls)
        gather = Gather(net, local, src, out, me)
        gather.start()
        gather.second()
        gather.third()
        gather.finish()
        net.finish()

    width = shard.shape[1]
    return remote_call(
        kernel, "gather_front", 0, [ANY], [((2, 4, 4, 64, width), BF, ANY)], [], GATHER_COPIES, 1
    )(shard)[0]


def spread_heads(qkv):
    def kernel(src, out, ss, rs, ls):
        me = here()
        c, y, z, x = me
        greet(y_peers(*me) + z_peers(*me))
        net, local = Net(ss, rs), Local(ls)
        kv = pl.ds(0, 2)
        owns = [local.copy(src.at[0, z], out.at[0, y, z]), local.copy(src.at[1, y], out.at[1, y, z])]
        first, second = {}, []
        for d in STEPS:
            first[0, d] = net.send(src.at[0, up(z, d)], out.at[0, y, z], at(c, y, z + d, x))
            first[1, d] = net.send(src.at[1, up(y, d)], out.at[1, y, z], at(c, y + d, z, x))
        for e in STEPS:
            second.append(net.send(src.at[0, z, kv], out.at[0, y, z, kv], at(c, y + e, z, x)))
            second.append(net.send(src.at[1, y, kv], out.at[1, y, z, kv], at(c, y, z + e, x)))
        for d in STEPS:
            first[0, d].wait_recv()
            piece = out.at[0, y, down(z, d), kv]
            for e in STEPS:
                second.append(net.send(piece, piece, at(c, y + e, z, x)))
            first[1, d].wait_recv()
            piece = out.at[1, down(y, d), z, kv]
            for e in STEPS:
                second.append(net.send(piece, piece, at(c, y, z + e, x)))
        for copy in second:
            copy.wait_recv()
        for copy in owns:
            copy.wait()
        net.finish()

    return remote_call(
        kernel, "spread_heads", 1, [ANY], [((2, 4, 4, 3, 256, 128), BF, ANY)], [], 6 + 6 + 18, 2
    )(qkv)[0]


def swap_rows(blocks, cid, name):
    def kernel(src, out, ss, rs, ls):
        me = here()
        c, y, z, x = me
        greet(y_peers(*me) + z_peers(*me))
        net, local = Net(ss, rs), Local(ls)
        owns = [local.copy(src.at[0, z], out.at[0, z]), local.copy(src.at[1, y], out.at[1, y])]
        copies = []
        for d in STEPS:
            copies.append(net.send(src.at[0, up(z, d)], out.at[0, z], at(c, y, z + d, x)))
            copies.append(net.send(src.at[1, up(y, d)], out.at[1, y], at(c, y + d, z, x)))
        for copy in copies:
            copy.wait_recv()
        for copy in owns:
            copy.wait()
        net.finish()

    return remote_call(kernel, name, cid, [ANY], [((2, 4, 256, 128), BF, ANY)], [], 6, 2)(blocks)[0]


def middle_forward(parts, inputs, gain, shift, shard):
    width = shard.shape[1]

    def kernel(parts, inputs, gain, shift, shard, hidden, second, weights, held, base, low, ss, rs, ls):
        me = here()
        c, y, z, x = me
        greet(y_peers(*me) + z_peers(*me) + core_peer(*me) + x_peers(*me))
        net, local = Net(ss, rs), Local(ls)
        sums = SumX(net, local, parts, held, me)
        sums.start()
        residual = local.copy(inputs.at[x], base)
        gather = Gather(net, local, shard, weights, me)
        gather.start()
        gather.second()
        residual.wait()
        sums.arrive()

        def step(rows):
            value = base[rows, :].astype(F32) + sums.total(rows)
            hidden[rows, :] = value
            norm, _ = normed(value)
            low[rows, :] = (norm * gain[...] + shift[...]).astype(BF)

        row_chunks(step)
        sums.gather(low, second)
        gather.third()
        gather.finish()
        sums.finish()
        net.finish()

    return remote_call(
        kernel,
        "middle_forward",
        3,
        [ANY, ANY, IN_VMEM, IN_VMEM, ANY],
        [
            ((128, D), F32, IN_VMEM),
            ((4, 128, D), BF, ANY),
            ((2, 4, 4, 64, width), BF, ANY),
        ],
        [pltpu.VMEM((4, 128, D), BF), pltpu.VMEM((128, D), BF), pltpu.VMEM((128, D), BF)],
        GATHER_COPIES + 6,
        4,
    )(parts, inputs, gain, shift, shard)


def middle_backward(parts, cotangent, hidden, gain, grads):
    widths = [g.shape[-1] for g in grads]
    count = len(grads)

    def kernel(parts, cotangent, hidden, gain, *rest):
        grad_refs = rest[:count]
        dhidden, hidden_low, vectors = rest[count : count + 3]
        outs = rest[count + 3 : 2 * count + 3]
        held, base, low = rest[2 * count + 3 : 2 * count + 6]
        scratch = rest[2 * count + 6 : -3]
        ss, rs, ls = rest[-3:]
        me = here()
        c, y, z, x = me
        greet(y_peers(*me) + z_peers(*me) + core_peer(*me) + x_peers(*me))
        net, local = Net(ss, rs), Local(ls)
        sums = SumX(net, local, parts, held, me)
        sums.start()
        upstream = local.copy(cotangent.at[x], base)
        scatters = [
            Scatter(net, local, grad_refs[k], outs[k], scratch[8 * k : 8 * k + 8], me)
            for k in range(count)
        ]
        for scatter in scatters:
            scatter.start()
        for scatter in scatters:
            scatter.first()
        upstream.wait()
        sums.arrive()
        vectors[...] = jnp.zeros_like(vectors)

        def step(rows):
            dsecond = sums.total(rows)
            norm, inverse = normed(hidden[rows, :])
            value = base[rows, :].astype(F32) + norm_pullback(dsecond, norm, inverse, gain[...])
            dhidden[rows, :] = value
            low[rows, :] = value.astype(BF)
            vectors[0:1, :] += jnp.sum(dsecond * norm, axis=0, keepdims=True)
            vectors[1:2, :] += jnp.sum(dsecond, axis=0, keepdims=True)

        row_chunks(step)
        sums.gather(low, hidden_low)
        for scatter in scatters:
            scatter.second()
        for scatter in scatters:
            scatter.third()
        sums.finish()
        net.finish()

    scratch = [pltpu.VMEM((4, 128, D), BF), pltpu.VMEM((128, D), BF), pltpu.VMEM((128, D), BF)]
    for width in widths:
        scratch += scatter_scratch(width)
    return remote_call(
        kernel,
        "middle_backward",
        4,
        [ANY, ANY, IN_VMEM, IN_VMEM] + [ANY] * count,
        [((128, D), F32, IN_VMEM), ((4, 128, D), BF, ANY), ((2, D), F32, IN_VMEM)]
        + [((64, width), F32, IN_VMEM) for width in widths],
        scratch,
        6 + SCATTER_COPIES * count,
        3 + count,
    )(parts, cotangent, hidden, gain, *grads)


def collect_heads(dkv, dq, parts, hidden):
    def kernel(dkv, dq, parts, hidden, dproject, outputs, got, mine, summed, held, low, ss, rs, ls):
        me = here()
        c, y, z, x = me
        greet(y_peers(*me) + z_peers(*me) + x_peers(*me))
        net, local = Net(ss, rs), Local(ls)
        kv = pl.ds(0, 2)
        one, two = {}, []
        owns = [
            local.copy(dkv.at[0, y], mine.at[0]),
            local.copy(dkv.at[1, :, z], mine.at[1]),
        ]
        for i in (1, 3, 2, 0):
            for d in STEPS:
                one[0, i, d] = net.send(
                    dkv.at[0, up(y, d), up(z, i)], got.at[0, d - 1, up(z, i)], at(c, y + d, z, x)
                )
                one[1, i, d] = net.send(
                    dkv.at[1, up(y, i), up(z, d)], got.at[1, d - 1, up(y, i)], at(c, y, z + d, x)
                )
        sums = SumX(net, local, parts, held, me)
        sums.start()
        lates = [
            local.copy(dq.at[0, z], dproject.at[0, z, 2]),
            local.copy(dq.at[1, y], dproject.at[1, y, 2]),
        ]
        for d in STEPS:
            two.append(net.send(dq.at[0, up(z, d)], dproject.at[0, z, 2], at(c, y, z + d, x)))
            two.append(net.send(dq.at[1, up(y, d)], dproject.at[1, y, 2], at(c, y + d, z, x)))
        for copy in owns:
            copy.wait()
        for i in (1, 3, 2, 0):
            for m, spot in ((0, z), (1, y)):
                for d in STEPS:
                    one[m, i, d].wait_recv()
                block = up(spot, i)

                def add(r, carry, m=m, block=block):
                    k, rows = r // 8, pl.ds(pl.multiple_of(lax.rem(r, 8) * 32, 32), 32)
                    total = mine[m, block, k, rows, :].astype(F32)
                    for n in range(3):
                        total += got[m, n, block, k, rows, :].astype(F32)
                    summed[m, block, k, rows, :] = total.astype(BF)
                    return carry

                lax.fori_loop(0, 16, add, 0)
            if i:
                two.append(
                    net.send(
                        summed.at[0, up(z, i)], dproject.at[0, z, kv], at(c, y, z + i, x)
                    )
                )
                two.append(
                    net.send(
                        summed.at[1, up(y, i)], dproject.at[1, y, kv], at(c, y + i, z, x)
                    )
                )
            else:
                lates.append(local.copy(summed.at[0, z], dproject.at[0, z, kv]))
                lates.append(local.copy(summed.at[1, y], dproject.at[1, y, kv]))
        sums.arrive()

        def step(rows):
            low[rows, :] = (hidden[rows, :] + sums.total(rows)).astype(BF)

        row_chunks(step)
        sums.gather(low, outputs)
        for copy in two:
            copy.wait_recv()
        for copy in lates:
            copy.wait()
        sums.finish()
        net.finish()

    return remote_call(
        kernel,
        "collect_heads",
        6,
        [ANY, ANY, ANY, IN_VMEM],
        [((2, 4, 3, 256, 128), BF, ANY), ((4, 128, D), BF, ANY)],
        [
            pltpu.VMEM((2, 3, 4, 2, 256, 128), BF),
            pltpu.VMEM((2, 4, 2, 256, 128), BF),
            pltpu.VMEM((2, 4, 2, 256, 128), BF),
            pltpu.VMEM((4, 128, D), BF),
            pltpu.VMEM((128, D), BF),
        ],
        24 + 6 + 6 + 6,
        8,
    )(dkv, dq, parts, hidden)


def last_backward(parts, inputs, dhidden, gain, vectors, grads):
    widths = [g.shape[-1] for g in grads]
    count = len(grads)

    def kernel(parts, inputs, dhidden, gain, vectors, *rest):
        grad_refs = rest[:count]
        input_grad, sums_out = rest[count : count + 2]
        outs = rest[count + 2 : 2 * count + 2]
        held, base, low, small, got = rest[2 * count + 2 : 2 * count + 7]
        scratch = rest[2 * count + 7 : -3]
        ss, rs, ls = rest[-3:]
        me = here()
        c, y, z, x = me
        greet(y_peers(*me) + z_peers(*me) + core_peer(*me) + x_peers(*me))
        net, local = Net(ss, rs), Local(ls)
        sums = SumX(net, local, parts, held, me)
        sums.start()
        residual = local.copy(inputs.at[x], base)
        scatters = [
            Scatter(net, local, grad_refs[k], outs[k], scratch[8 * k : 8 * k + 8], me)
            for k in range(count)
        ]
        for scatter in scatters:
            scatter.start()
        for scatter in scatters:
            scatter.first()
        residual.wait()
        sums.arrive()
        small[0, ...] = vectors[...]

        def step(rows):
            dfirst = sums.total(rows)
            norm, inverse = normed(base[rows, :].astype(F32))
            value = dhidden[rows, :] + norm_pullback(dfirst, norm, inverse, gain[...])
            low[rows, :] = value.astype(BF)
            small[0, 0:1, :] += jnp.sum(dfirst * norm, axis=0, keepdims=True)
            small[0, 1:2, :] += jnp.sum(dfirst, axis=0, keepdims=True)

        row_chunks(step)
        copies = [
            net.send(small.at[0], got.at[0, d - 1], at(c, y, z, x + d)) for d in STEPS
        ]
        sums.gather(low, input_grad)
        for scatter in scatters:
            scatter.second()
        for copy in copies:
            copy.wait_recv()
        small[1, ...] = small[0, ...]
        for n in range(3):
            small[1, 0:4, :] += got[0, n, 0:4, :]
        copies = [
            net.send(small.at[1], got.at[1, d - 1], at(c, y + d, z, x)) for d in STEPS
        ]
        for copy in copies:
            copy.wait_recv()
        small[2, ...] = small[1, ...] + got[1, 0] + got[1, 1] + got[1, 2]
        copies = [
            net.send(small.at[2], got.at[2, d - 1], at(c, y, z + d, x)) for d in STEPS
        ]
        for copy in copies:
            copy.wait_recv()
        small[3, ...] = small[2, ...] + got[2, 0] + got[2, 1] + got[2, 2]
        copy = net.send(small.at[3], got.at[3, 0], at(1 - c, y, z, x))
        for scatter in scatters:
            scatter.third()
        copy.wait_recv()
        sums_out[...] = small[3, ...] + got[3, 0]
        sums.finish()
        net.finish()

    scratch = [
        pltpu.VMEM((4, 128, D), BF),
        pltpu.VMEM((128, D), BF),
        pltpu.VMEM((128, D), BF),
        pltpu.VMEM((4, 8, D), F32),
        pltpu.VMEM((4, 3, 8, D), F32),
    ]
    for width in widths:
        scratch += scatter_scratch(width)
    return remote_call(
        kernel,
        "last_backward",
        7,
        [ANY, ANY, IN_VMEM, IN_VMEM, IN_VMEM] + [ANY] * count,
        [((4, 128, D), BF, ANY), ((8, D), F32, IN_VMEM)]
        + [((64, width), F32, IN_VMEM) for width in widths],
        scratch,
        6 + 10 + SCATTER_COPIES * count,
        3 + count,
    )(parts, inputs, dhidden, gain, vectors, *grads)


def turn(values, cosine, minus_sine, plus_sine):
    return (
        values * cosine
        + pltpu.roll(values, 120, 1) * minus_sine
        + pltpu.roll(values, 8, 1) * plus_sine
    )


def project_heads(tokens, gain, shift, weights, bias, tables):
    def kernel(x_ref, gain_ref, shift_ref, w_ref, b_ref, t_ref, out_ref, low_ref):
        j = pl.program_id(0)

        @pl.when(j == 0)
        def _():
            def step(i, carry):
                rows = pl.ds(pl.multiple_of(i * 16, 16), 16)
                norm, _ = normed(x_ref[rows, :].astype(F32))
                low_ref[rows, :] = (norm * gain_ref[...] + shift_ref[...]).astype(BF)
                return carry

            lax.fori_loop(0, 32, step, 0)

        for m in range(2):
            acc = jnp.dot(low_ref[m * 256 : m * 256 + 256, :], w_ref[...], preferred_element_type=F32)
            acc = acc + b_ref[0]
            for h in range(2):
                part = acc[:, h * 128 : h * 128 + 128]

                @pl.when(j < 4)
                def _():
                    out_ref[m, h, 0] = turn(part, t_ref[0], t_ref[1], t_ref[2]).astype(BF)

                @pl.when(j >= 4)
                def _():
                    out_ref[m, h, 0] = part.astype(BF)

    return pl.pallas_call(
        kernel,
        name="project_heads",
        grid=(6,),
        in_specs=[
            pl.BlockSpec((512, D), lambda j: (0, 0)),
            pl.BlockSpec((1, D), lambda j: (0, 0)),
            pl.BlockSpec((1, D), lambda j: (0, 0)),
            pl.BlockSpec((D, 256), lambda j: (0, j)),
            pl.BlockSpec((1, 1, 256), lambda j: (j, 0, 0)),
            pl.BlockSpec((3, 256, 128), lambda j: (0, 0, 0)),
        ],
        out_specs=[
            pl.BlockSpec((2, 2, 1, 256, 128), lambda j: (0, j % 2, (j // 2 + 2) % 3, 0, 0)),
            pl.BlockSpec((512, D), lambda j: (0, 0)),
        ],
        out_shape=[
            jax.ShapeDtypeStruct((2, 4, 3, 256, 128), BF),
            jax.ShapeDtypeStruct((512, D), BF),
        ],
        compiler_params=pltpu.CompilerParams(vmem_limit_bytes=VMEM_LIMIT),
    )(tokens, gain, shift, weights, bias, tables)


def two_heads(block):
    lane = lax.broadcasted_iota(jnp.int32, (128, 128), 1)
    value = block.astype(F32)
    return jnp.concatenate(
        [jnp.where(lane < HEAD_DIM, value, 0.0), jnp.where(lane >= HEAD_DIM, value, 0.0)], axis=0
    )


def one_block(stacked):
    feature = lax.broadcasted_iota(jnp.int32, (128, 128), 0)
    return jnp.where(feature < HEAD_DIM, stacked[:, :128], stacked[:, 128:]).T


def nt(left, right):
    return lax.dot_general(left, right, (((1,), (1,)), ((), ())), preferred_element_type=F32)


def masked_places(tile, place):
    key = tile * TILE + lax.broadcasted_iota(jnp.int32, (TILE, 256), 0)
    query = place * 128 + lax.rem(lax.broadcasted_iota(jnp.int32, (TILE, 256), 1), 128)
    return key <= query


def attend(slots, places, rows_of, spread):
    def kernel(slots, places, rows_of, k_ref, v_ref, q_ref, o_ref, full_ref, log_ref, keys, values_t):
        m, i = pl.program_id(0), pl.program_id(1)

        @pl.when(i == 0)
        def _():
            def lay(b, carry):
                slot = slots[b]
                rows = pl.ds(pl.multiple_of(lax.rem(slot, 2) * 128, 128), 128)
                to = pl.ds(pl.multiple_of(b * 128, 128), 128)
                keys[to, :] = k_ref[0, slot // 2, 0, rows, :]
                values_t[:, to] = v_ref[0, slot // 2, 0, rows, :].astype(F32).T.astype(BF)
                return carry

            lax.fori_loop(0, 32, lay, 0)

        for half in range(2):
            place = places[(m * 4 + i) * 2 + half]
            query = (two_heads(q_ref[0, 0, 0, half * 128 : half * 128 + 128, :]) * 0.125).astype(BF)

            def step(t, carry, masked):
                top, total, acc = carry
                span = pl.ds(pl.multiple_of(t * TILE, TILE), TILE)
                scores = nt(keys[span, :], query) * LOG2E
                if masked:
                    scores = jnp.where(masked_places(t, place), scores, LOW)
                new_top = jnp.maximum(top, jnp.max(scores, axis=0, keepdims=True))
                weights = jnp.exp2(scores - new_top)
                shrink = jnp.exp2(top - new_top)
                total = total * shrink + jnp.sum(weights, axis=0, keepdims=True)
                acc = acc * shrink + jnp.dot(
                    values_t[:, span], weights.astype(BF), preferred_element_type=F32
                )
                return new_top, total, acc

            carry = (
                jnp.full((1, 256), LOW, F32),
                jnp.zeros((1, 256), F32),
                jnp.zeros((128, 256), F32),
            )
            last = place // (TILE // 128)
            carry = lax.fori_loop(0, last, lambda t, s: step(t, s, False), carry)
            top, total, acc = step(last, carry, True)
            result = one_block(acc / total)
            full_ref[0, 0, half * 128 : half * 128 + 128, :] = result
            o_ref[0, 0, half * 128 : half * 128 + 128, :] = result.astype(BF)
            log_ref[0, 0, half : half + 1, :] = top + jnp.log2(total)

    grid_spec = pltpu.PrefetchScalarGridSpec(
        num_scalar_prefetch=3,
        grid=(2, 4),
        in_specs=[
            pl.BlockSpec((1, 16, 1, 256, 128), lambda m, i, s, p, r: (m, 0, 0, 0, 0)),
            pl.BlockSpec((1, 16, 1, 256, 128), lambda m, i, s, p, r: (m, 0, 1, 0, 0)),
            pl.BlockSpec((1, 1, 1, 256, 128), lambda m, i, s, p, r: (m, r[m * 4 + i], 2, 0, 0)),
        ],
        out_specs=[
            pl.BlockSpec((1, 1, 256, 128), lambda m, i, s, p, r: (m, i, 0, 0)),
            pl.BlockSpec((1, 1, 256, 128), lambda m, i, s, p, r: (m, i, 0, 0)),
            pl.BlockSpec((1, 1, 2, 256), lambda m, i, s, p, r: (m, i, 0, 0)),
        ],
        scratch_shapes=[pltpu.VMEM((4096, 128), BF), pltpu.VMEM((128, 4096), BF)],
    )
    return pl.pallas_call(
        kernel,
        name="attend",
        grid_spec=grid_spec,
        out_shape=[
            jax.ShapeDtypeStruct((2, 4, 256, 128), BF),
            jax.ShapeDtypeStruct((2, 4, 256, 128), F32),
            jax.ShapeDtypeStruct((2, 4, 2, 256), F32),
        ],
        compiler_params=pltpu.CompilerParams(vmem_limit_bytes=VMEM_LIMIT),
    )(slots, places, rows_of, spread, spread, spread)


def attend_back(slots, places, rows_of, spread, full, logs, upstream, tables):
    def kernel(
        slots, places, rows_of, k_ref, v_ref, q_ref, full_ref, log_ref, up_ref, t_ref, dq_ref, dkv_ref,
        keys, keys_t, values, dkeys, dvalues,
    ):
        m, i = pl.program_id(0), pl.program_id(1)

        @pl.when(i == 0)
        def _():
            def lay(b, carry):
                slot = slots[b]
                rows = pl.ds(pl.multiple_of(lax.rem(slot, 2) * 128, 128), 128)
                to = pl.ds(pl.multiple_of(b * 128, 128), 128)
                keys[to, :] = k_ref[0, slot // 2, 0, rows, :]
                keys_t[:, to] = k_ref[0, slot // 2, 0, rows, :].astype(F32).T.astype(BF)
                values[to, :] = v_ref[0, slot // 2, 0, rows, :]
                dkeys[to, :] = jnp.zeros((128, 128), F32)
                dvalues[to, :] = jnp.zeros((128, 128), F32)
                return carry

            lax.fori_loop(0, 32, lay, 0)

        for half in range(2):
            rows = slice(half * 128, half * 128 + 128)
            place = places[(m * 4 + i) * 2 + half]
            query = (two_heads(q_ref[0, 0, 0, rows, :]) * 0.125).astype(BF)
            ups = up_ref[0, 0, rows, :]
            grad = two_heads(ups).astype(BF)
            product = (ups.astype(F32) * full_ref[0, 0, rows, :]).T
            delta = jnp.concatenate(
                [
                    jnp.sum(product[:HEAD_DIM], axis=0, keepdims=True),
                    jnp.sum(product[HEAD_DIM:], axis=0, keepdims=True),
                ],
                axis=1,
            )
            logs = log_ref[0, 0, half : half + 1, :]

            def step(t, dquery, masked):
                span = pl.ds(pl.multiple_of(t * TILE, TILE), TILE)
                scores = nt(keys[span, :], query) * LOG2E
                probs = jnp.exp2(scores - logs)
                if masked:
                    probs = jnp.where(masked_places(t, place), probs, 0.0)
                dprobs = nt(values[span, :], grad)
                dscores = (probs * (dprobs - delta)).astype(BF)
                dvalues[span, :] += jnp.dot(probs.astype(BF), grad, preferred_element_type=F32)
                dkeys[span, :] += jnp.dot(dscores, query, preferred_element_type=F32)
                return dquery + jnp.dot(keys_t[:, span], dscores, preferred_element_type=F32)

            last = place // (TILE // 128)
            dquery = lax.fori_loop(
                0, last, lambda t, s: step(t, s, False), jnp.zeros((128, 256), F32)
            )
            dquery = one_block(step(last, dquery, True)) * 0.125
            own = pl.ds(pl.multiple_of(place * 128, 128), 128)
            dq_ref[0, 0, rows, :] = turn(
                dquery, t_ref[0, own, :], -t_ref[1, own, :], -t_ref[2, own, :]
            ).astype(BF)

        @pl.when(i == 3)
        def _():
            def flush(b, carry):
                slot = slots[b]
                rows = pl.ds(pl.multiple_of(lax.rem(slot, 2) * 128, 128), 128)
                to = pl.ds(pl.multiple_of(b * 128, 128), 128)
                dkv_ref[0, slot // 2, 0, rows, :] = turn(
                    dkeys[to, :], t_ref[0, to, :], -t_ref[1, to, :], -t_ref[2, to, :]
                ).astype(BF)
                dkv_ref[0, slot // 2, 1, rows, :] = dvalues[to, :].astype(BF)
                return carry

            lax.fori_loop(0, 32, flush, 0)

    grid_spec = pltpu.PrefetchScalarGridSpec(
        num_scalar_prefetch=3,
        grid=(2, 4),
        in_specs=[
            pl.BlockSpec((1, 16, 1, 256, 128), lambda m, i, s, p, r: (m, 0, 0, 0, 0)),
            pl.BlockSpec((1, 16, 1, 256, 128), lambda m, i, s, p, r: (m, 0, 1, 0, 0)),
            pl.BlockSpec((1, 1, 1, 256, 128), lambda m, i, s, p, r: (m, r[m * 4 + i], 2, 0, 0)),
            pl.BlockSpec((1, 1, 256, 128), lambda m, i, s, p, r: (m, i, 0, 0)),
            pl.BlockSpec((1, 1, 2, 256), lambda m, i, s, p, r: (m, i, 0, 0)),
            pl.BlockSpec((1, 1, 256, 128), lambda m, i, s, p, r: (m, i, 0, 0)),
            pl.BlockSpec((3, 4096, 128), lambda m, i, s, p, r: (0, 0, 0)),
        ],
        out_specs=[
            pl.BlockSpec((1, 1, 256, 128), lambda m, i, s, p, r: (m, i, 0, 0)),
            pl.BlockSpec((1, 16, 2, 256, 128), lambda m, i, s, p, r: (m, 0, 0, 0, 0)),
        ],
        scratch_shapes=[
            pltpu.VMEM((4096, 128), BF),
            pltpu.VMEM((128, 4096), BF),
            pltpu.VMEM((4096, 128), BF),
            pltpu.VMEM((4096, 128), F32),
            pltpu.VMEM((4096, 128), F32),
        ],
    )
    return pl.pallas_call(
        kernel,
        name="attend_back",
        grid_spec=grid_spec,
        out_shape=[
            jax.ShapeDtypeStruct((2, 4, 256, 128), BF),
            jax.ShapeDtypeStruct((2, 16, 2, 256, 128), BF),
        ],
        compiler_params=pltpu.CompilerParams(vmem_limit_bytes=VMEM_LIMIT),
    )(slots, places, rows_of, spread, spread, spread, full, logs, upstream, tables)


def rotary_tables(places):
    frequency = 10000.0 ** (-jnp.arange(0, ROT, 2, dtype=F32) / ROT)
    angles = places.astype(F32)[:, None] * frequency[None, :]
    cosine, sine = jnp.cos(angles), jnp.sin(angles)
    rows, half = places.shape[0], ROT // 2
    rest = HEAD_DIM - ROT
    zeros, ones = jnp.zeros((rows, half), F32), jnp.ones((rows, rest), F32)
    tables = (
        jnp.concatenate([cosine, cosine, ones], axis=1),
        jnp.concatenate([-sine, zeros, 0.0 * ones], axis=1),
        jnp.concatenate([zeros, sine, 0.0 * ones], axis=1),
    )
    return jnp.stack([jnp.concatenate([t, t], axis=1) for t in tables])


def body(
    inputs,
    cotangent,
    group_place,
    attend_gain,
    attend_shift,
    project_weight,
    project_bias,
    output_weight,
    mixer_gain,
    mixer_shift,
    gate_weight,
    up_weight,
    down_weight,
):
    ctx = lax.axis_index("ctx")
    y, z = ctx // 4, lax.rem(ctx, 4)
    shard_index = lax.axis_index("dp") * 16 + ctx

    blocks = jnp.arange(32, dtype=jnp.int32)
    hits = group_place[None, :] == blocks[:, None]
    slots = jnp.sum(jnp.where(hits, blocks[None, :], 0), axis=1)
    four = jnp.arange(4, dtype=jnp.int32)
    rows_of = jnp.concatenate([y * 4 + four, four * 4 + z])
    held_slots = (rows_of[:, None] * 2 + jnp.arange(2, dtype=jnp.int32)[None, :]).reshape(16)
    chosen = held_slots[:, None] == blocks[None, :]
    places = jnp.sum(jnp.where(chosen, group_place[None, :], 0), axis=1)
    own_slots = ctx * 2 + jnp.arange(2, dtype=jnp.int32)
    own_blocks = jnp.sum(
        jnp.where(own_slots[:, None] == blocks[None, :], group_place[None, :], 0), axis=1
    )
    own_places = (own_blocks[:, None] * 128 + jnp.arange(128, dtype=jnp.int32)[None, :]).reshape(256)
    own_tables = rotary_tables(own_places)
    all_tables = rotary_tables(jnp.arange(4096, dtype=jnp.int32))

    vectors = jnp.concatenate(
        [
            jnp.stack([attend_gain, attend_shift, mixer_gain, mixer_shift], axis=1),
            jnp.pad(project_bias.reshape(1, 48), ((0, 63), (0, 0))),
            jnp.zeros((64, 76), BF),
        ],
        axis=1,
    )
    front_shard = jnp.concatenate(
        [project_weight.reshape(64, 1536), output_weight.T, vectors], axis=1
    )
    back_shard = jnp.concatenate([gate_weight, up_weight, down_weight.T], axis=1)
    front = gather_front(front_shard).reshape(D, 2176)
    gains = front[:, 2048:2052].astype(F32).T
    first_gain, first_shift = gains[0:1], gains[1:2]
    second_gain, second_shift = gains[2:3], gains[3:4]
    bias = (
        front.reshape(32, 64, 2176)[:, 0, 2052:2100]
        .reshape(32, 3, 8, 2)
        .transpose(1, 2, 0, 3)
        .astype(F32)
        .reshape(6, 1, 256)
    )
    output_t = front[:, 1536:2048]
    project_flat = front[:, :1536]

    tokens = inputs.reshape(512, D)
    quarters = inputs.reshape(4, 128, D)
    qkv, first_low = project_heads(tokens, first_gain, first_shift, front, bias, own_tables)
    spread = spread_heads(qkv).reshape(2, 16, 3, 256, 128)
    attended_heads, attended_full, logs = attend(slots, places, rows_of, spread)
    attended_low = (
        swap_rows(attended_heads, 2, "attended_back").transpose(0, 2, 1, 3).reshape(512, 512)
    )
    branch = nt(attended_low, output_t).astype(BF).reshape(4, 128, D)
    hidden, second_low, back = middle_forward(branch, quarters, second_gain, second_shift, back_shard)

    second_low = second_low.reshape(512, D)
    back = back.reshape(D, 3 * UNITS)
    gate_w, up_w, down_t = back[:, :UNITS], back[:, UNITS : 2 * UNITS], back[:, 2 * UNITS :]
    dy = cotangent.reshape(512, D)
    gate_value = jnp.dot(second_low, gate_w, preferred_element_type=F32)
    up_value = jnp.dot(second_low, up_w, preferred_element_type=F32)
    dmixed = jnp.dot(dy, down_t, preferred_element_type=F32)
    sigmoid = jax.nn.sigmoid(gate_value)
    mixed = (gate_value * sigmoid * up_value).astype(BF)
    dgate = (dmixed * up_value * sigmoid * (1.0 + gate_value * (1.0 - sigmoid))).astype(BF)
    dup = (dmixed * gate_value * sigmoid).astype(BF)
    mixer_part = nt(mixed, down_t).astype(BF).reshape(4, 128, D)
    second_part = (nt(dgate, gate_w) + nt(dup, up_w)).astype(BF).reshape(4, 128, D)

    def tn(left, right):
        return lax.dot_general(left, right, (((0,), (0,)), ((), ())), preferred_element_type=F32)

    def shards(grad):
        return grad.astype(BF).reshape(2, 4, 4, 64, grad.shape[1])

    dhidden, hidden_low, mixer_vectors, gate_grad, up_grad, down_grad = middle_backward(
        second_part,
        cotangent.reshape(4, 128, D),
        hidden,
        second_gain,
        [shards(tn(second_low, dgate)), shards(tn(second_low, dup)), shards(tn(dy, mixed))],
    )

    hidden_low = hidden_low.reshape(512, D)
    dattended = jnp.dot(hidden_low, output_t, preferred_element_type=F32).astype(BF)
    upstream = swap_rows(
        dattended.reshape(2, 256, 4, 128).transpose(0, 2, 1, 3), 5, "dattended_out"
    )
    output_grad = shards(tn(hidden_low, attended_low))
    dq, dkv = attend_back(
        slots, places, rows_of, spread, attended_full, logs, upstream, all_tables
    )
    dproject, outputs = collect_heads(dkv.reshape(2, 4, 4, 2, 256, 128), dq, mixer_part, hidden)
    ordered = jnp.concatenate([dproject[:, :, 2:], dproject[:, :, :2]], axis=2)
    dproject = ordered.transpose(0, 3, 2, 1, 4).reshape(512, 1536)
    first_part = nt(dproject, project_flat).astype(BF).reshape(4, 128, D)
    project_grad = shards(tn(first_low, dproject))
    bias_part = jnp.sum(dproject.astype(F32), axis=0)
    small = jnp.concatenate(
        [
            jnp.zeros((2, D), F32),
            mixer_vectors,
            jnp.pad(bias_part, (0, D - 1536))[None],
            jnp.zeros((3, D), F32),
        ]
    )
    input_grad, small, project_grad, output_grad = last_backward(
        first_part, quarters, dhidden, first_gain, small, [project_grad, output_grad]
    )
    own = lax.dynamic_slice(small, (0, shard_index * 64), (4, 64))
    bias_grad = lax.dynamic_slice(
        small[4, :1536].reshape(3, 8, 64), (0, 0, shard_index * 2), (3, 8, 2)
    )
    shape = inputs.shape
    return (
        outputs.reshape(shape),
        input_grad.reshape(shape),
        own[0],
        own[1],
        project_grad.reshape(64, 3, 512),
        bias_grad,
        output_grad.T,
        own[2],
        own[3],
        gate_grad,
        up_grad,
        down_grad.T,
    )


def solution(mesh):
    weight = ("dp", "ctx")
    rows = P(None, "dp", "ctx", None)
    vector = P(weight)
    matrix = P(weight, "tensor")
    turned = P("tensor", weight)
    project = P(weight, None, "tensor")
    bias = P(None, "tensor", weight)
    params = (vector, vector, project, bias, turned, vector, vector, matrix, matrix, turned)
    return jax.shard_map(
        body,
        mesh=mesh,
        in_specs=(rows, rows, P()) + params,
        out_specs=(rows, rows) + params,
        check_vma=False,
    )
```

```python
import functools

import jax
import jax.numpy as jnp
import numpy as np
from jax import lax
from jax.experimental import pallas as pl
from jax.experimental.pallas import tpu as pltpu
from jax.sharding import PartitionSpec as P

MESH = pl.DeviceIdType.MESH
D = 2048
UNITS = 1408
HEAD_DIM = 64
ROT = 16
EPSILON = 1e-05
LOG2E = 1.4426950408889634
LOW = -1e30
TILE = 512
VMEM_LIMIT = 58 * 2**20
STEPS = (1, 3, 2)
BF = jnp.bfloat16
F32 = jnp.float32


def here():
    ctx = lax.axis_index("ctx")
    return (lax.axis_index("dp"), ctx // 4, lax.rem(ctx, 4), lax.axis_index("tensor"))


def at(c, y, z, x):
    return (c, lax.rem(y, 4) * 4 + lax.rem(z, 4), lax.rem(x, 4))


def up(i, d):
    return lax.rem(i + d, 4)


def down(i, d):
    return lax.rem(i + 4 - d, 4)


class Net:
    def __init__(self, send_sems, recv_sems):
        self.send_sems, self.recv_sems = send_sems, recv_sems
        self.sent = []

    def send(self, src, dst, device):
        n = len(self.sent)
        copy = pltpu.make_async_remote_copy(
            src_ref=src,
            dst_ref=dst,
            send_sem=self.send_sems.at[n],
            recv_sem=self.recv_sems.at[n],
            device_id=device,
            device_id_type=MESH,
        )
        copy.start()
        self.sent.append(copy)
        return copy

    def finish(self):
        for copy in self.sent:
            copy.wait_send()


class Local:
    def __init__(self, sems):
        self.sems, self.n = sems, 0

    def copy(self, src, dst):
        copy = pltpu.make_async_copy(src, dst, self.sems.at[self.n])
        copy.start()
        self.n += 1
        return copy


def greet(peers):
    barrier = pltpu.get_barrier_semaphore()
    for peer in peers:
        pl.semaphore_signal(barrier, inc=1, device_id=peer, device_id_type=MESH)
    pl.semaphore_wait(barrier, len(peers))


def y_peers(c, y, z, x):
    return [at(c, y + d, z, x) for d in (1, 2, 3)]


def z_peers(c, y, z, x):
    return [at(c, y, z + d, x) for d in (1, 2, 3)]


def x_peers(c, y, z, x):
    return [at(c, y, z, x + d) for d in (1, 2, 3)]


def core_peer(c, y, z, x):
    return [at(1 - c, y, z, x)]


class RingSum:
    def __init__(self, net, device, mine, spare, add):
        self.net, self.device, self.mine, self.spare, self.add = net, device, mine, spare, add

    def start(self):
        send, mine, spare = self.net.send, self.mine, self.spare
        ahead, back = self.device(1), self.device(3)
        self.far_ahead = send(mine(2, 0), spare.at[0], ahead)
        self.far_back = send(mine(2, 1), spare.at[1], back)
        self.near = [send(mine(1, 1), spare.at[3], ahead), send(mine(3, 0), spare.at[2], back)]

    def middle(self):
        send, spare = self.net.send, self.spare
        self.far_ahead.wait_recv()
        self.add(spare.at[0], self.mine(1, 0))
        self.near.append(send(spare.at[0], spare.at[4], self.device(1)))
        self.far_back.wait_recv()
        self.add(spare.at[1], self.mine(3, 1))
        self.near.append(send(spare.at[1], spare.at[5], self.device(3)))

    def arrive(self):
        for copy in self.near:
            copy.wait_recv()

    def terms(self, half):
        return [self.spare.at[4 if half == 0 else 3], self.spare.at[2 if half == 0 else 5]]


RING_SUM = 6


class RingGather:
    def __init__(self, net, device, out):
        self.net, self.device, self.out = net, device, out

    def start(self, block):
        self.ahead = self.net.send(block, self.out(0), self.device(1))
        self.back = self.net.send(block, self.out(0), self.device(3))

    def from_back(self):
        self.ahead.wait_recv()
        piece = self.out(3, 0)
        self.far_ahead = self.net.send(piece, piece, self.device(1))

    def from_ahead(self):
        self.back.wait_recv()
        piece = self.out(1, 1)
        self.far_back = self.net.send(piece, piece, self.device(3))

    def arrive(self):
        self.far_ahead.wait_recv()
        self.far_back.wait_recv()


RING_GATHER = 4


class Gather:
    def __init__(self, net, local, src, out, me):
        self.net, self.local, self.src, self.out, self.me = net, local, src, out, me
        self.core = []
        c, y, z, x = me
        along_y = lambda d: at(c, y + d, z, x)
        along_z = lambda d: at(c, y, z + d, x)

        def rows(first, half):
            return pl.ds(first, 32) if half is None else pl.ds(first + 16 * half, 16)

        self.one = (
            RingGather(net, along_y, lambda d, half=None: out.at[c, up(y, d), z, rows(0, half)]),
            RingGather(net, along_z, lambda d, half=None: out.at[c, y, up(z, d), rows(32, half)]),
        )
        self.two = {}
        for k in range(4):
            self.two[0, k] = RingGather(
                net, along_z, lambda d, half=None, k=k: out.at[c, up(y, k), up(z, d), rows(0, half)]
            )
            self.two[1, k] = RingGather(
                net, along_y, lambda d, half=None, k=k: out.at[c, up(y, d), up(z, k), rows(32, half)]
            )

    def hand_over(self, piece):
        c, y, z, x = self.me
        self.core.append(self.net.send(piece, piece, at(1 - c, y, z, x)))

    def start(self):
        c, y, z, x = self.me
        src = self.src
        self.own = self.local.copy(src, self.out.at[c, y, z])
        halves = (src.at[pl.ds(0, 32)], src.at[pl.ds(32, 32)])
        for way in range(2):
            self.one[way].start(halves[way])
        for way in range(2):
            self.two[way, 0].start(halves[way])
        self.core.append(self.net.send(src, self.out.at[c, y, z], at(1 - c, y, z, x)))

    def near(self):
        for way in range(2):
            self.one[way].from_back()
            self.two[way, 3].start(self.one[way].out(3))
        for way in range(2):
            self.one[way].from_ahead()
            self.two[way, 1].start(self.one[way].out(1))
        for k in (3, 1):
            for way in range(2):
                self.hand_over(self.one[way].out(k))
        self.pass_on(0)
        for way in range(2):
            self.one[way].arrive()
            self.two[way, 2].start(self.one[way].out(2))
            self.hand_over(self.one[way].out(2))

    def pass_on(self, k):
        for way in range(2):
            self.two[way, k].from_back()
            self.two[way, k].from_ahead()
            self.hand_over(self.two[way, k].out(3))
            self.hand_over(self.two[way, k].out(1))

    def far(self):
        for k in (3, 1, 2):
            self.pass_on(k)
        for k in (0, 3, 1, 2):
            for way in range(2):
                self.two[way, k].arrive()
                self.hand_over(self.two[way, k].out(2))

    def finish(self):
        for copy in self.core:
            copy.wait_recv()
        self.own.wait()


GATHER_COPIES = 10 * RING_GATHER + 31


def scatter_scratch(width):
    return [
        pltpu.VMEM((4, 4, 64, width), BF),
        pltpu.VMEM((4, 4, 64, width), BF),
        pltpu.VMEM((6, 4, 16, width), BF),
        pltpu.VMEM((6, 4, 16, width), BF),
        pltpu.VMEM((4, 32, width), BF),
        pltpu.VMEM((4, 32, width), BF),
        pltpu.VMEM((6, 16, width), BF),
        pltpu.VMEM((6, 16, width), BF),
    ]


SCATTER_COPIES = 1 + 4 * RING_SUM


def add_blocks(total, term):
    if len(total.shape) == 2:
        total[...] = (total[...].astype(F32) + term[...].astype(F32)).astype(BF)
        return

    def one(i, carry):
        total[i] = (total[i].astype(F32) + term[i].astype(F32)).astype(BF)
        return carry

    lax.fori_loop(0, total.shape[0], one, 0)


class Scatter:
    def __init__(self, net, local, grads, out, scratch, me):
        self.net, self.local, self.grads, self.out, self.me = net, local, grads, out, me
        (held, self.other, one_a, one_b, self.sum_a, self.sum_b, two_a, two_b) = scratch
        self.held = held
        c, y, z, x = me
        along_y = lambda d: at(c, y + d, z, x)
        along_z = lambda d: at(c, y, z + d, x)
        self.one_a = RingSum(
            net, along_z, lambda d, half: held.at[:, up(z, d), pl.ds(16 * half, 16)], one_a, add_blocks
        )
        self.one_b = RingSum(
            net, along_y, lambda d, half: held.at[up(y, d), :, pl.ds(32 + 16 * half, 16)], one_b, add_blocks
        )
        self.two_a = RingSum(
            net, along_y, lambda d, half: self.sum_a.at[up(y, d), pl.ds(16 * half, 16)], two_a, add_blocks
        )
        self.two_b = RingSum(
            net, along_z, lambda d, half: self.sum_b.at[up(z, d), pl.ds(16 * half, 16)], two_b, add_blocks
        )

    def start(self):
        c, y, z, x = self.me
        self.own = self.local.copy(self.grads.at[c], self.held)
        self.zero = self.net.send(self.grads.at[1 - c], self.other, at(1 - c, y, z, x))

    def first(self):
        self.own.wait()
        self.zero.wait_recv()
        held, other = self.held, self.other

        def add(i, carry):
            for q in range(4):
                rows = pl.ds(q * 16, 16)
                held[i // 4, lax.rem(i, 4), rows, :] = (
                    held[i // 4, lax.rem(i, 4), rows, :].astype(F32)
                    + other[i // 4, lax.rem(i, 4), rows, :].astype(F32)
                ).astype(BF)
            return carry

        lax.fori_loop(0, 16, add, 0)
        self.one_a.start()
        self.one_b.start()

    def first_middle(self):
        self.one_a.middle()
        self.one_b.middle()

    def second(self):
        for one, two, total in ((self.one_a, self.two_a, self.sum_a), (self.one_b, self.two_b, self.sum_b)):
            one.arrive()
            for half in range(2):
                own, terms = one.mine(0, half), one.terms(half)

                def add(i, carry, half=half, own=own, terms=terms, total=total):
                    value = own[i].astype(F32)
                    for term in terms:
                        value += term[i].astype(F32)
                    total[i, pl.ds(16 * half, 16), :] = value.astype(BF)
                    return carry

                lax.fori_loop(0, 4, add, 0)
            two.start()

    def second_middle(self):
        self.two_a.middle()
        self.two_b.middle()

    def third(self):
        for first, two in ((0, self.two_a), (32, self.two_b)):
            two.arrive()
            for half in range(2):
                value = two.mine(0, half)[...].astype(F32)
                for term in two.terms(half):
                    value += term[...].astype(F32)
                self.out[pl.ds(first + 16 * half, 16), :] = value


class SumX:
    def __init__(self, net, local, parts, held, spare, me):
        c, y, z, x = me
        self.local, self.parts, self.held, self.x, self.net = local, parts, held, x, net
        self.along = lambda d: at(c, y, z, x + d)
        self.ring = RingSum(
            net, self.along, lambda d, half: held.at[up(x, d), pl.ds(64 * half, 64)], spare, self.add
        )

    def add(self, total, term):
        def one(i, carry):
            rows = pl.ds(pl.multiple_of(i * 16, 16), 16)
            total[rows, :] = (total[rows, :].astype(F32) + term[rows, :].astype(F32)).astype(BF)
            return carry

        lax.fori_loop(0, 4, one, 0)

    def load(self):
        self.loads = [self.local.copy(self.parts.at[up(self.x, d)], self.held.at[up(self.x, d)]) for d in (2, 1, 3, 0)]

    def start(self):
        for copy in self.loads:
            copy.wait()
        self.ring.start()

    def middle(self):
        self.ring.middle()

    def totals(self, step):
        self.ring.arrive()
        for half in range(2):
            terms = self.ring.terms(half)

            def loop(i, carry, half=half, terms=terms):
                rows = pl.ds(pl.multiple_of(i * 16, 16), 16)
                own = pl.ds(pl.multiple_of(64 * half + i * 16, 16), 16)
                value = self.held[self.x, own, :].astype(F32)
                for term in terms:
                    value += term[rows, :].astype(F32)
                step(own, value)
                return carry

            lax.fori_loop(0, 4, loop, 0)

    def gather(self, block, out):
        x = self.x

        def piece(d, half=None):
            whole = out.at[up(x, d)]
            return whole if half is None else out.at[up(x, d), pl.ds(64 * half, 64)]

        self.back = RingGather(self.net, self.along, piece)
        self.mine = self.local.copy(block, out.at[x])
        self.back.start(block)

    def gather_middle(self):
        self.back.from_back()
        self.back.from_ahead()

    def finish(self):
        self.mine.wait()
        self.back.arrive()


SUM_COPIES = RING_SUM + RING_GATHER
SUM_LOCALS = 5


def sum_scratch():
    return [pltpu.VMEM((4, 128, D), BF), pltpu.VMEM((6, 64, D), BF)]


def normed(values):
    centre = jnp.mean(values, axis=-1, keepdims=True)
    spread = values - centre
    inverse = lax.rsqrt(jnp.mean(spread * spread, axis=-1, keepdims=True) + EPSILON)
    return spread * inverse, inverse


def norm_pullback(upstream, norm, inverse, gain):
    scaled = upstream * gain
    first = jnp.mean(scaled, axis=-1, keepdims=True)
    second = jnp.mean(scaled * norm, axis=-1, keepdims=True)
    return inverse * (scaled - first - norm * second)


ANY = pl.BlockSpec(memory_space=pl.ANY)
IN_VMEM = pl.BlockSpec(memory_space=pltpu.VMEM)


def remote_call(body, name, cid, ins, outs, scratch, copies, locals_):
    return pl.pallas_call(
        body,
        name=name,
        in_specs=ins,
        out_specs=[spec for _, _, spec in outs],
        out_shape=[jax.ShapeDtypeStruct(shape, dtype) for shape, dtype, _ in outs],
        scratch_shapes=scratch
        + [
            pltpu.SemaphoreType.DMA((copies,)),
            pltpu.SemaphoreType.DMA((copies,)),
            pltpu.SemaphoreType.DMA((locals_,)),
        ],
        compiler_params=pltpu.CompilerParams(
            collective_id=cid, has_side_effects=True, vmem_limit_bytes=VMEM_LIMIT
        ),
    )


def gather_front(shard):
    def kernel(src, out, ss, rs, ls):
        me = here()
        greet(y_peers(*me) + z_peers(*me) + core_peer(*me))
        net, local = Net(ss, rs), Local(ls)
        gather = Gather(net, local, src, out, me)
        gather.start()
        gather.near()
        gather.far()
        gather.finish()
        net.finish()

    width = shard.shape[1]
    return remote_call(
        kernel, "gather_front", 0, [ANY], [((2, 4, 4, 64, width), BF, ANY)], [], GATHER_COPIES, 1
    )(shard)[0]


def spread_heads(qkv):
    def kernel(src, out, ss, rs, ls):
        me = here()
        c, y, z, x = me
        greet(y_peers(*me) + z_peers(*me))
        net, local = Net(ss, rs), Local(ls)
        kv = pl.ds(0, 2)
        owns = [local.copy(src.at[0, z], out.at[0, y, z]), local.copy(src.at[1, y], out.at[1, y, z])]
        first, second = {}, {}
        along_y = lambda d: at(c, y + d, z, x)
        along_z = lambda d: at(c, y, z + d, x)

        def part(half):
            return kv if half is None else half

        for k in range(4):
            second[0, k] = RingGather(
                net, along_y, lambda d, half=None, k=k: out.at[0, up(y, d), up(z, k), part(half)]
            )
            second[1, k] = RingGather(
                net, along_z, lambda d, half=None, k=k: out.at[1, up(y, k), up(z, d), part(half)]
            )
        for d in STEPS:
            first[0, d] = net.send(src.at[0, up(z, d)], out.at[0, y, z], along_z(d))
            first[1, d] = net.send(src.at[1, up(y, d)], out.at[1, y, z], along_y(d))
        second[0, 0].start(src.at[0, z, kv])
        second[1, 0].start(src.at[1, y, kv])
        for d in STEPS:
            for m in range(2):
                first[m, d].wait_recv()
                ring = second[m, 4 - d]
                ring.start(ring.out(0))
        for k in (0, 3, 1, 2):
            for m in range(2):
                second[m, k].from_back()
                second[m, k].from_ahead()
        for ring in second.values():
            ring.arrive()
        for copy in owns:
            copy.wait()
        net.finish()

    return remote_call(
        kernel, "spread_heads", 1, [ANY], [((2, 4, 4, 3, 256, 128), BF, ANY)], [], 6 + 8 * RING_GATHER, 2
    )(qkv)[0]


def swap_rows(blocks, cid, name):
    def kernel(src, out, ss, rs, ls):
        me = here()
        c, y, z, x = me
        greet(y_peers(*me) + z_peers(*me))
        net, local = Net(ss, rs), Local(ls)
        owns = [local.copy(src.at[0, z], out.at[0, z]), local.copy(src.at[1, y], out.at[1, y])]
        copies = []
        for d in STEPS:
            copies.append(net.send(src.at[0, up(z, d)], out.at[0, z], at(c, y, z + d, x)))
            copies.append(net.send(src.at[1, up(y, d)], out.at[1, y], at(c, y + d, z, x)))
        for copy in copies:
            copy.wait_recv()
        for copy in owns:
            copy.wait()
        net.finish()

    return remote_call(kernel, name, cid, [ANY], [((2, 4, 256, 128), BF, ANY)], [], 6, 2)(blocks)[0]


def middle_forward(parts, inputs, gain, shift, shard):
    width = shard.shape[1]

    def kernel(parts, inputs, gain, shift, shard, hidden, second, weights, held, spare, base, low, ss, rs, ls):
        me = here()
        c, y, z, x = me
        net, local = Net(ss, rs), Local(ls)
        sums = SumX(net, local, parts, held, spare, me)
        sums.load()
        residual = local.copy(inputs.at[x], base)
        greet(y_peers(*me) + z_peers(*me) + core_peer(*me) + x_peers(*me))
        gather = Gather(net, local, shard, weights, me)
        gather.start()
        sums.start()
        gather.near()
        sums.middle()
        residual.wait()

        def step(rows, total):
            value = base[rows, :].astype(F32) + total
            hidden[rows, :] = value
            norm, _ = normed(value)
            low[rows, :] = (norm * gain[...] + shift[...]).astype(BF)

        sums.totals(step)
        sums.gather(low, second)
        gather.far()
        sums.gather_middle()
        gather.finish()
        sums.finish()
        net.finish()

    return remote_call(
        kernel,
        "middle_forward",
        3,
        [ANY, ANY, IN_VMEM, IN_VMEM, ANY],
        [
            ((128, D), F32, IN_VMEM),
            ((4, 128, D), BF, ANY),
            ((2, 4, 4, 64, width), BF, ANY),
        ],
        sum_scratch() + [pltpu.VMEM((128, D), BF), pltpu.VMEM((128, D), BF)],
        GATHER_COPIES + SUM_COPIES,
        SUM_LOCALS + 2,
    )(parts, inputs, gain, shift, shard)


def middle_backward(parts, cotangent, hidden, gain, grads):
    widths = [g.shape[-1] for g in grads]
    count = len(grads)

    def kernel(parts, cotangent, hidden, gain, *rest):
        grad_refs = rest[:count]
        dhidden, hidden_low, vectors = rest[count : count + 3]
        outs = rest[count + 3 : 2 * count + 3]
        held, spare, base, low = rest[2 * count + 3 : 2 * count + 7]
        scratch = rest[2 * count + 7 : -3]
        ss, rs, ls = rest[-3:]
        me = here()
        c, y, z, x = me
        net, local = Net(ss, rs), Local(ls)
        sums = SumX(net, local, parts, held, spare, me)
        sums.load()
        upstream = local.copy(cotangent.at[x], base)
        greet(y_peers(*me) + z_peers(*me) + core_peer(*me) + x_peers(*me))
        scatters = [
            Scatter(net, local, grad_refs[k], outs[k], scratch[8 * k : 8 * k + 8], me)
            for k in range(count)
        ]
        for scatter in scatters:
            scatter.start()
        sums.start()
        for scatter in scatters:
            scatter.first()
        sums.middle()
        for scatter in scatters:
            scatter.first_middle()
        upstream.wait()
        vectors[...] = jnp.zeros_like(vectors)

        def step(rows, dsecond):
            norm, inverse = normed(hidden[rows, :])
            value = base[rows, :].astype(F32) + norm_pullback(dsecond, norm, inverse, gain[...])
            dhidden[rows, :] = value
            low[rows, :] = value.astype(BF)
            vectors[0:1, :] += jnp.sum(dsecond * norm, axis=0, keepdims=True)
            vectors[1:2, :] += jnp.sum(dsecond, axis=0, keepdims=True)

        sums.totals(step)
        sums.gather(low, hidden_low)
        scatters[0].second()
        sums.gather_middle()
        for scatter in scatters[1:]:
            scatter.second()
        for scatter in scatters:
            scatter.second_middle()
        for scatter in scatters:
            scatter.third()
        sums.finish()
        net.finish()

    scratch = sum_scratch() + [pltpu.VMEM((128, D), BF), pltpu.VMEM((128, D), BF)]
    for width in widths:
        scratch += scatter_scratch(width)
    return remote_call(
        kernel,
        "middle_backward",
        4,
        [ANY, ANY, IN_VMEM, IN_VMEM] + [ANY] * count,
        [((128, D), F32, IN_VMEM), ((4, 128, D), BF, ANY), ((2, D), F32, IN_VMEM)]
        + [((64, width), F32, IN_VMEM) for width in widths],
        scratch,
        SUM_COPIES + SCATTER_COPIES * count,
        SUM_LOCALS + 1 + count,
    )(parts, cotangent, hidden, gain, *grads)


def collect_heads(dkv, dq, parts, hidden):
    def kernel(dkv, dq, parts, hidden, dproject, outputs, mine, got, summed, held, spare, low, ss, rs, ls):
        me = here()
        c, y, z, x = me
        net, local = Net(ss, rs), Local(ls)
        order = (1, 3, 2, 0)
        loads = [local.copy(dkv.at[m], mine.at[m]) for m in range(2)]
        sums = SumX(net, local, parts, held, spare, me)
        sums.load()
        greet(y_peers(*me) + z_peers(*me) + x_peers(*me))
        kv = pl.ds(0, 2)
        along_y = lambda d: at(c, y + d, z, x)
        along_z = lambda d: at(c, y, z + d, x)

        def add(total, term):
            def one(i, carry):
                rows = pl.ds(pl.multiple_of(i * 64, 64), 64)
                total[rows, :] = (total[rows, :].astype(F32) + term[rows, :].astype(F32)).astype(BF)
                return carry

            lax.fori_loop(0, 4, one, 0)

        rings = {}
        for k in order:
            rings[0, k] = RingSum(
                net, along_y, lambda d, half, k=k: mine.at[0, up(y, d), up(z, k), half], got.at[0, k], add
            )
            rings[1, k] = RingSum(
                net, along_z, lambda d, half, k=k: mine.at[1, up(y, k), up(z, d), half], got.at[1, k], add
            )
        for copy in loads:
            copy.wait()
        for ring in rings.values():
            ring.start()
        sums.start()
        lates = [
            local.copy(dq.at[0, z], dproject.at[0, z, 2]),
            local.copy(dq.at[1, y], dproject.at[1, y, 2]),
        ]
        two = []
        for d in STEPS:
            two.append(net.send(dq.at[0, up(z, d)], dproject.at[0, z, 2], along_z(d)))
            two.append(net.send(dq.at[1, up(y, d)], dproject.at[1, y, 2], along_y(d)))
        for ring in rings.values():
            ring.middle()
        sums.middle()
        for k in order:
            for m, spot in ((0, z), (1, y)):
                ring = rings[m, k]
                ring.arrive()
                for half in range(2):
                    own, terms = ring.mine(0, half), ring.terms(half)

                    def total(i, carry, m=m, k=k, half=half, own=own, terms=terms):
                        rows = pl.ds(pl.multiple_of(i * 64, 64), 64)
                        value = own[rows, :].astype(F32)
                        for term in terms:
                            value += term[rows, :].astype(F32)
                        summed[m, k, half, rows, :] = value.astype(BF)
                        return carry

                    lax.fori_loop(0, 4, total, 0)
            if k:
                two.append(net.send(summed.at[0, k], dproject.at[0, z, kv], along_z(k)))
                two.append(net.send(summed.at[1, k], dproject.at[1, y, kv], along_y(k)))
            else:
                lates.append(local.copy(summed.at[0, 0], dproject.at[0, z, kv]))
                lates.append(local.copy(summed.at[1, 0], dproject.at[1, y, kv]))

        def step(rows, total):
            low[rows, :] = (hidden[rows, :] + total).astype(BF)

        sums.totals(step)
        sums.gather(low, outputs)
        sums.gather_middle()
        for copy in two:
            copy.wait_recv()
        for copy in lates:
            copy.wait()
        sums.finish()
        net.finish()

    return remote_call(
        kernel,
        "collect_heads",
        6,
        [ANY, ANY, ANY, IN_VMEM],
        [((2, 4, 3, 256, 128), BF, ANY), ((4, 128, D), BF, ANY)],
        [
            pltpu.VMEM((2, 4, 4, 2, 256, 128), BF),
            pltpu.VMEM((2, 4, 6, 256, 128), BF),
            pltpu.VMEM((2, 4, 2, 256, 128), BF),
        ]
        + sum_scratch()
        + [pltpu.VMEM((128, D), BF)],
        8 * RING_SUM + 6 + 6 + SUM_COPIES,
        2 + 4 + SUM_LOCALS,
    )(dkv, dq, parts, hidden)


def last_backward(parts, inputs, dhidden, gain, vectors, grads):
    widths = [g.shape[-1] for g in grads]
    count = len(grads)

    def kernel(parts, inputs, dhidden, gain, vectors, *rest):
        grad_refs = rest[:count]
        input_grad, sums_out = rest[count : count + 2]
        outs = rest[count + 2 : 2 * count + 2]
        held, spare, base, low, small, got = rest[2 * count + 2 : 2 * count + 8]
        scratch = rest[2 * count + 8 : -3]
        ss, rs, ls = rest[-3:]
        me = here()
        c, y, z, x = me
        net, local = Net(ss, rs), Local(ls)
        sums = SumX(net, local, parts, held, spare, me)
        sums.load()
        residual = local.copy(inputs.at[x], base)
        greet(y_peers(*me) + z_peers(*me) + core_peer(*me) + x_peers(*me))
        scatters = [
            Scatter(net, local, grad_refs[k], outs[k], scratch[8 * k : 8 * k + 8], me)
            for k in range(count)
        ]
        for scatter in scatters:
            scatter.start()
        sums.start()
        for scatter in scatters:
            scatter.first()
        sums.middle()
        for scatter in scatters:
            scatter.first_middle()
        residual.wait()
        small[0, ...] = vectors[...]

        def step(rows, dfirst):
            norm, inverse = normed(base[rows, :].astype(F32))
            value = dhidden[rows, :] + norm_pullback(dfirst, norm, inverse, gain[...])
            low[rows, :] = value.astype(BF)
            small[0, 0:1, :] += jnp.sum(dfirst * norm, axis=0, keepdims=True)
            small[0, 1:2, :] += jnp.sum(dfirst, axis=0, keepdims=True)

        sums.totals(step)
        copies = [
            net.send(small.at[0], got.at[0, d - 1], at(c, y, z, x + d)) for d in STEPS
        ]
        sums.gather(low, input_grad)
        for scatter in scatters:
            scatter.second()
        sums.gather_middle()
        for copy in copies:
            copy.wait_recv()
        small[1, ...] = small[0, ...]
        for n in range(3):
            small[1, 0:4, :] += got[0, n, 0:4, :]
        copies = [
            net.send(small.at[1], got.at[1, d - 1], at(c, y + d, z, x)) for d in STEPS
        ]
        for copy in copies:
            copy.wait_recv()
        small[2, ...] = small[1, ...] + got[1, 0] + got[1, 1] + got[1, 2]
        copies = [
            net.send(small.at[2], got.at[2, d - 1], at(c, y, z + d, x)) for d in STEPS
        ]
        for copy in copies:
            copy.wait_recv()
        small[3, ...] = small[2, ...] + got[2, 0] + got[2, 1] + got[2, 2]
        copy = net.send(small.at[3], got.at[3, 0], at(1 - c, y, z, x))
        for scatter in scatters:
            scatter.second_middle()
        for scatter in scatters:
            scatter.third()
        copy.wait_recv()
        sums_out[...] = small[3, ...] + got[3, 0]
        sums.finish()
        net.finish()

    scratch = sum_scratch() + [
        pltpu.VMEM((128, D), BF),
        pltpu.VMEM((128, D), BF),
        pltpu.VMEM((4, 8, D), F32),
        pltpu.VMEM((4, 3, 8, D), F32),
    ]
    for width in widths:
        scratch += scatter_scratch(width)
    return remote_call(
        kernel,
        "last_backward",
        7,
        [ANY, ANY, IN_VMEM, IN_VMEM, IN_VMEM] + [ANY] * count,
        [((4, 128, D), BF, ANY), ((8, D), F32, IN_VMEM)]
        + [((64, width), F32, IN_VMEM) for width in widths],
        scratch,
        SUM_COPIES + 10 + SCATTER_COPIES * count,
        SUM_LOCALS + 1 + count,
    )(parts, inputs, dhidden, gain, vectors, *grads)


def turn(values, cosine, sine):
    lane = lax.rem(lax.broadcasted_iota(jnp.int32, values.shape, 1), HEAD_DIM)
    swapped = jnp.where(lane < ROT // 2, -pltpu.roll(values, 120, 1), pltpu.roll(values, 8, 1))
    return values * cosine + swapped * sine


def project_heads(tokens, gain, shift, front, bias, tables):
    def kernel(x_ref, gain_ref, shift_ref, w_hbm, b_ref, t_ref, out_ref, low_ref, weights, sems):
        loads = []
        for t in range(3):
            columns = pl.ds(t * 512, 512)
            loads.append(pltpu.make_async_copy(w_hbm.at[:, columns], weights.at[t], sems.at[t]))
            loads[t].start()

        def step(i, carry):
            rows = pl.ds(pl.multiple_of(i * 32, 32), 32)
            norm, _ = normed(x_ref[rows, :].astype(F32))
            low_ref[rows, :] = (norm * gain_ref[...] + shift_ref[...]).astype(BF)
            return carry

        lax.fori_loop(0, 16, step, 0)
        for t in (1, 2, 0):
            loads[t].wait()
            for m in range(2):
                acc = jnp.dot(
                    low_ref[m * 256 : m * 256 + 256, :], weights[t], preferred_element_type=F32
                )
                acc = acc + b_ref[:, t * 512 : t * 512 + 512]
                for h in range(4):
                    part = acc[:, h * 128 : h * 128 + 128]
                    if t < 2:
                        part = turn(part, t_ref[0], t_ref[1])
                    out_ref[m, h, (t + 2) % 3] = part.astype(BF)

    return pl.pallas_call(
        kernel,
        name="project_heads",
        in_specs=[IN_VMEM, IN_VMEM, IN_VMEM, ANY, IN_VMEM, IN_VMEM],
        out_specs=[IN_VMEM, IN_VMEM],
        out_shape=[
            jax.ShapeDtypeStruct((2, 4, 3, 256, 128), BF),
            jax.ShapeDtypeStruct((512, D), BF),
        ],
        scratch_shapes=[pltpu.VMEM((3, D, 512), BF), pltpu.SemaphoreType.DMA((3,))],
        compiler_params=pltpu.CompilerParams(vmem_limit_bytes=VMEM_LIMIT),
    )(tokens, gain, shift, front, bias, tables)


def two_heads(block):
    lane = lax.broadcasted_iota(jnp.int32, (128, 128), 1)
    value = block.astype(F32)
    return jnp.concatenate(
        [jnp.where(lane < HEAD_DIM, value, 0.0), jnp.where(lane >= HEAD_DIM, value, 0.0)], axis=0
    )


def two_heads_t(block):
    feature = lax.broadcasted_iota(jnp.int32, (128, 128), 0)
    value = block.astype(F32).T
    return jnp.concatenate(
        [jnp.where(feature < HEAD_DIM, value, 0.0), jnp.where(feature >= HEAD_DIM, value, 0.0)], axis=1
    )


def one_block(stacked):
    feature = lax.broadcasted_iota(jnp.int32, (128, 128), 0)
    return jnp.where(feature < HEAD_DIM, stacked[:, :128], stacked[:, 128:]).T


def nt(left, right):
    return lax.dot_general(left, right, (((1,), (1,)), ((), ())), preferred_element_type=F32)


def unit_of(places, m, n):
    pair, rest = n // 9, lax.rem(n, 9)
    ahead = places[m * 8 + pair * 2] // (TILE // 128) + 1
    late = rest >= ahead
    block = pair * 2 + jnp.where(late, 1, 0)
    tile = rest - jnp.where(late, ahead, 0)
    return block, tile, places[m * 8 + block] * 128 - tile * TILE


def key_minus_query():
    return lax.broadcasted_iota(jnp.int32, (TILE, 256), 0) - lax.rem(
        lax.broadcasted_iota(jnp.int32, (TILE, 256), 1), 128
    )


def tile_of(t):
    return pl.ds(pl.multiple_of(t * TILE, TILE), TILE)


def lay_blocks(slots, lay):
    def some(n, carry):
        for k in range(4):
            b = n * 4 + k
            slot = slots[b]
            rows = pl.ds(pl.multiple_of(lax.rem(slot, 2) * 128, 128), 128)
            lay(slot // 2, rows, pl.ds(pl.multiple_of(b * 128, 128), 128))
        return carry

    lax.fori_loop(0, 8, some, 0)


UNITS_EACH = 36


def attend(slots, places, rows_of, spread):
    def kernel(
        slots, places, rows_of, k_ref, v_ref, q_ref, o_ref, full_ref, log_ref,
        keys, values_t, queries, scores_0, scores_1, weights_0, weights_1, results, sums,
    ):
        scores, weights = (scores_0, scores_1), (weights_0, weights_1)
        m = pl.program_id(0)

        def lay(slot, rows, to):
            keys[to, :] = k_ref[0, slot, 0, rows, :]
            values_t[:, to] = v_ref[0, slot, 0, rows, :].T

        lay_blocks(slots, lay)
        for b in range(8):
            row = rows_of[m * 4 + b // 2]
            block = q_ref[0, row, 0, (b % 2) * 128 : (b % 2) * 128 + 128, :]
            queries[b] = (two_heads_t(block) * 0.125).astype(BF)
        offset = key_minus_query()

        def multiply(n, odd):
            block, tile, _ = unit_of(places, m, n)
            scores[odd][...] = jnp.dot(
                keys[tile_of(tile), :], queries[block], preferred_element_type=F32
            )

        def soften(n, odd, top, total):
            block, tile, limit = unit_of(places, m, n)
            value = jnp.where(offset <= limit, scores[odd][...] * LOG2E, LOW)
            first = tile == 0
            top = jnp.where(first, LOW, top)
            new_top = jnp.maximum(top, jnp.max(value, axis=0, keepdims=True))
            exps = jnp.exp2(value - new_top)
            shrink = jnp.exp2(top - new_top)
            total = total * shrink + jnp.sum(exps, axis=0, keepdims=True)
            weights[odd][...] = exps.astype(BF)
            sums[block, 0:1, :] = new_top
            sums[block, 1:2, :] = total
            return new_top, total, shrink

        def gather(n, odd, shrink, acc):
            block, tile, _ = unit_of(places, m, n)
            acc = acc * shrink + jnp.dot(
                values_t[:, tile_of(tile)], weights[odd][...], preferred_element_type=F32
            )
            results[block] = acc
            return acc

        row = jnp.zeros((1, 256), F32)
        multiply(0, 0)
        multiply(1, 1)
        top, total, shrink = soften(0, 0, row, row)

        def step(k, carry):
            top, total, shrink, acc = carry
            for n, odd in ((2 * k + 1, 1), (2 * k + 2, 0)):
                multiply(n + 1, 1 - odd)
                acc = gather(n - 1, 1 - odd, shrink, acc)
                top, total, shrink = soften(n, odd, top, total)
            return top, total, shrink, acc

        carry = (top, total, shrink, jnp.zeros((128, 256), F32))
        top, total, shrink, acc = lax.fori_loop(0, UNITS_EACH // 2 - 1, step, carry)
        last = UNITS_EACH - 1
        acc = gather(last - 1, 0, shrink, acc)
        _, _, shrink = soften(last, 1, top, total)
        gather(last, 1, shrink, acc)
        for b in range(8):
            rows = slice((b % 2) * 128, (b % 2) * 128 + 128)
            total = sums[b, 1:2, :]
            result = one_block(results[b] / total)
            full_ref[0, b // 2, rows, :] = result
            o_ref[0, b // 2, rows, :] = result.astype(BF)
            log_ref[0, b : b + 1, :] = sums[b, 0:1, :] + jnp.log2(total)

    grid_spec = pltpu.PrefetchScalarGridSpec(
        num_scalar_prefetch=3,
        grid=(2,),
        in_specs=[
            pl.BlockSpec((1, 16, 1, 256, 128), lambda m, s, p, r: (m, 0, 0, 0, 0)),
            pl.BlockSpec((1, 16, 1, 256, 128), lambda m, s, p, r: (m, 0, 1, 0, 0)),
            pl.BlockSpec((1, 16, 1, 256, 128), lambda m, s, p, r: (m, 0, 2, 0, 0)),
        ],
        out_specs=[
            pl.BlockSpec((1, 4, 256, 128), lambda m, s, p, r: (m, 0, 0, 0)),
            pl.BlockSpec((1, 4, 256, 128), lambda m, s, p, r: (m, 0, 0, 0)),
            pl.BlockSpec((1, 8, 256), lambda m, s, p, r: (m, 0, 0)),
        ],
        scratch_shapes=[
            pltpu.VMEM((4096, 128), BF),
            pltpu.VMEM((128, 4096), BF),
            pltpu.VMEM((8, 128, 256), BF),
            pltpu.VMEM((TILE, 256), F32),
            pltpu.VMEM((TILE, 256), F32),
            pltpu.VMEM((TILE, 256), BF),
            pltpu.VMEM((TILE, 256), BF),
            pltpu.VMEM((8, 128, 256), F32),
            pltpu.VMEM((8, 8, 256), F32),
        ],
    )
    return pl.pallas_call(
        kernel,
        name="attend",
        grid_spec=grid_spec,
        out_shape=[
            jax.ShapeDtypeStruct((2, 4, 256, 128), BF),
            jax.ShapeDtypeStruct((2, 4, 256, 128), F32),
            jax.ShapeDtypeStruct((2, 8, 256), F32),
        ],
        compiler_params=pltpu.CompilerParams(vmem_limit_bytes=VMEM_LIMIT),
    )(slots, places, rows_of, spread, spread, spread)


def attend_back(slots, places, rows_of, spread, full, logs, upstream, tables):
    base, steps = tables

    def kernel(
        slots, places, rows_of, k_ref, v_ref, q_ref, full_ref, log_ref, up_ref, base_ref, steps_ref,
        dq_ref, dkv_ref,
        keys, keys_t, values, dkeys, dvalues, queries, queries_t, grads, grads_t, delta,
        scores_0, scores_1, dprobs_0, dprobs_1, probs_0, probs_1, dscores_0, dscores_1, results,
    ):
        scores, dprobs = (scores_0, scores_1), (dprobs_0, dprobs_1)
        probs_low, dscores = (probs_0, probs_1), (dscores_0, dscores_1)
        m = pl.program_id(0)

        def lay(slot, rows, to):
            block = k_ref[0, slot, 0, rows, :]
            keys[to, :] = block
            keys_t[:, to] = block.T
            values[to, :] = v_ref[0, slot, 0, rows, :]
            dkeys[to, :] = jnp.zeros((128, 128), F32)
            dvalues[to, :] = jnp.zeros((128, 128), F32)

        lay_blocks(slots, lay)
        for b in range(8):
            rows = slice((b % 2) * 128, (b % 2) * 128 + 128)
            block = q_ref[0, rows_of[m * 4 + b // 2], 0, rows, :]
            queries[b] = (two_heads(block) * 0.125).astype(BF)
            queries_t[b] = (two_heads_t(block) * 0.125).astype(BF)
            ups = up_ref[0, b // 2, rows, :]
            grads[b] = two_heads(ups).astype(BF)
            grads_t[b] = two_heads_t(ups).astype(BF)
            product = (ups.astype(F32) * full_ref[0, b // 2, rows, :]).T
            delta[b, 0:1, :128] = jnp.sum(product[:HEAD_DIM], axis=0, keepdims=True)
            delta[b, 0:1, 128:] = jnp.sum(product[HEAD_DIM:], axis=0, keepdims=True)
        offset = key_minus_query()

        def multiply(n, odd):
            block, tile, _ = unit_of(places, m, n)
            scores[odd][...] = jnp.dot(
                keys[tile_of(tile), :], queries_t[block], preferred_element_type=F32
            )
            dprobs[odd][...] = jnp.dot(
                values[tile_of(tile), :], grads_t[block], preferred_element_type=F32
            )

        def soften(n, odd):
            block, _, limit = unit_of(places, m, n)
            value = jnp.exp2(scores[odd][...] * LOG2E - log_ref[0, pl.ds(block, 1), :])
            value = jnp.where(offset <= limit, value, 0.0)
            probs_low[odd][...] = value.astype(BF)
            dscores[odd][...] = (
                value * (dprobs[odd][...] - delta[block, 0:1, :])
            ).astype(BF)

        def gather(n, odd, acc):
            block, tile, _ = unit_of(places, m, n)
            span = tile_of(tile)
            dvalues[span, :] += jnp.dot(probs_low[odd][...], grads[block], preferred_element_type=F32)
            dkeys[span, :] += jnp.dot(dscores[odd][...], queries[block], preferred_element_type=F32)
            acc = jnp.where(tile == 0, 0.0, acc) + jnp.dot(
                keys_t[:, span], dscores[odd][...], preferred_element_type=F32
            )
            results[block] = acc
            return acc

        multiply(0, 0)
        multiply(1, 1)
        soften(0, 0)

        def step(k, acc):
            for n, odd in ((2 * k + 1, 1), (2 * k + 2, 0)):
                multiply(n + 1, 1 - odd)
                acc = gather(n - 1, 1 - odd, acc)
                soften(n, odd)
            return acc

        last = UNITS_EACH - 1
        acc = lax.fori_loop(0, UNITS_EACH // 2 - 1, step, jnp.zeros((128, 256), F32))
        acc = gather(last - 1, 0, acc)
        soften(last, 1)
        gather(last, 1, acc)

        def turned_back(values, place):
            cosine, sine = base_ref[0], base_ref[1]
            far_cosine, far_sine = steps_ref[0, pl.ds(place, 1), :], steps_ref[1, pl.ds(place, 1), :]
            return turn(
                values,
                far_cosine * cosine - far_sine * sine,
                -(far_sine * cosine + far_cosine * sine),
            )

        for b in range(8):
            rows = slice((b % 2) * 128, (b % 2) * 128 + 128)
            dquery = one_block(results[b]) * 0.125
            dq_ref[0, b // 2, rows, :] = turned_back(dquery, places[m * 8 + b]).astype(BF)

        def flush(n, carry):
            for k in range(2):
                b = n * 2 + k
                slot = slots[b]
                rows = pl.ds(pl.multiple_of(lax.rem(slot, 2) * 128, 128), 128)
                to = pl.ds(pl.multiple_of(b * 128, 128), 128)
                dkv_ref[0, slot // 2, 0, rows, :] = turned_back(dkeys[to, :], b).astype(BF)
                dkv_ref[0, slot // 2, 1, rows, :] = dvalues[to, :].astype(BF)
            return carry

        lax.fori_loop(0, 16, flush, 0)

    grid_spec = pltpu.PrefetchScalarGridSpec(
        num_scalar_prefetch=3,
        grid=(2,),
        in_specs=[
            pl.BlockSpec((1, 16, 1, 256, 128), lambda m, s, p, r: (m, 0, 0, 0, 0)),
            pl.BlockSpec((1, 16, 1, 256, 128), lambda m, s, p, r: (m, 0, 1, 0, 0)),
            pl.BlockSpec((1, 16, 1, 256, 128), lambda m, s, p, r: (m, 0, 2, 0, 0)),
            pl.BlockSpec((1, 4, 256, 128), lambda m, s, p, r: (m, 0, 0, 0)),
            pl.BlockSpec((1, 8, 256), lambda m, s, p, r: (m, 0, 0)),
            pl.BlockSpec((1, 4, 256, 128), lambda m, s, p, r: (m, 0, 0, 0)),
            pl.BlockSpec((2, 128, 128), lambda m, s, p, r: (0, 0, 0)),
            pl.BlockSpec((2, 32, 128), lambda m, s, p, r: (0, 0, 0)),
        ],
        out_specs=[
            pl.BlockSpec((1, 4, 256, 128), lambda m, s, p, r: (m, 0, 0, 0)),
            pl.BlockSpec((1, 16, 2, 256, 128), lambda m, s, p, r: (m, 0, 0, 0, 0)),
        ],
        scratch_shapes=[
            pltpu.VMEM((4096, 128), BF),
            pltpu.VMEM((128, 4096), BF),
            pltpu.VMEM((4096, 128), BF),
            pltpu.VMEM((4096, 128), F32),
            pltpu.VMEM((4096, 128), F32),
            pltpu.VMEM((8, 256, 128), BF),
            pltpu.VMEM((8, 128, 256), BF),
            pltpu.VMEM((8, 256, 128), BF),
            pltpu.VMEM((8, 128, 256), BF),
            pltpu.VMEM((8, 8, 256), F32),
            pltpu.VMEM((TILE, 256), F32),
            pltpu.VMEM((TILE, 256), F32),
            pltpu.VMEM((TILE, 256), F32),
            pltpu.VMEM((TILE, 256), F32),
            pltpu.VMEM((TILE, 256), BF),
            pltpu.VMEM((TILE, 256), BF),
            pltpu.VMEM((TILE, 256), BF),
            pltpu.VMEM((TILE, 256), BF),
            pltpu.VMEM((8, 128, 256), F32),
        ],
    )
    return pl.pallas_call(
        kernel,
        name="attend_back",
        grid_spec=grid_spec,
        out_shape=[
            jax.ShapeDtypeStruct((2, 4, 256, 128), BF),
            jax.ShapeDtypeStruct((2, 16, 2, 256, 128), BF),
        ],
        compiler_params=pltpu.CompilerParams(vmem_limit_bytes=VMEM_LIMIT),
    )(slots, places, rows_of, spread, spread, spread, full, logs, upstream, base, steps)


def tn(left, right):
    return lax.dot_general(left, right, (((0,), (0,)), ((), ())), preferred_element_type=F32)


def feed_forward(second_low, dy, weights):
    def kernel(
        low_hbm, dy_hbm, w_hbm, branch, dsecond, gate_out, up_out, down_out,
        low, dys, gate_w, up_w, down_w, gate, up, dmixed, mixed, dgate, dup, chunks, sems, chunk_sems,
    ):
        def load(n, src, dst):
            copy = pltpu.make_async_copy(src, dst, sems.at[n])
            copy.start()
            return copy

        def columns(k):
            return w_hbm.at[:, pl.ds(k * UNITS, UNITS)]

        loads = [
            load(0, low_hbm, low),
            load(1, columns(0), gate_w),
            load(2, columns(1), up_w),
            load(3, dy_hbm, dys),
            load(4, columns(2), down_w),
        ]
        loads[0].wait()
        loads[1].wait()
        gate[...] = jnp.dot(low[...], gate_w[...], preferred_element_type=F32)
        loads[2].wait()
        up[...] = jnp.dot(low[...], up_w[...], preferred_element_type=F32)
        loads[3].wait()
        loads[4].wait()
        dmixed[...] = jnp.dot(dys[...], down_w[...], preferred_element_type=F32)

        def step(i, carry):
            rows = pl.ds(pl.multiple_of(i * 16, 16), 16)
            g, u, d = gate[rows, :], up[rows, :], dmixed[rows, :]
            s = jax.nn.sigmoid(g)
            silu = g * s
            mixed[rows, :] = (silu * u).astype(BF)
            dgate[rows, :] = (d * u * s * (1.0 + g * (1.0 - s))).astype(BF)
            dup[rows, :] = (d * silu).astype(BF)
            return carry

        lax.fori_loop(0, 32, step, 0)
        dsecond[...] = (nt(dgate[...], gate_w[...]) + nt(dup[...], up_w[...])).astype(BF)
        busy = {}
        n = 0
        for left, right, out in ((low, dgate, gate_out), (low, dup, up_out), (dys, mixed, down_out)):
            for k in range(4):
                rows = pl.ds(k * 512, 512)
                slot = n % 2
                if slot in busy:
                    busy[slot].wait()
                chunks[slot] = tn(left[:, rows], right[...]).astype(BF)
                busy[slot] = pltpu.make_async_copy(chunks.at[slot], out.at[rows, :], chunk_sems.at[slot])
                busy[slot].start()
                n += 1
        branch[...] = nt(mixed[...], down_w[...]).astype(BF)
        busy[0].wait()
        busy[1].wait()

    return pl.pallas_call(
        kernel,
        name="feed_forward",
        in_specs=[ANY, ANY, ANY],
        out_specs=[IN_VMEM, IN_VMEM, ANY, ANY, ANY],
        out_shape=[jax.ShapeDtypeStruct((512, D), BF)] * 2 + [jax.ShapeDtypeStruct((D, UNITS), BF)] * 3,
        scratch_shapes=[pltpu.VMEM((512, D), BF)] * 2
        + [pltpu.VMEM((D, UNITS), BF)] * 3
        + [pltpu.VMEM((512, UNITS), F32)] * 3
        + [pltpu.VMEM((512, UNITS), BF)] * 3
        + [
            pltpu.VMEM((2, 512, UNITS), BF),
            pltpu.SemaphoreType.DMA((5,)),
            pltpu.SemaphoreType.DMA((2,)),
        ],
        compiler_params=pltpu.CompilerParams(vmem_limit_bytes=VMEM_LIMIT),
    )(second_low, dy, weights)


def project_back(dproject, first_low, front):
    def kernel(dp_ref, low_ref, w_hbm, dfirst, grad_out, bias_out, wide, weights, chunks, sems, chunk_sems):
        load = pltpu.make_async_copy(w_hbm.at[:, pl.ds(0, 1536)], weights, sems.at[0])
        load.start()
        for m in range(2):
            for t in range(3):
                for h in range(4):
                    to = t * 512 + h * 128
                    wide[m * 256 : m * 256 + 256, to : to + 128] = dp_ref[m, h, (t + 2) % 3]
        bias_out[...] = jnp.sum(wide[...].astype(F32), axis=0, keepdims=True)
        busy = {}
        for k in range(4):
            rows = pl.ds(k * 512, 512)
            slot = k % 2
            if slot in busy:
                busy[slot].wait()
            chunks[slot] = tn(low_ref[:, rows], wide[...]).astype(BF)
            busy[slot] = pltpu.make_async_copy(chunks.at[slot], grad_out.at[rows, :], chunk_sems.at[slot])
            busy[slot].start()
        load.wait()
        dfirst[...] = nt(wide[...], weights[...]).astype(BF)
        busy[0].wait()
        busy[1].wait()

    return pl.pallas_call(
        kernel,
        name="project_back",
        in_specs=[IN_VMEM, IN_VMEM, ANY],
        out_specs=[IN_VMEM, ANY, IN_VMEM],
        out_shape=[
            jax.ShapeDtypeStruct((512, D), BF),
            jax.ShapeDtypeStruct((D, 1536), BF),
            jax.ShapeDtypeStruct((1, 1536), F32),
        ],
        scratch_shapes=[
            pltpu.VMEM((512, 1536), BF),
            pltpu.VMEM((D, 1536), BF),
            pltpu.VMEM((2, 512, 1536), BF),
            pltpu.SemaphoreType.DMA((1,)),
            pltpu.SemaphoreType.DMA((2,)),
        ],
        compiler_params=pltpu.CompilerParams(vmem_limit_bytes=VMEM_LIMIT),
    )(dproject, first_low, front)


def rotary_tables(places):
    lane = np.arange(128) % HEAD_DIM
    power = 10000.0 ** (-jnp.arange(0, ROT, 2, dtype=F32) / ROT)
    hot = (lane[None, :] % (ROT // 2) == np.arange(ROT // 2)[:, None]) & (lane[None, :] < ROT)
    frequency = jnp.sum(jnp.where(hot, power[:, None], 0.0), axis=0)
    angles = places.astype(F32)[:, None] * frequency[None, :]
    return jnp.stack([jnp.cos(angles), jnp.sin(angles)])


def angle_tables():
    near = jnp.arange(128, dtype=jnp.int32)
    return rotary_tables(near), rotary_tables(near[:32] * 128)


def body(
    inputs,
    cotangent,
    group_place,
    attend_gain,
    attend_shift,
    project_weight,
    project_bias,
    output_weight,
    mixer_gain,
    mixer_shift,
    gate_weight,
    up_weight,
    down_weight,
):
    ctx = lax.axis_index("ctx")
    y, z = ctx // 4, lax.rem(ctx, 4)
    shard_index = lax.axis_index("dp") * 16 + ctx

    blocks = jnp.arange(32, dtype=jnp.int32)
    hits = group_place[None, :] == blocks[:, None]
    slots = jnp.sum(jnp.where(hits, blocks[None, :], 0), axis=1)
    four = jnp.arange(4, dtype=jnp.int32)
    rows_of = jnp.concatenate([y * 4 + four, four * 4 + z])
    held_slots = (rows_of[:, None] * 2 + jnp.arange(2, dtype=jnp.int32)[None, :]).reshape(16)
    chosen = held_slots[:, None] == blocks[None, :]
    places = jnp.sum(jnp.where(chosen, group_place[None, :], 0), axis=1)
    own_slots = ctx * 2 + jnp.arange(2, dtype=jnp.int32)
    own_blocks = jnp.sum(
        jnp.where(own_slots[:, None] == blocks[None, :], group_place[None, :], 0), axis=1
    )
    own_places = (own_blocks[:, None] * 128 + jnp.arange(128, dtype=jnp.int32)[None, :]).reshape(256)
    own_tables = rotary_tables(own_places)
    all_tables = angle_tables()

    vectors = jnp.concatenate(
        [
            jnp.stack([attend_gain, attend_shift, mixer_gain, mixer_shift], axis=1),
            jnp.pad(project_bias.reshape(1, 48), ((0, 63), (0, 0))),
            jnp.zeros((64, 76), BF),
        ],
        axis=1,
    )
    front_shard = jnp.concatenate(
        [project_weight.reshape(64, 1536), output_weight.T, vectors], axis=1
    )
    back_shard = jnp.concatenate([gate_weight, up_weight, down_weight.T], axis=1)
    front = gather_front(front_shard).reshape(D, 2176)
    gains = front[:, 2048:2052].astype(F32).T
    first_gain, first_shift = gains[0:1], gains[1:2]
    second_gain, second_shift = gains[2:3], gains[3:4]
    bias = (
        front.reshape(32, 64, 2176)[:, 0, 2052:2100]
        .reshape(32, 3, 8, 2)
        .transpose(1, 2, 0, 3)
        .astype(F32)
        .reshape(1, 1536)
    )
    output_t = front[:, 1536:2048]

    tokens = inputs.reshape(512, D)
    quarters = inputs.reshape(4, 128, D)
    qkv, first_low = project_heads(tokens, first_gain, first_shift, front, bias, own_tables)
    spread = spread_heads(qkv).reshape(2, 16, 3, 256, 128)
    attended_heads, attended_full, logs = attend(slots, places, rows_of, spread)
    attended_low = (
        swap_rows(attended_heads, 2, "attended_back").transpose(0, 2, 1, 3).reshape(512, 512)
    )
    branch = nt(attended_low, output_t).astype(BF).reshape(4, 128, D)
    hidden, second_low, back = middle_forward(branch, quarters, second_gain, second_shift, back_shard)

    mixer_part, second_part, gate_grad, up_grad, down_grad = feed_forward(
        second_low.reshape(512, D), cotangent.reshape(512, D), back.reshape(D, 3 * UNITS)
    )

    def shards(grad):
        return grad.reshape(2, 4, 4, 64, grad.shape[1])

    dhidden, hidden_low, mixer_vectors, gate_grad, up_grad, down_grad = middle_backward(
        second_part.reshape(4, 128, D),
        cotangent.reshape(4, 128, D),
        hidden,
        second_gain,
        [shards(gate_grad), shards(up_grad), shards(down_grad)],
    )

    hidden_low = hidden_low.reshape(512, D)
    dattended = jnp.dot(hidden_low, output_t, preferred_element_type=F32).astype(BF)
    upstream = swap_rows(
        dattended.reshape(2, 256, 4, 128).transpose(0, 2, 1, 3), 5, "dattended_out"
    )
    output_grad = shards(tn(hidden_low, attended_low).astype(BF))
    dq, dkv = attend_back(
        slots, places, rows_of, spread, attended_full, logs, upstream, all_tables
    )
    dproject, outputs = collect_heads(dkv.reshape(2, 4, 4, 2, 256, 128), dq, mixer_part.reshape(4, 128, D), hidden)
    first_part, project_grad, bias_part = project_back(dproject, first_low, front)
    small = jnp.concatenate(
        [
            jnp.zeros((2, D), F32),
            mixer_vectors,
            jnp.pad(bias_part, ((0, 0), (0, D - 1536))),
            jnp.zeros((3, D), F32),
        ]
    )
    input_grad, small, project_grad, output_grad = last_backward(
        first_part.reshape(4, 128, D),
        quarters,
        dhidden,
        first_gain,
        small,
        [shards(project_grad), output_grad],
    )
    own = lax.dynamic_slice(small, (0, shard_index * 64), (4, 64))
    bias_grad = lax.dynamic_slice(
        small[4, :1536].reshape(3, 8, 64), (0, 0, shard_index * 2), (3, 8, 2)
    )
    shape = inputs.shape
    return (
        outputs.reshape(shape),
        input_grad.reshape(shape),
        own[0],
        own[1],
        project_grad.reshape(64, 3, 512),
        bias_grad,
        output_grad.T,
        own[2],
        own[3],
        gate_grad,
        up_grad,
        down_grad.T,
    )


def solution(mesh):
    weight = ("dp", "ctx")
    rows = P(None, "dp", "ctx", None)
    vector = P(weight)
    matrix = P(weight, "tensor")
    turned = P("tensor", weight)
    project = P(weight, None, "tensor")
    bias = P(None, "tensor", weight)
    params = (vector, vector, project, bias, turned, vector, vector, matrix, matrix, turned)
    return jax.shard_map(
        body,
        mesh=mesh,
        in_specs=(rows, rows, P()) + params,
        out_specs=(rows, rows) + params,
        check_vma=False,
    )
```

```python
import functools

import jax
import jax.numpy as jnp
import numpy as np
from jax import lax
from jax.experimental import pallas as pl
from jax.experimental.pallas import tpu as pltpu
from jax.sharding import PartitionSpec as P

MESH = pl.DeviceIdType.MESH
D = 2048
UNITS = 1408
HEAD_DIM = 64
ROT = 16
EPSILON = 1e-05
LOG2E = 1.4426950408889634
LOW = -1e30
TILE = 512
VMEM_LIMIT = 58 * 2**20
STEPS = (1, 3, 2)
BF = jnp.bfloat16
F32 = jnp.float32


def here():
    ctx = lax.axis_index("ctx")
    return (lax.axis_index("dp"), ctx // 4, lax.rem(ctx, 4), lax.axis_index("tensor"))


def at(c, y, z, x):
    return (c, lax.rem(y, 4) * 4 + lax.rem(z, 4), lax.rem(x, 4))


def up(i, d):
    return lax.rem(i + d, 4)


def down(i, d):
    return lax.rem(i + 4 - d, 4)


class Net:
    def __init__(self, send_sems, recv_sems):
        self.send_sems, self.recv_sems = send_sems, recv_sems
        self.sent = []

    def send(self, src, dst, device):
        n = len(self.sent)
        copy = pltpu.make_async_remote_copy(
            src_ref=src,
            dst_ref=dst,
            send_sem=self.send_sems.at[n],
            recv_sem=self.recv_sems.at[n],
            device_id=device,
            device_id_type=MESH,
        )
        copy.start()
        self.sent.append(copy)
        return copy

    def finish(self):
        for copy in self.sent:
            copy.wait_send()


class Local:
    def __init__(self, sems):
        self.sems, self.n = sems, 0

    def copy(self, src, dst):
        copy = pltpu.make_async_copy(src, dst, self.sems.at[self.n])
        copy.start()
        self.n += 1
        return copy


def greet(peers):
    barrier = pltpu.get_barrier_semaphore()
    for peer in peers:
        pl.semaphore_signal(barrier, inc=1, device_id=peer, device_id_type=MESH)
    pl.semaphore_wait(barrier, len(peers))


def y_peers(c, y, z, x):
    return [at(c, y + d, z, x) for d in (1, 2, 3)]


def z_peers(c, y, z, x):
    return [at(c, y, z + d, x) for d in (1, 2, 3)]


def x_peers(c, y, z, x):
    return [at(c, y, z, x + d) for d in (1, 2, 3)]


def core_peer(c, y, z, x):
    return [at(1 - c, y, z, x)]


class RingSum:
    def __init__(self, net, device, mine, spare, add):
        self.net, self.device, self.mine, self.spare, self.add = net, device, mine, spare, add

    def start(self):
        send, mine, spare = self.net.send, self.mine, self.spare
        ahead, back = self.device(1), self.device(3)
        self.far_ahead = send(mine(2, 0), spare.at[0], ahead)
        self.far_back = send(mine(2, 1), spare.at[1], back)
        self.near = [send(mine(1, 1), spare.at[3], ahead), send(mine(3, 0), spare.at[2], back)]

    def middle(self):
        send, spare = self.net.send, self.spare
        self.far_ahead.wait_recv()
        self.add(spare.at[0], self.mine(1, 0))
        self.near.append(send(spare.at[0], spare.at[4], self.device(1)))
        self.far_back.wait_recv()
        self.add(spare.at[1], self.mine(3, 1))
        self.near.append(send(spare.at[1], spare.at[5], self.device(3)))

    def arrive(self):
        for copy in self.near:
            copy.wait_recv()

    def terms(self, half):
        return [self.spare.at[4 if half == 0 else 3], self.spare.at[2 if half == 0 else 5]]


RING_SUM = 6


class RingGather:
    def __init__(self, net, device, out):
        self.net, self.device, self.out = net, device, out

    def start(self, block):
        self.ahead = self.net.send(block, self.out(0), self.device(1))
        self.back = self.net.send(block, self.out(0), self.device(3))

    def from_back(self):
        self.ahead.wait_recv()
        piece = self.out(3, 0)
        self.far_ahead = self.net.send(piece, piece, self.device(1))

    def from_ahead(self):
        self.back.wait_recv()
        piece = self.out(1, 1)
        self.far_back = self.net.send(piece, piece, self.device(3))

    def arrive(self):
        self.far_ahead.wait_recv()
        self.far_back.wait_recv()


RING_GATHER = 4


class Gather:
    def __init__(self, net, local, src, place, me):
        self.net, self.local, self.src, self.place, self.me = net, local, src, place, me
        self.core = []
        c, y, z, x = me
        along_y = lambda d: at(c, y + d, z, x)
        along_z = lambda d: at(c, y, z + d, x)

        def spot(far_y, far_z, first, half):
            if half is None:
                return place(c, up(y, far_y), up(z, far_z), first, 32)
            return place(c, up(y, far_y), up(z, far_z), first + 16 * half, 16)

        self.one = (
            RingGather(net, along_y, lambda d, half=None: spot(d, 0, 0, half)),
            RingGather(net, along_z, lambda d, half=None: spot(0, d, 32, half)),
        )
        self.two = {}
        for k in range(4):
            self.two[0, k] = RingGather(net, along_z, lambda d, half=None, k=k: spot(k, d, 0, half))
            self.two[1, k] = RingGather(net, along_y, lambda d, half=None, k=k: spot(d, k, 32, half))

    def hand_over(self, piece):
        c, y, z, x = self.me
        self.core.append(self.net.send(piece, piece, at(1 - c, y, z, x)))

    def start(self):
        c, y, z, x = self.me
        src, own = self.src, self.place(c, y, z, 0, 64)
        self.own = self.local.copy(src, own)
        halves = (src.at[pl.ds(0, 32)], src.at[pl.ds(32, 32)])
        for way in range(2):
            self.one[way].start(halves[way])
        for way in range(2):
            self.two[way, 0].start(halves[way])
        self.core.append(self.net.send(src, own, at(1 - c, y, z, x)))

    def near(self):
        for way in range(2):
            self.one[way].from_back()
            self.two[way, 3].start(self.one[way].out(3))
        for way in range(2):
            self.one[way].from_ahead()
            self.two[way, 1].start(self.one[way].out(1))
        for k in (3, 1):
            for way in range(2):
                self.hand_over(self.one[way].out(k))

    def middle(self):
        self.pass_on(0)
        for way in range(2):
            self.one[way].arrive()
            self.two[way, 2].start(self.one[way].out(2))
            self.hand_over(self.one[way].out(2))

    def pass_on(self, k):
        for way in range(2):
            self.two[way, k].from_back()
            self.two[way, k].from_ahead()
            self.hand_over(self.two[way, k].out(3))
            self.hand_over(self.two[way, k].out(1))

    def far(self):
        for k in (3, 1, 2):
            self.pass_on(k)
        for k in (0, 3, 1, 2):
            for way in range(2):
                self.two[way, k].arrive()
                self.hand_over(self.two[way, k].out(2))

    def finish(self):
        for copy in self.core:
            copy.wait_recv()
        self.own.wait()


def flat_rows(ref):
    def place(c, y, z, first, count):
        return ref.at[pl.ds(pl.multiple_of(((c * 4 + y) * 4 + z) * 64 + first, 16), count)]

    return place


GATHER_COPIES = 10 * RING_GATHER + 31


def scatter_scratch(width):
    return [
        pltpu.VMEM((4, 4, 64, width), BF),
        pltpu.VMEM((4, 4, 64, width), BF),
        pltpu.VMEM((6, 4, 16, width), BF),
        pltpu.VMEM((6, 4, 16, width), BF),
        pltpu.VMEM((4, 32, width), BF),
        pltpu.VMEM((4, 32, width), BF),
        pltpu.VMEM((6, 16, width), BF),
        pltpu.VMEM((6, 16, width), BF),
    ]


SCATTER_COPIES = 1 + 4 * RING_SUM


def add_blocks(total, term):
    if len(total.shape) == 2:
        total[...] = (total[...].astype(F32) + term[...].astype(F32)).astype(BF)
        return

    def one(i, carry):
        total[i] = (total[i].astype(F32) + term[i].astype(F32)).astype(BF)
        return carry

    lax.fori_loop(0, total.shape[0], one, 0)


class Scatter:
    def __init__(self, net, local, grads, out, scratch, me):
        self.net, self.local, self.grads, self.out, self.me = net, local, grads, out, me
        (held, self.other, one_a, one_b, self.sum_a, self.sum_b, two_a, two_b) = scratch
        self.held = held
        c, y, z, x = me
        along_y = lambda d: at(c, y + d, z, x)
        along_z = lambda d: at(c, y, z + d, x)
        self.one_a = RingSum(
            net, along_z, lambda d, half: held.at[:, up(z, d), pl.ds(16 * half, 16)], one_a, add_blocks
        )
        self.one_b = RingSum(
            net, along_y, lambda d, half: held.at[up(y, d), :, pl.ds(32 + 16 * half, 16)], one_b, add_blocks
        )
        self.two_a = RingSum(
            net, along_y, lambda d, half: self.sum_a.at[up(y, d), pl.ds(16 * half, 16)], two_a, add_blocks
        )
        self.two_b = RingSum(
            net, along_z, lambda d, half: self.sum_b.at[up(z, d), pl.ds(16 * half, 16)], two_b, add_blocks
        )

    def start(self):
        c, y, z, x = self.me
        self.own = self.local.copy(self.grads.at[c], self.held)
        self.zero = self.net.send(self.grads.at[1 - c], self.other, at(1 - c, y, z, x))

    def first(self):
        self.own.wait()
        self.zero.wait_recv()
        held, other = self.held, self.other

        def add(i, carry):
            for q in range(4):
                rows = pl.ds(q * 16, 16)
                held[i // 4, lax.rem(i, 4), rows, :] = (
                    held[i // 4, lax.rem(i, 4), rows, :].astype(F32)
                    + other[i // 4, lax.rem(i, 4), rows, :].astype(F32)
                ).astype(BF)
            return carry

        lax.fori_loop(0, 16, add, 0)
        self.one_a.start()
        self.one_b.start()

    def first_middle(self):
        self.one_a.middle()
        self.one_b.middle()

    def second(self):
        for one, two, total in ((self.one_a, self.two_a, self.sum_a), (self.one_b, self.two_b, self.sum_b)):
            one.arrive()
            for half in range(2):
                own, terms = one.mine(0, half), one.terms(half)

                def add(i, carry, half=half, own=own, terms=terms, total=total):
                    value = own[i].astype(F32)
                    for term in terms:
                        value += term[i].astype(F32)
                    total[i, pl.ds(16 * half, 16), :] = value.astype(BF)
                    return carry

                lax.fori_loop(0, 4, add, 0)
            two.start()

    def second_middle(self):
        self.two_a.middle()
        self.two_b.middle()

    def third(self):
        for first, two in ((0, self.two_a), (32, self.two_b)):
            two.arrive()
            for half in range(2):
                value = two.mine(0, half)[...].astype(F32)
                for term in two.terms(half):
                    value += term[...].astype(F32)
                self.out[pl.ds(first + 16 * half, 16), :] = value


class SumX:
    def __init__(self, net, local, parts, held, spare, me):
        c, y, z, x = me
        self.local, self.parts, self.held, self.x, self.net = local, parts, held, x, net
        self.along = lambda d: at(c, y, z, x + d)
        self.ring = RingSum(
            net, self.along, lambda d, half: held.at[up(x, d), pl.ds(64 * half, 64)], spare, self.add
        )

    def add(self, total, term):
        def one(i, carry):
            rows = pl.ds(pl.multiple_of(i * 16, 16), 16)
            total[rows, :] = (total[rows, :].astype(F32) + term[rows, :].astype(F32)).astype(BF)
            return carry

        lax.fori_loop(0, 4, one, 0)

    def load(self):
        self.loads = [self.local.copy(self.parts.at[up(self.x, d)], self.held.at[up(self.x, d)]) for d in (2, 1, 3, 0)]

    def start(self):
        for copy in self.loads:
            copy.wait()
        self.ring.start()

    def start_held(self):
        self.ring.start()

    def middle(self):
        self.ring.middle()

    def totals(self, step):
        self.ring.arrive()
        for half in range(2):
            terms = self.ring.terms(half)

            def loop(i, carry, half=half, terms=terms):
                rows = pl.ds(pl.multiple_of(i * 32, 32), 32)
                own = pl.ds(pl.multiple_of(64 * half + i * 32, 32), 32)
                value = self.held[self.x, own, :].astype(F32)
                for term in terms:
                    value += term[rows, :].astype(F32)
                step(own, value)
                return carry

            lax.fori_loop(0, 2, loop, 0)

    def gather(self, block, out):
        x = self.x

        def piece(d, half=None):
            whole = out.at[up(x, d)]
            return whole if half is None else out.at[up(x, d), pl.ds(64 * half, 64)]

        self.back = RingGather(self.net, self.along, piece)
        self.mine = self.local.copy(block, out.at[x])
        self.back.start(block)

    def gather_middle(self):
        self.back.from_back()
        self.back.from_ahead()

    def finish(self):
        self.mine.wait()
        self.back.arrive()


SUM_COPIES = RING_SUM + RING_GATHER
SUM_LOCALS = 5


def sum_scratch():
    return [pltpu.VMEM((4, 128, D), BF), pltpu.VMEM((6, 64, D), BF)]


def normed(values):
    centre = jnp.mean(values, axis=-1, keepdims=True)
    spread = values - centre
    inverse = lax.rsqrt(jnp.mean(spread * spread, axis=-1, keepdims=True) + EPSILON)
    return spread * inverse, inverse


def norm_pullback(upstream, norm, inverse, gain):
    scaled = upstream * gain
    first = jnp.mean(scaled, axis=-1, keepdims=True)
    second = jnp.mean(scaled * norm, axis=-1, keepdims=True)
    return inverse * (scaled - first - norm * second)


ANY = pl.BlockSpec(memory_space=pl.ANY)
IN_VMEM = pl.BlockSpec(memory_space=pltpu.VMEM)


def remote_call(body, name, cid, ins, outs, scratch, copies, locals_):
    return pl.pallas_call(
        body,
        name=name,
        in_specs=ins,
        out_specs=[spec for _, _, spec in outs],
        out_shape=[jax.ShapeDtypeStruct(shape, dtype) for shape, dtype, _ in outs],
        scratch_shapes=scratch
        + [
            pltpu.SemaphoreType.DMA((copies,)),
            pltpu.SemaphoreType.DMA((copies,)),
            pltpu.SemaphoreType.DMA((locals_,)),
        ],
        compiler_params=pltpu.CompilerParams(
            collective_id=cid, has_side_effects=True, vmem_limit_bytes=VMEM_LIMIT
        ),
    )


def assemble_vectors(weights, gains, bias, spots):
    for s in range(32):
        block = weights[s * 64 : s * 64 + 16, 2048:2176].astype(F32)
        for k in range(4):
            side = (k % 2) * 64
            gains[k : k + 1, s * 64 : s * 64 + 64] = block[k // 2 : k // 2 + 1, side : side + 64]
        spots[s : s + 1, :] = block[2:3, :]
    values = spots[...].astype(BF)
    shard = lax.broadcasted_iota(jnp.int32, (32, 64), 0)
    lane = lax.broadcasted_iota(jnp.int32, (32, 64), 1)
    total = jnp.zeros((24, 64), F32)
    for e in range(2):
        pick = jnp.where(lane == 2 * shard + e, 1.0, 0.0).astype(BF)
        total += tn(values, pick)[e * 24 : e * 24 + 24]
    for n in range(24):
        bias[0:1, n * 64 : n * 64 + 64] = total[n : n + 1]


def front_forward(shard, tokens, tables):
    def kernel(src, x_ref, t_ref, front, gains, low, out, weights, norm, blocks, bias, spots, ss, rs, ls):
        me = here()
        c, y, z, x = me
        net, local = Net(ss, rs), Local(ls)
        greet(y_peers(*me) + z_peers(*me) + core_peer(*me))
        gather = Gather(net, local, src, flat_rows(weights), me)
        gather.start()

        def centre(i, carry):
            rows = pl.ds(pl.multiple_of(i * 32, 32), 32)
            norm[rows, :] = normed(x_ref[rows, :].astype(F32))[0]
            return carry

        lax.fori_loop(0, 4, centre, 0)
        gather.near()
        lax.fori_loop(4, 8, centre, 0)
        gather.middle()
        lax.fori_loop(8, 16, centre, 0)
        gather.far()
        gather.finish()
        keep = local.copy(weights, front)
        assemble_vectors(weights, gains, bias, spots)

        def scale(i, carry):
            rows = pl.ds(pl.multiple_of(i * 32, 32), 32)
            low[rows, :] = (norm[rows, :] * gains[0:1, :] + gains[1:2, :]).astype(BF)
            return carry

        lax.fori_loop(0, 16, scale, 0)

        def project(t):
            columns = slice(t * 512, t * 512 + 512)
            for m in range(2):
                acc = jnp.dot(low[m * 256 : m * 256 + 256, :], weights[:, columns], preferred_element_type=F32)
                acc = acc + bias[:, columns]
                for h in range(4):
                    part = acc[:, h * 128 : h * 128 + 128]
                    if t < 2:
                        part = turn(part, t_ref[0], t_ref[1])
                    blocks[m, h, (t + 2) % 3] = part.astype(BF)

        along_y = lambda d: at(c, y + d, z, x)
        along_z = lambda d: at(c, y, z + d, x)
        kv = pl.ds(0, 2)

        def part(half):
            return kv if half is None else half

        rings = {}
        for k in range(4):
            rings[0, k] = RingGather(
                net, along_y, lambda d, half=None, k=k: out.at[0, up(y, d), up(z, k), part(half)]
            )
            rings[1, k] = RingGather(
                net, along_z, lambda d, half=None, k=k: out.at[1, up(y, k), up(z, d), part(half)]
            )
        project(1)
        project(2)
        first = {}
        for d in STEPS:
            first[0, d] = net.send(blocks.at[0, up(z, d), kv], out.at[0, y, z, kv], along_z(d))
            first[1, d] = net.send(blocks.at[1, up(y, d), kv], out.at[1, y, z, kv], along_y(d))
        rings[0, 0].start(blocks.at[0, z, kv])
        rings[1, 0].start(blocks.at[1, y, kv])
        project(0)
        last = []
        for d in STEPS:
            last.append(net.send(blocks.at[0, up(z, d), 2], out.at[0, y, z, 2], along_z(d)))
            last.append(net.send(blocks.at[1, up(y, d), 2], out.at[1, y, z, 2], along_y(d)))
        owns = [local.copy(blocks.at[0, z], out.at[0, y, z]), local.copy(blocks.at[1, y], out.at[1, y, z])]
        for d in STEPS:
            for m in range(2):
                first[m, d].wait_recv()
                ring = rings[m, 4 - d]
                ring.start(ring.out(0))
        for k in (0, 3, 1, 2):
            for m in range(2):
                rings[m, k].from_back()
                rings[m, k].from_ahead()
        for ring in rings.values():
            ring.arrive()
        for copy in last:
            copy.wait_recv()
        for copy in owns:
            copy.wait()
        keep.wait()
        net.finish()

    width = shard.shape[1]
    return remote_call(
        kernel,
        "front_forward",
        0,
        [ANY, IN_VMEM, IN_VMEM],
        [
            ((D, width), BF, ANY),
            ((4, D), F32, IN_VMEM),
            ((512, D), BF, IN_VMEM),
            ((2, 4, 4, 3, 256, 128), BF, ANY),
        ],
        [
            pltpu.VMEM((D, width), BF),
            pltpu.VMEM((512, D), F32),
            pltpu.VMEM((2, 4, 3, 256, 128), BF),
            pltpu.VMEM((1, 1536), F32),
            pltpu.VMEM((32, 128), F32),
        ],
        GATHER_COPIES + 12 + 8 * RING_GATHER,
        4,
    )(shard, tokens, tables)


class Swap:
    def __init__(self, net, local, src, out, me):
        c, y, z, x = me
        self.owns = [local.copy(src.at[0, z], out.at[0, z]), local.copy(src.at[1, y], out.at[1, y])]
        self.copies = []
        for d in STEPS:
            self.copies.append(net.send(src.at[0, up(z, d)], out.at[0, z], at(c, y, z + d, x)))
            self.copies.append(net.send(src.at[1, up(y, d)], out.at[1, y], at(c, y + d, z, x)))

    def arrive(self):
        for copy in self.copies:
            copy.wait_recv()
        for copy in self.owns:
            copy.wait()


SWAP_COPIES, SWAP_LOCALS = 6, 2
TURNED = pl.ds(1536, 512)


def middle_forward(heads, front, inputs, gains, shard):
    width = shard.shape[1]

    def kernel(
        heads, front, inputs, gains, shard, attended, hidden, second, weights,
        swapped, out_w, held, spare, base, low, ss, rs, ls,
    ):
        me = here()
        c, y, z, x = me
        net, local = Net(ss, rs), Local(ls)
        sums = SumX(net, local, None, held, spare, me)
        load = local.copy(front.at[:, TURNED], out_w)
        residual = local.copy(inputs.at[x], base)
        greet(y_peers(*me) + z_peers(*me) + core_peer(*me) + x_peers(*me))
        swap = Swap(net, local, heads, swapped, me)
        gather = Gather(net, local, shard, flat_rows(weights), me)
        gather.start()
        load.wait()
        swap.arrive()
        for m in range(2):
            for h in range(4):
                attended[m * 256 : m * 256 + 256, h * 128 : h * 128 + 128] = swapped[m, h]
        for q in range(4):
            held[q] = nt(attended[q * 128 : q * 128 + 128, :], out_w[...]).astype(BF)
        sums.start_held()
        gather.near()
        sums.middle()
        gather.middle()
        residual.wait()

        def step(rows, total):
            value = base[rows, :].astype(F32) + total
            hidden[rows, :] = value
            norm, _ = normed(value)
            low[rows, :] = (norm * gains[2:3, :] + gains[3:4, :]).astype(BF)

        sums.totals(step)
        sums.gather(low, second)
        gather.far()
        sums.gather_middle()
        gather.finish()
        sums.finish()
        net.finish()

    return remote_call(
        kernel,
        "middle_forward",
        3,
        [ANY, ANY, ANY, IN_VMEM, ANY],
        [
            ((512, 512), BF, IN_VMEM),
            ((128, D), F32, IN_VMEM),
            ((4, 128, D), BF, ANY),
            ((D, width), BF, ANY),
        ],
        [pltpu.VMEM((2, 4, 256, 128), BF), pltpu.VMEM((D, 512), BF)]
        + sum_scratch()
        + [pltpu.VMEM((128, D), BF), pltpu.VMEM((128, D), BF)],
        SWAP_COPIES + GATHER_COPIES + SUM_COPIES,
        SWAP_LOCALS + SUM_LOCALS + 3,
    )(heads, front, inputs, gains, shard)


def middle_backward(parts, cotangent, hidden, gains, attended, front, grads):
    widths = [g.shape[-1] for g in grads]
    count = len(grads)

    def kernel(parts, cotangent, hidden, gains, attended, front, *rest):
        grad_refs = rest[:count]
        dhidden, vectors, output_grad, upstream = rest[count : count + 4]
        outs = rest[count + 4 : 2 * count + 4]
        held, spare, base, low, hidden_low, out_w, blocks = rest[2 * count + 4 : 2 * count + 11]
        scratch = rest[2 * count + 11 : -3]
        ss, rs, ls = rest[-3:]
        me = here()
        c, y, z, x = me
        net, local = Net(ss, rs), Local(ls)
        sums = SumX(net, local, parts, held, spare, me)
        sums.load()
        upper = local.copy(cotangent.at[x], base)
        load = local.copy(front.at[:, TURNED], out_w)
        greet(y_peers(*me) + z_peers(*me) + core_peer(*me) + x_peers(*me))
        scatters = [
            Scatter(net, local, grad_refs[k], outs[k], scratch[8 * k : 8 * k + 8], me)
            for k in range(count)
        ]
        sums.start()
        for scatter in scatters:
            scatter.start()
        scatters[0].first()
        sums.middle()
        for scatter in scatters[1:]:
            scatter.first()
        scatters[0].first_middle()
        upper.wait()
        vectors[...] = jnp.zeros_like(vectors)

        def step(rows, dsecond):
            norm, inverse = normed(hidden[rows, :])
            value = base[rows, :].astype(F32) + norm_pullback(dsecond, norm, inverse, gains[2:3, :])
            dhidden[rows, :] = value
            low[rows, :] = value.astype(BF)
            vectors[0:1, :] += jnp.sum(dsecond * norm, axis=0, keepdims=True)
            vectors[1:2, :] += jnp.sum(dsecond, axis=0, keepdims=True)

        sums.totals(step)
        sums.gather(low, hidden_low)
        for scatter in scatters[1:]:
            scatter.first_middle()
        scatters[0].second()
        sums.gather_middle()
        for scatter in scatters[1:]:
            scatter.second()
        load.wait()
        sums.finish()
        for q in range(4):
            rows = slice((q % 2) * 128, (q % 2) * 128 + 128)
            result = jnp.dot(hidden_low[q], out_w[...], preferred_element_type=F32).astype(BF)
            for h in range(4):
                blocks[q // 2, h, rows, :] = result[:, h * 128 : h * 128 + 128]
        swap = Swap(net, local, blocks, upstream, me)
        for scatter in scatters:
            scatter.second_middle()
        whole = hidden_low[...].reshape(512, D)
        output_grad[...] = tn(whole, attended[...]).astype(BF)
        for scatter in scatters:
            scatter.third()
        swap.arrive()
        net.finish()

    scratch = sum_scratch() + [
        pltpu.VMEM((128, D), BF),
        pltpu.VMEM((128, D), BF),
        pltpu.VMEM((4, 128, D), BF),
        pltpu.VMEM((D, 512), BF),
        pltpu.VMEM((2, 4, 256, 128), BF),
    ]
    for width in widths:
        scratch += scatter_scratch(width)
    return remote_call(
        kernel,
        "middle_backward",
        4,
        [ANY, ANY, IN_VMEM, IN_VMEM, IN_VMEM, ANY] + [ANY] * count,
        [
            ((128, D), F32, IN_VMEM),
            ((2, D), F32, IN_VMEM),
            ((D, 512), BF, IN_VMEM),
            ((2, 4, 256, 128), BF, ANY),
        ]
        + [((64, width), F32, IN_VMEM) for width in widths],
        scratch,
        SUM_COPIES + SCATTER_COPIES * count + SWAP_COPIES,
        SUM_LOCALS + SWAP_LOCALS + 2 + count,
    )(parts, cotangent, hidden, gains, attended, front, *grads)


def collect_heads(dkv, dq, parts, hidden):
    def kernel(dkv, dq, parts, hidden, dproject, outputs, mine, got, summed, held, spare, low, ss, rs, ls):
        me = here()
        c, y, z, x = me
        net, local = Net(ss, rs), Local(ls)
        order = (1, 3, 2, 0)
        loads = [local.copy(dkv.at[m], mine.at[m]) for m in range(2)]
        sums = SumX(net, local, parts, held, spare, me)
        sums.load()
        greet(y_peers(*me) + z_peers(*me) + x_peers(*me))
        kv = pl.ds(0, 2)
        along_y = lambda d: at(c, y + d, z, x)
        along_z = lambda d: at(c, y, z + d, x)

        def add(total, term):
            def one(i, carry):
                rows = pl.ds(pl.multiple_of(i * 64, 64), 64)
                total[rows, :] = (total[rows, :].astype(F32) + term[rows, :].astype(F32)).astype(BF)
                return carry

            lax.fori_loop(0, 4, one, 0)

        rings = {}
        for k in order:
            rings[0, k] = RingSum(
                net, along_y, lambda d, half, k=k: mine.at[0, up(y, d), up(z, k), half], got.at[0, k], add
            )
            rings[1, k] = RingSum(
                net, along_z, lambda d, half, k=k: mine.at[1, up(y, k), up(z, d), half], got.at[1, k], add
            )
        sums.start()
        for copy in loads:
            copy.wait()
        for ring in rings.values():
            ring.start()
        lates = [
            local.copy(dq.at[0, z], dproject.at[0, z, 2]),
            local.copy(dq.at[1, y], dproject.at[1, y, 2]),
        ]
        two = []
        for d in STEPS:
            two.append(net.send(dq.at[0, up(z, d)], dproject.at[0, z, 2], along_z(d)))
            two.append(net.send(dq.at[1, up(y, d)], dproject.at[1, y, 2], along_y(d)))
        sums.middle()
        for ring in rings.values():
            ring.middle()

        def step(rows, total):
            low[rows, :] = (hidden[rows, :] + total).astype(BF)

        sums.totals(step)
        sums.gather(low, outputs)
        for k in order:
            for m, spot in ((0, z), (1, y)):
                ring = rings[m, k]
                ring.arrive()
                for half in range(2):
                    own, terms = ring.mine(0, half), ring.terms(half)

                    def total(i, carry, m=m, k=k, half=half, own=own, terms=terms):
                        rows = pl.ds(pl.multiple_of(i * 64, 64), 64)
                        value = own[rows, :].astype(F32)
                        for term in terms:
                            value += term[rows, :].astype(F32)
                        summed[m, k, half, rows, :] = value.astype(BF)
                        return carry

                    lax.fori_loop(0, 4, total, 0)
            if k:
                two.append(net.send(summed.at[0, k], dproject.at[0, z, kv], along_z(k)))
                two.append(net.send(summed.at[1, k], dproject.at[1, y, kv], along_y(k)))
            else:
                lates.append(local.copy(summed.at[0, 0], dproject.at[0, z, kv]))
                lates.append(local.copy(summed.at[1, 0], dproject.at[1, y, kv]))

        sums.gather_middle()
        for copy in two:
            copy.wait_recv()
        for copy in lates:
            copy.wait()
        sums.finish()
        net.finish()

    return remote_call(
        kernel,
        "collect_heads",
        6,
        [ANY, ANY, ANY, IN_VMEM],
        [((2, 4, 3, 256, 128), BF, ANY), ((4, 128, D), BF, ANY)],
        [
            pltpu.VMEM((2, 4, 4, 2, 256, 128), BF),
            pltpu.VMEM((2, 4, 6, 256, 128), BF),
            pltpu.VMEM((2, 4, 2, 256, 128), BF),
        ]
        + sum_scratch()
        + [pltpu.VMEM((128, D), BF)],
        8 * RING_SUM + 6 + 6 + SUM_COPIES,
        2 + 4 + SUM_LOCALS,
    )(dkv, dq, parts, hidden)


def last_backward(parts, inputs, dhidden, gains, vectors, grads):
    widths = [g.shape[-1] for g in grads]
    count = len(grads)

    def kernel(parts, inputs, dhidden, gains, vectors, *rest):
        grad_refs = rest[:count]
        input_grad, sums_out = rest[count : count + 2]
        outs = rest[count + 2 : 2 * count + 2]
        held, spare, base, low, small, got = rest[2 * count + 2 : 2 * count + 8]
        scratch = rest[2 * count + 8 : -3]
        ss, rs, ls = rest[-3:]
        me = here()
        c, y, z, x = me
        net, local = Net(ss, rs), Local(ls)
        sums = SumX(net, local, parts, held, spare, me)
        sums.load()
        residual = local.copy(inputs.at[x], base)
        greet(y_peers(*me) + z_peers(*me) + core_peer(*me) + x_peers(*me))
        scatters = [
            Scatter(net, local, grad_refs[k], outs[k], scratch[8 * k : 8 * k + 8], me)
            for k in range(count)
        ]
        sums.start()
        for scatter in scatters:
            scatter.start()
        sums.middle()
        for scatter in scatters:
            scatter.first()
        residual.wait()
        small[0, ...] = vectors[...]

        def step(rows, dfirst):
            norm, inverse = normed(base[rows, :].astype(F32))
            value = dhidden[rows, :] + norm_pullback(dfirst, norm, inverse, gains[0:1, :])
            low[rows, :] = value.astype(BF)
            small[0, 0:1, :] += jnp.sum(dfirst * norm, axis=0, keepdims=True)
            small[0, 1:2, :] += jnp.sum(dfirst, axis=0, keepdims=True)

        sums.totals(step)
        copies = [
            net.send(small.at[0], got.at[0, d - 1], at(c, y, z, x + d)) for d in STEPS
        ]
        sums.gather(low, input_grad)
        for scatter in scatters:
            scatter.first_middle()
        for copy in copies:
            copy.wait_recv()
        small[1, ...] = small[0, ...]
        for n in range(3):
            small[1, 0:4, :] += got[0, n, 0:4, :]
        copies = [
            net.send(small.at[1], got.at[1, d - 1], at(c, y + d, z, x)) for d in STEPS
        ]
        sums.gather_middle()
        for scatter in scatters:
            scatter.second()
        for copy in copies:
            copy.wait_recv()
        small[2, ...] = small[1, ...] + got[1, 0] + got[1, 1] + got[1, 2]
        copies = [
            net.send(small.at[2], got.at[2, d - 1], at(c, y, z + d, x)) for d in STEPS
        ]
        for scatter in scatters:
            scatter.second_middle()
        for copy in copies:
            copy.wait_recv()
        small[3, ...] = small[2, ...] + got[2, 0] + got[2, 1] + got[2, 2]
        copy = net.send(small.at[3], got.at[3, 0], at(1 - c, y, z, x))
        for scatter in scatters:
            scatter.third()
        copy.wait_recv()
        sums_out[...] = small[3, ...] + got[3, 0]
        sums.finish()
        net.finish()

    scratch = sum_scratch() + [
        pltpu.VMEM((128, D), BF),
        pltpu.VMEM((128, D), BF),
        pltpu.VMEM((4, 8, D), F32),
        pltpu.VMEM((4, 3, 8, D), F32),
    ]
    for width in widths:
        scratch += scatter_scratch(width)
    return remote_call(
        kernel,
        "last_backward",
        7,
        [ANY, ANY, IN_VMEM, IN_VMEM, IN_VMEM] + [ANY] * count,
        [((4, 128, D), BF, ANY), ((8, D), F32, IN_VMEM)]
        + [((64, width), F32, IN_VMEM) for width in widths],
        scratch,
        SUM_COPIES + 10 + SCATTER_COPIES * count,
        SUM_LOCALS + 1 + count,
    )(parts, inputs, dhidden, gains, vectors, *grads)


def turn(values, cosine, sine):
    lane = lax.rem(lax.broadcasted_iota(jnp.int32, values.shape, 1), HEAD_DIM)
    swapped = jnp.where(lane < ROT // 2, -pltpu.roll(values, 120, 1), pltpu.roll(values, 8, 1))
    return values * cosine + swapped * sine


def two_heads(block):
    lane = lax.broadcasted_iota(jnp.int32, (128, 128), 1)
    value = block.astype(F32)
    return jnp.concatenate(
        [jnp.where(lane < HEAD_DIM, value, 0.0), jnp.where(lane >= HEAD_DIM, value, 0.0)], axis=0
    )


def two_heads_t(block):
    feature = lax.broadcasted_iota(jnp.int32, (128, 128), 0)
    value = block.astype(F32).T
    return jnp.concatenate(
        [jnp.where(feature < HEAD_DIM, value, 0.0), jnp.where(feature >= HEAD_DIM, value, 0.0)], axis=1
    )


def one_block(stacked):
    feature = lax.broadcasted_iota(jnp.int32, (128, 128), 0)
    return jnp.where(feature < HEAD_DIM, stacked[:, :128], stacked[:, 128:]).T


def nt(left, right):
    return lax.dot_general(left, right, (((1,), (1,)), ((), ())), preferred_element_type=F32)


def unit_of(places, m, n):
    pair, rest = n // 9, lax.rem(n, 9)
    ahead = places[m * 8 + pair * 2] // (TILE // 128) + 1
    late = rest >= ahead
    block = pair * 2 + jnp.where(late, 1, 0)
    tile = rest - jnp.where(late, ahead, 0)
    return block, tile, places[m * 8 + block] * 128 - tile * TILE


def key_minus_query():
    return lax.broadcasted_iota(jnp.int32, (TILE, 256), 0) - lax.rem(
        lax.broadcasted_iota(jnp.int32, (TILE, 256), 1), 128
    )


def tile_of(t):
    return pl.ds(pl.multiple_of(t * TILE, TILE), TILE)


def lay_blocks(slots, lay):
    def some(n, carry):
        for k in range(4):
            b = n * 4 + k
            slot = slots[b]
            rows = pl.ds(pl.multiple_of(lax.rem(slot, 2) * 128, 128), 128)
            lay(slot // 2, rows, pl.ds(pl.multiple_of(b * 128, 128), 128))
        return carry

    lax.fori_loop(0, 8, some, 0)


UNITS_EACH = 36


def attend(slots, places, rows_of, spread):
    def kernel(
        slots, places, rows_of, k_ref, v_ref, q_ref, o_ref, full_ref, log_ref,
        keys, values_t, queries, scores_0, scores_1, weights_0, weights_1, results, sums,
    ):
        scores, weights = (scores_0, scores_1), (weights_0, weights_1)
        m = pl.program_id(0)

        def lay(slot, rows, to):
            keys[to, :] = k_ref[0, slot, 0, rows, :]
            values_t[:, to] = v_ref[0, slot, 0, rows, :].T

        lay_blocks(slots, lay)
        for b in range(8):
            row = rows_of[m * 4 + b // 2]
            block = q_ref[0, row, 0, (b % 2) * 128 : (b % 2) * 128 + 128, :]
            queries[b] = (two_heads_t(block) * 0.125).astype(BF)
        offset = key_minus_query()

        def multiply(n, odd):
            block, tile, _ = unit_of(places, m, n)
            scores[odd][...] = jnp.dot(
                keys[tile_of(tile), :], queries[block], preferred_element_type=F32
            )

        def soften(n, odd, top, total):
            block, tile, limit = unit_of(places, m, n)
            value = jnp.where(offset <= limit, scores[odd][...] * LOG2E, LOW)
            first = tile == 0
            top = jnp.where(first, LOW, top)
            new_top = jnp.maximum(top, jnp.max(value, axis=0, keepdims=True))
            exps = jnp.exp2(value - new_top)
            shrink = jnp.exp2(top - new_top)
            total = total * shrink + jnp.sum(exps, axis=0, keepdims=True)
            weights[odd][...] = exps.astype(BF)
            sums[block, 0:1, :] = new_top
            sums[block, 1:2, :] = total
            return new_top, total, shrink

        def gather(n, odd, shrink, acc):
            block, tile, _ = unit_of(places, m, n)
            acc = acc * shrink + jnp.dot(
                values_t[:, tile_of(tile)], weights[odd][...], preferred_element_type=F32
            )
            results[block] = acc
            return acc

        row = jnp.zeros((1, 256), F32)
        multiply(0, 0)
        multiply(1, 1)
        top, total, shrink = soften(0, 0, row, row)

        def step(k, carry):
            top, total, shrink, acc = carry
            for n, odd in ((2 * k + 1, 1), (2 * k + 2, 0)):
                multiply(n + 1, 1 - odd)
                acc = gather(n - 1, 1 - odd, shrink, acc)
                top, total, shrink = soften(n, odd, top, total)
            return top, total, shrink, acc

        carry = (top, total, shrink, jnp.zeros((128, 256), F32))
        top, total, shrink, acc = lax.fori_loop(0, UNITS_EACH // 2 - 1, step, carry)
        last = UNITS_EACH - 1
        acc = gather(last - 1, 0, shrink, acc)
        _, _, shrink = soften(last, 1, top, total)
        gather(last, 1, shrink, acc)
        for b in range(8):
            rows = slice((b % 2) * 128, (b % 2) * 128 + 128)
            total = sums[b, 1:2, :]
            result = one_block(results[b] / total)
            full_ref[0, b // 2, rows, :] = result
            o_ref[0, b // 2, rows, :] = result.astype(BF)
            log_ref[0, b : b + 1, :] = sums[b, 0:1, :] + jnp.log2(total)

    grid_spec = pltpu.PrefetchScalarGridSpec(
        num_scalar_prefetch=3,
        grid=(2,),
        in_specs=[
            pl.BlockSpec((1, 16, 1, 256, 128), lambda m, s, p, r: (m, 0, 0, 0, 0)),
            pl.BlockSpec((1, 16, 1, 256, 128), lambda m, s, p, r: (m, 0, 1, 0, 0)),
            pl.BlockSpec((1, 16, 1, 256, 128), lambda m, s, p, r: (m, 0, 2, 0, 0)),
        ],
        out_specs=[
            pl.BlockSpec((1, 4, 256, 128), lambda m, s, p, r: (m, 0, 0, 0)),
            pl.BlockSpec((1, 4, 256, 128), lambda m, s, p, r: (m, 0, 0, 0)),
            pl.BlockSpec((1, 8, 256), lambda m, s, p, r: (m, 0, 0)),
        ],
        scratch_shapes=[
            pltpu.VMEM((4096, 128), BF),
            pltpu.VMEM((128, 4096), BF),
            pltpu.VMEM((8, 128, 256), BF),
            pltpu.VMEM((TILE, 256), F32),
            pltpu.VMEM((TILE, 256), F32),
            pltpu.VMEM((TILE, 256), BF),
            pltpu.VMEM((TILE, 256), BF),
            pltpu.VMEM((8, 128, 256), F32),
            pltpu.VMEM((8, 8, 256), F32),
        ],
    )
    return pl.pallas_call(
        kernel,
        name="attend",
        grid_spec=grid_spec,
        out_shape=[
            jax.ShapeDtypeStruct((2, 4, 256, 128), BF),
            jax.ShapeDtypeStruct((2, 4, 256, 128), F32),
            jax.ShapeDtypeStruct((2, 8, 256), F32),
        ],
        compiler_params=pltpu.CompilerParams(vmem_limit_bytes=VMEM_LIMIT),
    )(slots, places, rows_of, spread, spread, spread)


def attend_back(slots, places, rows_of, spread, full, logs, upstream, tables):
    base, steps = tables

    def kernel(
        slots, places, rows_of, k_ref, v_ref, q_ref, full_ref, log_ref, up_ref, base_ref, steps_ref,
        dq_ref, dkv_ref,
        keys, keys_t, values, dkeys, dvalues, queries, queries_t, grads, grads_t, delta,
        scores_0, scores_1, dprobs_0, dprobs_1, probs_0, probs_1, dscores_0, dscores_1, results,
    ):
        scores, dprobs = (scores_0, scores_1), (dprobs_0, dprobs_1)
        probs_low, dscores = (probs_0, probs_1), (dscores_0, dscores_1)
        m = pl.program_id(0)

        def lay(slot, rows, to):
            block = k_ref[0, slot, 0, rows, :]
            keys[to, :] = block
            keys_t[:, to] = block.T
            values[to, :] = v_ref[0, slot, 0, rows, :]
            dkeys[to, :] = jnp.zeros((128, 128), F32)
            dvalues[to, :] = jnp.zeros((128, 128), F32)

        lay_blocks(slots, lay)
        for b in range(8):
            rows = slice((b % 2) * 128, (b % 2) * 128 + 128)
            block = q_ref[0, rows_of[m * 4 + b // 2], 0, rows, :]
            queries[b] = (two_heads(block) * 0.125).astype(BF)
            queries_t[b] = (two_heads_t(block) * 0.125).astype(BF)
            ups = up_ref[0, b // 2, rows, :]
            grads[b] = two_heads(ups).astype(BF)
            grads_t[b] = two_heads_t(ups).astype(BF)
            product = (ups.astype(F32) * full_ref[0, b // 2, rows, :]).T
            delta[b, 0:1, :128] = jnp.sum(product[:HEAD_DIM], axis=0, keepdims=True)
            delta[b, 0:1, 128:] = jnp.sum(product[HEAD_DIM:], axis=0, keepdims=True)
        offset = key_minus_query()

        def multiply(n, odd):
            block, tile, _ = unit_of(places, m, n)
            scores[odd][...] = jnp.dot(
                keys[tile_of(tile), :], queries_t[block], preferred_element_type=F32
            )
            dprobs[odd][...] = jnp.dot(
                values[tile_of(tile), :], grads_t[block], preferred_element_type=F32
            )

        def soften(n, odd):
            block, _, limit = unit_of(places, m, n)
            value = jnp.exp2(scores[odd][...] * LOG2E - log_ref[0, pl.ds(block, 1), :])
            value = jnp.where(offset <= limit, value, 0.0)
            probs_low[odd][...] = value.astype(BF)
            dscores[odd][...] = (
                value * (dprobs[odd][...] - delta[block, 0:1, :])
            ).astype(BF)

        def gather(n, odd, acc):
            block, tile, _ = unit_of(places, m, n)
            span = tile_of(tile)
            dvalues[span, :] += jnp.dot(probs_low[odd][...], grads[block], preferred_element_type=F32)
            dkeys[span, :] += jnp.dot(dscores[odd][...], queries[block], preferred_element_type=F32)
            acc = jnp.where(tile == 0, 0.0, acc) + jnp.dot(
                keys_t[:, span], dscores[odd][...], preferred_element_type=F32
            )
            results[block] = acc
            return acc

        multiply(0, 0)
        multiply(1, 1)
        soften(0, 0)

        def step(k, acc):
            for n, odd in ((2 * k + 1, 1), (2 * k + 2, 0)):
                multiply(n + 1, 1 - odd)
                acc = gather(n - 1, 1 - odd, acc)
                soften(n, odd)
            return acc

        last = UNITS_EACH - 1
        acc = lax.fori_loop(0, UNITS_EACH // 2 - 1, step, jnp.zeros((128, 256), F32))
        acc = gather(last - 1, 0, acc)
        soften(last, 1)
        gather(last, 1, acc)

        def turned_back(values, place):
            cosine, sine = base_ref[0], base_ref[1]
            far_cosine, far_sine = steps_ref[0, pl.ds(place, 1), :], steps_ref[1, pl.ds(place, 1), :]
            return turn(
                values,
                far_cosine * cosine - far_sine * sine,
                -(far_sine * cosine + far_cosine * sine),
            )

        for b in range(8):
            rows = slice((b % 2) * 128, (b % 2) * 128 + 128)
            dquery = one_block(results[b]) * 0.125
            dq_ref[0, b // 2, rows, :] = turned_back(dquery, places[m * 8 + b]).astype(BF)

        def flush(n, carry):
            for k in range(2):
                b = n * 2 + k
                slot = slots[b]
                rows = pl.ds(pl.multiple_of(lax.rem(slot, 2) * 128, 128), 128)
                to = pl.ds(pl.multiple_of(b * 128, 128), 128)
                dkv_ref[0, slot // 2, 0, rows, :] = turned_back(dkeys[to, :], b).astype(BF)
                dkv_ref[0, slot // 2, 1, rows, :] = dvalues[to, :].astype(BF)
            return carry

        lax.fori_loop(0, 16, flush, 0)

    grid_spec = pltpu.PrefetchScalarGridSpec(
        num_scalar_prefetch=3,
        grid=(2,),
        in_specs=[
            pl.BlockSpec((1, 16, 1, 256, 128), lambda m, s, p, r: (m, 0, 0, 0, 0)),
            pl.BlockSpec((1, 16, 1, 256, 128), lambda m, s, p, r: (m, 0, 1, 0, 0)),
            pl.BlockSpec((1, 16, 1, 256, 128), lambda m, s, p, r: (m, 0, 2, 0, 0)),
            pl.BlockSpec((1, 4, 256, 128), lambda m, s, p, r: (m, 0, 0, 0)),
            pl.BlockSpec((1, 8, 256), lambda m, s, p, r: (m, 0, 0)),
            pl.BlockSpec((1, 4, 256, 128), lambda m, s, p, r: (m, 0, 0, 0)),
            pl.BlockSpec((2, 128, 128), lambda m, s, p, r: (0, 0, 0)),
            pl.BlockSpec((2, 32, 128), lambda m, s, p, r: (0, 0, 0)),
        ],
        out_specs=[
            pl.BlockSpec((1, 4, 256, 128), lambda m, s, p, r: (m, 0, 0, 0)),
            pl.BlockSpec((1, 16, 2, 256, 128), lambda m, s, p, r: (m, 0, 0, 0, 0)),
        ],
        scratch_shapes=[
            pltpu.VMEM((4096, 128), BF),
            pltpu.VMEM((128, 4096), BF),
            pltpu.VMEM((4096, 128), BF),
            pltpu.VMEM((4096, 128), F32),
            pltpu.VMEM((4096, 128), F32),
            pltpu.VMEM((8, 256, 128), BF),
            pltpu.VMEM((8, 128, 256), BF),
            pltpu.VMEM((8, 256, 128), BF),
            pltpu.VMEM((8, 128, 256), BF),
            pltpu.VMEM((8, 8, 256), F32),
            pltpu.VMEM((TILE, 256), F32),
            pltpu.VMEM((TILE, 256), F32),
            pltpu.VMEM((TILE, 256), F32),
            pltpu.VMEM((TILE, 256), F32),
            pltpu.VMEM((TILE, 256), BF),
            pltpu.VMEM((TILE, 256), BF),
            pltpu.VMEM((TILE, 256), BF),
            pltpu.VMEM((TILE, 256), BF),
            pltpu.VMEM((8, 128, 256), F32),
        ],
    )
    return pl.pallas_call(
        kernel,
        name="attend_back",
        grid_spec=grid_spec,
        out_shape=[
            jax.ShapeDtypeStruct((2, 4, 256, 128), BF),
            jax.ShapeDtypeStruct((2, 16, 2, 256, 128), BF),
        ],
        compiler_params=pltpu.CompilerParams(vmem_limit_bytes=VMEM_LIMIT),
    )(slots, places, rows_of, spread, spread, spread, full, logs, upstream, base, steps)


def tn(left, right):
    return lax.dot_general(left, right, (((0,), (0,)), ((), ())), preferred_element_type=F32)


def feed_forward(second_low, dy, weights):
    def kernel(
        low_hbm, dy_hbm, w_hbm, branch, dsecond, gate_out, up_out, down_out,
        low, dys, gate_w, up_w, down_w, gate, up, dmixed, mixed, dgate, dup, chunks, sems, chunk_sems,
    ):
        def load(n, src, dst):
            copy = pltpu.make_async_copy(src, dst, sems.at[n])
            copy.start()
            return copy

        def columns(k):
            return w_hbm.at[:, pl.ds(k * UNITS, UNITS)]

        loads = [
            load(0, low_hbm, low),
            load(1, columns(0), gate_w),
            load(2, columns(1), up_w),
            load(3, dy_hbm, dys),
            load(4, columns(2), down_w),
        ]
        loads[0].wait()
        loads[1].wait()
        gate[...] = jnp.dot(low[...], gate_w[...], preferred_element_type=F32)
        loads[2].wait()
        up[...] = jnp.dot(low[...], up_w[...], preferred_element_type=F32)
        loads[3].wait()
        loads[4].wait()
        dmixed[...] = jnp.dot(dys[...], down_w[...], preferred_element_type=F32)

        def step(i, carry):
            rows = pl.ds(pl.multiple_of(i * 16, 16), 16)
            g, u, d = gate[rows, :], up[rows, :], dmixed[rows, :]
            s = jax.nn.sigmoid(g)
            silu = g * s
            mixed[rows, :] = (silu * u).astype(BF)
            dgate[rows, :] = (d * u * s * (1.0 + g * (1.0 - s))).astype(BF)
            dup[rows, :] = (d * silu).astype(BF)
            return carry

        lax.fori_loop(0, 32, step, 0)
        dsecond[...] = (nt(dgate[...], gate_w[...]) + nt(dup[...], up_w[...])).astype(BF)
        busy = {}
        n = 0
        for left, right, out in ((low, dgate, gate_out), (low, dup, up_out), (dys, mixed, down_out)):
            for k in range(4):
                rows = pl.ds(k * 512, 512)
                slot = n % 2
                if slot in busy:
                    busy[slot].wait()
                chunks[slot] = tn(left[:, rows], right[...]).astype(BF)
                busy[slot] = pltpu.make_async_copy(chunks.at[slot], out.at[rows, :], chunk_sems.at[slot])
                busy[slot].start()
                n += 1
        branch[...] = nt(mixed[...], down_w[...]).astype(BF)
        busy[0].wait()
        busy[1].wait()

    return pl.pallas_call(
        kernel,
        name="feed_forward",
        in_specs=[ANY, ANY, ANY],
        out_specs=[IN_VMEM, IN_VMEM, ANY, ANY, ANY],
        out_shape=[jax.ShapeDtypeStruct((512, D), BF)] * 2 + [jax.ShapeDtypeStruct((D, UNITS), BF)] * 3,
        scratch_shapes=[pltpu.VMEM((512, D), BF)] * 2
        + [pltpu.VMEM((D, UNITS), BF)] * 3
        + [pltpu.VMEM((512, UNITS), F32)] * 3
        + [pltpu.VMEM((512, UNITS), BF)] * 3
        + [
            pltpu.VMEM((2, 512, UNITS), BF),
            pltpu.SemaphoreType.DMA((5,)),
            pltpu.SemaphoreType.DMA((2,)),
        ],
        compiler_params=pltpu.CompilerParams(vmem_limit_bytes=VMEM_LIMIT),
    )(second_low, dy, weights)


def project_back(dproject, first_low, front):
    def kernel(dp_ref, low_ref, w_hbm, dfirst, grad_out, bias_out, wide, weights, chunks, sems, chunk_sems):
        load = pltpu.make_async_copy(w_hbm.at[:, pl.ds(0, 1536)], weights, sems.at[0])
        load.start()
        for m in range(2):
            for t in range(3):
                for h in range(4):
                    to = t * 512 + h * 128
                    wide[m * 256 : m * 256 + 256, to : to + 128] = dp_ref[m, h, (t + 2) % 3]
        bias_out[...] = jnp.sum(wide[...].astype(F32), axis=0, keepdims=True)
        busy = {}
        for k in range(4):
            rows = pl.ds(k * 512, 512)
            slot = k % 2
            if slot in busy:
                busy[slot].wait()
            chunks[slot] = tn(low_ref[:, rows], wide[...]).astype(BF)
            busy[slot] = pltpu.make_async_copy(chunks.at[slot], grad_out.at[rows, :], chunk_sems.at[slot])
            busy[slot].start()
        load.wait()
        dfirst[...] = nt(wide[...], weights[...]).astype(BF)
        busy[0].wait()
        busy[1].wait()

    return pl.pallas_call(
        kernel,
        name="project_back",
        in_specs=[IN_VMEM, IN_VMEM, ANY],
        out_specs=[IN_VMEM, ANY, IN_VMEM],
        out_shape=[
            jax.ShapeDtypeStruct((512, D), BF),
            jax.ShapeDtypeStruct((D, 1536), BF),
            jax.ShapeDtypeStruct((1, 1536), F32),
        ],
        scratch_shapes=[
            pltpu.VMEM((512, 1536), BF),
            pltpu.VMEM((D, 1536), BF),
            pltpu.VMEM((2, 512, 1536), BF),
            pltpu.SemaphoreType.DMA((1,)),
            pltpu.SemaphoreType.DMA((2,)),
        ],
        compiler_params=pltpu.CompilerParams(vmem_limit_bytes=VMEM_LIMIT),
    )(dproject, first_low, front)


def rotary_tables(places):
    lane = np.arange(128) % HEAD_DIM
    power = 10000.0 ** (-jnp.arange(0, ROT, 2, dtype=F32) / ROT)
    hot = (lane[None, :] % (ROT // 2) == np.arange(ROT // 2)[:, None]) & (lane[None, :] < ROT)
    frequency = jnp.sum(jnp.where(hot, power[:, None], 0.0), axis=0)
    angles = places.astype(F32)[:, None] * frequency[None, :]
    return jnp.stack([jnp.cos(angles), jnp.sin(angles)])


def angle_tables():
    near = jnp.arange(128, dtype=jnp.int32)
    return rotary_tables(near), rotary_tables(near[:32] * 128)


def body(
    inputs,
    cotangent,
    group_place,
    attend_gain,
    attend_shift,
    project_weight,
    project_bias,
    output_weight,
    mixer_gain,
    mixer_shift,
    gate_weight,
    up_weight,
    down_weight,
):
    ctx = lax.axis_index("ctx")
    y, z = ctx // 4, lax.rem(ctx, 4)
    shard_index = lax.axis_index("dp") * 16 + ctx

    blocks = jnp.arange(32, dtype=jnp.int32)
    hits = group_place[None, :] == blocks[:, None]
    slots = jnp.sum(jnp.where(hits, blocks[None, :], 0), axis=1)
    four = jnp.arange(4, dtype=jnp.int32)
    rows_of = jnp.concatenate([y * 4 + four, four * 4 + z])
    held_slots = (rows_of[:, None] * 2 + jnp.arange(2, dtype=jnp.int32)[None, :]).reshape(16)
    chosen = held_slots[:, None] == blocks[None, :]
    places = jnp.sum(jnp.where(chosen, group_place[None, :], 0), axis=1)
    own_slots = ctx * 2 + jnp.arange(2, dtype=jnp.int32)
    own_blocks = jnp.sum(
        jnp.where(own_slots[:, None] == blocks[None, :], group_place[None, :], 0), axis=1
    )
    own_places = (own_blocks[:, None] * 128 + jnp.arange(128, dtype=jnp.int32)[None, :]).reshape(256)
    own_tables = rotary_tables(own_places)
    all_tables = angle_tables()

    vectors = jnp.concatenate(
        [
            attend_gain,
            attend_shift,
            mixer_gain,
            mixer_shift,
            project_bias.transpose(2, 0, 1).reshape(48),
            jnp.zeros((80,), BF),
        ]
    ).reshape(3, 128)
    front_shard = jnp.concatenate(
        [project_weight.reshape(64, 1536), output_weight.T, jnp.pad(vectors, ((0, 61), (0, 0)))], axis=1
    )
    back_shard = jnp.concatenate([gate_weight, up_weight, down_weight.T], axis=1)

    tokens = inputs.reshape(512, D)
    quarters = inputs.reshape(4, 128, D)
    front, gains, first_low, spread = front_forward(front_shard, tokens, own_tables)
    spread = spread.reshape(2, 16, 3, 256, 128)
    attended_heads, attended_full, logs = attend(slots, places, rows_of, spread)
    attended_low, hidden, second_low, back = middle_forward(
        attended_heads, front, quarters, gains, back_shard
    )

    mixer_part, second_part, gate_grad, up_grad, down_grad = feed_forward(
        second_low.reshape(512, D), cotangent.reshape(512, D), back
    )

    def shards(grad):
        return grad.reshape(2, 4, 4, 64, grad.shape[1])

    dhidden, mixer_vectors, output_grad, upstream, gate_grad, up_grad, down_grad = middle_backward(
        second_part.reshape(4, 128, D),
        cotangent.reshape(4, 128, D),
        hidden,
        gains,
        attended_low,
        front,
        [shards(gate_grad), shards(up_grad), shards(down_grad)],
    )

    dq, dkv = attend_back(
        slots, places, rows_of, spread, attended_full, logs, upstream, all_tables
    )
    dproject, outputs = collect_heads(dkv.reshape(2, 4, 4, 2, 256, 128), dq, mixer_part.reshape(4, 128, D), hidden)
    first_part, project_grad, bias_part = project_back(dproject, first_low, front)
    small = jnp.concatenate(
        [
            jnp.zeros((2, D), F32),
            mixer_vectors,
            jnp.pad(bias_part, ((0, 0), (0, D - 1536))),
            jnp.zeros((3, D), F32),
        ]
    )
    input_grad, small, project_grad, output_grad = last_backward(
        first_part.reshape(4, 128, D),
        quarters,
        dhidden,
        gains,
        small,
        [shards(project_grad), shards(output_grad)],
    )
    own = lax.dynamic_slice(small, (0, shard_index * 64), (4, 64))
    bias_grad = lax.dynamic_slice(
        small[4, :1536].reshape(3, 8, 64), (0, 0, shard_index * 2), (3, 8, 2)
    )
    shape = inputs.shape
    return (
        outputs.reshape(shape),
        input_grad.reshape(shape),
        own[0],
        own[1],
        project_grad.reshape(64, 3, 512),
        bias_grad,
        output_grad.T,
        own[2],
        own[3],
        gate_grad,
        up_grad,
        down_grad.T,
    )


def solution(mesh):
    weight = ("dp", "ctx")
    rows = P(None, "dp", "ctx", None)
    vector = P(weight)
    matrix = P(weight, "tensor")
    turned = P("tensor", weight)
    project = P(weight, None, "tensor")
    bias = P(None, "tensor", weight)
    params = (vector, vector, project, bias, turned, vector, vector, matrix, matrix, turned)
    return jax.shard_map(
        body,
        mesh=mesh,
        in_specs=(rows, rows, P()) + params,
        out_specs=(rows, rows) + params,
        check_vma=False,
    )
```

```python
import functools

import jax
import jax.numpy as jnp
import numpy as np
from jax import lax
from jax.experimental import pallas as pl
from jax.experimental.pallas import tpu as pltpu
from jax.sharding import PartitionSpec as P

MESH = pl.DeviceIdType.MESH
D = 2048
UNITS = 1408
HEAD_DIM = 64
ROT = 16
EPSILON = 1e-05
LOG2E = 1.4426950408889634
LOW = -1e30
TILE = 512
VMEM_LIMIT = 58 * 2**20
STEPS = (1, 3, 2)
BF = jnp.bfloat16
F32 = jnp.float32


def here():
    ctx = lax.axis_index("ctx")
    return (lax.axis_index("dp"), ctx // 4, lax.rem(ctx, 4), lax.axis_index("tensor"))


def at(c, y, z, x):
    return (c, lax.rem(y, 4) * 4 + lax.rem(z, 4), lax.rem(x, 4))


def up(i, d):
    return lax.rem(i + d, 4)


def down(i, d):
    return lax.rem(i + 4 - d, 4)


class Net:
    def __init__(self, send_sems, recv_sems):
        self.send_sems, self.recv_sems = send_sems, recv_sems
        self.sent, self.gone = [], set()

    def send(self, src, dst, device):
        n = len(self.sent)
        copy = pltpu.make_async_remote_copy(
            src_ref=src,
            dst_ref=dst,
            send_sem=self.send_sems.at[n],
            recv_sem=self.recv_sems.at[n],
            device_id=device,
            device_id_type=MESH,
        )
        copy.start()
        self.sent.append(copy)
        return copy

    def finish(self):
        for n, copy in enumerate(self.sent):
            if n not in self.gone:
                copy.wait_send()

    def wait_sent(self, copy):
        copy.wait_send()
        self.gone.add([other is copy for other in self.sent].index(True))


class Local:
    def __init__(self, sems):
        self.sems, self.n = sems, 0

    def copy(self, src, dst):
        copy = pltpu.make_async_copy(src, dst, self.sems.at[self.n])
        copy.start()
        self.n += 1
        return copy


def greet(peers):
    barrier = pltpu.get_barrier_semaphore()
    for peer in peers:
        pl.semaphore_signal(barrier, inc=1, device_id=peer, device_id_type=MESH)
    pl.semaphore_wait(barrier, len(peers))


def y_peers(c, y, z, x):
    return [at(c, y + d, z, x) for d in (1, 2, 3)]


def z_peers(c, y, z, x):
    return [at(c, y, z + d, x) for d in (1, 2, 3)]


def x_peers(c, y, z, x):
    return [at(c, y, z, x + d) for d in (1, 2, 3)]


def core_peer(c, y, z, x):
    return [at(1 - c, y, z, x)]


class RingSum:
    def __init__(self, net, device, mine, spare, add):
        self.net, self.device, self.mine, self.spare, self.add = net, device, mine, spare, add

    def start(self):
        self.start_far()
        self.start_near()

    def start_far(self):
        send, mine, spare = self.net.send, self.mine, self.spare
        ahead, back = self.device(1), self.device(3)
        self.far_ahead = send(mine(2, 0), spare.at[0], ahead)
        self.far_back = send(mine(2, 1), spare.at[1], back)

    def start_near(self):
        send, mine, spare = self.net.send, self.mine, self.spare
        ahead, back = self.device(1), self.device(3)
        self.near = [send(mine(1, 1), spare.at[3], ahead), send(mine(3, 0), spare.at[2], back)]

    def middle(self):
        send, spare = self.net.send, self.spare
        self.far_ahead.wait_recv()
        self.add(spare.at[0], self.mine(1, 0))
        self.near.append(send(spare.at[0], spare.at[4], self.device(1)))
        self.far_back.wait_recv()
        self.add(spare.at[1], self.mine(3, 1))
        self.near.append(send(spare.at[1], spare.at[5], self.device(3)))

    def arrive(self):
        for copy in self.near:
            copy.wait_recv()

    def sent(self):
        for copy in [self.far_ahead, self.far_back] + self.near:
            self.net.wait_sent(copy)

    def terms(self, half):
        return [self.spare.at[4 if half == 0 else 3], self.spare.at[2 if half == 0 else 5]]


RING_SUM = 6


class RingGather:
    def __init__(self, net, device, out):
        self.net, self.device, self.out = net, device, out

    def start(self, block):
        self.ahead = self.net.send(block, self.out(0), self.device(1))
        self.back = self.net.send(block, self.out(0), self.device(3))

    def from_back(self):
        self.ahead.wait_recv()
        piece = self.out(3, 0)
        self.far_ahead = self.net.send(piece, piece, self.device(1))

    def from_ahead(self):
        self.back.wait_recv()
        piece = self.out(1, 1)
        self.far_back = self.net.send(piece, piece, self.device(3))

    def arrive(self):
        self.far_ahead.wait_recv()
        self.far_back.wait_recv()


RING_GATHER = 4


class Gather:
    def __init__(self, net, local, src, place, me):
        self.net, self.local, self.src, self.place, self.me = net, local, src, place, me
        self.core = []
        c, y, z, x = me
        along_y = lambda d: at(c, y + d, z, x)
        along_z = lambda d: at(c, y, z + d, x)

        def spot(far_y, far_z, first, half):
            if half is None:
                return place(c, up(y, far_y), up(z, far_z), first, 32)
            return place(c, up(y, far_y), up(z, far_z), first + 16 * half, 16)

        self.one = (
            RingGather(net, along_y, lambda d, half=None: spot(d, 0, 0, half)),
            RingGather(net, along_z, lambda d, half=None: spot(0, d, 32, half)),
        )
        self.two = {}
        for k in range(4):
            self.two[0, k] = RingGather(net, along_z, lambda d, half=None, k=k: spot(k, d, 0, half))
            self.two[1, k] = RingGather(net, along_y, lambda d, half=None, k=k: spot(d, k, 32, half))

    def hand_over(self, piece):
        c, y, z, x = self.me
        self.core.append(self.net.send(piece, piece, at(1 - c, y, z, x)))

    def start(self):
        c, y, z, x = self.me
        src, own = self.src, self.place(c, y, z, 0, 64)
        self.own = self.local.copy(src, own)
        halves = (src.at[pl.ds(0, 32)], src.at[pl.ds(32, 32)])
        for way in range(2):
            self.one[way].start(halves[way])
        for way in range(2):
            self.two[way, 0].start(halves[way])
        self.core.append(self.net.send(src, own, at(1 - c, y, z, x)))

    def near(self):
        for way in range(2):
            self.one[way].from_back()
            self.two[way, 3].start(self.one[way].out(3))
        for way in range(2):
            self.one[way].from_ahead()
            self.two[way, 1].start(self.one[way].out(1))
        for k in (3, 1):
            for way in range(2):
                self.hand_over(self.one[way].out(k))

    def middle(self):
        self.pass_on(0)
        for way in range(2):
            self.one[way].arrive()
            self.two[way, 2].start(self.one[way].out(2))
            self.hand_over(self.one[way].out(2))

    def pass_on(self, k):
        for way in range(2):
            self.two[way, k].from_back()
            self.two[way, k].from_ahead()
            self.hand_over(self.two[way, k].out(3))
            self.hand_over(self.two[way, k].out(1))

    def far(self):
        for k in (3, 1, 2):
            self.pass_on(k)
        for k in (0, 3, 1, 2):
            for way in range(2):
                self.two[way, k].arrive()
                self.hand_over(self.two[way, k].out(2))

    def finish(self):
        for copy in self.core:
            copy.wait_recv()
        self.own.wait()


def flat_rows(ref):
    def place(c, y, z, first, count):
        return ref.at[pl.ds(pl.multiple_of(((c * 4 + y) * 4 + z) * 64 + first, 16), count)]

    return place


GATHER_COPIES = 10 * RING_GATHER + 31


def scatter_scratch(width):
    return [
        pltpu.VMEM((4, 4, 64, width), BF),
        pltpu.VMEM((4, 4, 64, width), BF),
        pltpu.VMEM((6, 4, 16, width), BF),
        pltpu.VMEM((6, 4, 16, width), BF),
        pltpu.VMEM((4, 32, width), BF),
        pltpu.VMEM((4, 32, width), BF),
        pltpu.VMEM((6, 16, width), BF),
        pltpu.VMEM((6, 16, width), BF),
    ]


SCATTER_COPIES = 1 + 4 * RING_SUM


def add_blocks(total, term):
    if len(total.shape) == 2:
        total[...] = (total[...].astype(F32) + term[...].astype(F32)).astype(BF)
        return

    def one(i, carry):
        total[i] = (total[i].astype(F32) + term[i].astype(F32)).astype(BF)
        return carry

    lax.fori_loop(0, total.shape[0], one, 0)


class Scatter:
    def __init__(self, net, local, grads, out, scratch, me):
        self.net, self.local, self.grads, self.out, self.me = net, local, grads, out, me
        (held, self.other, one_a, one_b, self.sum_a, self.sum_b, two_a, two_b) = scratch
        self.held = held
        c, y, z, x = me
        along_y = lambda d: at(c, y + d, z, x)
        along_z = lambda d: at(c, y, z + d, x)
        self.one_a = RingSum(
            net, along_z, lambda d, half: held.at[:, up(z, d), pl.ds(16 * half, 16)], one_a, add_blocks
        )
        self.one_b = RingSum(
            net, along_y, lambda d, half: held.at[up(y, d), :, pl.ds(32 + 16 * half, 16)], one_b, add_blocks
        )
        self.two_a = RingSum(
            net, along_y, lambda d, half: self.sum_a.at[up(y, d), pl.ds(16 * half, 16)], two_a, add_blocks
        )
        self.two_b = RingSum(
            net, along_z, lambda d, half: self.sum_b.at[up(z, d), pl.ds(16 * half, 16)], two_b, add_blocks
        )

    def start(self):
        c, y, z, x = self.me
        self.own = self.local.copy(self.grads.at[c], self.held)
        self.zero = self.net.send(self.grads.at[1 - c], self.other, at(1 - c, y, z, x))

    def send_filled(self, block):
        c, y, z, x = self.me
        self.own = None
        self.zero = self.net.send(block, self.other, at(1 - c, y, z, x))

    def first(self):
        if self.own is not None:
            self.own.wait()
        self.zero.wait_recv()
        held, other = self.held, self.other

        def add(i, carry):
            for q in range(4):
                rows = pl.ds(q * 16, 16)
                held[i // 4, lax.rem(i, 4), rows, :] = (
                    held[i // 4, lax.rem(i, 4), rows, :].astype(F32)
                    + other[i // 4, lax.rem(i, 4), rows, :].astype(F32)
                ).astype(BF)
            return carry

        lax.fori_loop(0, 16, add, 0)
        self.one_a.start()
        self.one_b.start()

    def first_middle(self):
        self.one_a.middle()
        self.one_b.middle()

    def second(self):
        for one, two, total in ((self.one_a, self.two_a, self.sum_a), (self.one_b, self.two_b, self.sum_b)):
            one.arrive()
            for half in range(2):
                own, terms = one.mine(0, half), one.terms(half)

                def add(i, carry, half=half, own=own, terms=terms, total=total):
                    value = own[i].astype(F32)
                    for term in terms:
                        value += term[i].astype(F32)
                    total[i, pl.ds(16 * half, 16), :] = value.astype(BF)
                    return carry

                lax.fori_loop(0, 4, add, 0)
            two.start()

    def second_middle(self):
        self.two_a.middle()
        self.two_b.middle()

    def third(self):
        for first, two in ((0, self.two_a), (32, self.two_b)):
            two.arrive()
            for half in range(2):
                value = two.mine(0, half)[...].astype(F32)
                for term in two.terms(half):
                    value += term[...].astype(F32)
                self.out[pl.ds(first + 16 * half, 16), :] = value


def quarters_of(net, out, me):
    c, y, z, x = me

    def piece(d, half=None):
        return out.at[up(x, d)] if half is None else out.at[up(x, d), pl.ds(64 * half, 64)]

    return RingGather(net, lambda d: at(c, y, z, x + d), piece)


class SumX:
    def __init__(self, net, local, parts, held, spare, me):
        c, y, z, x = me
        self.local, self.parts, self.held, self.x, self.net, self.me = local, parts, held, x, net, me
        self.along = lambda d: at(c, y, z, x + d)
        self.ring = RingSum(
            net, self.along, lambda d, half: held.at[up(x, d), pl.ds(64 * half, 64)], spare, self.add
        )

    def add(self, total, term):
        def one(i, carry):
            rows = pl.ds(pl.multiple_of(i * 16, 16), 16)
            total[rows, :] = (total[rows, :].astype(F32) + term[rows, :].astype(F32)).astype(BF)
            return carry

        lax.fori_loop(0, 4, one, 0)

    def load(self):
        self.loads = [self.local.copy(self.parts.at[up(self.x, d)], self.held.at[up(self.x, d)]) for d in (2, 1, 3, 0)]

    def start(self):
        for copy in self.loads:
            copy.wait()
        self.ring.start()

    def start_held(self):
        self.ring.start()

    def middle(self):
        self.ring.middle()

    def totals(self, step):
        self.ring.arrive()
        for half in range(2):
            terms = self.ring.terms(half)

            def loop(i, carry, half=half, terms=terms):
                rows = pl.ds(pl.multiple_of(i * 32, 32), 32)
                own = pl.ds(pl.multiple_of(64 * half + i * 32, 32), 32)
                value = self.held[self.x, own, :].astype(F32)
                for term in terms:
                    value += term[rows, :].astype(F32)
                step(own, value)
                return carry

            lax.fori_loop(0, 2, loop, 0)

    def gather(self, block, out):
        x = self.x
        self.back = quarters_of(self.net, out, self.me)
        self.mine = self.local.copy(block, out.at[x])
        self.back.start(block)

    def gather_middle(self):
        self.back.from_back()
        self.back.from_ahead()

    def finish(self):
        self.mine.wait()
        self.back.arrive()


SUM_COPIES = RING_SUM + RING_GATHER
SUM_LOCALS = 5


def sum_scratch():
    return [pltpu.VMEM((4, 128, D), BF), pltpu.VMEM((6, 64, D), BF)]


def normed(values):
    centre = jnp.mean(values, axis=-1, keepdims=True)
    spread = values - centre
    inverse = lax.rsqrt(jnp.mean(spread * spread, axis=-1, keepdims=True) + EPSILON)
    return spread * inverse, inverse


def norm_pullback(upstream, norm, inverse, gain):
    scaled = upstream * gain
    first = jnp.mean(scaled, axis=-1, keepdims=True)
    second = jnp.mean(scaled * norm, axis=-1, keepdims=True)
    return inverse * (scaled - first - norm * second)


ANY = pl.BlockSpec(memory_space=pl.ANY)
IN_VMEM = pl.BlockSpec(memory_space=pltpu.VMEM)
IN_SMEM = pl.BlockSpec(memory_space=pltpu.SMEM)


def remote_call(body, name, cid, ins, outs, scratch, copies, locals_):
    return pl.pallas_call(
        body,
        name=name,
        in_specs=ins,
        out_specs=[spec for _, _, spec in outs],
        out_shape=[jax.ShapeDtypeStruct(shape, dtype) for shape, dtype, _ in outs],
        scratch_shapes=scratch
        + [
            pltpu.SemaphoreType.DMA((copies,)),
            pltpu.SemaphoreType.DMA((copies,)),
            pltpu.SemaphoreType.DMA((locals_,)),
        ],
        compiler_params=pltpu.CompilerParams(
            collective_id=cid, has_side_effects=True, vmem_limit_bytes=VMEM_LIMIT
        ),
    )


def assemble_vectors(weights, gains, bias, spots):
    for s in range(32):
        block = weights[s * 64 : s * 64 + 16, 2048:2176].astype(F32)
        gains[0:4, s * 64 : s * 64 + 64] = block[0:4, :64]
        spots[s : s + 1, :] = block[4:5, :]
    values = spots[...].astype(BF)
    head = lax.broadcasted_iota(jnp.int32, (32, 128), 0)
    held = lax.broadcasted_iota(jnp.int32, (32, 128), 1)
    shard = lax.broadcasted_iota(jnp.int32, (32, 64), 0)
    lane = lax.broadcasted_iota(jnp.int32, (32, 64), 1)
    total = jnp.zeros((32, 64), F32)
    for e in range(2):
        pick = jnp.where((held == 2 * head + e) & (head < 24), 1.0, 0.0).astype(BF)
        spread = jnp.where(lane == 2 * shard + e, 1.0, 0.0).astype(BF)
        total += jnp.dot(nt(pick, values).astype(BF), spread, preferred_element_type=F32)
    for n in range(24):
        bias[0:1, n * 64 : n * 64 + 64] = total[n : n + 1]


def front_forward(shard, tokens, group_place, base, steps):
    def kernel(
        src, x_ref, group_ref, base_ref, steps_ref, front, gains, low, out,
        weights, norm, blocks, bias, spots, turns, ss, rs, ls,
    ):
        me = here()
        c, y, z, x = me
        net, local = Net(ss, rs), Local(ls)
        greet(y_peers(*me) + z_peers(*me) + core_peer(*me))
        gather = Gather(net, local, src, flat_rows(weights), me)
        gather.start()
        for n in range(2):
            rows = slice(n * 128, n * 128 + 128)
            cosine, sine = turn_tables(base_ref, steps_ref, group_ref[(y * 4 + z) * 2 + n])
            turns[0, rows, :] = cosine
            turns[1, rows, :] = sine

        def centre(i, carry):
            rows = pl.ds(pl.multiple_of(i * 32, 32), 32)
            norm[rows, :] = normed(x_ref[rows, :].astype(F32))[0]
            return carry

        lax.fori_loop(0, 4, centre, 0)
        gather.near()
        lax.fori_loop(4, 8, centre, 0)
        gather.middle()
        lax.fori_loop(8, 16, centre, 0)
        gather.far()
        gather.finish()
        keep = local.copy(weights, front)
        assemble_vectors(weights, gains, bias, spots)

        def scale(i, carry):
            rows = pl.ds(pl.multiple_of(i * 32, 32), 32)
            low[rows, :] = (norm[rows, :] * gains[0:1, :] + gains[1:2, :]).astype(BF)
            return carry

        lax.fori_loop(0, 16, scale, 0)

        def project(t):
            columns = slice(t * 512, t * 512 + 512)
            for m in range(2):
                acc = jnp.dot(low[m * 256 : m * 256 + 256, :], weights[:, columns], preferred_element_type=F32)
                acc = acc + bias[:, columns]
                for h in range(4):
                    part = acc[:, h * 128 : h * 128 + 128]
                    if t < 2:
                        part = turn(part, turns[0], turns[1])
                    blocks[m, h, (t + 2) % 3] = part.astype(BF)

        along_y = lambda d: at(c, y + d, z, x)
        along_z = lambda d: at(c, y, z + d, x)
        kv = pl.ds(0, 2)

        def part(half):
            return kv if half is None else half

        rings = {}
        for k in range(4):
            rings[0, k] = RingGather(
                net, along_y, lambda d, half=None, k=k: out.at[0, up(y, d), up(z, k), part(half)]
            )
            rings[1, k] = RingGather(
                net, along_z, lambda d, half=None, k=k: out.at[1, up(y, k), up(z, d), part(half)]
            )
        project(1)
        project(2)
        first = {}
        for d in STEPS:
            first[0, d] = net.send(blocks.at[0, up(z, d), kv], out.at[0, y, z, kv], along_z(d))
            first[1, d] = net.send(blocks.at[1, up(y, d), kv], out.at[1, y, z, kv], along_y(d))
        rings[0, 0].start(blocks.at[0, z, kv])
        rings[1, 0].start(blocks.at[1, y, kv])
        project(0)
        last = []
        for d in STEPS:
            last.append(net.send(blocks.at[0, up(z, d), 2], out.at[0, y, z, 2], along_z(d)))
            last.append(net.send(blocks.at[1, up(y, d), 2], out.at[1, y, z, 2], along_y(d)))
        owns = [local.copy(blocks.at[0, z], out.at[0, y, z]), local.copy(blocks.at[1, y], out.at[1, y, z])]
        for d in STEPS:
            for m in range(2):
                first[m, d].wait_recv()
                ring = rings[m, 4 - d]
                ring.start(ring.out(0))
        for k in (0, 3, 1, 2):
            for m in range(2):
                rings[m, k].from_back()
                rings[m, k].from_ahead()
        for ring in rings.values():
            ring.arrive()
        for copy in last:
            copy.wait_recv()
        for copy in owns:
            copy.wait()
        keep.wait()
        net.finish()

    width = shard.shape[1]
    return remote_call(
        kernel,
        "front_forward",
        0,
        [ANY, IN_VMEM, IN_SMEM, IN_VMEM, IN_VMEM],
        [
            ((D, width), BF, ANY),
            ((4, D), F32, IN_VMEM),
            ((512, D), BF, IN_VMEM),
            ((2, 4, 4, 3, 256, 128), BF, ANY),
        ],
        [
            pltpu.VMEM((D, width), BF),
            pltpu.VMEM((512, D), F32),
            pltpu.VMEM((2, 4, 3, 256, 128), BF),
            pltpu.VMEM((1, 1536), F32),
            pltpu.VMEM((32, 128), F32),
            pltpu.VMEM((2, 256, 128), F32),
        ],
        GATHER_COPIES + 12 + 8 * RING_GATHER,
        4,
    )(shard, tokens, group_place, base, steps)


class Swap:
    def __init__(self, net, local, src, out, me):
        c, y, z, x = me
        self.owns = [local.copy(src.at[0, z], out.at[0, z]), local.copy(src.at[1, y], out.at[1, y])]
        self.copies = []
        for d in STEPS:
            self.copies.append(net.send(src.at[0, up(z, d)], out.at[0, z], at(c, y, z + d, x)))
            self.copies.append(net.send(src.at[1, up(y, d)], out.at[1, y], at(c, y + d, z, x)))

    def arrive(self):
        for copy in self.copies:
            copy.wait_recv()
        for copy in self.owns:
            copy.wait()


SWAP_COPIES, SWAP_LOCALS = 6, 2
TURNED = pl.ds(1536, 512)


def middle_forward(heads, front, inputs, gains, shard):
    width = shard.shape[1]

    def kernel(
        heads, front, inputs, gains, shard, attended, hidden, second, weights,
        swapped, out_w, held, spare, base, low, ss, rs, ls,
    ):
        me = here()
        c, y, z, x = me
        net, local = Net(ss, rs), Local(ls)
        sums = SumX(net, local, None, held, spare, me)
        load = local.copy(front.at[:, TURNED], out_w)
        residual = local.copy(inputs.at[x], base)
        greet(y_peers(*me) + z_peers(*me) + core_peer(*me) + x_peers(*me))
        swap = Swap(net, local, heads, swapped, me)
        gather = Gather(net, local, shard, flat_rows(weights), me)
        gather.start()
        load.wait()
        swap.arrive()
        for m in range(2):
            for h in range(4):
                attended[m * 256 : m * 256 + 256, h * 128 : h * 128 + 128] = swapped[m, h]
        for q in range(4):
            held[q] = nt(attended[q * 128 : q * 128 + 128, :], out_w[...]).astype(BF)
        sums.start_held()
        gather.near()
        sums.middle()
        gather.middle()
        residual.wait()

        def step(rows, total):
            value = base[rows, :].astype(F32) + total
            hidden[rows, :] = value
            norm, _ = normed(value)
            low[rows, :] = (norm * gains[2:3, :] + gains[3:4, :]).astype(BF)

        sums.totals(step)
        sums.gather(low, second)
        gather.far()
        sums.gather_middle()
        gather.finish()
        sums.finish()
        net.finish()

    return remote_call(
        kernel,
        "middle_forward",
        3,
        [ANY, ANY, ANY, IN_VMEM, ANY],
        [
            ((512, 512), BF, IN_VMEM),
            ((128, D), F32, IN_VMEM),
            ((4, 128, D), BF, ANY),
            ((D, width), BF, ANY),
        ],
        [pltpu.VMEM((2, 4, 256, 128), BF), pltpu.VMEM((D, 512), BF)]
        + sum_scratch()
        + [pltpu.VMEM((128, D), BF), pltpu.VMEM((128, D), BF)],
        SWAP_COPIES + GATHER_COPIES + SUM_COPIES,
        SWAP_LOCALS + SUM_LOCALS + 3,
    )(heads, front, inputs, gains, shard)


def other_half(c, k, size):
    core = 1 - c if k < 2 else c
    return pl.ds(pl.multiple_of(core * 1024 + (k % 2) * size, size), size)


def shard_block(k):
    return pl.ds((k % 2) * 2, 2)


def middle_backward(parts, cotangent, hidden, gains, attended, front, second_low, dup, mixed, branch, gate_grad):
    def kernel(
        parts, cotangent, hidden, gains, attended, front, second_low, dup, mixed, branch, gate_grad,
        dhidden, vectors, output_grad, upstream, out_block, gate_out, up_out, down_out,
        held, spare, low, hidden_low, out_w, blocks, lows, dys, extra, *rest,
    ):
        scratch, (ss, rs, ls) = rest[:-3], rest[-3:]
        me = here()
        c, y, z, x = me
        net, local = Net(ss, rs), Local(ls)
        sums = SumX(net, local, parts, held, spare, me)
        sums.load()
        loads = [local.copy(second_low, lows), local.copy(cotangent, dys)]
        load = local.copy(front.at[:, TURNED], out_w)
        greet(y_peers(*me) + z_peers(*me) + core_peer(*me) + x_peers(*me))
        gate, up_, down_ = [
            Scatter(net, local, grads, out, scratch[8 * k : 8 * k + 8], me)
            for k, (grads, out) in enumerate(((gate_grad, gate_out), (None, up_out), (None, down_out)))
        ]
        gate.start()
        sums.start()

        def multiply(left, right, k, to):
            value = tn(left[:, other_half(c, k, 512)], right[...]).astype(BF)
            to[shard_block(k)] = value.reshape(2, 4, 64, UNITS)

        loads[0].wait()
        for k in range(2):
            multiply(lows, dup, k, down_.held)
        up_.send_filled(down_.held)
        gate.first()
        sums.middle()
        for k in range(2, 4):
            multiply(lows, dup, k, up_.held)
        loads[1].wait()
        for k in range(2):
            multiply(dys, mixed, k, extra)
        down_.send_filled(extra)
        up_.first()
        net.wait_sent(up_.zero)
        gate.first_middle()
        vectors[...] = jnp.zeros_like(vectors)

        def step(rows, dsecond):
            norm, inverse = normed(hidden[rows, :])
            upper = dys[pl.ds(pl.multiple_of(x * 128 + rows.start, 32), 32), :].astype(F32)
            value = upper + norm_pullback(dsecond, norm, inverse, gains[2:3, :])
            dhidden[rows, :] = value
            low[rows, :] = value.astype(BF)
            vectors[0:1, :] += jnp.sum(dsecond * norm, axis=0, keepdims=True)
            vectors[1:2, :] += jnp.sum(dsecond, axis=0, keepdims=True)

        sums.totals(step)
        sums.ring.sent()
        sums.gather(low, hidden_low)
        for k in range(2, 4):
            multiply(dys, mixed, k, down_.held)
        down_.first()
        up_.first_middle()
        gate.second()
        sums.gather_middle()
        late = SumX(net, local, branch, held, spare, me)
        late.load()
        late.start()
        down_.first_middle()
        up_.second()
        load.wait()
        sums.finish()
        for q in range(4):
            rows = slice((q % 2) * 128, (q % 2) * 128 + 128)
            result = jnp.dot(hidden_low[q], out_w[...], preferred_element_type=F32).astype(BF)
            for h in range(4):
                blocks[q // 2, h, rows, :] = result[:, h * 128 : h * 128 + 128]
        swap = Swap(net, local, blocks, upstream, me)
        late.middle()
        gate.second_middle()
        down_.second()
        whole = hidden_low[...].reshape(512, D)
        output_grad[...] = tn(whole, attended[...]).astype(BF)
        up_.second_middle()
        gate.third()
        down_.second_middle()

        def last(rows, total):
            out_block[rows, :] = (hidden[rows, :] + total).astype(BF)

        late.totals(last)
        up_.third()
        down_.third()
        swap.arrive()
        net.finish()

    scratch = sum_scratch() + [
        pltpu.VMEM((128, D), BF),
        pltpu.VMEM((4, 128, D), BF),
        pltpu.VMEM((D, 512), BF),
        pltpu.VMEM((2, 4, 256, 128), BF),
        pltpu.VMEM((512, D), BF),
        pltpu.VMEM((512, D), BF),
        pltpu.VMEM((4, 4, 64, UNITS), BF),
    ]
    return remote_call(
        kernel,
        "middle_backward",
        4,
        [ANY, ANY, IN_VMEM, IN_VMEM, IN_VMEM, ANY, ANY, IN_VMEM, IN_VMEM, ANY, ANY],
        [
            ((128, D), F32, IN_VMEM),
            ((2, D), F32, IN_VMEM),
            ((D, 512), BF, IN_VMEM),
            ((2, 4, 256, 128), BF, ANY),
            ((128, D), BF, IN_VMEM),
        ]
        + [((64, UNITS), F32, IN_VMEM)] * 3,
        scratch + scatter_scratch(UNITS) * 3,
        SUM_COPIES + RING_SUM + SCATTER_COPIES * 3 + SWAP_COPIES,
        SUM_LOCALS + 4 + SWAP_LOCALS + 3 + 1,
    )(parts, cotangent, hidden, gains, attended, front, second_low, dup, mixed, branch, gate_grad)


def collect_heads(dkv, dq, block):
    def kernel(dkv, dq, block, dproject, outputs, mine, got, summed, ss, rs, ls):
        me = here()
        c, y, z, x = me
        net, local = Net(ss, rs), Local(ls)
        order = (1, 3, 2, 0)
        loads = [local.copy(dkv.at[m], mine.at[m]) for m in range(2)]
        greet(y_peers(*me) + z_peers(*me) + x_peers(*me))
        kv = pl.ds(0, 2)
        along_y = lambda d: at(c, y + d, z, x)
        along_z = lambda d: at(c, y, z + d, x)

        def add(total, term):
            def one(i, carry):
                rows = pl.ds(pl.multiple_of(i * 64, 64), 64)
                total[rows, :] = (total[rows, :].astype(F32) + term[rows, :].astype(F32)).astype(BF)
                return carry

            lax.fori_loop(0, 4, one, 0)

        rings = {}
        for k in order:
            rings[0, k] = RingSum(
                net, along_y, lambda d, half, k=k: mine.at[0, up(y, d), up(z, k), half], got.at[0, k], add
            )
            rings[1, k] = RingSum(
                net, along_z, lambda d, half, k=k: mine.at[1, up(y, k), up(z, d), half], got.at[1, k], add
            )
        whole = quarters_of(net, outputs, me)
        own = local.copy(block, outputs.at[x])
        whole.start(block)
        for copy in loads:
            copy.wait()
        for ring in rings.values():
            ring.start()
        lates = [
            local.copy(dq.at[0, z], dproject.at[0, z, 2]),
            local.copy(dq.at[1, y], dproject.at[1, y, 2]),
        ]
        two = []
        for d in STEPS:
            two.append(net.send(dq.at[0, up(z, d)], dproject.at[0, z, 2], along_z(d)))
            two.append(net.send(dq.at[1, up(y, d)], dproject.at[1, y, 2], along_y(d)))
        for ring in rings.values():
            ring.middle()
        for k in order:
            for m, spot in ((0, z), (1, y)):
                ring = rings[m, k]
                ring.arrive()
                for half in range(2):
                    kept, terms = ring.mine(0, half), ring.terms(half)

                    def total(i, carry, m=m, k=k, half=half, kept=kept, terms=terms):
                        rows = pl.ds(pl.multiple_of(i * 64, 64), 64)
                        value = kept[rows, :].astype(F32)
                        for term in terms:
                            value += term[rows, :].astype(F32)
                        summed[m, k, half, rows, :] = value.astype(BF)
                        return carry

                    lax.fori_loop(0, 4, total, 0)
            if k:
                two.append(net.send(summed.at[0, k], dproject.at[0, z, kv], along_z(k)))
                two.append(net.send(summed.at[1, k], dproject.at[1, y, kv], along_y(k)))
            else:
                lates.append(local.copy(summed.at[0, 0], dproject.at[0, z, kv]))
                lates.append(local.copy(summed.at[1, 0], dproject.at[1, y, kv]))

        whole.from_back()
        whole.from_ahead()
        for copy in two:
            copy.wait_recv()
        for copy in lates:
            copy.wait()
        own.wait()
        whole.arrive()
        net.finish()

    return remote_call(
        kernel,
        "collect_heads",
        6,
        [ANY, ANY, IN_VMEM],
        [((2, 4, 3, 256, 128), BF, ANY), ((4, 128, D), BF, ANY)],
        [
            pltpu.VMEM((2, 4, 4, 2, 256, 128), BF),
            pltpu.VMEM((2, 4, 6, 256, 128), BF),
            pltpu.VMEM((2, 4, 2, 256, 128), BF),
        ],
        8 * RING_SUM + 6 + 6 + RING_GATHER,
        2 + 4 + 1,
    )(dkv, dq, block)


def last_backward(dproject, first_low, front, inputs, dhidden, gains, mixer_vectors, output_grad):
    def kernel(
        dproject, first_low, front, inputs, dhidden, gains, mixer_vectors, output_grad,
        input_grad, sums_out, project_out, output_out,
        wide, weights, lows, held, spare, base, low, extra, small, got, *rest,
    ):
        scratch, (ss, rs, ls) = rest[:-3], rest[-3:]
        me = here()
        c, y, z, x = me
        net, local = Net(ss, rs), Local(ls)
        load = local.copy(front.at[:, pl.ds(0, 1536)], weights)
        load_low = local.copy(first_low, lows)
        residual = local.copy(inputs.at[x], base)
        greet(y_peers(*me) + z_peers(*me) + core_peer(*me) + x_peers(*me))
        project = Scatter(net, local, None, project_out, scratch[:8], me)
        output = Scatter(net, local, output_grad, output_out, scratch[8:], me)
        output.start()
        sums = SumX(net, local, None, held, spare, me)
        for m in range(2):
            for t in range(3):
                for h in range(4):
                    to = t * 512 + h * 128
                    wide[m * 256 : m * 256 + 256, to : to + 128] = dproject[m, h, (t + 2) % 3]
        load.wait()

        def quarter(d):
            q = up(x, d)
            rows = wide[pl.ds(pl.multiple_of(q * 128, 128), 128), :]
            held[q] = nt(rows, weights[...]).astype(BF)

        quarter(2)
        sums.ring.start_far()
        quarter(1)
        quarter(3)
        sums.ring.start_near()

        def multiply(k, to):
            value = tn(lows[:, other_half(c, k, 512)], wide[...]).astype(BF)
            to[shard_block(k)] = value.reshape(2, 4, 64, 1536)

        load_low.wait()
        for k in range(2):
            multiply(k, extra)
        project.send_filled(extra)
        sums.middle()
        quarter(0)
        for k in range(2, 4):
            multiply(k, project.held)
        output.first()
        small[0, ...] = jnp.zeros_like(small[0])
        small[0, 2:4, :] = mixer_vectors[...]
        small[0, 4:5, 0:1536] = jnp.sum(wide[...].astype(F32), axis=0, keepdims=True)
        project.first()
        residual.wait()

        def step(rows, dfirst):
            norm, inverse = normed(base[rows, :].astype(F32))
            value = dhidden[rows, :] + norm_pullback(dfirst, norm, inverse, gains[0:1, :])
            low[rows, :] = value.astype(BF)
            small[0, 0:1, :] += jnp.sum(dfirst * norm, axis=0, keepdims=True)
            small[0, 1:2, :] += jnp.sum(dfirst, axis=0, keepdims=True)

        sums.totals(step)
        copies = [net.send(small.at[0], got.at[0, d - 1], at(c, y, z, x + d)) for d in STEPS]
        sums.gather(low, input_grad)
        output.first_middle()
        project.first_middle()
        for copy in copies:
            copy.wait_recv()
        small[1, ...] = small[0, ...]
        for n in range(3):
            small[1, 0:4, :] += got[0, n, 0:4, :]
        copies = [net.send(small.at[1], got.at[1, d - 1], at(c, y + d, z, x)) for d in STEPS]
        sums.gather_middle()
        output.second()
        project.second()
        for copy in copies:
            copy.wait_recv()
        small[2, ...] = small[1, ...] + got[1, 0] + got[1, 1] + got[1, 2]
        copies = [net.send(small.at[2], got.at[2, d - 1], at(c, y, z + d, x)) for d in STEPS]
        output.second_middle()
        project.second_middle()
        for copy in copies:
            copy.wait_recv()
        small[3, ...] = small[2, ...] + got[2, 0] + got[2, 1] + got[2, 2]
        copy = net.send(small.at[3], got.at[3, 0], at(1 - c, y, z, x))
        output.third()
        project.third()
        copy.wait_recv()
        sums_out[...] = small[3, ...] + got[3, 0]
        sums.finish()
        net.finish()

    scratch = (
        [pltpu.VMEM((512, 1536), BF), pltpu.VMEM((D, 1536), BF), pltpu.VMEM((512, D), BF)]
        + sum_scratch()
        + [
            pltpu.VMEM((128, D), BF),
            pltpu.VMEM((128, D), BF),
            pltpu.VMEM((4, 4, 64, 1536), BF),
            pltpu.VMEM((4, 8, D), F32),
            pltpu.VMEM((4, 3, 8, D), F32),
        ]
    )
    return remote_call(
        kernel,
        "last_backward",
        7,
        [IN_VMEM, ANY, ANY, ANY, IN_VMEM, IN_VMEM, IN_VMEM, ANY],
        [
            ((4, 128, D), BF, ANY),
            ((8, D), F32, IN_VMEM),
            ((64, 1536), F32, IN_VMEM),
            ((64, 512), F32, IN_VMEM),
        ],
        scratch + scatter_scratch(1536) + scatter_scratch(512),
        SUM_COPIES + 10 + SCATTER_COPIES * 2,
        SUM_LOCALS + 4,
    )(dproject, first_low, front, inputs, dhidden, gains, mixer_vectors, output_grad)


def turn(values, cosine, sine):
    lane = lax.rem(lax.broadcasted_iota(jnp.int32, values.shape, 1), HEAD_DIM)
    swapped = jnp.where(lane < ROT // 2, -pltpu.roll(values, 120, 1), pltpu.roll(values, 8, 1))
    return values * cosine + swapped * sine


def turn_tables(base, steps, block):
    cosine, sine = base[0], base[1]
    far_cosine, far_sine = steps[0, pl.ds(block, 1), :], steps[1, pl.ds(block, 1), :]
    return far_cosine * cosine - far_sine * sine, far_sine * cosine + far_cosine * sine


def two_heads(block):
    lane = lax.broadcasted_iota(jnp.int32, (128, 128), 1)
    value = block.astype(F32)
    return jnp.concatenate(
        [jnp.where(lane < HEAD_DIM, value, 0.0), jnp.where(lane >= HEAD_DIM, value, 0.0)], axis=0
    )


def two_heads_t(block):
    feature = lax.broadcasted_iota(jnp.int32, (128, 128), 0)
    value = block.astype(F32).T
    return jnp.concatenate(
        [jnp.where(feature < HEAD_DIM, value, 0.0), jnp.where(feature >= HEAD_DIM, value, 0.0)], axis=1
    )


def one_block(stacked):
    feature = lax.broadcasted_iota(jnp.int32, (128, 128), 0)
    return jnp.where(feature < HEAD_DIM, stacked[:, :128], stacked[:, 128:]).T


def nt(left, right):
    return lax.dot_general(left, right, (((1,), (1,)), ((), ())), preferred_element_type=F32)


def plan_blocks(group_place, slots, places):
    _, y, z, _ = here()

    def one(j, carry):
        slots[group_place[j]] = j
        return carry

    lax.fori_loop(0, 32, one, 0)
    for b in range(8):
        places[b] = group_place[(y * 4 + b // 2) * 2 + b % 2]
        places[8 + b] = group_place[((b // 2) * 4 + z) * 2 + b % 2]


def row_of(m, i):
    _, y, z, _ = here()
    return jnp.where(m == 0, y * 4 + i, i * 4 + z)


def unit_of(places, m, n):
    pair, rest = n // 9, lax.rem(n, 9)
    ahead = places[m * 8 + pair * 2] // (TILE // 128) + 1
    late = rest >= ahead
    block = pair * 2 + jnp.where(late, 1, 0)
    tile = rest - jnp.where(late, ahead, 0)
    return block, tile, places[m * 8 + block] * 128 - tile * TILE


def key_minus_query():
    return lax.broadcasted_iota(jnp.int32, (TILE, 256), 0) - lax.rem(
        lax.broadcasted_iota(jnp.int32, (TILE, 256), 1), 128
    )


def tile_of(t):
    return pl.ds(pl.multiple_of(t * TILE, TILE), TILE)


def lay_blocks(slots, lay):
    def some(n, carry):
        for k in range(4):
            b = n * 4 + k
            slot = slots[b]
            rows = pl.ds(pl.multiple_of(lax.rem(slot, 2) * 128, 128), 128)
            lay(slot // 2, rows, pl.ds(pl.multiple_of(b * 128, 128), 128))
        return carry

    lax.fori_loop(0, 8, some, 0)


UNITS_EACH = 36


def attend(group_place, spread):
    def kernel(
        group_ref, k_ref, v_ref, q_ref, o_ref, full_ref, log_ref,
        slots, places, keys, values_t, queries, scores_0, scores_1, weights_0, weights_1, results, sums,
    ):
        scores, weights = (scores_0, scores_1), (weights_0, weights_1)
        m = pl.program_id(0)
        plan_blocks(group_ref, slots, places)

        def lay(slot, rows, to):
            keys[to, :] = k_ref[0, slot, 0, rows, :]
            values_t[:, to] = v_ref[0, slot, 0, rows, :].T

        lay_blocks(slots, lay)
        for b in range(8):
            row = row_of(m, b // 2)
            block = q_ref[0, row, 0, (b % 2) * 128 : (b % 2) * 128 + 128, :]
            queries[b] = (two_heads_t(block) * 0.125).astype(BF)
        offset = key_minus_query()

        def multiply(n, odd):
            block, tile, _ = unit_of(places, m, n)
            scores[odd][...] = jnp.dot(
                keys[tile_of(tile), :], queries[block], preferred_element_type=F32
            )

        def soften(n, odd, top, total):
            block, tile, limit = unit_of(places, m, n)
            value = jnp.where(offset <= limit, scores[odd][...] * LOG2E, LOW)
            first = tile == 0
            top = jnp.where(first, LOW, top)
            new_top = jnp.maximum(top, jnp.max(value, axis=0, keepdims=True))
            exps = jnp.exp2(value - new_top)
            shrink = jnp.exp2(top - new_top)
            total = total * shrink + jnp.sum(exps, axis=0, keepdims=True)
            weights[odd][...] = exps.astype(BF)
            sums[block, 0:1, :] = new_top
            sums[block, 1:2, :] = total
            return new_top, total, shrink

        def gather(n, odd, shrink, acc):
            block, tile, _ = unit_of(places, m, n)
            acc = acc * shrink + jnp.dot(
                values_t[:, tile_of(tile)], weights[odd][...], preferred_element_type=F32
            )
            results[block] = acc
            return acc

        row = jnp.zeros((1, 256), F32)
        multiply(0, 0)
        multiply(1, 1)
        top, total, shrink = soften(0, 0, row, row)

        def step(k, carry):
            top, total, shrink, acc = carry
            for n, odd in ((2 * k + 1, 1), (2 * k + 2, 0)):
                multiply(n + 1, 1 - odd)
                acc = gather(n - 1, 1 - odd, shrink, acc)
                top, total, shrink = soften(n, odd, top, total)
            return top, total, shrink, acc

        carry = (top, total, shrink, jnp.zeros((128, 256), F32))
        top, total, shrink, acc = lax.fori_loop(0, UNITS_EACH // 2 - 1, step, carry)
        last = UNITS_EACH - 1
        acc = gather(last - 1, 0, shrink, acc)
        _, _, shrink = soften(last, 1, top, total)
        gather(last, 1, shrink, acc)
        for b in range(8):
            rows = slice((b % 2) * 128, (b % 2) * 128 + 128)
            total = sums[b, 1:2, :]
            result = one_block(results[b] / total)
            full_ref[0, b // 2, rows, :] = result
            o_ref[0, b // 2, rows, :] = result.astype(BF)
            log_ref[0, b : b + 1, :] = sums[b, 0:1, :] + jnp.log2(total)

    grid_spec = pltpu.PrefetchScalarGridSpec(
        num_scalar_prefetch=1,
        grid=(2,),
        in_specs=[
            pl.BlockSpec((1, 16, 1, 256, 128), lambda m, g: (m, 0, 0, 0, 0)),
            pl.BlockSpec((1, 16, 1, 256, 128), lambda m, g: (m, 0, 1, 0, 0)),
            pl.BlockSpec((1, 16, 1, 256, 128), lambda m, g: (m, 0, 2, 0, 0)),
        ],
        out_specs=[
            pl.BlockSpec((1, 4, 256, 128), lambda m, g: (m, 0, 0, 0)),
            pl.BlockSpec((1, 4, 256, 128), lambda m, g: (m, 0, 0, 0)),
            pl.BlockSpec((1, 8, 256), lambda m, g: (m, 0, 0)),
        ],
        scratch_shapes=[
            pltpu.SMEM((32,), jnp.int32),
            pltpu.SMEM((16,), jnp.int32),
            pltpu.VMEM((4096, 128), BF),
            pltpu.VMEM((128, 4096), BF),
            pltpu.VMEM((8, 128, 256), BF),
            pltpu.VMEM((TILE, 256), F32),
            pltpu.VMEM((TILE, 256), F32),
            pltpu.VMEM((TILE, 256), BF),
            pltpu.VMEM((TILE, 256), BF),
            pltpu.VMEM((8, 128, 256), F32),
            pltpu.VMEM((8, 8, 256), F32),
        ],
    )
    return pl.pallas_call(
        kernel,
        name="attend",
        grid_spec=grid_spec,
        out_shape=[
            jax.ShapeDtypeStruct((2, 4, 256, 128), BF),
            jax.ShapeDtypeStruct((2, 4, 256, 128), F32),
            jax.ShapeDtypeStruct((2, 8, 256), F32),
        ],
        compiler_params=pltpu.CompilerParams(vmem_limit_bytes=VMEM_LIMIT),
    )(group_place, spread, spread, spread)


def attend_back(group_place, spread, full, logs, upstream, base, steps):
    def kernel(
        group_ref, k_ref, v_ref, q_ref, full_ref, log_ref, up_ref, base_ref, steps_ref,
        dq_ref, dkv_ref,
        slots, places, keys, keys_t, values, dkeys, dvalues, queries, queries_t, grads, grads_t, delta,
        scores_0, scores_1, dprobs_0, dprobs_1, probs_0, probs_1, dscores_0, dscores_1, results,
    ):
        scores, dprobs = (scores_0, scores_1), (dprobs_0, dprobs_1)
        probs_low, dscores = (probs_0, probs_1), (dscores_0, dscores_1)
        m = pl.program_id(0)
        plan_blocks(group_ref, slots, places)

        def lay(slot, rows, to):
            block = k_ref[0, slot, 0, rows, :]
            keys[to, :] = block
            keys_t[:, to] = block.T
            values[to, :] = v_ref[0, slot, 0, rows, :]
            dkeys[to, :] = jnp.zeros((128, 128), F32)
            dvalues[to, :] = jnp.zeros((128, 128), F32)

        lay_blocks(slots, lay)
        for b in range(8):
            rows = slice((b % 2) * 128, (b % 2) * 128 + 128)
            block = q_ref[0, row_of(m, b // 2), 0, rows, :]
            queries[b] = (two_heads(block) * 0.125).astype(BF)
            queries_t[b] = (two_heads_t(block) * 0.125).astype(BF)
            ups = up_ref[0, b // 2, rows, :]
            grads[b] = two_heads(ups).astype(BF)
            grads_t[b] = two_heads_t(ups).astype(BF)
            product = (ups.astype(F32) * full_ref[0, b // 2, rows, :]).T
            delta[b, 0:1, :128] = jnp.sum(product[:HEAD_DIM], axis=0, keepdims=True)
            delta[b, 0:1, 128:] = jnp.sum(product[HEAD_DIM:], axis=0, keepdims=True)
        offset = key_minus_query()

        def multiply(n, odd):
            block, tile, _ = unit_of(places, m, n)
            scores[odd][...] = jnp.dot(
                keys[tile_of(tile), :], queries_t[block], preferred_element_type=F32
            )
            dprobs[odd][...] = jnp.dot(
                values[tile_of(tile), :], grads_t[block], preferred_element_type=F32
            )

        def soften(n, odd):
            block, _, limit = unit_of(places, m, n)
            value = jnp.exp2(scores[odd][...] * LOG2E - log_ref[0, pl.ds(block, 1), :])
            value = jnp.where(offset <= limit, value, 0.0)
            probs_low[odd][...] = value.astype(BF)
            dscores[odd][...] = (
                value * (dprobs[odd][...] - delta[block, 0:1, :])
            ).astype(BF)

        def gather(n, odd, acc):
            block, tile, _ = unit_of(places, m, n)
            span = tile_of(tile)
            dvalues[span, :] += jnp.dot(probs_low[odd][...], grads[block], preferred_element_type=F32)
            dkeys[span, :] += jnp.dot(dscores[odd][...], queries[block], preferred_element_type=F32)
            acc = jnp.where(tile == 0, 0.0, acc) + jnp.dot(
                keys_t[:, span], dscores[odd][...], preferred_element_type=F32
            )
            results[block] = acc
            return acc

        multiply(0, 0)
        multiply(1, 1)
        soften(0, 0)

        def step(k, acc):
            for n, odd in ((2 * k + 1, 1), (2 * k + 2, 0)):
                multiply(n + 1, 1 - odd)
                acc = gather(n - 1, 1 - odd, acc)
                soften(n, odd)
            return acc

        last = UNITS_EACH - 1
        acc = lax.fori_loop(0, UNITS_EACH // 2 - 1, step, jnp.zeros((128, 256), F32))
        acc = gather(last - 1, 0, acc)
        soften(last, 1)
        gather(last, 1, acc)

        def turned_back(values, place):
            cosine, sine = turn_tables(base_ref, steps_ref, place)
            return turn(values, cosine, -sine)

        for b in range(8):
            rows = slice((b % 2) * 128, (b % 2) * 128 + 128)
            dquery = one_block(results[b]) * 0.125
            dq_ref[0, b // 2, rows, :] = turned_back(dquery, places[m * 8 + b]).astype(BF)

        def flush(n, carry):
            for k in range(2):
                b = n * 2 + k
                slot = slots[b]
                rows = pl.ds(pl.multiple_of(lax.rem(slot, 2) * 128, 128), 128)
                to = pl.ds(pl.multiple_of(b * 128, 128), 128)
                dkv_ref[0, slot // 2, 0, rows, :] = turned_back(dkeys[to, :], b).astype(BF)
                dkv_ref[0, slot // 2, 1, rows, :] = dvalues[to, :].astype(BF)
            return carry

        lax.fori_loop(0, 16, flush, 0)

    grid_spec = pltpu.PrefetchScalarGridSpec(
        num_scalar_prefetch=1,
        grid=(2,),
        in_specs=[
            pl.BlockSpec((1, 16, 1, 256, 128), lambda m, g: (m, 0, 0, 0, 0)),
            pl.BlockSpec((1, 16, 1, 256, 128), lambda m, g: (m, 0, 1, 0, 0)),
            pl.BlockSpec((1, 16, 1, 256, 128), lambda m, g: (m, 0, 2, 0, 0)),
            pl.BlockSpec((1, 4, 256, 128), lambda m, g: (m, 0, 0, 0)),
            pl.BlockSpec((1, 8, 256), lambda m, g: (m, 0, 0)),
            pl.BlockSpec((1, 4, 256, 128), lambda m, g: (m, 0, 0, 0)),
            pl.BlockSpec((2, 128, 128), lambda m, g: (0, 0, 0)),
            pl.BlockSpec((2, 32, 128), lambda m, g: (0, 0, 0)),
        ],
        out_specs=[
            pl.BlockSpec((1, 4, 256, 128), lambda m, g: (m, 0, 0, 0)),
            pl.BlockSpec((1, 16, 2, 256, 128), lambda m, g: (m, 0, 0, 0, 0)),
        ],
        scratch_shapes=[
            pltpu.SMEM((32,), jnp.int32),
            pltpu.SMEM((16,), jnp.int32),
            pltpu.VMEM((4096, 128), BF),
            pltpu.VMEM((128, 4096), BF),
            pltpu.VMEM((4096, 128), BF),
            pltpu.VMEM((4096, 128), F32),
            pltpu.VMEM((4096, 128), F32),
            pltpu.VMEM((8, 256, 128), BF),
            pltpu.VMEM((8, 128, 256), BF),
            pltpu.VMEM((8, 256, 128), BF),
            pltpu.VMEM((8, 128, 256), BF),
            pltpu.VMEM((8, 8, 256), F32),
            pltpu.VMEM((TILE, 256), F32),
            pltpu.VMEM((TILE, 256), F32),
            pltpu.VMEM((TILE, 256), F32),
            pltpu.VMEM((TILE, 256), F32),
            pltpu.VMEM((TILE, 256), BF),
            pltpu.VMEM((TILE, 256), BF),
            pltpu.VMEM((TILE, 256), BF),
            pltpu.VMEM((TILE, 256), BF),
            pltpu.VMEM((8, 128, 256), F32),
        ],
    )
    return pl.pallas_call(
        kernel,
        name="attend_back",
        grid_spec=grid_spec,
        out_shape=[
            jax.ShapeDtypeStruct((2, 4, 256, 128), BF),
            jax.ShapeDtypeStruct((2, 16, 2, 256, 128), BF),
        ],
        compiler_params=pltpu.CompilerParams(vmem_limit_bytes=VMEM_LIMIT),
    )(group_place, spread, spread, spread, full, logs, upstream, base, steps)


def tn(left, right):
    return lax.dot_general(left, right, (((0,), (0,)), ((), ())), preferred_element_type=F32)


def feed_forward(second_low, dy, weights):
    def kernel(
        low_hbm, dy_hbm, w_hbm, branch, dsecond, gate_out, dup, mixed,
        low, dys, gate_w, up_w, down_w, gate, up, dmixed, dgate, chunks, sems, chunk_sems,
    ):
        def load(n, src, dst):
            copy = pltpu.make_async_copy(src, dst, sems.at[n])
            copy.start()
            return copy

        def columns(k):
            return w_hbm.at[:, pl.ds(k * UNITS, UNITS)]

        loads = [
            load(0, low_hbm, low),
            load(1, columns(0), gate_w),
            load(2, columns(1), up_w),
            load(3, dy_hbm, dys),
            load(4, columns(2), down_w),
        ]
        loads[0].wait()
        loads[1].wait()
        gate[...] = jnp.dot(low[...], gate_w[...], preferred_element_type=F32)
        loads[2].wait()
        up[...] = jnp.dot(low[...], up_w[...], preferred_element_type=F32)
        loads[3].wait()
        loads[4].wait()
        dmixed[...] = jnp.dot(dys[...], down_w[...], preferred_element_type=F32)

        def step(i, carry):
            rows = pl.ds(pl.multiple_of(i * 16, 16), 16)
            g, u, d = gate[rows, :], up[rows, :], dmixed[rows, :]
            s = jax.nn.sigmoid(g)
            silu = g * s
            mixed[rows, :] = (silu * u).astype(BF)
            dgate[rows, :] = (d * u * s * (1.0 + g * (1.0 - s))).astype(BF)
            dup[rows, :] = (d * silu).astype(BF)
            return carry

        lax.fori_loop(0, 32, step, 0)
        dsecond[...] = (nt(dgate[...], gate_w[...]) + nt(dup[...], up_w[...])).astype(BF)
        busy = {}
        for k in range(4):
            rows = pl.ds(k * 512, 512)
            slot = k % 2
            if slot in busy:
                busy[slot].wait()
            chunks[slot] = tn(low[:, rows], dgate[...]).astype(BF)
            busy[slot] = pltpu.make_async_copy(chunks.at[slot], gate_out.at[rows, :], chunk_sems.at[slot])
            busy[slot].start()
        branch[...] = nt(mixed[...], down_w[...]).astype(BF)
        busy[0].wait()
        busy[1].wait()

    return pl.pallas_call(
        kernel,
        name="feed_forward",
        in_specs=[ANY, ANY, ANY],
        out_specs=[IN_VMEM, IN_VMEM, ANY, IN_VMEM, IN_VMEM],
        out_shape=[jax.ShapeDtypeStruct((512, D), BF)] * 2
        + [jax.ShapeDtypeStruct((D, UNITS), BF)]
        + [jax.ShapeDtypeStruct((512, UNITS), BF)] * 2,
        scratch_shapes=[pltpu.VMEM((512, D), BF)] * 2
        + [pltpu.VMEM((D, UNITS), BF)] * 3
        + [pltpu.VMEM((512, UNITS), F32)] * 3
        + [
            pltpu.VMEM((512, UNITS), BF),
            pltpu.VMEM((2, 512, UNITS), BF),
            pltpu.SemaphoreType.DMA((5,)),
            pltpu.SemaphoreType.DMA((2,)),
        ],
        compiler_params=pltpu.CompilerParams(vmem_limit_bytes=VMEM_LIMIT),
    )(second_low, dy, weights)


def angle_tables():
    lane = np.arange(128) % HEAD_DIM
    power = 10000.0 ** (-2.0 * (lane % (ROT // 2)) / ROT)
    frequency = np.where(lane < ROT, power, 0.0)
    tables = []
    for places in (np.arange(128), np.arange(32) * 128):
        angles = places[:, None] * frequency[None, :]
        tables.append(jnp.asarray(np.stack([np.cos(angles), np.sin(angles)]).astype(np.float32)))
    return tables


def body(
    inputs,
    cotangent,
    group_place,
    attend_gain,
    attend_shift,
    project_weight,
    project_bias,
    output_weight,
    mixer_gain,
    mixer_shift,
    gate_weight,
    up_weight,
    down_weight,
):
    shard_index = lax.axis_index("dp") * 16 + lax.axis_index("ctx")
    base, steps = angle_tables()

    vectors = jnp.stack([attend_gain, attend_shift, mixer_gain, mixer_shift])
    vectors = jnp.concatenate(
        [
            jnp.pad(vectors, ((0, 0), (0, 64))),
            jnp.pad(project_bias.reshape(1, 48), ((0, 0), (0, 80))),
            jnp.zeros((59, 128), BF),
        ]
    )
    front_shard = jnp.concatenate(
        [project_weight.reshape(64, 1536), output_weight.T, vectors], axis=1
    )
    back_shard = jnp.concatenate([gate_weight, up_weight, down_weight.T], axis=1)

    tokens = inputs.reshape(512, D)
    quarters = inputs.reshape(4, 128, D)
    front, gains, first_low, spread = front_forward(front_shard, tokens, group_place, base, steps)
    spread = spread.reshape(2, 16, 3, 256, 128)
    attended_heads, attended_full, logs = attend(group_place, spread)
    attended_low, hidden, second_low, back = middle_forward(
        attended_heads, front, quarters, gains, back_shard
    )

    second_low = second_low.reshape(512, D)
    dy = cotangent.reshape(512, D)
    branch, second_part, gate_grad, dup, mixed = feed_forward(second_low, dy, back)
    dhidden, mixer_vectors, output_grad, upstream, out_block, gate_grad, up_grad, down_grad = middle_backward(
        second_part.reshape(4, 128, D),
        dy,
        hidden,
        gains,
        attended_low,
        front,
        second_low,
        dup,
        mixed,
        branch.reshape(4, 128, D),
        gate_grad.reshape(2, 4, 4, 64, UNITS),
    )

    dq, dkv = attend_back(group_place, spread, attended_full, logs, upstream, base, steps)
    dproject, outputs = collect_heads(dkv.reshape(2, 4, 4, 2, 256, 128), dq, out_block)
    input_grad, small, project_grad, output_grad = last_backward(
        dproject, first_low, front, quarters, dhidden, gains, mixer_vectors, output_grad.reshape(2, 4, 4, 64, 512)
    )
    own = lax.dynamic_slice(small, (0, shard_index * 64), (4, 64))
    bias_grad = lax.dynamic_slice(
        small[4, :1536].reshape(3, 8, 64), (0, 0, shard_index * 2), (3, 8, 2)
    )
    shape = inputs.shape
    return (
        outputs.reshape(shape),
        input_grad.reshape(shape),
        own[0],
        own[1],
        project_grad.reshape(64, 3, 512),
        bias_grad,
        output_grad.T,
        own[2],
        own[3],
        gate_grad,
        up_grad,
        down_grad.T,
    )


def solution(mesh):
    weight = ("dp", "ctx")
    rows = P(None, "dp", "ctx", None)
    vector = P(weight)
    matrix = P(weight, "tensor")
    turned = P("tensor", weight)
    project = P(weight, None, "tensor")
    bias = P(None, "tensor", weight)
    params = (vector, vector, project, bias, turned, vector, vector, matrix, matrix, turned)
    return jax.shard_map(
        body,
        mesh=mesh,
        in_specs=(rows, rows, P()) + params,
        out_specs=(rows, rows) + params,
        check_vma=False,
    )
```

```python
import functools

import jax
import jax.numpy as jnp
import numpy as np
from jax import lax
from jax.experimental import pallas as pl
from jax.experimental.pallas import tpu as pltpu
from jax.sharding import PartitionSpec as P

MESH = pl.DeviceIdType.MESH
D = 2048
UNITS = 1408
GATE_SPLIT = 512
HEAD_DIM = 64
ROT = 16
EPSILON = 1e-05
LOG2E = 1.4426950408889634
LOW = -1e30
TILE = 512
VMEM_LIMIT = 58 * 2**20
STEPS = (1, 3, 2)
BF = jnp.bfloat16
F32 = jnp.float32


def here():
    ctx = lax.axis_index("ctx")
    return (lax.axis_index("dp"), ctx // 4, lax.rem(ctx, 4), lax.axis_index("tensor"))


def at(c, y, z, x):
    return (c, lax.rem(y, 4) * 4 + lax.rem(z, 4), lax.rem(x, 4))


def up(i, d):
    return lax.rem(i + d, 4)


def down(i, d):
    return lax.rem(i + 4 - d, 4)


class Net:
    def __init__(self, send_sems, recv_sems):
        self.send_sems, self.recv_sems = send_sems, recv_sems
        self.sent, self.gone = [], set()

    def send(self, src, dst, device):
        n = len(self.sent)
        copy = pltpu.make_async_remote_copy(
            src_ref=src,
            dst_ref=dst,
            send_sem=self.send_sems.at[n],
            recv_sem=self.recv_sems.at[n],
            device_id=device,
            device_id_type=MESH,
        )
        copy.start()
        self.sent.append(copy)
        return copy

    def finish(self):
        for n, copy in enumerate(self.sent):
            if n not in self.gone:
                copy.wait_send()

    def wait_sent(self, copy):
        copy.wait_send()
        self.gone.add([other is copy for other in self.sent].index(True))


class Local:
    def __init__(self, sems):
        self.sems, self.n = sems, 0

    def copy(self, src, dst):
        copy = pltpu.make_async_copy(src, dst, self.sems.at[self.n])
        copy.start()
        self.n += 1
        return copy


def greet(peers):
    barrier = pltpu.get_barrier_semaphore()
    for peer in peers:
        pl.semaphore_signal(barrier, inc=1, device_id=peer, device_id_type=MESH)
    pl.semaphore_wait(barrier, len(peers))


def y_peers(c, y, z, x):
    return [at(c, y + d, z, x) for d in (1, 2, 3)]


def z_peers(c, y, z, x):
    return [at(c, y, z + d, x) for d in (1, 2, 3)]


def x_peers(c, y, z, x):
    return [at(c, y, z, x + d) for d in (1, 2, 3)]


def core_peer(c, y, z, x):
    return [at(1 - c, y, z, x)]


class RingSum:
    def __init__(self, net, device, mine, spare, add):
        self.net, self.device, self.mine, self.spare, self.add = net, device, mine, spare, add

    def start(self):
        self.start_far()
        self.start_near()

    def start_far(self):
        send, mine, spare = self.net.send, self.mine, self.spare
        ahead, back = self.device(1), self.device(3)
        self.far_ahead = send(mine(2, 0), spare.at[0], ahead)
        self.far_back = send(mine(2, 1), spare.at[1], back)

    def start_near(self):
        send, mine, spare = self.net.send, self.mine, self.spare
        ahead, back = self.device(1), self.device(3)
        self.near = [send(mine(1, 1), spare.at[3], ahead), send(mine(3, 0), spare.at[2], back)]

    def middle(self):
        send, spare = self.net.send, self.spare
        self.far_ahead.wait_recv()
        self.add(spare.at[0], self.mine(1, 0))
        self.near.append(send(spare.at[0], spare.at[4], self.device(1)))
        self.far_back.wait_recv()
        self.add(spare.at[1], self.mine(3, 1))
        self.near.append(send(spare.at[1], spare.at[5], self.device(3)))

    def arrive(self):
        for copy in self.near:
            copy.wait_recv()

    def sent(self):
        for copy in [self.far_ahead, self.far_back] + self.near:
            self.net.wait_sent(copy)

    def terms(self, half):
        return [self.spare.at[4 if half == 0 else 3], self.spare.at[2 if half == 0 else 5]]


RING_SUM = 6


class RingGather:
    def __init__(self, net, device, out):
        self.net, self.device, self.out = net, device, out

    def start(self, block):
        self.ahead = self.net.send(block, self.out(0), self.device(1))
        self.back = self.net.send(block, self.out(0), self.device(3))

    def from_back(self):
        self.ahead.wait_recv()
        piece = self.out(3, 0)
        self.far_ahead = self.net.send(piece, piece, self.device(1))

    def from_ahead(self):
        self.back.wait_recv()
        piece = self.out(1, 1)
        self.far_back = self.net.send(piece, piece, self.device(3))

    def arrive(self):
        self.far_ahead.wait_recv()
        self.far_back.wait_recv()


RING_GATHER = 4


class Gather:
    def __init__(self, net, local, src, place, me):
        self.net, self.local, self.src, self.place, self.me = net, local, src, place, me
        self.core = []
        c, y, z, x = me
        along_y = lambda d: at(c, y + d, z, x)
        along_z = lambda d: at(c, y, z + d, x)

        def spot(far_y, far_z, first, half):
            if half is None:
                return place(c, up(y, far_y), up(z, far_z), first, 32)
            return place(c, up(y, far_y), up(z, far_z), first + 16 * half, 16)

        self.one = (
            RingGather(net, along_y, lambda d, half=None: spot(d, 0, 0, half)),
            RingGather(net, along_z, lambda d, half=None: spot(0, d, 32, half)),
        )
        self.two = {}
        for k in range(4):
            self.two[0, k] = RingGather(net, along_z, lambda d, half=None, k=k: spot(k, d, 0, half))
            self.two[1, k] = RingGather(net, along_y, lambda d, half=None, k=k: spot(d, k, 32, half))

    def hand_over(self, piece):
        c, y, z, x = self.me
        self.core.append(self.net.send(piece, piece, at(1 - c, y, z, x)))

    def start(self):
        c, y, z, x = self.me
        src, own = self.src, self.place(c, y, z, 0, 64)
        self.own = self.local.copy(src, own)
        halves = (src.at[pl.ds(0, 32)], src.at[pl.ds(32, 32)])
        for way in range(2):
            self.one[way].start(halves[way])
        for way in range(2):
            self.two[way, 0].start(halves[way])
        self.core.append(self.net.send(src, own, at(1 - c, y, z, x)))

    def near(self):
        for way in range(2):
            self.one[way].from_back()
            self.two[way, 3].start(self.one[way].out(3))
        for way in range(2):
            self.one[way].from_ahead()
            self.two[way, 1].start(self.one[way].out(1))
        for k in (3, 1):
            for way in range(2):
                self.hand_over(self.one[way].out(k))

    def middle(self):
        self.pass_on(0)
        for way in range(2):
            self.one[way].arrive()
            self.two[way, 2].start(self.one[way].out(2))
            self.hand_over(self.one[way].out(2))

    def pass_on(self, k):
        for way in range(2):
            self.two[way, k].from_back()
            self.two[way, k].from_ahead()
            self.hand_over(self.two[way, k].out(3))
            self.hand_over(self.two[way, k].out(1))

    def far(self):
        for k in (0, 3, 1, 2):
            for way in range(2):
                self.two[way, k].arrive()
                self.hand_over(self.two[way, k].out(2))

    def finish(self):
        for copy in self.core:
            copy.wait_recv()
        self.own.wait()


def flat_rows(ref):
    def place(c, y, z, first, count):
        return ref.at[pl.ds(pl.multiple_of(((c * 4 + y) * 4 + z) * 64 + first, 16), count)]

    return place


GATHER_COPIES = 10 * RING_GATHER + 31


def scatter_scratch(width):
    return [
        pltpu.VMEM((4, 4, 64, width), BF),
        pltpu.VMEM((4, 4, 64, width), BF),
        pltpu.VMEM((6, 4, 16, width), BF),
        pltpu.VMEM((6, 4, 16, width), BF),
        pltpu.VMEM((4, 32, width), BF),
        pltpu.VMEM((4, 32, width), BF),
        pltpu.VMEM((6, 16, width), BF),
        pltpu.VMEM((6, 16, width), BF),
    ]


SCATTER_COPIES = 1 + 4 * RING_SUM


def add_blocks(total, term):
    if len(total.shape) == 2:
        total[...] = (total[...].astype(F32) + term[...].astype(F32)).astype(BF)
        return

    def one(i, carry):
        total[i] = (total[i].astype(F32) + term[i].astype(F32)).astype(BF)
        return carry

    lax.fori_loop(0, total.shape[0], one, 0)


class Scatter:
    def __init__(self, net, local, grads, out, scratch, me):
        self.net, self.local, self.grads, self.out, self.me = net, local, grads, out, me
        (held, self.other, one_a, one_b, self.sum_a, self.sum_b, two_a, two_b) = scratch
        self.held = held
        c, y, z, x = me
        along_y = lambda d: at(c, y + d, z, x)
        along_z = lambda d: at(c, y, z + d, x)
        self.one_a = RingSum(
            net, along_z, lambda d, half: held.at[:, up(z, d), pl.ds(16 * half, 16)], one_a, add_blocks
        )
        self.one_b = RingSum(
            net, along_y, lambda d, half: held.at[up(y, d), :, pl.ds(32 + 16 * half, 16)], one_b, add_blocks
        )
        self.two_a = RingSum(
            net, along_y, lambda d, half: self.sum_a.at[up(y, d), pl.ds(16 * half, 16)], two_a, add_blocks
        )
        self.two_b = RingSum(
            net, along_z, lambda d, half: self.sum_b.at[up(z, d), pl.ds(16 * half, 16)], two_b, add_blocks
        )

    def start(self):
        c, y, z, x = self.me
        self.own = self.local.copy(self.grads.at[c], self.held)
        self.zero = self.net.send(self.grads.at[1 - c], self.other, at(1 - c, y, z, x))

    def send_filled(self, block):
        c, y, z, x = self.me
        self.own = None
        self.zero = self.net.send(block, self.other, at(1 - c, y, z, x))

    def first(self):
        if self.own is not None:
            self.own.wait()
        self.zero.wait_recv()
        held, other = self.held, self.other

        def add(i, carry):
            for q in range(4):
                rows = pl.ds(q * 16, 16)
                held[i // 4, lax.rem(i, 4), rows, :] = (
                    held[i // 4, lax.rem(i, 4), rows, :].astype(F32)
                    + other[i // 4, lax.rem(i, 4), rows, :].astype(F32)
                ).astype(BF)
            return carry

        lax.fori_loop(0, 16, add, 0)
        self.one_a.start()
        self.one_b.start()

    def first_middle(self):
        self.one_a.middle()
        self.one_b.middle()

    def second(self):
        for one, two, total in ((self.one_a, self.two_a, self.sum_a), (self.one_b, self.two_b, self.sum_b)):
            one.arrive()
            for half in range(2):
                own, terms = one.mine(0, half), one.terms(half)

                def add(i, carry, half=half, own=own, terms=terms, total=total):
                    value = own[i].astype(F32)
                    for term in terms:
                        value += term[i].astype(F32)
                    total[i, pl.ds(16 * half, 16), :] = value.astype(BF)
                    return carry

                lax.fori_loop(0, 4, add, 0)
            two.start()

    def second_middle(self):
        self.two_a.middle()
        self.two_b.middle()

    def third(self):
        for first, two in ((0, self.two_a), (32, self.two_b)):
            two.arrive()
            for half in range(2):
                value = two.mine(0, half)[...].astype(F32)
                for term in two.terms(half):
                    value += term[...].astype(F32)
                self.out[pl.ds(first + 16 * half, 16), :] = value


class SumX:
    def __init__(self, net, local, parts, held, spare, me, first=0, count=128):
        c, y, z, x = me
        self.local, self.parts, self.held, self.x, self.net = local, parts, held, x, net
        self.first, self.count = first, count
        self.along = lambda d: at(c, y, z, x + d)
        self.ring = RingSum(net, self.along, lambda d, half: self.piece(held, d, half), spare, self.add)

    def piece(self, ref, d, half=None):
        size = self.count // 2
        start, rows = (self.first, self.count) if half is None else (self.first + size * half, size)
        return ref.at[up(self.x, d), pl.ds(start, rows)]

    def add(self, total, term):
        def one(i, carry):
            rows = pl.ds(pl.multiple_of(i * 16, 16), 16)
            total[rows, :] = (total[rows, :].astype(F32) + term[rows, :].astype(F32)).astype(BF)
            return carry

        lax.fori_loop(0, self.count // 32, one, 0)

    def load(self):
        self.loads = [
            self.local.copy(self.piece(self.parts, d), self.piece(self.held, d)) for d in (2, 1, 3, 0)
        ]

    def start(self):
        for copy in self.loads:
            copy.wait()
        self.ring.start()

    def start_held(self):
        self.ring.start()

    def middle(self):
        self.ring.middle()

    def totals(self, step):
        self.ring.arrive()
        for half in range(2):
            terms = self.ring.terms(half)

            def loop(i, carry, half=half, terms=terms):
                rows = pl.ds(pl.multiple_of(i * 32, 32), 32)
                own = pl.ds(pl.multiple_of(self.first + self.count // 2 * half + i * 32, 32), 32)
                value = self.held[self.x, own, :].astype(F32)
                for term in terms:
                    value += term[rows, :].astype(F32)
                step(own, value)
                return carry

            lax.fori_loop(0, self.count // 64, loop, 0)

    def gather(self, block, out):
        self.back = RingGather(self.net, self.along, lambda d, half=None: self.piece(out, d, half))
        rows = block.at[pl.ds(self.first, self.count)]
        self.mine = self.local.copy(rows, self.piece(out, 0))
        self.back.start(rows)

    def gather_middle(self):
        self.back.from_back()
        self.back.from_ahead()

    def finish(self):
        self.mine.wait()
        self.back.arrive()


SUM_COPIES = RING_SUM + RING_GATHER
SUM_LOCALS = 5


def sum_scratch():
    return [pltpu.VMEM((4, 128, D), BF), pltpu.VMEM((6, 64, D), BF)]


def two_sums_scratch():
    return [pltpu.VMEM((4, 128, D), BF), pltpu.VMEM((6, 32, D), BF), pltpu.VMEM((6, 32, D), BF)]


def two_sums(net, local, held, spares, me):
    return [SumX(net, local, None, held, spares[n], me, 64 * n, 64) for n in range(2)]


def normed(values):
    centre = jnp.mean(values, axis=-1, keepdims=True)
    spread = values - centre
    inverse = lax.rsqrt(jnp.mean(spread * spread, axis=-1, keepdims=True) + EPSILON)
    return spread * inverse, inverse


def norm_pullback(upstream, norm, inverse, gain):
    scaled = upstream * gain
    first = jnp.mean(scaled, axis=-1, keepdims=True)
    second = jnp.mean(scaled * norm, axis=-1, keepdims=True)
    return inverse * (scaled - first - norm * second)


ANY = pl.BlockSpec(memory_space=pl.ANY)
IN_VMEM = pl.BlockSpec(memory_space=pltpu.VMEM)
IN_SMEM = pl.BlockSpec(memory_space=pltpu.SMEM)


def remote_call(body, name, cid, ins, outs, scratch, copies, locals_):
    return pl.pallas_call(
        body,
        name=name,
        in_specs=ins,
        out_specs=[spec for _, _, spec in outs],
        out_shape=[jax.ShapeDtypeStruct(shape, dtype) for shape, dtype, _ in outs],
        scratch_shapes=scratch
        + [
            pltpu.SemaphoreType.DMA((copies,)),
            pltpu.SemaphoreType.DMA((copies,)),
            pltpu.SemaphoreType.DMA((locals_,)),
        ],
        compiler_params=pltpu.CompilerParams(
            collective_id=cid, has_side_effects=True, vmem_limit_bytes=VMEM_LIMIT
        ),
    )


def assemble_vectors(weights, gains, bias, spots):
    for s in range(32):
        block = weights[s * 64 : s * 64 + 16, 2048:2176].astype(F32)
        gains[0:4, s * 64 : s * 64 + 64] = block[0:4, :64]
        spots[s : s + 1, :] = block[4:5, :]
    values = spots[...].astype(BF)
    head = lax.broadcasted_iota(jnp.int32, (32, 128), 0)
    held = lax.broadcasted_iota(jnp.int32, (32, 128), 1)
    shard = lax.broadcasted_iota(jnp.int32, (32, 64), 0)
    lane = lax.broadcasted_iota(jnp.int32, (32, 64), 1)
    total = jnp.zeros((32, 64), F32)
    for e in range(2):
        pick = jnp.where((held == 2 * head + e) & (head < 24), 1.0, 0.0).astype(BF)
        spread = jnp.where(lane == 2 * shard + e, 1.0, 0.0).astype(BF)
        total += jnp.dot(nt(pick, values).astype(BF), spread, preferred_element_type=F32)
    for n in range(24):
        bias[0:1, n * 64 : n * 64 + 64] = total[n : n + 1]


def front_forward(shard, tokens, group_place, base, steps):
    def kernel(
        src, x_ref, group_ref, base_ref, steps_ref, front, gains, low, out,
        weights, norm, blocks, bias, spots, turns, ss, rs, ls,
    ):
        me = here()
        c, y, z, x = me
        net, local = Net(ss, rs), Local(ls)
        greet(y_peers(*me) + z_peers(*me) + core_peer(*me))
        gather = Gather(net, local, src, flat_rows(weights), me)
        gather.start()
        for n in range(2):
            rows = slice(n * 128, n * 128 + 128)
            cosine, sine = turn_tables(base_ref, steps_ref, group_ref[(y * 4 + z) * 2 + n])
            turns[0, rows, :] = cosine
            turns[1, rows, :] = sine

        def centre(i, carry):
            rows = pl.ds(pl.multiple_of(i * 32, 32), 32)
            norm[rows, :] = normed(x_ref[rows, :].astype(F32))[0]
            return carry

        lax.fori_loop(0, 4, centre, 0)
        gather.near()
        lax.fori_loop(4, 8, centre, 0)
        gather.middle()
        lax.fori_loop(8, 16, centre, 0)
        for k in (3, 1, 2):
            gather.pass_on(k)
        gather.far()
        gather.finish()
        keep = local.copy(weights, front)
        assemble_vectors(weights, gains, bias, spots)

        def scale(i, carry):
            rows = pl.ds(pl.multiple_of(i * 32, 32), 32)
            low[rows, :] = (norm[rows, :] * gains[0:1, :] + gains[1:2, :]).astype(BF)
            return carry

        lax.fori_loop(0, 16, scale, 0)

        def project(t):
            columns = slice(t * 512, t * 512 + 512)
            for m in range(2):
                acc = jnp.dot(low[m * 256 : m * 256 + 256, :], weights[:, columns], preferred_element_type=F32)
                acc = acc + bias[:, columns]
                for h in range(4):
                    part = acc[:, h * 128 : h * 128 + 128]
                    if t < 2:
                        part = turn(part, turns[0], turns[1])
                    blocks[m, h, (t + 2) % 3] = part.astype(BF)

        along_y = lambda d: at(c, y + d, z, x)
        along_z = lambda d: at(c, y, z + d, x)
        kv = pl.ds(0, 2)

        def part(half):
            return kv if half is None else half

        rings = {}
        for k in range(4):
            rings[0, k] = RingGather(
                net, along_y, lambda d, half=None, k=k: out.at[0, up(y, d), up(z, k), part(half)]
            )
            rings[1, k] = RingGather(
                net, along_z, lambda d, half=None, k=k: out.at[1, up(y, k), up(z, d), part(half)]
            )
        project(1)
        project(2)
        first = {}
        for d in STEPS:
            first[0, d] = net.send(blocks.at[0, up(z, d), kv], out.at[0, y, z, kv], along_z(d))
            first[1, d] = net.send(blocks.at[1, up(y, d), kv], out.at[1, y, z, kv], along_y(d))
        rings[0, 0].start(blocks.at[0, z, kv])
        rings[1, 0].start(blocks.at[1, y, kv])
        project(0)
        last = []
        for d in STEPS:
            last.append(net.send(blocks.at[0, up(z, d), 2], out.at[0, y, z, 2], along_z(d)))
            last.append(net.send(blocks.at[1, up(y, d), 2], out.at[1, y, z, 2], along_y(d)))
        owns = [local.copy(blocks.at[0, z], out.at[0, y, z]), local.copy(blocks.at[1, y], out.at[1, y, z])]
        for d in STEPS:
            for m in range(2):
                first[m, d].wait_recv()
                ring = rings[m, 4 - d]
                ring.start(ring.out(0))
        for k in (0, 3, 1, 2):
            for m in range(2):
                rings[m, k].from_back()
                rings[m, k].from_ahead()
        for ring in rings.values():
            ring.arrive()
        for copy in last:
            copy.wait_recv()
        for copy in owns:
            copy.wait()
        keep.wait()
        net.finish()

    width = shard.shape[1]
    return remote_call(
        kernel,
        "front_forward",
        0,
        [ANY, IN_VMEM, IN_SMEM, IN_VMEM, IN_VMEM],
        [
            ((D, width), BF, ANY),
            ((4, D), F32, IN_VMEM),
            ((512, D), BF, IN_VMEM),
            ((2, 4, 4, 3, 256, 128), BF, ANY),
        ],
        [
            pltpu.VMEM((D, width), BF),
            pltpu.VMEM((512, D), F32),
            pltpu.VMEM((2, 4, 3, 256, 128), BF),
            pltpu.VMEM((1, 1536), F32),
            pltpu.VMEM((32, 128), F32),
            pltpu.VMEM((2, 256, 128), F32),
        ],
        GATHER_COPIES + 12 + 8 * RING_GATHER,
        4,
    )(shard, tokens, group_place, base, steps)


class Swap:
    def __init__(self, net, local, src, out, me):
        c, y, z, x = me
        self.owns = [local.copy(src.at[0, z], out.at[0, z]), local.copy(src.at[1, y], out.at[1, y])]
        self.copies = []
        for d in STEPS:
            self.copies.append(net.send(src.at[0, up(z, d)], out.at[0, z], at(c, y, z + d, x)))
            self.copies.append(net.send(src.at[1, up(y, d)], out.at[1, y], at(c, y + d, z, x)))

    def arrive(self):
        for copy in self.copies:
            copy.wait_recv()
        for copy in self.owns:
            copy.wait()


SWAP_COPIES, SWAP_LOCALS = 6, 2
TURNED = pl.ds(1536, 512)


def middle_forward(heads, front, inputs, gains, shard):
    width = shard.shape[1]

    def kernel(
        heads, front, inputs, gains, shard, attended, hidden, second, weights,
        swapped, out_w, held, spare_0, spare_1, base, low, ss, rs, ls,
    ):
        me = here()
        c, y, z, x = me
        net, local = Net(ss, rs), Local(ls)
        early, late = two_sums(net, local, held, (spare_0, spare_1), me)
        load = local.copy(front.at[:, TURNED], out_w)
        residual = local.copy(inputs.at[x], base)
        greet(y_peers(*me) + z_peers(*me) + core_peer(*me) + x_peers(*me))
        swap = Swap(net, local, heads, swapped, me)
        gather = Gather(net, local, shard, flat_rows(weights), me)
        gather.start()
        load.wait()
        swap.arrive()
        for m in range(2):
            for h in range(4):
                attended[m * 256 : m * 256 + 256, h * 128 : h * 128 + 128] = swapped[m, h]
        for q in range(4):
            held[q] = nt(attended[q * 128 : q * 128 + 128, :], out_w[...]).astype(BF)
        early.start_held()
        gather.near()
        early.middle()
        late.start_held()
        gather.middle()
        residual.wait()

        def step(rows, total):
            value = base[rows, :].astype(F32) + total
            hidden[rows, :] = value
            norm, _ = normed(value)
            low[rows, :] = (norm * gains[2:3, :] + gains[3:4, :]).astype(BF)

        early.totals(step)
        early.gather(low, second)
        late.middle()
        gather.pass_on(3)
        late.totals(step)
        late.gather(low, second)
        gather.pass_on(1)
        early.gather_middle()
        gather.pass_on(2)
        late.gather_middle()
        gather.far()
        gather.finish()
        early.finish()
        late.finish()
        net.finish()

    return remote_call(
        kernel,
        "middle_forward",
        3,
        [ANY, ANY, ANY, IN_VMEM, ANY],
        [
            ((512, 512), BF, IN_VMEM),
            ((128, D), F32, IN_VMEM),
            ((4, 128, D), BF, ANY),
            ((D, width), BF, ANY),
        ],
        [pltpu.VMEM((2, 4, 256, 128), BF), pltpu.VMEM((D, 512), BF)]
        + two_sums_scratch()
        + [pltpu.VMEM((128, D), BF), pltpu.VMEM((128, D), BF)],
        SWAP_COPIES + GATHER_COPIES + 2 * SUM_COPIES,
        SWAP_LOCALS + SUM_LOCALS + 3,
    )(heads, front, inputs, gains, shard)


def other_half(c, k, size):
    core = 1 - c if k < 2 else c
    return pl.ds(pl.multiple_of(core * 1024 + (k % 2) * size, size), size)


def shard_block(k):
    return pl.ds((k % 2) * 2, 2)


def middle_backward(parts, cotangent, hidden, gains, attended, front, second_low, dup, mixed, branch, gate_grad):
    def kernel(
        parts, cotangent, hidden, gains, attended, front, second_low, dup, mixed, branch, gate_grad,
        dhidden, vectors, output_grad, upstream, out_block, gate_out, up_out, down_out,
        held, spare, low, hidden_low, out_w, blocks, lows, dys, extra, *rest,
    ):
        scratch, (ss, rs, ls) = rest[:-3], rest[-3:]
        me = here()
        c, y, z, x = me
        net, local = Net(ss, rs), Local(ls)
        sums = SumX(net, local, parts, held, spare, me)
        sums.load()
        loads = [local.copy(second_low, lows), local.copy(cotangent, dys)]
        load = local.copy(front.at[:, TURNED], out_w)
        greet(y_peers(*me) + z_peers(*me) + core_peer(*me) + x_peers(*me))
        left, right = pl.ds(0, GATE_SPLIT), pl.ds(GATE_SPLIT, UNITS - GATE_SPLIT)
        gate, gate_two, up_, down_ = [
            Scatter(net, local, grads, out, scratch[8 * k : 8 * k + 8], me)
            for k, (grads, out) in enumerate(
                (
                    (gate_grad.at[:, :, :, :, left], gate_out.at[:, left]),
                    (gate_grad.at[:, :, :, :, right], gate_out.at[:, right]),
                    (None, up_out),
                    (None, down_out),
                )
            )
        ]
        gate.start()
        gate_two.start()
        sums.start()

        def multiply(left, right, k, to):
            value = tn(left[:, other_half(c, k, 512)], right[...]).astype(BF)
            to[shard_block(k)] = value.reshape(2, 4, 64, UNITS)

        loads[0].wait()
        for k in range(2):
            multiply(lows, dup, k, down_.held)
        up_.send_filled(down_.held)
        gate.first()
        gate_two.first()
        sums.middle()
        for k in range(2, 4):
            multiply(lows, dup, k, up_.held)
        loads[1].wait()
        for k in range(2):
            multiply(dys, mixed, k, extra)
        down_.send_filled(extra)
        up_.first()
        net.wait_sent(up_.zero)
        gate.first_middle()
        gate_two.first_middle()
        vectors[...] = jnp.zeros_like(vectors)

        def step(rows, dsecond):
            norm, inverse = normed(hidden[rows, :])
            upper = dys[pl.ds(pl.multiple_of(x * 128 + rows.start, 32), 32), :].astype(F32)
            value = upper + norm_pullback(dsecond, norm, inverse, gains[2:3, :])
            dhidden[rows, :] = value
            low[rows, :] = value.astype(BF)
            vectors[0:1, :] += jnp.sum(dsecond * norm, axis=0, keepdims=True)
            vectors[1:2, :] += jnp.sum(dsecond, axis=0, keepdims=True)

        sums.totals(step)
        sums.ring.sent()
        sums.gather(low, hidden_low)
        for k in range(2, 4):
            multiply(dys, mixed, k, down_.held)
        down_.first()
        up_.first_middle()
        gate.second()
        gate_two.second()
        sums.gather_middle()
        late = SumX(net, local, branch, held, spare, me)
        late.load()
        late.start()
        down_.first_middle()
        up_.second()
        load.wait()
        sums.finish()
        for q in range(4):
            rows = slice((q % 2) * 128, (q % 2) * 128 + 128)
            result = jnp.dot(hidden_low[q], out_w[...], preferred_element_type=F32).astype(BF)
            for h in range(4):
                blocks[q // 2, h, rows, :] = result[:, h * 128 : h * 128 + 128]
        swap = Swap(net, local, blocks, upstream, me)
        late.middle()
        gate.second_middle()
        gate_two.second_middle()
        down_.second()
        whole = hidden_low[...].reshape(512, D)
        output_grad[...] = tn(whole, attended[...]).astype(BF)
        up_.second_middle()
        gate.third()
        gate_two.third()
        down_.second_middle()

        def last(rows, total):
            out_block[rows, :] = (hidden[rows, :] + total).astype(BF)

        late.totals(last)
        up_.third()
        down_.third()
        swap.arrive()
        net.finish()

    scratch = sum_scratch() + [
        pltpu.VMEM((128, D), BF),
        pltpu.VMEM((4, 128, D), BF),
        pltpu.VMEM((D, 512), BF),
        pltpu.VMEM((2, 4, 256, 128), BF),
        pltpu.VMEM((512, D), BF),
        pltpu.VMEM((512, D), BF),
        pltpu.VMEM((4, 4, 64, UNITS), BF),
    ]
    return remote_call(
        kernel,
        "middle_backward",
        4,
        [ANY, ANY, IN_VMEM, IN_VMEM, IN_VMEM, ANY, ANY, IN_VMEM, IN_VMEM, ANY, ANY],
        [
            ((128, D), F32, IN_VMEM),
            ((2, D), F32, IN_VMEM),
            ((D, 512), BF, IN_VMEM),
            ((2, 4, 256, 128), BF, ANY),
            ((128, D), BF, IN_VMEM),
        ]
        + [((64, UNITS), F32, IN_VMEM)] * 3,
        scratch
        + scatter_scratch(GATE_SPLIT)
        + scatter_scratch(UNITS - GATE_SPLIT)
        + scatter_scratch(UNITS) * 2,
        SUM_COPIES + RING_SUM + SCATTER_COPIES * 4 + SWAP_COPIES,
        SUM_LOCALS + 4 + SWAP_LOCALS + 4 + 2,
    )(parts, cotangent, hidden, gains, attended, front, second_low, dup, mixed, branch, gate_grad)


def collect_heads(dkv, dq, block):
    def kernel(dkv, dq, block, dproject, outputs, mine, got, summed, ss, rs, ls):
        me = here()
        c, y, z, x = me
        net, local = Net(ss, rs), Local(ls)
        order = (1, 3, 2, 0)
        loads = [local.copy(dkv.at[m], mine.at[m]) for m in range(2)]
        greet(y_peers(*me) + z_peers(*me) + x_peers(*me))
        kv = pl.ds(0, 2)
        along_y = lambda d: at(c, y + d, z, x)
        along_z = lambda d: at(c, y, z + d, x)

        def add(total, term):
            def one(i, carry):
                rows = pl.ds(pl.multiple_of(i * 64, 64), 64)
                total[rows, :] = (total[rows, :].astype(F32) + term[rows, :].astype(F32)).astype(BF)
                return carry

            lax.fori_loop(0, 4, one, 0)

        rings = {}
        for k in order:
            rings[0, k] = RingSum(
                net, along_y, lambda d, half, k=k: mine.at[0, up(y, d), up(z, k), half], got.at[0, k], add
            )
            rings[1, k] = RingSum(
                net, along_z, lambda d, half, k=k: mine.at[1, up(y, k), up(z, d), half], got.at[1, k], add
            )
        whole = SumX(net, local, None, None, None, me)
        whole.gather(block, outputs)
        for copy in loads:
            copy.wait()
        for ring in rings.values():
            ring.start()
        lates = [
            local.copy(dq.at[0, z], dproject.at[0, z, 2]),
            local.copy(dq.at[1, y], dproject.at[1, y, 2]),
        ]
        two = []
        for d in STEPS:
            two.append(net.send(dq.at[0, up(z, d)], dproject.at[0, z, 2], along_z(d)))
            two.append(net.send(dq.at[1, up(y, d)], dproject.at[1, y, 2], along_y(d)))
        for ring in rings.values():
            ring.middle()
        for k in order:
            for m, spot in ((0, z), (1, y)):
                ring = rings[m, k]
                ring.arrive()
                for half in range(2):
                    kept, terms = ring.mine(0, half), ring.terms(half)

                    def total(i, carry, m=m, k=k, half=half, kept=kept, terms=terms):
                        rows = pl.ds(pl.multiple_of(i * 64, 64), 64)
                        value = kept[rows, :].astype(F32)
                        for term in terms:
                            value += term[rows, :].astype(F32)
                        summed[m, k, half, rows, :] = value.astype(BF)
                        return carry

                    lax.fori_loop(0, 4, total, 0)
            if k:
                two.append(net.send(summed.at[0, k], dproject.at[0, z, kv], along_z(k)))
                two.append(net.send(summed.at[1, k], dproject.at[1, y, kv], along_y(k)))
            else:
                lates.append(local.copy(summed.at[0, 0], dproject.at[0, z, kv]))
                lates.append(local.copy(summed.at[1, 0], dproject.at[1, y, kv]))

        whole.gather_middle()
        for copy in two:
            copy.wait_recv()
        for copy in lates:
            copy.wait()
        whole.finish()
        net.finish()

    return remote_call(
        kernel,
        "collect_heads",
        6,
        [ANY, ANY, IN_VMEM],
        [((2, 4, 3, 256, 128), BF, ANY), ((4, 128, D), BF, ANY)],
        [
            pltpu.VMEM((2, 4, 4, 2, 256, 128), BF),
            pltpu.VMEM((2, 4, 6, 256, 128), BF),
            pltpu.VMEM((2, 4, 2, 256, 128), BF),
        ],
        8 * RING_SUM + 6 + 6 + RING_GATHER,
        2 + 4 + 1,
    )(dkv, dq, block)


def last_backward(dproject, first_low, front, inputs, dhidden, gains, mixer_vectors, output_grad):
    def kernel(
        dproject, first_low, front, inputs, dhidden, gains, mixer_vectors, output_grad,
        input_grad, sums_out, project_out, output_out,
        wide, weights, lows, held, spare_0, spare_1, base, low, extra, small, got, *rest,
    ):
        scratch, (ss, rs, ls) = rest[:-3], rest[-3:]
        me = here()
        c, y, z, x = me
        net, local = Net(ss, rs), Local(ls)
        load = local.copy(front.at[:, pl.ds(0, 1536)], weights)
        load_low = local.copy(first_low, lows)
        residual = local.copy(inputs.at[x], base)
        greet(y_peers(*me) + z_peers(*me) + core_peer(*me) + x_peers(*me))
        project = Scatter(net, local, None, project_out, scratch[:8], me)
        output = Scatter(net, local, output_grad, output_out, scratch[8:], me)
        output.start()
        early, late = two_sums(net, local, held, (spare_0, spare_1), me)
        for m in range(2):
            for t in range(3):
                for h in range(4):
                    to = t * 512 + h * 128
                    wide[m * 256 : m * 256 + 256, to : to + 128] = dproject[m, h, (t + 2) % 3]
        load.wait()

        def quarter(d):
            q = up(x, d)
            rows = wide[pl.ds(pl.multiple_of(q * 128, 128), 128), :]
            held[q] = nt(rows, weights[...]).astype(BF)

        quarter(2)
        early.ring.start_far()
        quarter(1)
        quarter(3)
        early.ring.start_near()

        def multiply(k, to):
            value = tn(lows[:, other_half(c, k, 512)], wide[...]).astype(BF)
            to[shard_block(k)] = value.reshape(2, 4, 64, 1536)

        load_low.wait()
        for k in range(2):
            multiply(k, extra)
        project.send_filled(extra)
        early.middle()
        late.ring.start_far()
        late.ring.start_near()
        quarter(0)
        small[0, ...] = jnp.zeros_like(small[0])
        small[0, 2:4, :] = mixer_vectors[...]
        small[0, 4:5, 0:1536] = jnp.sum(wide[...].astype(F32), axis=0, keepdims=True)
        residual.wait()

        def step(rows, dfirst):
            norm, inverse = normed(base[rows, :].astype(F32))
            value = dhidden[rows, :] + norm_pullback(dfirst, norm, inverse, gains[0:1, :])
            low[rows, :] = value.astype(BF)
            small[0, 0:1, :] += jnp.sum(dfirst * norm, axis=0, keepdims=True)
            small[0, 1:2, :] += jnp.sum(dfirst, axis=0, keepdims=True)

        early.totals(step)
        early.gather(low, input_grad)
        late.middle()
        for k in range(2, 4):
            multiply(k, project.held)
        output.first()
        project.first()
        late.totals(step)
        late.gather(low, input_grad)
        copies = [net.send(small.at[0], got.at[0, d - 1], at(c, y, z, x + d)) for d in STEPS]
        output.first_middle()
        project.first_middle()
        early.gather_middle()
        for copy in copies:
            copy.wait_recv()
        small[1, ...] = small[0, ...]
        for n in range(3):
            small[1, 0:4, :] += got[0, n, 0:4, :]
        copies = [net.send(small.at[1], got.at[1, d - 1], at(c, y + d, z, x)) for d in STEPS]
        late.gather_middle()
        output.second()
        project.second()
        for copy in copies:
            copy.wait_recv()
        small[2, ...] = small[1, ...] + got[1, 0] + got[1, 1] + got[1, 2]
        copies = [net.send(small.at[2], got.at[2, d - 1], at(c, y, z + d, x)) for d in STEPS]
        output.second_middle()
        project.second_middle()
        for copy in copies:
            copy.wait_recv()
        small[3, ...] = small[2, ...] + got[2, 0] + got[2, 1] + got[2, 2]
        copy = net.send(small.at[3], got.at[3, 0], at(1 - c, y, z, x))
        output.third()
        project.third()
        copy.wait_recv()
        sums_out[...] = small[3, ...] + got[3, 0]
        early.finish()
        late.finish()
        net.finish()

    scratch = (
        [pltpu.VMEM((512, 1536), BF), pltpu.VMEM((D, 1536), BF), pltpu.VMEM((512, D), BF)]
        + two_sums_scratch()
        + [
            pltpu.VMEM((128, D), BF),
            pltpu.VMEM((128, D), BF),
            pltpu.VMEM((4, 4, 64, 1536), BF),
            pltpu.VMEM((4, 8, D), F32),
            pltpu.VMEM((4, 3, 8, D), F32),
        ]
    )
    return remote_call(
        kernel,
        "last_backward",
        7,
        [IN_VMEM, ANY, ANY, ANY, IN_VMEM, IN_VMEM, IN_VMEM, ANY],
        [
            ((4, 128, D), BF, ANY),
            ((8, D), F32, IN_VMEM),
            ((64, 1536), F32, IN_VMEM),
            ((64, 512), F32, IN_VMEM),
        ],
        scratch + scatter_scratch(1536) + scatter_scratch(512),
        2 * SUM_COPIES + 10 + SCATTER_COPIES * 2,
        SUM_LOCALS + 4,
    )(dproject, first_low, front, inputs, dhidden, gains, mixer_vectors, output_grad)


def turn(values, cosine, sine):
    lane = lax.rem(lax.broadcasted_iota(jnp.int32, values.shape, 1), HEAD_DIM)
    swapped = jnp.where(lane < ROT // 2, -pltpu.roll(values, 120, 1), pltpu.roll(values, 8, 1))
    return values * cosine + swapped * sine


def turn_tables(base, steps, block):
    cosine, sine = base[0], base[1]
    far_cosine, far_sine = steps[0, pl.ds(block, 1), :], steps[1, pl.ds(block, 1), :]
    return far_cosine * cosine - far_sine * sine, far_sine * cosine + far_cosine * sine


def two_heads(block):
    lane = lax.broadcasted_iota(jnp.int32, (128, 128), 1)
    value = block.astype(F32)
    return jnp.concatenate(
        [jnp.where(lane < HEAD_DIM, value, 0.0), jnp.where(lane >= HEAD_DIM, value, 0.0)], axis=0
    )


def two_heads_t(block):
    feature = lax.broadcasted_iota(jnp.int32, (128, 128), 0)
    value = block.astype(F32).T
    return jnp.concatenate(
        [jnp.where(feature < HEAD_DIM, value, 0.0), jnp.where(feature >= HEAD_DIM, value, 0.0)], axis=1
    )


def one_block(stacked):
    feature = lax.broadcasted_iota(jnp.int32, (128, 128), 0)
    return jnp.where(feature < HEAD_DIM, stacked[:, :128], stacked[:, 128:]).T


def nt(left, right):
    return lax.dot_general(left, right, (((1,), (1,)), ((), ())), preferred_element_type=F32)


def plan_blocks(group_place, slots, places):
    _, y, z, _ = here()

    def one(j, carry):
        slots[group_place[j]] = j
        return carry

    lax.fori_loop(0, 32, one, 0)
    for b in range(8):
        places[b] = group_place[(y * 4 + b // 2) * 2 + b % 2]
        places[8 + b] = group_place[((b // 2) * 4 + z) * 2 + b % 2]


def row_of(m, i):
    _, y, z, _ = here()
    return jnp.where(m == 0, y * 4 + i, i * 4 + z)


def unit_of(places, m, n):
    pair, rest = n // 9, lax.rem(n, 9)
    ahead = places[m * 8 + pair * 2] // (TILE // 128) + 1
    late = rest >= ahead
    block = pair * 2 + jnp.where(late, 1, 0)
    tile = rest - jnp.where(late, ahead, 0)
    return block, tile, places[m * 8 + block] * 128 - tile * TILE


def lay_mask(steps, bars):
    row = lax.broadcasted_iota(jnp.int32, (1024, 128), 0) - 513
    lane = lax.broadcasted_iota(jnp.int32, (1024, 128), 1)
    steps[...] = jnp.where(jnp.minimum(row, 127) == lane, 1.0, 0.0).astype(BF)
    bar = lax.broadcasted_iota(jnp.int32, (128, 256), 0)
    query = lax.rem(lax.broadcasted_iota(jnp.int32, (128, 256), 1), 128)
    bars[...] = jnp.where(bar >= query, LOW, 0.0).astype(BF)


def with_mask(keys, steps, behind):
    first = 512 - jnp.minimum(behind, 512)
    return jnp.concatenate([keys, steps[pl.ds(pl.multiple_of(first, 128), TILE), :]], axis=1)


def tile_of(t):
    return pl.ds(pl.multiple_of(t * TILE, TILE), TILE)


def lay_blocks(slots, lay):
    def some(n, carry):
        for k in range(4):
            b = n * 4 + k
            slot = slots[b]
            rows = pl.ds(pl.multiple_of(lax.rem(slot, 2) * 128, 128), 128)
            lay(slot // 2, rows, pl.ds(pl.multiple_of(b * 128, 128), 128))
        return carry

    lax.fori_loop(0, 8, some, 0)


UNITS_EACH = 36


def attend(group_place, spread):
    def kernel(
        group_ref, k_ref, v_ref, q_ref, o_ref, full_ref, log_ref,
        slots, places, keys, values_t, queries, scores_0, scores_1, weights_0, weights_1, results, tops, steps, bars,
    ):
        scores, weights = (scores_0, scores_1), (weights_0, weights_1)
        m = pl.program_id(0)
        plan_blocks(group_ref, slots, places)

        def lay(slot, rows, to):
            keys[to, :] = k_ref[0, slot, 0, rows, :]
            values_t[:128, to] = v_ref[0, slot, 0, rows, :].T

        lay_blocks(slots, lay)
        for b in range(8):
            row = row_of(m, b // 2)
            block = q_ref[0, row, 0, (b % 2) * 128 : (b % 2) * 128 + 128, :]
            queries[b, :128] = (two_heads_t(block) * 0.125).astype(BF)
        lay_mask(steps, bars)
        for b in range(8):
            queries[b, 128:] = bars[...]
        values_t[128:, :] = jnp.ones((16, 4096), BF)

        def multiply(n, odd):
            block, tile, behind = unit_of(places, m, n)
            scores[odd][...] = jnp.dot(
                with_mask(keys[tile_of(tile), :], steps, behind), queries[block], preferred_element_type=F32
            )

        def soften(n, odd, top):
            block, tile, _ = unit_of(places, m, n)
            value = scores[odd][...] * LOG2E
            top = jnp.where(tile == 0, LOW, top)
            new_top = jnp.maximum(top, jnp.max(value, axis=0, keepdims=True))
            weights[odd][...] = jnp.exp2(value - new_top).astype(BF)
            tops[block, 0:1, :] = new_top
            return new_top, jnp.exp2(top - new_top)

        def gather(n, odd, shrink, acc):
            block, tile, _ = unit_of(places, m, n)
            acc = acc * shrink + jnp.dot(
                values_t[:, tile_of(tile)], weights[odd][...], preferred_element_type=F32
            )
            results[block] = acc
            return acc

        multiply(0, 0)
        multiply(1, 1)
        top, shrink = soften(0, 0, jnp.zeros((1, 256), F32))

        def step(k, carry):
            top, shrink, acc = carry
            for n, odd in ((2 * k + 1, 1), (2 * k + 2, 0)):
                multiply(n + 1, 1 - odd)
                acc = gather(n - 1, 1 - odd, shrink, acc)
                top, shrink = soften(n, odd, top)
            return top, shrink, acc

        carry = (top, shrink, jnp.zeros((144, 256), F32))
        top, shrink, acc = lax.fori_loop(0, UNITS_EACH // 2 - 1, step, carry)
        last = UNITS_EACH - 1
        acc = gather(last - 1, 0, shrink, acc)
        _, shrink = soften(last, 1, top)
        gather(last, 1, shrink, acc)
        for b in range(8):
            rows = slice((b % 2) * 128, (b % 2) * 128 + 128)
            total = results[b, 128:129, :]
            result = one_block(results[b, :128, :] / total)
            full_ref[0, b // 2, rows, :] = result
            o_ref[0, b // 2, rows, :] = result.astype(BF)
            log_ref[0, b : b + 1, :] = tops[b, 0:1, :] + jnp.log2(total)

    grid_spec = pltpu.PrefetchScalarGridSpec(
        num_scalar_prefetch=1,
        grid=(2,),
        in_specs=[
            pl.BlockSpec((1, 16, 1, 256, 128), lambda m, g: (m, 0, 0, 0, 0)),
            pl.BlockSpec((1, 16, 1, 256, 128), lambda m, g: (m, 0, 1, 0, 0)),
            pl.BlockSpec((1, 16, 1, 256, 128), lambda m, g: (m, 0, 2, 0, 0)),
        ],
        out_specs=[
            pl.BlockSpec((1, 4, 256, 128), lambda m, g: (m, 0, 0, 0)),
            pl.BlockSpec((1, 4, 256, 128), lambda m, g: (m, 0, 0, 0)),
            pl.BlockSpec((1, 8, 256), lambda m, g: (m, 0, 0)),
        ],
        scratch_shapes=[
            pltpu.SMEM((32,), jnp.int32),
            pltpu.SMEM((16,), jnp.int32),
            pltpu.VMEM((4096, 128), BF),
            pltpu.VMEM((144, 4096), BF),
            pltpu.VMEM((8, 256, 256), BF),
            pltpu.VMEM((TILE, 256), F32),
            pltpu.VMEM((TILE, 256), F32),
            pltpu.VMEM((TILE, 256), BF),
            pltpu.VMEM((TILE, 256), BF),
            pltpu.VMEM((8, 144, 256), F32),
            pltpu.VMEM((8, 8, 256), F32),
            pltpu.VMEM((1024, 128), BF),
            pltpu.VMEM((128, 256), BF),
        ],
    )
    return pl.pallas_call(
        kernel,
        name="attend",
        grid_spec=grid_spec,
        out_shape=[
            jax.ShapeDtypeStruct((2, 4, 256, 128), BF),
            jax.ShapeDtypeStruct((2, 4, 256, 128), F32),
            jax.ShapeDtypeStruct((2, 8, 256), F32),
        ],
        compiler_params=pltpu.CompilerParams(vmem_limit_bytes=VMEM_LIMIT),
    )(group_place, spread, spread, spread)


def attend_back(group_place, spread, full, logs, upstream, base, steps):
    def kernel(
        group_ref, k_ref, v_ref, q_ref, full_ref, log_ref, up_ref, base_ref, steps_ref,
        dq_ref, dkv_ref,
        slots, places, keys, keys_t, values, dkeys, dvalues, queries, queries_t, grads, grads_t, delta,
        scores_0, scores_1, dprobs_0, dprobs_1, probs_0, probs_1, dscores_0, dscores_1, results, steps, bars,
    ):
        scores, dprobs = (scores_0, scores_1), (dprobs_0, dprobs_1)
        probs_low, dscores = (probs_0, probs_1), (dscores_0, dscores_1)
        m = pl.program_id(0)
        plan_blocks(group_ref, slots, places)

        def lay(slot, rows, to):
            block = k_ref[0, slot, 0, rows, :]
            keys[to, :] = block
            keys_t[:, to] = block.T
            values[to, :] = v_ref[0, slot, 0, rows, :]
            dkeys[to, :] = jnp.zeros((128, 128), F32)
            dvalues[to, :] = jnp.zeros((128, 128), F32)

        lay_blocks(slots, lay)
        for b in range(8):
            rows = slice((b % 2) * 128, (b % 2) * 128 + 128)
            block = q_ref[0, row_of(m, b // 2), 0, rows, :]
            queries[b] = (two_heads(block) * 0.125).astype(BF)
            queries_t[b, :128] = (two_heads_t(block) * 0.125).astype(BF)
            ups = up_ref[0, b // 2, rows, :]
            grads[b] = two_heads(ups).astype(BF)
            grads_t[b] = two_heads_t(ups).astype(BF)
            product = (ups.astype(F32) * full_ref[0, b // 2, rows, :]).T
            delta[b, 0:1, :128] = jnp.sum(product[:HEAD_DIM], axis=0, keepdims=True)
            delta[b, 0:1, 128:] = jnp.sum(product[HEAD_DIM:], axis=0, keepdims=True)
        lay_mask(steps, bars)
        for b in range(8):
            queries_t[b, 128:] = bars[...]

        def multiply(n, odd):
            block, tile, behind = unit_of(places, m, n)
            scores[odd][...] = jnp.dot(
                with_mask(keys[tile_of(tile), :], steps, behind), queries_t[block], preferred_element_type=F32
            )
            dprobs[odd][...] = jnp.dot(
                values[tile_of(tile), :], grads_t[block], preferred_element_type=F32
            )

        def soften(n, odd):
            block, _, _ = unit_of(places, m, n)
            value = jnp.exp2(scores[odd][...] * LOG2E - log_ref[0, pl.ds(block, 1), :])
            probs_low[odd][...] = value.astype(BF)
            dscores[odd][...] = (
                value * (dprobs[odd][...] - delta[block, 0:1, :])
            ).astype(BF)

        def gather(n, odd, acc):
            block, tile, _ = unit_of(places, m, n)
            span = tile_of(tile)
            dvalues[span, :] += jnp.dot(probs_low[odd][...], grads[block], preferred_element_type=F32)
            dkeys[span, :] += jnp.dot(dscores[odd][...], queries[block], preferred_element_type=F32)
            acc = jnp.where(tile == 0, 0.0, acc) + jnp.dot(
                keys_t[:, span], dscores[odd][...], preferred_element_type=F32
            )
            results[block] = acc
            return acc

        multiply(0, 0)
        multiply(1, 1)
        soften(0, 0)

        def step(k, acc):
            for n, odd in ((2 * k + 1, 1), (2 * k + 2, 0)):
                multiply(n + 1, 1 - odd)
                acc = gather(n - 1, 1 - odd, acc)
                soften(n, odd)
            return acc

        last = UNITS_EACH - 1
        acc = lax.fori_loop(0, UNITS_EACH // 2 - 1, step, jnp.zeros((128, 256), F32))
        acc = gather(last - 1, 0, acc)
        soften(last, 1)
        gather(last, 1, acc)

        def turned_back(values, place):
            cosine, sine = turn_tables(base_ref, steps_ref, place)
            return turn(values, cosine, -sine)

        for b in range(8):
            rows = slice((b % 2) * 128, (b % 2) * 128 + 128)
            dquery = one_block(results[b]) * 0.125
            dq_ref[0, b // 2, rows, :] = turned_back(dquery, places[m * 8 + b]).astype(BF)

        def flush(n, carry):
            for k in range(2):
                b = n * 2 + k
                slot = slots[b]
                rows = pl.ds(pl.multiple_of(lax.rem(slot, 2) * 128, 128), 128)
                to = pl.ds(pl.multiple_of(b * 128, 128), 128)
                dkv_ref[0, slot // 2, 0, rows, :] = turned_back(dkeys[to, :], b).astype(BF)
                dkv_ref[0, slot // 2, 1, rows, :] = dvalues[to, :].astype(BF)
            return carry

        lax.fori_loop(0, 16, flush, 0)

    grid_spec = pltpu.PrefetchScalarGridSpec(
        num_scalar_prefetch=1,
        grid=(2,),
        in_specs=[
            pl.BlockSpec((1, 16, 1, 256, 128), lambda m, g: (m, 0, 0, 0, 0)),
            pl.BlockSpec((1, 16, 1, 256, 128), lambda m, g: (m, 0, 1, 0, 0)),
            pl.BlockSpec((1, 16, 1, 256, 128), lambda m, g: (m, 0, 2, 0, 0)),
            pl.BlockSpec((1, 4, 256, 128), lambda m, g: (m, 0, 0, 0)),
            pl.BlockSpec((1, 8, 256), lambda m, g: (m, 0, 0)),
            pl.BlockSpec((1, 4, 256, 128), lambda m, g: (m, 0, 0, 0)),
            pl.BlockSpec((2, 128, 128), lambda m, g: (0, 0, 0)),
            pl.BlockSpec((2, 32, 128), lambda m, g: (0, 0, 0)),
        ],
        out_specs=[
            pl.BlockSpec((1, 4, 256, 128), lambda m, g: (m, 0, 0, 0)),
            pl.BlockSpec((1, 16, 2, 256, 128), lambda m, g: (m, 0, 0, 0, 0)),
        ],
        scratch_shapes=[
            pltpu.SMEM((32,), jnp.int32),
            pltpu.SMEM((16,), jnp.int32),
            pltpu.VMEM((4096, 128), BF),
            pltpu.VMEM((128, 4096), BF),
            pltpu.VMEM((4096, 128), BF),
            pltpu.VMEM((4096, 128), F32),
            pltpu.VMEM((4096, 128), F32),
            pltpu.VMEM((8, 256, 128), BF),
            pltpu.VMEM((8, 256, 256), BF),
            pltpu.VMEM((8, 256, 128), BF),
            pltpu.VMEM((8, 128, 256), BF),
            pltpu.VMEM((8, 8, 256), F32),
            pltpu.VMEM((TILE, 256), F32),
            pltpu.VMEM((TILE, 256), F32),
            pltpu.VMEM((TILE, 256), F32),
            pltpu.VMEM((TILE, 256), F32),
            pltpu.VMEM((TILE, 256), BF),
            pltpu.VMEM((TILE, 256), BF),
            pltpu.VMEM((TILE, 256), BF),
            pltpu.VMEM((TILE, 256), BF),
            pltpu.VMEM((8, 128, 256), F32),
            pltpu.VMEM((1024, 128), BF),
            pltpu.VMEM((128, 256), BF),
        ],
    )
    return pl.pallas_call(
        kernel,
        name="attend_back",
        grid_spec=grid_spec,
        out_shape=[
            jax.ShapeDtypeStruct((2, 4, 256, 128), BF),
            jax.ShapeDtypeStruct((2, 16, 2, 256, 128), BF),
        ],
        compiler_params=pltpu.CompilerParams(vmem_limit_bytes=VMEM_LIMIT),
    )(group_place, spread, spread, spread, full, logs, upstream, base, steps)


def tn(left, right):
    return lax.dot_general(left, right, (((0,), (0,)), ((), ())), preferred_element_type=F32)


def feed_forward(second_low, dy, weights):
    def kernel(
        low_hbm, dy_hbm, w_hbm, branch, dsecond, gate_out, dup, mixed,
        low, dys, gate_w, up_w, down_w, gate, up, dmixed, dgate, chunks, sems, chunk_sems,
    ):
        def load(n, src, dst):
            copy = pltpu.make_async_copy(src, dst, sems.at[n])
            copy.start()
            return copy

        def columns(k):
            return w_hbm.at[:, pl.ds(k * UNITS, UNITS)]

        loads = [
            load(0, low_hbm, low),
            load(1, columns(0), gate_w),
            load(2, columns(1), up_w),
            load(3, dy_hbm, dys),
            load(4, columns(2), down_w),
        ]
        loads[0].wait()
        loads[1].wait()
        gate[...] = jnp.dot(low[...], gate_w[...], preferred_element_type=F32)
        loads[2].wait()
        up[...] = jnp.dot(low[...], up_w[...], preferred_element_type=F32)
        loads[3].wait()
        loads[4].wait()
        dmixed[...] = jnp.dot(dys[...], down_w[...], preferred_element_type=F32)

        def step(i, carry):
            rows = pl.ds(pl.multiple_of(i * 16, 16), 16)
            g, u, d = gate[rows, :], up[rows, :], dmixed[rows, :]
            s = jax.nn.sigmoid(g)
            silu = g * s
            mixed[rows, :] = (silu * u).astype(BF)
            dgate[rows, :] = (d * u * s * (1.0 + g * (1.0 - s))).astype(BF)
            dup[rows, :] = (d * silu).astype(BF)
            return carry

        lax.fori_loop(0, 32, step, 0)
        dsecond[...] = (nt(dgate[...], gate_w[...]) + nt(dup[...], up_w[...])).astype(BF)
        busy = {}
        for k in range(4):
            rows = pl.ds(k * 512, 512)
            slot = k % 2
            if slot in busy:
                busy[slot].wait()
            chunks[slot] = tn(low[:, rows], dgate[...]).astype(BF)
            busy[slot] = pltpu.make_async_copy(chunks.at[slot], gate_out.at[rows, :], chunk_sems.at[slot])
            busy[slot].start()
        branch[...] = nt(mixed[...], down_w[...]).astype(BF)
        busy[0].wait()
        busy[1].wait()

    return pl.pallas_call(
        kernel,
        name="feed_forward",
        in_specs=[ANY, ANY, ANY],
        out_specs=[IN_VMEM, IN_VMEM, ANY, IN_VMEM, IN_VMEM],
        out_shape=[jax.ShapeDtypeStruct((512, D), BF)] * 2
        + [jax.ShapeDtypeStruct((D, UNITS), BF)]
        + [jax.ShapeDtypeStruct((512, UNITS), BF)] * 2,
        scratch_shapes=[pltpu.VMEM((512, D), BF)] * 2
        + [pltpu.VMEM((D, UNITS), BF)] * 3
        + [pltpu.VMEM((512, UNITS), F32)] * 3
        + [
            pltpu.VMEM((512, UNITS), BF),
            pltpu.VMEM((2, 512, UNITS), BF),
            pltpu.SemaphoreType.DMA((5,)),
            pltpu.SemaphoreType.DMA((2,)),
        ],
        compiler_params=pltpu.CompilerParams(vmem_limit_bytes=VMEM_LIMIT),
    )(second_low, dy, weights)


def angle_tables():
    lane = np.arange(128) % HEAD_DIM
    power = 10000.0 ** (-2.0 * (lane % (ROT // 2)) / ROT)
    frequency = np.where(lane < ROT, power, 0.0)
    tables = []
    for places in (np.arange(128), np.arange(32) * 128):
        angles = places[:, None] * frequency[None, :]
        tables.append(jnp.asarray(np.stack([np.cos(angles), np.sin(angles)]).astype(np.float32)))
    return tables


def body(
    inputs,
    cotangent,
    group_place,
    attend_gain,
    attend_shift,
    project_weight,
    project_bias,
    output_weight,
    mixer_gain,
    mixer_shift,
    gate_weight,
    up_weight,
    down_weight,
):
    shard_index = lax.axis_index("dp") * 16 + lax.axis_index("ctx")
    base, steps = angle_tables()

    vectors = jnp.stack([attend_gain, attend_shift, mixer_gain, mixer_shift])
    vectors = jnp.concatenate(
        [
            jnp.pad(vectors, ((0, 0), (0, 64))),
            jnp.pad(project_bias.reshape(1, 48), ((0, 0), (0, 80))),
            jnp.zeros((59, 128), BF),
        ]
    )
    front_shard = jnp.concatenate(
        [project_weight.reshape(64, 1536), output_weight.T, vectors], axis=1
    )
    back_shard = jnp.concatenate([gate_weight, up_weight, down_weight.T], axis=1)

    tokens = inputs.reshape(512, D)
    quarters = inputs.reshape(4, 128, D)
    front, gains, first_low, spread = front_forward(front_shard, tokens, group_place, base, steps)
    spread = spread.reshape(2, 16, 3, 256, 128)
    attended_heads, attended_full, logs = attend(group_place, spread)
    attended_low, hidden, second_low, back = middle_forward(
        attended_heads, front, quarters, gains, back_shard
    )

    second_low = second_low.reshape(512, D)
    dy = cotangent.reshape(512, D)
    branch, second_part, gate_grad, dup, mixed = feed_forward(second_low, dy, back)
    dhidden, mixer_vectors, output_grad, upstream, out_block, gate_grad, up_grad, down_grad = middle_backward(
        second_part.reshape(4, 128, D),
        dy,
        hidden,
        gains,
        attended_low,
        front,
        second_low,
        dup,
        mixed,
        branch.reshape(4, 128, D),
        gate_grad.reshape(2, 4, 4, 64, UNITS),
    )

    dq, dkv = attend_back(group_place, spread, attended_full, logs, upstream, base, steps)
    dproject, outputs = collect_heads(dkv.reshape(2, 4, 4, 2, 256, 128), dq, out_block)
    input_grad, small, project_grad, output_grad = last_backward(
        dproject, first_low, front, quarters, dhidden, gains, mixer_vectors, output_grad.reshape(2, 4, 4, 64, 512)
    )
    own = lax.dynamic_slice(small, (0, shard_index * 64), (4, 64))
    bias_grad = lax.dynamic_slice(
        small[4, :1536].reshape(3, 8, 64), (0, 0, shard_index * 2), (3, 8, 2)
    )
    shape = inputs.shape
    return (
        outputs.reshape(shape),
        input_grad.reshape(shape),
        own[0],
        own[1],
        project_grad.reshape(64, 3, 512),
        bias_grad,
        output_grad.T,
        own[2],
        own[3],
        gate_grad,
        up_grad,
        down_grad.T,
    )


def solution(mesh):
    weight = ("dp", "ctx")
    rows = P(None, "dp", "ctx", None)
    vector = P(weight)
    matrix = P(weight, "tensor")
    turned = P("tensor", weight)
    project = P(weight, None, "tensor")
    bias = P(None, "tensor", weight)
    params = (vector, vector, project, bias, turned, vector, vector, matrix, matrix, turned)
    return jax.shard_map(
        body,
        mesh=mesh,
        in_specs=(rows, rows, P()) + params,
        out_specs=(rows, rows) + params,
        check_vma=False,
    )
```

```python
import functools

import jax
import jax.numpy as jnp
import numpy as np
from jax import lax
from jax.experimental import pallas as pl
from jax.experimental.pallas import tpu as pltpu
from jax.sharding import PartitionSpec as P

MESH = pl.DeviceIdType.MESH
D = 2048
UNITS = 1408
HEAD_DIM = 64
ROT = 16
EPSILON = 1e-05
LOG2E = 1.4426950408889634
LOW = -1e30
TILE = 512
ROWS = 64
AT_ONCE = 34
VMEM_LIMIT = 58 * 2**20
STEPS = (1, 3, 2)
BF = jnp.bfloat16
F32 = jnp.float32


def here():
    ctx = lax.axis_index("ctx")
    return (lax.axis_index("dp"), ctx // 4, lax.rem(ctx, 4), lax.axis_index("tensor"))


def at(c, y, z, x):
    return (c, lax.rem(y, 4) * 4 + lax.rem(z, 4), lax.rem(x, 4))


def up(i, d):
    return lax.rem(i + d, 4)


def down(i, d):
    return lax.rem(i + 4 - d, 4)


class Net:
    def __init__(self, send_sems, recv_sems):
        self.send_sems, self.recv_sems = send_sems, recv_sems
        self.sent, self.gone = [], set()

    def send(self, src, dst, device):
        n = len(self.sent)
        copy = pltpu.make_async_remote_copy(
            src_ref=src,
            dst_ref=dst,
            send_sem=self.send_sems.at[n],
            recv_sem=self.recv_sems.at[n],
            device_id=device,
            device_id_type=MESH,
        )
        copy.start()
        self.sent.append(copy)
        return copy

    def finish(self):
        for n, copy in enumerate(self.sent):
            if n not in self.gone:
                copy.wait_send()

    def wait_sent(self, copy):
        copy.wait_send()
        self.gone.add([other is copy for other in self.sent].index(True))


class Local:
    def __init__(self, sems):
        self.sems, self.n = sems, 0

    def copy(self, src, dst):
        copy = pltpu.make_async_copy(src, dst, self.sems.at[self.n])
        copy.start()
        self.n += 1
        return copy


def greet(peers):
    barrier = pltpu.get_barrier_semaphore()
    for peer in peers:
        pl.semaphore_signal(barrier, inc=1, device_id=peer, device_id_type=MESH)
    pl.semaphore_wait(barrier, len(peers))


def y_peers(c, y, z, x):
    return [at(c, y + d, z, x) for d in (1, 2, 3)]


def z_peers(c, y, z, x):
    return [at(c, y, z + d, x) for d in (1, 2, 3)]


def x_peers(c, y, z, x):
    return [at(c, y, z, x + d) for d in (1, 2, 3)]


def core_peer(c, y, z, x):
    return [at(1 - c, y, z, x)]


class RingSum:
    def __init__(self, net, device, mine, spare, add):
        self.net, self.device, self.mine, self.spare, self.add = net, device, mine, spare, add

    def start(self):
        self.start_far()
        self.start_near()

    def start_far(self):
        send, mine, spare = self.net.send, self.mine, self.spare
        ahead, back = self.device(1), self.device(3)
        self.far_ahead = send(mine(2, 0), spare.at[0], ahead)
        self.far_back = send(mine(2, 1), spare.at[1], back)

    def start_near(self):
        send, mine, spare = self.net.send, self.mine, self.spare
        ahead, back = self.device(1), self.device(3)
        self.near = [send(mine(1, 1), spare.at[3], ahead), send(mine(3, 0), spare.at[2], back)]

    def middle(self):
        send, spare = self.net.send, self.spare
        self.far_ahead.wait_recv()
        self.add(spare.at[0], self.mine(1, 0))
        self.near.append(send(spare.at[0], spare.at[4], self.device(1)))
        self.far_back.wait_recv()
        self.add(spare.at[1], self.mine(3, 1))
        self.near.append(send(spare.at[1], spare.at[5], self.device(3)))

    def arrive(self):
        for copy in self.near:
            copy.wait_recv()

    def sent(self):
        for copy in [self.far_ahead, self.far_back] + self.near:
            self.net.wait_sent(copy)

    def terms(self, half):
        return [self.spare.at[4 if half == 0 else 3], self.spare.at[2 if half == 0 else 5]]


RING_SUM = 6


class RingGather:
    def __init__(self, net, device, out):
        self.net, self.device, self.out = net, device, out

    def start(self, block):
        self.ahead = self.net.send(block, self.out(0), self.device(1))
        self.back = self.net.send(block, self.out(0), self.device(3))

    def from_back(self):
        self.ahead.wait_recv()
        piece = self.out(3, 0)
        self.far_ahead = self.net.send(piece, piece, self.device(1))

    def from_ahead(self):
        self.back.wait_recv()
        piece = self.out(1, 1)
        self.far_back = self.net.send(piece, piece, self.device(3))

    def arrive(self):
        self.far_ahead.wait_recv()
        self.far_back.wait_recv()


RING_GATHER = 4


class Gather:
    def __init__(self, net, local, src, place, me):
        self.net, self.local, self.src, self.place, self.me = net, local, src, place, me
        self.core = []
        c, y, z, x = me
        along_y = lambda d: at(c, y + d, z, x)
        along_z = lambda d: at(c, y, z + d, x)

        def spot(far_y, far_z, first, half):
            if half is None:
                return place(c, up(y, far_y), up(z, far_z), first, 32)
            return place(c, up(y, far_y), up(z, far_z), first + 16 * half, 16)

        self.one = (
            RingGather(net, along_y, lambda d, half=None: spot(d, 0, 0, half)),
            RingGather(net, along_z, lambda d, half=None: spot(0, d, 32, half)),
        )
        self.two = {}
        for k in range(4):
            self.two[0, k] = RingGather(net, along_z, lambda d, half=None, k=k: spot(k, d, 0, half))
            self.two[1, k] = RingGather(net, along_y, lambda d, half=None, k=k: spot(d, k, 32, half))

    def hand_over(self, piece):
        c, y, z, x = self.me
        self.core.append(self.net.send(piece, piece, at(1 - c, y, z, x)))

    def start(self):
        c, y, z, x = self.me
        src, own = self.src, self.place(c, y, z, 0, 64)
        self.own = self.local.copy(src, own)
        halves = (src.at[pl.ds(0, 32)], src.at[pl.ds(32, 32)])
        for way in range(2):
            self.one[way].start(halves[way])
        for way in range(2):
            self.two[way, 0].start(halves[way])
        self.core.append(self.net.send(src, own, at(1 - c, y, z, x)))

    def near(self):
        for way in range(2):
            self.one[way].from_back()
            self.two[way, 3].start(self.one[way].out(3))
        for way in range(2):
            self.one[way].from_ahead()
            self.two[way, 1].start(self.one[way].out(1))
        for k in (3, 1):
            for way in range(2):
                self.hand_over(self.one[way].out(k))

    def middle(self):
        self.pass_on(0)
        for way in range(2):
            self.one[way].arrive()
            self.two[way, 2].start(self.one[way].out(2))
            self.hand_over(self.one[way].out(2))

    def pass_on(self, k):
        for way in range(2):
            self.two[way, k].from_back()
            self.two[way, k].from_ahead()
            self.hand_over(self.two[way, k].out(3))
            self.hand_over(self.two[way, k].out(1))

    def far(self):
        for k in (0, 3, 1, 2):
            for way in range(2):
                self.two[way, k].arrive()
                self.hand_over(self.two[way, k].out(2))

    def finish(self):
        for copy in self.core:
            copy.wait_recv()
        self.own.wait()


def flat_rows(ref):
    def place(c, y, z, first, count):
        return ref.at[pl.ds(pl.multiple_of(((c * 4 + y) * 4 + z) * 64 + first, 16), count)]

    return place


GATHER_COPIES = 10 * RING_GATHER + 31


def scatter_scratch(width):
    return [
        pltpu.VMEM((4, 4, 64, width), BF),
        pltpu.VMEM((4, 4, 64, width), BF),
        pltpu.VMEM((6, 4, 16, width), BF),
        pltpu.VMEM((6, 4, 16, width), BF),
        pltpu.VMEM((4, 32, width), BF),
        pltpu.VMEM((4, 32, width), BF),
        pltpu.VMEM((6, 16, width), BF),
        pltpu.VMEM((6, 16, width), BF),
    ]


SCATTER_COPIES = 1 + 4 * RING_SUM


def add_blocks(total, term):
    if len(total.shape) == 2:
        total[...] = (total[...].astype(F32) + term[...].astype(F32)).astype(BF)
        return

    def one(i, carry):
        total[i] = (total[i].astype(F32) + term[i].astype(F32)).astype(BF)
        return carry

    lax.fori_loop(0, total.shape[0], one, 0)


class Scatter:
    def __init__(self, net, local, grads, out, scratch, me):
        self.net, self.local, self.grads, self.out, self.me = net, local, grads, out, me
        (held, self.other, one_a, one_b, self.sum_a, self.sum_b, two_a, two_b) = scratch
        self.held = held
        c, y, z, x = me
        along_y = lambda d: at(c, y + d, z, x)
        along_z = lambda d: at(c, y, z + d, x)
        self.one_a = RingSum(
            net, along_z, lambda d, half: held.at[:, up(z, d), pl.ds(16 * half, 16)], one_a, add_blocks
        )
        self.one_b = RingSum(
            net, along_y, lambda d, half: held.at[up(y, d), :, pl.ds(32 + 16 * half, 16)], one_b, add_blocks
        )
        self.two_a = RingSum(
            net, along_y, lambda d, half: self.sum_a.at[up(y, d), pl.ds(16 * half, 16)], two_a, add_blocks
        )
        self.two_b = RingSum(
            net, along_z, lambda d, half: self.sum_b.at[up(z, d), pl.ds(16 * half, 16)], two_b, add_blocks
        )

    def start(self):
        c, y, z, x = self.me
        self.own = self.local.copy(self.grads.at[c], self.held)
        self.zero = self.net.send(self.grads.at[1 - c], self.other, at(1 - c, y, z, x))

    def send_filled(self, block):
        c, y, z, x = self.me
        self.own = None
        self.zero = self.net.send(block, self.other, at(1 - c, y, z, x))

    def first(self):
        if self.own is not None:
            self.own.wait()
        self.zero.wait_recv()
        held, other = self.held, self.other

        def add(i, carry):
            for q in range(4):
                rows = pl.ds(q * 16, 16)
                held[i // 4, lax.rem(i, 4), rows, :] = (
                    held[i // 4, lax.rem(i, 4), rows, :].astype(F32)
                    + other[i // 4, lax.rem(i, 4), rows, :].astype(F32)
                ).astype(BF)
            return carry

        lax.fori_loop(0, 16, add, 0)
        self.one_a.start()
        self.one_b.start()

    def first_middle(self):
        self.one_a.middle()
        self.one_b.middle()

    def second(self):
        for one, two, total in ((self.one_a, self.two_a, self.sum_a), (self.one_b, self.two_b, self.sum_b)):
            one.arrive()
            for half in range(2):
                own, terms = one.mine(0, half), one.terms(half)

                def add(i, carry, half=half, own=own, terms=terms, total=total):
                    value = own[i].astype(F32)
                    for term in terms:
                        value += term[i].astype(F32)
                    total[i, pl.ds(16 * half, 16), :] = value.astype(BF)
                    return carry

                lax.fori_loop(0, 4, add, 0)
            two.start()

    def second_middle(self):
        self.two_a.middle()
        self.two_b.middle()

    def third(self):
        for first, two in ((0, self.two_a), (32, self.two_b)):
            two.arrive()
            for half in range(2):
                value = two.mine(0, half)[...].astype(F32)
                for term in two.terms(half):
                    value += term[...].astype(F32)
                self.out[pl.ds(first + 16 * half, 16), :] = value


def quarters_of(net, out, me):
    c, y, z, x = me

    def piece(d, half=None):
        return out.at[up(x, d)] if half is None else out.at[up(x, d), pl.ds(64 * half, 64)]

    return RingGather(net, lambda d: at(c, y, z, x + d), piece)


class SumX:
    def __init__(self, net, local, parts, held, spare, me):
        c, y, z, x = me
        self.local, self.parts, self.held, self.x, self.net, self.me = local, parts, held, x, net, me
        self.along = lambda d: at(c, y, z, x + d)
        self.ring = RingSum(
            net, self.along, lambda d, half: held.at[up(x, d), pl.ds(64 * half, 64)], spare, self.add
        )

    def add(self, total, term):
        def one(i, carry):
            rows = pl.ds(pl.multiple_of(i * 16, 16), 16)
            total[rows, :] = (total[rows, :].astype(F32) + term[rows, :].astype(F32)).astype(BF)
            return carry

        lax.fori_loop(0, 4, one, 0)

    def load(self):
        self.loads = [self.local.copy(self.parts.at[up(self.x, d)], self.held.at[up(self.x, d)]) for d in (2, 1, 3, 0)]

    def start(self):
        for copy in self.loads:
            copy.wait()
        self.ring.start()

    def start_held(self):
        self.ring.start()

    def middle(self):
        self.ring.middle()

    def totals(self, step):
        self.ring.arrive()
        for half in range(2):
            terms = self.ring.terms(half)

            def loop(i, carry, half=half, terms=terms):
                rows = pl.ds(pl.multiple_of(i * 32, 32), 32)
                own = pl.ds(pl.multiple_of(64 * half + i * 32, 32), 32)
                value = self.held[self.x, own, :].astype(F32)
                for term in terms:
                    value += term[rows, :].astype(F32)
                step(own, value)
                return carry

            lax.fori_loop(0, 2, loop, 0)

    def gather(self, block, out):
        x = self.x
        self.back = quarters_of(self.net, out, self.me)
        self.mine = self.local.copy(block, out.at[x])
        self.back.start(block)

    def gather_middle(self):
        self.back.from_back()
        self.back.from_ahead()

    def finish(self):
        self.mine.wait()
        self.back.arrive()


SUM_COPIES = RING_SUM + RING_GATHER
SUM_LOCALS = 5


def sum_scratch():
    return [pltpu.VMEM((4, 128, D), BF), pltpu.VMEM((6, 64, D), BF)]


def normed(values):
    centre = jnp.mean(values, axis=-1, keepdims=True)
    spread = values - centre
    inverse = lax.rsqrt(jnp.mean(spread * spread, axis=-1, keepdims=True) + EPSILON)
    return spread * inverse, inverse


def norm_pullback(upstream, norm, inverse, gain):
    scaled = upstream * gain
    first = jnp.mean(scaled, axis=-1, keepdims=True)
    second = jnp.mean(scaled * norm, axis=-1, keepdims=True)
    return inverse * (scaled - first - norm * second)


ANY = pl.BlockSpec(memory_space=pl.ANY)
IN_VMEM = pl.BlockSpec(memory_space=pltpu.VMEM)
IN_SMEM = pl.BlockSpec(memory_space=pltpu.SMEM)


def remote_call(body, name, cid, ins, outs, scratch, copies, locals_):
    return pl.pallas_call(
        body,
        name=name,
        in_specs=ins,
        out_specs=[spec for _, _, spec in outs],
        out_shape=[jax.ShapeDtypeStruct(shape, dtype) for shape, dtype, _ in outs],
        scratch_shapes=scratch
        + [
            pltpu.SemaphoreType.DMA((copies,)),
            pltpu.SemaphoreType.DMA((copies,)),
            pltpu.SemaphoreType.DMA((locals_,)),
        ],
        compiler_params=pltpu.CompilerParams(
            collective_id=cid, has_side_effects=True, vmem_limit_bytes=VMEM_LIMIT
        ),
    )


def assemble_vectors(weights, gains, bias, spots):
    for s in range(32):
        block = weights[s * 64 : s * 64 + 16, 2048:2176].astype(F32)
        gains[0:4, s * 64 : s * 64 + 64] = block[0:4, :64]
        spots[s : s + 1, :] = block[4:5, :]
    values = spots[...].astype(BF)
    head = lax.broadcasted_iota(jnp.int32, (32, 128), 0)
    held = lax.broadcasted_iota(jnp.int32, (32, 128), 1)
    shard = lax.broadcasted_iota(jnp.int32, (32, 64), 0)
    lane = lax.broadcasted_iota(jnp.int32, (32, 64), 1)
    total = jnp.zeros((32, 64), F32)
    for e in range(2):
        pick = jnp.where((held == 2 * head + e) & (head < 24), 1.0, 0.0).astype(BF)
        spread = jnp.where(lane == 2 * shard + e, 1.0, 0.0).astype(BF)
        total += jnp.dot(nt(pick, values).astype(BF), spread, preferred_element_type=F32)
    for n in range(24):
        bias[0:1, n * 64 : n * 64 + 64] = total[n : n + 1]


def front_forward(shard, tokens, group_place, base, steps):
    def kernel(
        src, x_ref, group_ref, base_ref, steps_ref, front, gains, low, out,
        weights, norm, blocks, bias, spots, turns, ss, rs, ls,
    ):
        me = here()
        c, y, z, x = me
        net, local = Net(ss, rs), Local(ls)
        greet(y_peers(*me) + z_peers(*me) + core_peer(*me))
        gather = Gather(net, local, src, flat_rows(weights), me)
        gather.start()
        for n in range(2):
            rows = slice(n * 128, n * 128 + 128)
            cosine, sine = turn_tables(base_ref, steps_ref, group_ref[(y * 4 + z) * 2 + n])
            turns[0, rows, :] = cosine
            turns[1, rows, :] = sine

        def centre(i, carry):
            rows = pl.ds(pl.multiple_of(i * 32, 32), 32)
            norm[rows, :] = normed(x_ref[rows, :].astype(F32))[0]
            return carry

        lax.fori_loop(0, 4, centre, 0)
        gather.near()
        lax.fori_loop(4, 8, centre, 0)
        gather.middle()
        lax.fori_loop(8, 16, centre, 0)
        for k in (3, 1, 2):
            gather.pass_on(k)
        gather.far()
        gather.finish()
        keep = local.copy(weights, front)
        assemble_vectors(weights, gains, bias, spots)

        def scale(i, carry):
            rows = pl.ds(pl.multiple_of(i * 32, 32), 32)
            low[rows, :] = (norm[rows, :] * gains[0:1, :] + gains[1:2, :]).astype(BF)
            return carry

        lax.fori_loop(0, 16, scale, 0)

        def project(t):
            columns = slice(t * 512, t * 512 + 512)
            for m in range(2):
                acc = jnp.dot(low[m * 256 : m * 256 + 256, :], weights[:, columns], preferred_element_type=F32)
                acc = acc + bias[:, columns]
                for h in range(4):
                    part = acc[:, h * 128 : h * 128 + 128]
                    if t < 2:
                        part = turn(part, turns[0], turns[1])
                    blocks[m, h, (t + 2) % 3] = part.astype(BF)

        along_y = lambda d: at(c, y + d, z, x)
        along_z = lambda d: at(c, y, z + d, x)
        kv = pl.ds(0, 2)

        def part(half):
            return kv if half is None else half

        rings = {}
        for k in range(4):
            rings[0, k] = RingGather(
                net, along_y, lambda d, half=None, k=k: out.at[0, up(y, d), up(z, k), part(half)]
            )
            rings[1, k] = RingGather(
                net, along_z, lambda d, half=None, k=k: out.at[1, up(y, k), up(z, d), part(half)]
            )
        project(1)
        project(2)
        first = {}
        for d in STEPS:
            first[0, d] = net.send(blocks.at[0, up(z, d), kv], out.at[0, y, z, kv], along_z(d))
            first[1, d] = net.send(blocks.at[1, up(y, d), kv], out.at[1, y, z, kv], along_y(d))
        rings[0, 0].start(blocks.at[0, z, kv])
        rings[1, 0].start(blocks.at[1, y, kv])
        project(0)
        last = []
        for d in STEPS:
            last.append(net.send(blocks.at[0, up(z, d), 2], out.at[0, y, z, 2], along_z(d)))
            last.append(net.send(blocks.at[1, up(y, d), 2], out.at[1, y, z, 2], along_y(d)))
        owns = [local.copy(blocks.at[0, z], out.at[0, y, z]), local.copy(blocks.at[1, y], out.at[1, y, z])]
        for d in STEPS:
            for m in range(2):
                first[m, d].wait_recv()
                ring = rings[m, 4 - d]
                ring.start(ring.out(0))
        for k in (0, 3, 1, 2):
            for m in range(2):
                rings[m, k].from_back()
                rings[m, k].from_ahead()
        for ring in rings.values():
            ring.arrive()
        for copy in last:
            copy.wait_recv()
        for copy in owns:
            copy.wait()
        keep.wait()
        net.finish()

    width = shard.shape[1]
    return remote_call(
        kernel,
        "front_forward",
        0,
        [ANY, IN_VMEM, IN_SMEM, IN_VMEM, IN_VMEM],
        [
            ((D, width), BF, ANY),
            ((4, D), F32, IN_VMEM),
            ((512, D), BF, IN_VMEM),
            ((2, 4, 4, 3, 256, 128), BF, ANY),
        ],
        [
            pltpu.VMEM((D, width), BF),
            pltpu.VMEM((512, D), F32),
            pltpu.VMEM((2, 4, 3, 256, 128), BF),
            pltpu.VMEM((1, 1536), F32),
            pltpu.VMEM((32, 128), F32),
            pltpu.VMEM((2, 256, 128), F32),
        ],
        GATHER_COPIES + 12 + 8 * RING_GATHER,
        4,
    )(shard, tokens, group_place, base, steps)


class Swap:
    def __init__(self, net, local, src, out, me):
        c, y, z, x = me
        self.owns = [local.copy(src.at[0, z], out.at[0, z]), local.copy(src.at[1, y], out.at[1, y])]
        self.copies = []
        for d in STEPS:
            self.copies.append(net.send(src.at[0, up(z, d)], out.at[0, z], at(c, y, z + d, x)))
            self.copies.append(net.send(src.at[1, up(y, d)], out.at[1, y], at(c, y + d, z, x)))

    def arrive(self):
        for copy in self.copies:
            copy.wait_recv()
        for copy in self.owns:
            copy.wait()


SWAP_COPIES, SWAP_LOCALS = 6, 2
TURNED = pl.ds(1536, 512)


def middle_forward(heads, front, inputs, gains, shard):
    width = shard.shape[1]

    def kernel(
        heads, front, inputs, gains, shard, attended, hidden, second, weights,
        swapped, out_w, held, spare, base, low, ss, rs, ls,
    ):
        me = here()
        c, y, z, x = me
        net, local = Net(ss, rs), Local(ls)
        sums = SumX(net, local, None, held, spare, me)
        load = local.copy(front.at[:, TURNED], out_w)
        residual = local.copy(inputs.at[x], base)
        greet(y_peers(*me) + z_peers(*me) + core_peer(*me) + x_peers(*me))
        swap = Swap(net, local, heads, swapped, me)
        gather = Gather(net, local, shard, flat_rows(weights), me)
        gather.start()
        load.wait()
        swap.arrive()
        for m in range(2):
            for h in range(4):
                attended[m * 256 : m * 256 + 256, h * 128 : h * 128 + 128] = swapped[m, h]
        for q in range(4):
            held[q] = nt(attended[q * 128 : q * 128 + 128, :], out_w[...]).astype(BF)
        sums.start_held()
        gather.near()
        sums.middle()
        gather.middle()
        gather.pass_on(3)
        residual.wait()

        def step(rows, total):
            value = base[rows, :].astype(F32) + total
            hidden[rows, :] = value
            norm, _ = normed(value)
            low[rows, :] = (norm * gains[2:3, :] + gains[3:4, :]).astype(BF)

        sums.totals(step)
        sums.gather(low, second)
        gather.pass_on(1)
        gather.pass_on(2)
        sums.gather_middle()
        gather.far()
        gather.finish()
        sums.finish()
        net.finish()

    return remote_call(
        kernel,
        "middle_forward",
        3,
        [ANY, ANY, ANY, IN_VMEM, ANY],
        [
            ((512, 512), BF, IN_VMEM),
            ((128, D), F32, IN_VMEM),
            ((4, 128, D), BF, ANY),
            ((D, width), BF, ANY),
        ],
        [pltpu.VMEM((2, 4, 256, 128), BF), pltpu.VMEM((D, 512), BF)]
        + sum_scratch()
        + [pltpu.VMEM((128, D), BF), pltpu.VMEM((128, D), BF)],
        SWAP_COPIES + GATHER_COPIES + SUM_COPIES,
        SWAP_LOCALS + SUM_LOCALS + 3,
    )(heads, front, inputs, gains, shard)


def other_half(c, k, size):
    core = 1 - c if k < 2 else c
    return pl.ds(pl.multiple_of(core * 1024 + (k % 2) * size, size), size)


def shard_block(k):
    return pl.ds((k % 2) * 2, 2)


def middle_backward(parts, cotangent, hidden, gains, attended, front, second_low, dup, mixed, branch, gate_grad):
    def kernel(
        parts, cotangent, hidden, gains, attended, front, second_low, dup, mixed, branch, gate_grad,
        dhidden, vectors, output_grad, upstream, out_block, gate_out, up_out, down_out,
        held, spare, low, hidden_low, out_w, blocks, lows, dys, extra, *rest,
    ):
        scratch, (ss, rs, ls) = rest[:-3], rest[-3:]
        me = here()
        c, y, z, x = me
        net, local = Net(ss, rs), Local(ls)
        sums = SumX(net, local, parts, held, spare, me)
        sums.load()
        loads = [local.copy(second_low, lows), local.copy(cotangent, dys)]
        load = local.copy(front.at[:, TURNED], out_w)
        greet(y_peers(*me) + z_peers(*me) + core_peer(*me) + x_peers(*me))
        gate, up_, down_ = [
            Scatter(net, local, grads, out, scratch[8 * k : 8 * k + 8], me)
            for k, (grads, out) in enumerate(((gate_grad, gate_out), (None, up_out), (None, down_out)))
        ]
        gate.start()
        sums.start()

        def multiply(left, right, k, to):
            value = tn(left[:, other_half(c, k, 512)], right[...]).astype(BF)
            to[shard_block(k)] = value.reshape(2, 4, 64, UNITS)

        loads[0].wait()
        for k in range(2):
            multiply(lows, dup, k, down_.held)
        up_.send_filled(down_.held)
        gate.first()
        sums.middle()
        for k in range(2, 4):
            multiply(lows, dup, k, up_.held)
        loads[1].wait()
        for k in range(2):
            multiply(dys, mixed, k, extra)
        down_.send_filled(extra)
        up_.first()
        net.wait_sent(up_.zero)
        gate.first_middle()
        vectors[...] = jnp.zeros_like(vectors)

        def step(rows, dsecond):
            norm, inverse = normed(hidden[rows, :])
            upper = dys[pl.ds(pl.multiple_of(x * 128 + rows.start, 32), 32), :].astype(F32)
            value = upper + norm_pullback(dsecond, norm, inverse, gains[2:3, :])
            dhidden[rows, :] = value
            low[rows, :] = value.astype(BF)
            vectors[0:1, :] += jnp.sum(dsecond * norm, axis=0, keepdims=True)
            vectors[1:2, :] += jnp.sum(dsecond, axis=0, keepdims=True)

        sums.totals(step)
        sums.ring.sent()
        sums.gather(low, hidden_low)
        for k in range(2, 4):
            multiply(dys, mixed, k, down_.held)
        down_.first()
        up_.first_middle()
        gate.second()
        sums.gather_middle()
        late = SumX(net, local, branch, held, spare, me)
        late.load()
        late.start()
        down_.first_middle()
        up_.second()
        load.wait()
        sums.finish()
        for q in range(4):
            rows = slice((q % 2) * 128, (q % 2) * 128 + 128)
            result = jnp.dot(hidden_low[q], out_w[...], preferred_element_type=F32).astype(BF)
            for h in range(4):
                blocks[q // 2, h, rows, :] = result[:, h * 128 : h * 128 + 128]
        swap = Swap(net, local, blocks, upstream, me)
        late.middle()
        gate.second_middle()
        down_.second()
        whole = hidden_low[...].reshape(512, D)
        output_grad[...] = tn(whole, attended[...]).astype(BF)
        up_.second_middle()
        gate.third()
        down_.second_middle()

        def last(rows, total):
            out_block[rows, :] = (hidden[rows, :] + total).astype(BF)

        late.totals(last)
        up_.third()
        down_.third()
        swap.arrive()
        net.finish()

    scratch = sum_scratch() + [
        pltpu.VMEM((128, D), BF),
        pltpu.VMEM((4, 128, D), BF),
        pltpu.VMEM((D, 512), BF),
        pltpu.VMEM((2, 4, 256, 128), BF),
        pltpu.VMEM((512, D), BF),
        pltpu.VMEM((512, D), BF),
        pltpu.VMEM((4, 4, 64, UNITS), BF),
    ]
    return remote_call(
        kernel,
        "middle_backward",
        4,
        [ANY, ANY, IN_VMEM, IN_VMEM, IN_VMEM, ANY, ANY, IN_VMEM, IN_VMEM, ANY, ANY],
        [
            ((128, D), F32, IN_VMEM),
            ((2, D), F32, IN_VMEM),
            ((D, 512), BF, IN_VMEM),
            ((2, 4, 256, 128), BF, ANY),
            ((128, D), BF, IN_VMEM),
        ]
        + [((64, UNITS), F32, IN_VMEM)] * 3,
        scratch + scatter_scratch(UNITS) * 3,
        SUM_COPIES + RING_SUM + SCATTER_COPIES * 3 + SWAP_COPIES,
        SUM_LOCALS + 4 + SWAP_LOCALS + 3 + 1,
    )(parts, cotangent, hidden, gains, attended, front, second_low, dup, mixed, branch, gate_grad)


def collect_heads(dkv, dq, block):
    def kernel(dkv, dq, block, dproject, outputs, mine, got, summed, ss, rs, ls):
        me = here()
        c, y, z, x = me
        net, local = Net(ss, rs), Local(ls)
        order = (1, 3, 2, 0)
        loads = [local.copy(dkv.at[m], mine.at[m]) for m in range(2)]
        greet(y_peers(*me) + z_peers(*me) + x_peers(*me))
        kv = pl.ds(0, 2)
        along_y = lambda d: at(c, y + d, z, x)
        along_z = lambda d: at(c, y, z + d, x)

        def add(total, term):
            def one(i, carry):
                rows = pl.ds(pl.multiple_of(i * 64, 64), 64)
                total[rows, :] = (total[rows, :].astype(F32) + term[rows, :].astype(F32)).astype(BF)
                return carry

            lax.fori_loop(0, 4, one, 0)

        rings = {}
        for k in order:
            rings[0, k] = RingSum(
                net, along_y, lambda d, half, k=k: mine.at[0, up(y, d), up(z, k), half], got.at[0, k], add
            )
            rings[1, k] = RingSum(
                net, along_z, lambda d, half, k=k: mine.at[1, up(y, k), up(z, d), half], got.at[1, k], add
            )
        whole = quarters_of(net, outputs, me)
        own = local.copy(block, outputs.at[x])
        whole.start(block)
        for copy in loads:
            copy.wait()
        for ring in rings.values():
            ring.start()
        lates = [
            local.copy(dq.at[0, z], dproject.at[0, z, 2]),
            local.copy(dq.at[1, y], dproject.at[1, y, 2]),
        ]
        two = []
        for d in STEPS:
            two.append(net.send(dq.at[0, up(z, d)], dproject.at[0, z, 2], along_z(d)))
            two.append(net.send(dq.at[1, up(y, d)], dproject.at[1, y, 2], along_y(d)))
        for ring in rings.values():
            ring.middle()
        for k in order:
            for m, spot in ((0, z), (1, y)):
                ring = rings[m, k]
                ring.arrive()
                for half in range(2):
                    kept, terms = ring.mine(0, half), ring.terms(half)

                    def total(i, carry, m=m, k=k, half=half, kept=kept, terms=terms):
                        rows = pl.ds(pl.multiple_of(i * 64, 64), 64)
                        value = kept[rows, :].astype(F32)
                        for term in terms:
                            value += term[rows, :].astype(F32)
                        summed[m, k, half, rows, :] = value.astype(BF)
                        return carry

                    lax.fori_loop(0, 4, total, 0)
            if k:
                two.append(net.send(summed.at[0, k], dproject.at[0, z, kv], along_z(k)))
                two.append(net.send(summed.at[1, k], dproject.at[1, y, kv], along_y(k)))
            else:
                lates.append(local.copy(summed.at[0, 0], dproject.at[0, z, kv]))
                lates.append(local.copy(summed.at[1, 0], dproject.at[1, y, kv]))

        whole.from_back()
        whole.from_ahead()
        for copy in two:
            copy.wait_recv()
        for copy in lates:
            copy.wait()
        own.wait()
        whole.arrive()
        net.finish()

    return remote_call(
        kernel,
        "collect_heads",
        6,
        [ANY, ANY, IN_VMEM],
        [((2, 4, 3, 256, 128), BF, ANY), ((4, 128, D), BF, ANY)],
        [
            pltpu.VMEM((2, 4, 4, 2, 256, 128), BF),
            pltpu.VMEM((2, 4, 6, 256, 128), BF),
            pltpu.VMEM((2, 4, 2, 256, 128), BF),
        ],
        8 * RING_SUM + 6 + 6 + RING_GATHER,
        2 + 4 + 1,
    )(dkv, dq, block)


def last_backward(dproject, first_low, front, inputs, dhidden, gains, mixer_vectors, output_grad):
    def kernel(
        dproject, first_low, front, inputs, dhidden, gains, mixer_vectors, output_grad,
        input_grad, sums_out, project_out, output_out,
        wide, weights, lows, held, spare, base, low, extra, small, got, *rest,
    ):
        scratch, (ss, rs, ls) = rest[:-3], rest[-3:]
        me = here()
        c, y, z, x = me
        net, local = Net(ss, rs), Local(ls)
        load = local.copy(front.at[:, pl.ds(0, 1536)], weights)
        load_low = local.copy(first_low, lows)
        residual = local.copy(inputs.at[x], base)
        greet(y_peers(*me) + z_peers(*me) + core_peer(*me) + x_peers(*me))
        project = Scatter(net, local, None, project_out, scratch[:8], me)
        output = Scatter(net, local, output_grad, output_out, scratch[8:], me)
        output.start()
        sums = SumX(net, local, None, held, spare, me)
        for m in range(2):
            for t in range(3):
                for h in range(4):
                    to = t * 512 + h * 128
                    wide[m * 256 : m * 256 + 256, to : to + 128] = dproject[m, h, (t + 2) % 3]
        load.wait()

        def quarter(d):
            q = up(x, d)
            rows = wide[pl.ds(pl.multiple_of(q * 128, 128), 128), :]
            held[q] = nt(rows, weights[...]).astype(BF)

        quarter(2)
        sums.ring.start_far()
        quarter(1)
        quarter(3)
        sums.ring.start_near()

        def multiply(k, to):
            value = tn(lows[:, other_half(c, k, 512)], wide[...]).astype(BF)
            to[shard_block(k)] = value.reshape(2, 4, 64, 1536)

        load_low.wait()
        for k in range(2):
            multiply(k, extra)
        project.send_filled(extra)
        sums.middle()
        quarter(0)
        for k in range(2, 4):
            multiply(k, project.held)
        output.first()
        small[0, ...] = jnp.zeros_like(small[0])
        small[0, 2:4, :] = mixer_vectors[...]
        small[0, 4:5, 0:1536] = jnp.sum(wide[...].astype(F32), axis=0, keepdims=True)
        project.first()
        residual.wait()

        def step(rows, dfirst):
            norm, inverse = normed(base[rows, :].astype(F32))
            value = dhidden[rows, :] + norm_pullback(dfirst, norm, inverse, gains[0:1, :])
            low[rows, :] = value.astype(BF)
            small[0, 0:1, :] += jnp.sum(dfirst * norm, axis=0, keepdims=True)
            small[0, 1:2, :] += jnp.sum(dfirst, axis=0, keepdims=True)

        sums.totals(step)
        copies = [net.send(small.at[0], got.at[0, d - 1], at(c, y, z, x + d)) for d in STEPS]
        sums.gather(low, input_grad)
        output.first_middle()
        project.first_middle()
        for copy in copies:
            copy.wait_recv()
        small[1, ...] = small[0, ...]
        for n in range(3):
            small[1, 0:4, :] += got[0, n, 0:4, :]
        copies = [net.send(small.at[1], got.at[1, d - 1], at(c, y + d, z, x)) for d in STEPS]
        sums.gather_middle()
        output.second()
        project.second()
        for copy in copies:
            copy.wait_recv()
        small[2, ...] = small[1, ...] + got[1, 0] + got[1, 1] + got[1, 2]
        copies = [net.send(small.at[2], got.at[2, d - 1], at(c, y, z + d, x)) for d in STEPS]
        output.second_middle()
        project.second_middle()
        for copy in copies:
            copy.wait_recv()
        small[3, ...] = small[2, ...] + got[2, 0] + got[2, 1] + got[2, 2]
        copy = net.send(small.at[3], got.at[3, 0], at(1 - c, y, z, x))
        output.third()
        project.third()
        copy.wait_recv()
        sums_out[...] = small[3, ...] + got[3, 0]
        sums.finish()
        net.finish()

    scratch = (
        [pltpu.VMEM((512, 1536), BF), pltpu.VMEM((D, 1536), BF), pltpu.VMEM((512, D), BF)]
        + sum_scratch()
        + [
            pltpu.VMEM((128, D), BF),
            pltpu.VMEM((128, D), BF),
            pltpu.VMEM((4, 4, 64, 1536), BF),
            pltpu.VMEM((4, 8, D), F32),
            pltpu.VMEM((4, 3, 8, D), F32),
        ]
    )
    return remote_call(
        kernel,
        "last_backward",
        7,
        [IN_VMEM, ANY, ANY, ANY, IN_VMEM, IN_VMEM, IN_VMEM, ANY],
        [
            ((4, 128, D), BF, ANY),
            ((8, D), F32, IN_VMEM),
            ((64, 1536), F32, IN_VMEM),
            ((64, 512), F32, IN_VMEM),
        ],
        scratch + scatter_scratch(1536) + scatter_scratch(512),
        SUM_COPIES + 10 + SCATTER_COPIES * 2,
        SUM_LOCALS + 4,
    )(dproject, first_low, front, inputs, dhidden, gains, mixer_vectors, output_grad)


def turn(values, cosine, sine):
    lane = lax.broadcasted_iota(jnp.int32, values.shape, 1) & (HEAD_DIM - 1)
    swapped = jnp.where(lane < ROT // 2, -pltpu.roll(values, 120, 1), pltpu.roll(values, 8, 1))
    return values * cosine + swapped * sine


def turn_tables(base, steps, block):
    cosine, sine = base[0], base[1]
    far_cosine, far_sine = steps[0, pl.ds(block, 1), :], steps[1, pl.ds(block, 1), :]
    return far_cosine * cosine - far_sine * sine, far_sine * cosine + far_cosine * sine


def two_heads(block):
    lane = lax.broadcasted_iota(jnp.int32, (128, 128), 1)
    value = block.astype(F32)
    return jnp.concatenate(
        [jnp.where(lane < HEAD_DIM, value, 0.0), jnp.where(lane >= HEAD_DIM, value, 0.0)], axis=0
    )


def two_heads_t(block):
    feature = lax.broadcasted_iota(jnp.int32, (128, 128), 0)
    value = block.astype(F32).T
    return jnp.concatenate(
        [jnp.where(feature < HEAD_DIM, value, 0.0), jnp.where(feature >= HEAD_DIM, value, 0.0)], axis=1
    )


def one_block(stacked):
    feature = lax.broadcasted_iota(jnp.int32, (128, 128), 0)
    return jnp.where(feature < HEAD_DIM, stacked[:, :128], stacked[:, 128:]).T


def nt(left, right):
    return lax.dot_general(left, right, (((1,), (1,)), ((), ())), preferred_element_type=F32)


def plan_blocks(group_place, slots, places):
    _, y, z, _ = here()

    def one(j, carry):
        slots[group_place[j]] = j
        return carry

    lax.fori_loop(0, 32, one, 0)
    for b in range(8):
        places[b] = group_place[(y * 4 + b // 2) * 2 + b % 2]
        places[8 + b] = group_place[((b // 2) * 4 + z) * 2 + b % 2]


def row_of(m, i):
    _, y, z, _ = here()
    return jnp.where(m == 0, y * 4 + i, i * 4 + z)


def unit_of(places, m, n):
    pair, rest = n // 9, lax.rem(n, 9)
    ahead = places[m * 8 + pair * 2] // (TILE // 128) + 1
    late = rest >= ahead
    block = pair * 2 + jnp.where(late, 1, 0)
    tile = rest - jnp.where(late, ahead, 0)
    return block, tile, places[m * 8 + block] * 128 - tile * TILE


def lay_mask(steps, bars):
    row = lax.broadcasted_iota(jnp.int32, (1024, 128), 0) - 513
    lane = lax.broadcasted_iota(jnp.int32, (1024, 128), 1)
    steps[...] = jnp.where(jnp.minimum(row, 127) == lane, 1.0, 0.0).astype(BF)
    bar = lax.broadcasted_iota(jnp.int32, (128, 256), 0)
    query = lax.rem(lax.broadcasted_iota(jnp.int32, (128, 256), 1), 128)
    bars[...] = jnp.where(bar >= query, LOW, 0.0).astype(BF)


def with_mask(keys, steps, behind):
    first = 512 - jnp.minimum(behind, 512)
    return jnp.concatenate([keys, steps[pl.ds(pl.multiple_of(first, 128), TILE), :]], axis=1)


def tile_of(t):
    return pl.ds(pl.multiple_of(t * TILE, TILE), TILE)


def lay_blocks(slots, lay):
    def some(n, carry):
        for k in range(8):
            b = n * 8 + k
            slot = slots[b]
            rows = pl.ds(pl.multiple_of(lax.rem(slot, 2) * 128, 128), 128)
            lay(slot // 2, rows, pl.ds(pl.multiple_of(b * 128, 128), 128))
        return carry

    lax.fori_loop(0, 4, some, 0)


UNITS_EACH = 36


def attend(group_place, spread):
    def kernel(
        group_ref, k_ref, v_ref, q_ref, o_ref, full_ref, log_ref,
        slots, places, keys, values_t, queries, scores_0, scores_1, weights_0, weights_1, results, tops, steps, bars,
    ):
        scores, weights = (scores_0, scores_1), (weights_0, weights_1)
        m = pl.program_id(0)
        plan_blocks(group_ref, slots, places)

        def lay(slot, rows, to):
            keys[to, :] = k_ref[0, slot, 0, rows, :]
            values_t[:128, to] = v_ref[0, slot, 0, rows, :].T

        lay_blocks(slots, lay)
        for b in range(8):
            row = row_of(m, b // 2)
            block = q_ref[0, row, 0, (b % 2) * 128 : (b % 2) * 128 + 128, :]
            queries[b, :128] = (two_heads_t(block) * 0.125).astype(BF)
        lay_mask(steps, bars)
        for b in range(8):
            queries[b, 128:] = bars[...]
        values_t[128:, :] = jnp.ones((16, 4096), BF)

        def multiply(n, odd):
            block, tile, behind = unit_of(places, m, n)
            value = jnp.dot(
                with_mask(keys[tile_of(tile), :], steps, behind), queries[block], preferred_element_type=F32
            )
            scores[odd][...] = value
            return jnp.max(value, axis=0, keepdims=True) * LOG2E

        def soften(n, odd, top, most):
            block, tile, _ = unit_of(places, m, n)
            top = jnp.where(tile == 0, LOW, top)
            new_top = jnp.maximum(top, most)
            for r in range(0, TILE, ROWS):
                rows = slice(r, r + ROWS)
                weights[odd][rows, :] = jnp.exp2(scores[odd][rows, :] * LOG2E - new_top).astype(BF)
            tops[block, 0:1, :] = new_top
            return new_top, jnp.exp2(top - new_top)

        def gather(n, odd, shrink, acc):
            block, tile, _ = unit_of(places, m, n)
            acc = acc * shrink + jnp.dot(
                values_t[:, tile_of(tile)], weights[odd][...], preferred_element_type=F32
            )
            results[block] = acc
            return acc

        most = multiply(0, 0)
        after = multiply(1, 1)
        top, shrink = soften(0, 0, jnp.zeros((1, 256), F32), most)

        def step(k, carry):
            top, shrink, acc, most = carry
            for n, odd in [(AT_ONCE * k + 1 + j, 1 - j % 2) for j in range(AT_ONCE)]:
                after = multiply(n + 1, 1 - odd)
                acc = gather(n - 1, 1 - odd, shrink, acc)
                top, shrink = soften(n, odd, top, most)
                most = after
            return top, shrink, acc, most

        carry = (top, shrink, jnp.zeros((144, 256), F32), after)
        top, shrink, acc, most = lax.fori_loop(0, (UNITS_EACH - 2) // AT_ONCE, step, carry)
        last = UNITS_EACH - 1
        acc = gather(last - 1, 0, shrink, acc)
        _, shrink = soften(last, 1, top, most)
        gather(last, 1, shrink, acc)
        for b in range(8):
            rows = slice((b % 2) * 128, (b % 2) * 128 + 128)
            total = results[b, 128:129, :]
            result = one_block(results[b, :128, :] / total)
            full_ref[0, b // 2, rows, :] = result
            o_ref[0, b // 2, rows, :] = result.astype(BF)
            log_ref[0, b : b + 1, :] = tops[b, 0:1, :] + jnp.log2(total)

    grid_spec = pltpu.PrefetchScalarGridSpec(
        num_scalar_prefetch=1,
        grid=(2,),
        in_specs=[
            pl.BlockSpec((1, 16, 1, 256, 128), lambda m, g: (m, 0, 0, 0, 0)),
            pl.BlockSpec((1, 16, 1, 256, 128), lambda m, g: (m, 0, 1, 0, 0)),
            pl.BlockSpec((1, 16, 1, 256, 128), lambda m, g: (m, 0, 2, 0, 0)),
        ],
        out_specs=[
            pl.BlockSpec((1, 4, 256, 128), lambda m, g: (m, 0, 0, 0)),
            pl.BlockSpec((1, 4, 256, 128), lambda m, g: (m, 0, 0, 0)),
            pl.BlockSpec((1, 8, 256), lambda m, g: (m, 0, 0)),
        ],
        scratch_shapes=[
            pltpu.SMEM((32,), jnp.int32),
            pltpu.SMEM((16,), jnp.int32),
            pltpu.VMEM((4096, 128), BF),
            pltpu.VMEM((144, 4096), BF),
            pltpu.VMEM((8, 256, 256), BF),
            pltpu.VMEM((TILE, 256), F32),
            pltpu.VMEM((TILE, 256), F32),
            pltpu.VMEM((TILE, 256), BF),
            pltpu.VMEM((TILE, 256), BF),
            pltpu.VMEM((8, 144, 256), F32),
            pltpu.VMEM((8, 8, 256), F32),
            pltpu.VMEM((1024, 128), BF),
            pltpu.VMEM((128, 256), BF),
        ],
    )
    return pl.pallas_call(
        kernel,
        name="attend",
        grid_spec=grid_spec,
        out_shape=[
            jax.ShapeDtypeStruct((2, 4, 256, 128), BF),
            jax.ShapeDtypeStruct((2, 4, 256, 128), F32),
            jax.ShapeDtypeStruct((2, 8, 256), F32),
        ],
        compiler_params=pltpu.CompilerParams(vmem_limit_bytes=VMEM_LIMIT),
    )(group_place, spread, spread, spread)


def attend_back(group_place, spread, full, logs, upstream, base, steps):
    def kernel(
        group_ref, k_ref, v_ref, q_ref, full_ref, log_ref, up_ref, base_ref, steps_ref,
        dq_ref, dkv_ref,
        slots, places, keys, keys_t, values, dkeys, dvalues, queries, queries_t, grads, grads_t, delta,
        scores_0, scores_1, dprobs_0, dprobs_1, probs_0, probs_1, dscores_0, dscores_1, results, steps, bars,
    ):
        scores, dprobs = (scores_0, scores_1), (dprobs_0, dprobs_1)
        probs_low, dscores = (probs_0, probs_1), (dscores_0, dscores_1)
        m = pl.program_id(0)
        plan_blocks(group_ref, slots, places)

        def lay(slot, rows, to):
            block = k_ref[0, slot, 0, rows, :]
            keys[to, :] = block
            keys_t[:, to] = block.T
            values[to, :] = v_ref[0, slot, 0, rows, :]
            dkeys[to, :] = jnp.zeros((128, 128), F32)
            dvalues[to, :] = jnp.zeros((128, 128), F32)

        lay_blocks(slots, lay)
        for b in range(8):
            rows = slice((b % 2) * 128, (b % 2) * 128 + 128)
            block = q_ref[0, row_of(m, b // 2), 0, rows, :]
            queries[b] = (two_heads(block) * 0.125).astype(BF)
            queries_t[b, :128] = (two_heads_t(block) * 0.125).astype(BF)
            ups = up_ref[0, b // 2, rows, :]
            grads[b] = two_heads(ups).astype(BF)
            grads_t[b] = two_heads_t(ups).astype(BF)
            product = (ups.astype(F32) * full_ref[0, b // 2, rows, :]).T
            delta[b, 0:1, :128] = jnp.sum(product[:HEAD_DIM], axis=0, keepdims=True)
            delta[b, 0:1, 128:] = jnp.sum(product[HEAD_DIM:], axis=0, keepdims=True)
        lay_mask(steps, bars)
        for b in range(8):
            queries_t[b, 128:] = bars[...]

        def multiply(n, odd):
            block, tile, behind = unit_of(places, m, n)
            scores[odd][...] = jnp.dot(
                with_mask(keys[tile_of(tile), :], steps, behind), queries_t[block], preferred_element_type=F32
            )
            dprobs[odd][...] = jnp.dot(
                values[tile_of(tile), :], grads_t[block], preferred_element_type=F32
            )

        def soften(n, odd):
            block, _, _ = unit_of(places, m, n)
            logs, deltas = log_ref[0, pl.ds(block, 1), :], delta[block, 0:1, :]
            for r in range(0, TILE, ROWS):
                rows = slice(r, r + ROWS)
                value = jnp.exp2(scores[odd][rows, :] * LOG2E - logs)
                probs_low[odd][rows, :] = value.astype(BF)
                dscores[odd][rows, :] = (value * (dprobs[odd][rows, :] - deltas)).astype(BF)

        def gather(n, odd, acc):
            block, tile, _ = unit_of(places, m, n)
            span = tile_of(tile)
            dvalues[span, :] += jnp.dot(probs_low[odd][...], grads[block], preferred_element_type=F32)
            dkeys[span, :] += jnp.dot(dscores[odd][...], queries[block], preferred_element_type=F32)
            acc = jnp.where(tile == 0, 0.0, acc) + jnp.dot(
                keys_t[:, span], dscores[odd][...], preferred_element_type=F32
            )
            results[block] = acc
            return acc

        multiply(0, 0)
        multiply(1, 1)
        soften(0, 0)

        def step(k, acc):
            for n, odd in [(AT_ONCE * k + 1 + j, 1 - j % 2) for j in range(AT_ONCE)]:
                multiply(n + 1, 1 - odd)
                acc = gather(n - 1, 1 - odd, acc)
                soften(n, odd)
            return acc

        last = UNITS_EACH - 1
        acc = lax.fori_loop(0, (UNITS_EACH - 2) // AT_ONCE, step, jnp.zeros((128, 256), F32))
        acc = gather(last - 1, 0, acc)
        soften(last, 1)
        gather(last, 1, acc)

        def turned_back(values, place):
            cosine, sine = turn_tables(base_ref, steps_ref, place)
            return turn(values, cosine, -sine)

        for b in range(8):
            rows = slice((b % 2) * 128, (b % 2) * 128 + 128)
            dquery = one_block(results[b]) * 0.125
            dq_ref[0, b // 2, rows, :] = turned_back(dquery, places[m * 8 + b]).astype(BF)

        def flush(n, carry):
            for k in range(4):
                b = n * 4 + k
                slot = slots[b]
                rows = pl.ds(pl.multiple_of(lax.rem(slot, 2) * 128, 128), 128)
                to = pl.ds(pl.multiple_of(b * 128, 128), 128)
                dkv_ref[0, slot // 2, 0, rows, :] = turned_back(dkeys[to, :], b).astype(BF)
                dkv_ref[0, slot // 2, 1, rows, :] = dvalues[to, :].astype(BF)
            return carry

        lax.fori_loop(0, 8, flush, 0)

    grid_spec = pltpu.PrefetchScalarGridSpec(
        num_scalar_prefetch=1,
        grid=(2,),
        in_specs=[
            pl.BlockSpec((1, 16, 1, 256, 128), lambda m, g: (m, 0, 0, 0, 0)),
            pl.BlockSpec((1, 16, 1, 256, 128), lambda m, g: (m, 0, 1, 0, 0)),
            pl.BlockSpec((1, 16, 1, 256, 128), lambda m, g: (m, 0, 2, 0, 0)),
            pl.BlockSpec((1, 4, 256, 128), lambda m, g: (m, 0, 0, 0)),
            pl.BlockSpec((1, 8, 256), lambda m, g: (m, 0, 0)),
            pl.BlockSpec((1, 4, 256, 128), lambda m, g: (m, 0, 0, 0)),
            pl.BlockSpec((2, 128, 128), lambda m, g: (0, 0, 0)),
            pl.BlockSpec((2, 32, 128), lambda m, g: (0, 0, 0)),
        ],
        out_specs=[
            pl.BlockSpec((1, 4, 256, 128), lambda m, g: (m, 0, 0, 0)),
            pl.BlockSpec((1, 16, 2, 256, 128), lambda m, g: (m, 0, 0, 0, 0)),
        ],
        scratch_shapes=[
            pltpu.SMEM((32,), jnp.int32),
            pltpu.SMEM((16,), jnp.int32),
            pltpu.VMEM((4096, 128), BF),
            pltpu.VMEM((128, 4096), BF),
            pltpu.VMEM((4096, 128), BF),
            pltpu.VMEM((4096, 128), F32),
            pltpu.VMEM((4096, 128), F32),
            pltpu.VMEM((8, 256, 128), BF),
            pltpu.VMEM((8, 256, 256), BF),
            pltpu.VMEM((8, 256, 128), BF),
            pltpu.VMEM((8, 128, 256), BF),
            pltpu.VMEM((8, 8, 256), F32),
            pltpu.VMEM((TILE, 256), F32),
            pltpu.VMEM((TILE, 256), F32),
            pltpu.VMEM((TILE, 256), F32),
            pltpu.VMEM((TILE, 256), F32),
            pltpu.VMEM((TILE, 256), BF),
            pltpu.VMEM((TILE, 256), BF),
            pltpu.VMEM((TILE, 256), BF),
            pltpu.VMEM((TILE, 256), BF),
            pltpu.VMEM((8, 128, 256), F32),
            pltpu.VMEM((1024, 128), BF),
            pltpu.VMEM((128, 256), BF),
        ],
    )
    return pl.pallas_call(
        kernel,
        name="attend_back",
        grid_spec=grid_spec,
        out_shape=[
            jax.ShapeDtypeStruct((2, 4, 256, 128), BF),
            jax.ShapeDtypeStruct((2, 16, 2, 256, 128), BF),
        ],
        compiler_params=pltpu.CompilerParams(vmem_limit_bytes=VMEM_LIMIT),
    )(group_place, spread, spread, spread, full, logs, upstream, base, steps)


def tn(left, right):
    return lax.dot_general(left, right, (((0,), (0,)), ((), ())), preferred_element_type=F32)


def feed_forward(second_low, dy, weights):
    def kernel(
        low_hbm, dy_hbm, w_hbm, branch, dsecond, gate_out, dup, mixed,
        low, dys, gate_w, up_w, down_w, gate, up, dmixed, dgate, chunks, sems, chunk_sems,
    ):
        def load(n, src, dst):
            copy = pltpu.make_async_copy(src, dst, sems.at[n])
            copy.start()
            return copy

        def columns(k):
            return w_hbm.at[:, pl.ds(k * UNITS, UNITS)]

        loads = [
            load(0, low_hbm, low),
            load(1, columns(0), gate_w),
            load(2, columns(1), up_w),
            load(3, dy_hbm, dys),
            load(4, columns(2), down_w),
        ]
        loads[0].wait()
        loads[1].wait()
        gate[...] = jnp.dot(low[...], gate_w[...], preferred_element_type=F32)
        loads[2].wait()
        up[...] = jnp.dot(low[...], up_w[...], preferred_element_type=F32)
        loads[3].wait()
        loads[4].wait()
        dmixed[...] = jnp.dot(dys[...], down_w[...], preferred_element_type=F32)

        def step(i, carry):
            rows = pl.ds(pl.multiple_of(i * 16, 16), 16)
            g, u, d = gate[rows, :], up[rows, :], dmixed[rows, :]
            s = jax.nn.sigmoid(g)
            silu = g * s
            mixed[rows, :] = (silu * u).astype(BF)
            dgate[rows, :] = (d * u * s * (1.0 + g * (1.0 - s))).astype(BF)
            dup[rows, :] = (d * silu).astype(BF)
            return carry

        lax.fori_loop(0, 32, step, 0)
        dsecond[...] = (nt(dgate[...], gate_w[...]) + nt(dup[...], up_w[...])).astype(BF)
        busy = {}
        for k in range(4):
            rows = pl.ds(k * 512, 512)
            slot = k % 2
            if slot in busy:
                busy[slot].wait()
            chunks[slot] = tn(low[:, rows], dgate[...]).astype(BF)
            busy[slot] = pltpu.make_async_copy(chunks.at[slot], gate_out.at[rows, :], chunk_sems.at[slot])
            busy[slot].start()
        branch[...] = nt(mixed[...], down_w[...]).astype(BF)
        busy[0].wait()
        busy[1].wait()

    return pl.pallas_call(
        kernel,
        name="feed_forward",
        in_specs=[ANY, ANY, ANY],
        out_specs=[IN_VMEM, IN_VMEM, ANY, IN_VMEM, IN_VMEM],
        out_shape=[jax.ShapeDtypeStruct((512, D), BF)] * 2
        + [jax.ShapeDtypeStruct((D, UNITS), BF)]
        + [jax.ShapeDtypeStruct((512, UNITS), BF)] * 2,
        scratch_shapes=[pltpu.VMEM((512, D), BF)] * 2
        + [pltpu.VMEM((D, UNITS), BF)] * 3
        + [pltpu.VMEM((512, UNITS), F32)] * 3
        + [
            pltpu.VMEM((512, UNITS), BF),
            pltpu.VMEM((2, 512, UNITS), BF),
            pltpu.SemaphoreType.DMA((5,)),
            pltpu.SemaphoreType.DMA((2,)),
        ],
        compiler_params=pltpu.CompilerParams(vmem_limit_bytes=VMEM_LIMIT),
    )(second_low, dy, weights)


def angle_tables():
    lane = np.arange(128) % HEAD_DIM
    power = 10000.0 ** (-2.0 * (lane % (ROT // 2)) / ROT)
    frequency = np.where(lane < ROT, power, 0.0)
    tables = []
    for places in (np.arange(128), np.arange(32) * 128):
        angles = places[:, None] * frequency[None, :]
        tables.append(jnp.asarray(np.stack([np.cos(angles), np.sin(angles)]).astype(np.float32)))
    return tables


def body(
    inputs,
    cotangent,
    group_place,
    attend_gain,
    attend_shift,
    project_weight,
    project_bias,
    output_weight,
    mixer_gain,
    mixer_shift,
    gate_weight,
    up_weight,
    down_weight,
):
    shard_index = lax.axis_index("dp") * 16 + lax.axis_index("ctx")
    base, steps = angle_tables()

    vectors = jnp.stack([attend_gain, attend_shift, mixer_gain, mixer_shift])
    vectors = jnp.concatenate(
        [
            jnp.pad(vectors, ((0, 0), (0, 64))),
            jnp.pad(project_bias.reshape(1, 48), ((0, 0), (0, 80))),
            jnp.zeros((59, 128), BF),
        ]
    )
    front_shard = jnp.concatenate(
        [project_weight.reshape(64, 1536), output_weight.T, vectors], axis=1
    )
    back_shard = jnp.concatenate([gate_weight, up_weight, down_weight.T], axis=1)

    tokens = inputs.reshape(512, D)
    quarters = inputs.reshape(4, 128, D)
    front, gains, first_low, spread = front_forward(front_shard, tokens, group_place, base, steps)
    spread = spread.reshape(2, 16, 3, 256, 128)
    attended_heads, attended_full, logs = attend(group_place, spread)
    attended_low, hidden, second_low, back = middle_forward(
        attended_heads, front, quarters, gains, back_shard
    )

    second_low = second_low.reshape(512, D)
    dy = cotangent.reshape(512, D)
    branch, second_part, gate_grad, dup, mixed = feed_forward(second_low, dy, back)
    dhidden, mixer_vectors, output_grad, upstream, out_block, gate_grad, up_grad, down_grad = middle_backward(
        second_part.reshape(4, 128, D),
        dy,
        hidden,
        gains,
        attended_low,
        front,
        second_low,
        dup,
        mixed,
        branch.reshape(4, 128, D),
        gate_grad.reshape(2, 4, 4, 64, UNITS),
    )

    dq, dkv = attend_back(group_place, spread, attended_full, logs, upstream, base, steps)
    dproject, outputs = collect_heads(dkv.reshape(2, 4, 4, 2, 256, 128), dq, out_block)
    input_grad, small, project_grad, output_grad = last_backward(
        dproject, first_low, front, quarters, dhidden, gains, mixer_vectors, output_grad.reshape(2, 4, 4, 64, 512)
    )
    own = lax.dynamic_slice(small, (0, shard_index * 64), (4, 64))
    bias_grad = lax.dynamic_slice(
        small[4, :1536].reshape(3, 8, 64), (0, 0, shard_index * 2), (3, 8, 2)
    )
    shape = inputs.shape
    return (
        outputs.reshape(shape),
        input_grad.reshape(shape),
        own[0],
        own[1],
        project_grad.reshape(64, 3, 512),
        bias_grad,
        output_grad.T,
        own[2],
        own[3],
        gate_grad,
        up_grad,
        down_grad.T,
    )


def solution(mesh):
    weight = ("dp", "ctx")
    rows = P(None, "dp", "ctx", None)
    vector = P(weight)
    matrix = P(weight, "tensor")
    turned = P("tensor", weight)
    project = P(weight, None, "tensor")
    bias = P(None, "tensor", weight)
    params = (vector, vector, project, bias, turned, vector, vector, matrix, matrix, turned)
    return jax.shard_map(
        body,
        mesh=mesh,
        in_specs=(rows, rows, P()) + params,
        out_specs=(rows, rows) + params,
        check_vma=False,
    )
```

```python
import functools

import jax
import jax.numpy as jnp
import numpy as np
from jax import lax
from jax.experimental import pallas as pl
from jax.experimental.pallas import tpu as pltpu
from jax.sharding import PartitionSpec as P

MESH = pl.DeviceIdType.MESH
D = 2048
UNITS = 1408
HEAD_DIM = 64
ROT = 16
EPSILON = 1e-05
LOG2E = 1.4426950408889634
LOW = -1e30
TILE = 512
ROWS = 64
AT_ONCE = 34
VMEM_LIMIT = 58 * 2**20
STEPS = (1, 3, 2)
BF = jnp.bfloat16
F32 = jnp.float32


def here():
    ctx = lax.axis_index("ctx")
    return (lax.axis_index("dp"), ctx // 4, lax.rem(ctx, 4), lax.axis_index("tensor"))


def at(c, y, z, x):
    return (c, lax.rem(y, 4) * 4 + lax.rem(z, 4), lax.rem(x, 4))


def up(i, d):
    return lax.rem(i + d, 4)


def down(i, d):
    return lax.rem(i + 4 - d, 4)


class Net:
    def __init__(self, send_sems, recv_sems):
        self.send_sems, self.recv_sems = send_sems, recv_sems
        self.sent, self.gone = [], set()

    def send(self, src, dst, device):
        n = len(self.sent)
        copy = pltpu.make_async_remote_copy(
            src_ref=src,
            dst_ref=dst,
            send_sem=self.send_sems.at[n],
            recv_sem=self.recv_sems.at[n],
            device_id=device,
            device_id_type=MESH,
        )
        copy.start()
        self.sent.append(copy)
        return copy

    def finish(self):
        for n, copy in enumerate(self.sent):
            if n not in self.gone:
                copy.wait_send()

    def wait_sent(self, copy):
        copy.wait_send()
        self.gone.add([other is copy for other in self.sent].index(True))


class Local:
    def __init__(self, sems):
        self.sems, self.n = sems, 0

    def copy(self, src, dst):
        copy = pltpu.make_async_copy(src, dst, self.sems.at[self.n])
        copy.start()
        self.n += 1
        return copy


def greet(peers):
    barrier = pltpu.get_barrier_semaphore()
    for peer in peers:
        pl.semaphore_signal(barrier, inc=1, device_id=peer, device_id_type=MESH)
    pl.semaphore_wait(barrier, len(peers))


def y_peers(c, y, z, x):
    return [at(c, y + d, z, x) for d in (1, 2, 3)]


def z_peers(c, y, z, x):
    return [at(c, y, z + d, x) for d in (1, 2, 3)]


def x_peers(c, y, z, x):
    return [at(c, y, z, x + d) for d in (1, 2, 3)]


def core_peer(c, y, z, x):
    return [at(1 - c, y, z, x)]


class RingSum:
    def __init__(self, net, device, mine, spare, add):
        self.net, self.device, self.mine, self.spare, self.add = net, device, mine, spare, add

    def start(self):
        self.start_far()
        self.start_near()

    def start_far(self):
        send, mine, spare = self.net.send, self.mine, self.spare
        ahead, back = self.device(1), self.device(3)
        self.far_ahead = send(mine(2, 0), spare.at[0], ahead)
        self.far_back = send(mine(2, 1), spare.at[1], back)

    def start_near(self):
        send, mine, spare = self.net.send, self.mine, self.spare
        ahead, back = self.device(1), self.device(3)
        self.near = [send(mine(1, 1), spare.at[3], ahead), send(mine(3, 0), spare.at[2], back)]

    def middle(self):
        send, spare = self.net.send, self.spare
        self.far_ahead.wait_recv()
        self.add(spare.at[0], self.mine(1, 0))
        self.near.append(send(spare.at[0], spare.at[4], self.device(1)))
        self.far_back.wait_recv()
        self.add(spare.at[1], self.mine(3, 1))
        self.near.append(send(spare.at[1], spare.at[5], self.device(3)))

    def arrive(self):
        for copy in self.near:
            copy.wait_recv()

    def sent(self):
        for copy in [self.far_ahead, self.far_back] + self.near:
            self.net.wait_sent(copy)

    def terms(self, half):
        return [self.spare.at[4 if half == 0 else 3], self.spare.at[2 if half == 0 else 5]]


RING_SUM = 6


class RingGather:
    def __init__(self, net, device, out):
        self.net, self.device, self.out = net, device, out

    def start(self, block):
        self.ahead = self.net.send(block, self.out(0), self.device(1))
        self.back = self.net.send(block, self.out(0), self.device(3))

    def from_back(self):
        self.ahead.wait_recv()
        piece = self.out(3, 0)
        self.far_ahead = self.net.send(piece, piece, self.device(1))

    def from_ahead(self):
        self.back.wait_recv()
        piece = self.out(1, 1)
        self.far_back = self.net.send(piece, piece, self.device(3))

    def arrive(self):
        self.far_ahead.wait_recv()
        self.far_back.wait_recv()


RING_GATHER = 4


class Gather:
    def __init__(self, net, local, src, place, me):
        self.net, self.local, self.src, self.place, self.me = net, local, src, place, me
        self.core = []
        c, y, z, x = me
        along_y = lambda d: at(c, y + d, z, x)
        along_z = lambda d: at(c, y, z + d, x)

        def spot(far_y, far_z, first, half):
            if half is None:
                return place(c, up(y, far_y), up(z, far_z), first, 32)
            return place(c, up(y, far_y), up(z, far_z), first + 16 * half, 16)

        self.one = (
            RingGather(net, along_y, lambda d, half=None: spot(d, 0, 0, half)),
            RingGather(net, along_z, lambda d, half=None: spot(0, d, 32, half)),
        )
        self.two = {}
        for k in range(4):
            self.two[0, k] = RingGather(net, along_z, lambda d, half=None, k=k: spot(k, d, 0, half))
            self.two[1, k] = RingGather(net, along_y, lambda d, half=None, k=k: spot(d, k, 32, half))

    def hand_over(self, piece):
        c, y, z, x = self.me
        self.core.append(self.net.send(piece, piece, at(1 - c, y, z, x)))

    def start(self):
        c, y, z, x = self.me
        src, own = self.src, self.place(c, y, z, 0, 64)
        self.own = self.local.copy(src, own)
        halves = (src.at[pl.ds(0, 32)], src.at[pl.ds(32, 32)])
        for way in range(2):
            self.one[way].start(halves[way])
        for way in range(2):
            self.two[way, 0].start(halves[way])
        self.core.append(self.net.send(src, own, at(1 - c, y, z, x)))

    def near(self):
        for way in range(2):
            self.one[way].from_back()
            self.two[way, 3].start(self.one[way].out(3))
        for way in range(2):
            self.one[way].from_ahead()
            self.two[way, 1].start(self.one[way].out(1))
        for k in (3, 1):
            for way in range(2):
                self.hand_over(self.one[way].out(k))

    def middle(self):
        self.pass_on(0)
        for way in range(2):
            self.one[way].arrive()
            self.two[way, 2].start(self.one[way].out(2))
            self.hand_over(self.one[way].out(2))

    def pass_on(self, k):
        for way in range(2):
            self.two[way, k].from_back()
            self.two[way, k].from_ahead()
            self.hand_over(self.two[way, k].out(3))
            self.hand_over(self.two[way, k].out(1))

    def far(self):
        for k in (0, 3, 1, 2):
            for way in range(2):
                self.two[way, k].arrive()
                self.hand_over(self.two[way, k].out(2))

    def finish(self):
        for copy in self.core:
            copy.wait_recv()
        self.own.wait()


def flat_rows(ref):
    def place(c, y, z, first, count):
        return ref.at[pl.ds(pl.multiple_of(((c * 4 + y) * 4 + z) * 64 + first, 16), count)]

    return place


GATHER_COPIES = 10 * RING_GATHER + 31


def scatter_scratch(width):
    return [
        pltpu.VMEM((4, 4, 64, width), BF),
        pltpu.VMEM((4, 4, 64, width), BF),
        pltpu.VMEM((6, 4, 16, width), BF),
        pltpu.VMEM((6, 4, 16, width), BF),
        pltpu.VMEM((4, 32, width), BF),
        pltpu.VMEM((4, 32, width), BF),
        pltpu.VMEM((6, 16, width), BF),
        pltpu.VMEM((6, 16, width), BF),
    ]


SCATTER_COPIES = 1 + 4 * RING_SUM


def add_blocks(total, term):
    if len(total.shape) == 2:
        total[...] = (total[...].astype(F32) + term[...].astype(F32)).astype(BF)
        return

    def one(i, carry):
        total[i] = (total[i].astype(F32) + term[i].astype(F32)).astype(BF)
        return carry

    lax.fori_loop(0, total.shape[0], one, 0)


class Scatter:
    def __init__(self, net, local, grads, out, scratch, me):
        self.net, self.local, self.grads, self.out, self.me = net, local, grads, out, me
        (held, self.other, one_a, one_b, self.sum_a, self.sum_b, two_a, two_b) = scratch
        self.held = held
        c, y, z, x = me
        along_y = lambda d: at(c, y + d, z, x)
        along_z = lambda d: at(c, y, z + d, x)
        self.one_a = RingSum(
            net, along_z, lambda d, half: held.at[:, up(z, d), pl.ds(16 * half, 16)], one_a, add_blocks
        )
        self.one_b = RingSum(
            net, along_y, lambda d, half: held.at[up(y, d), :, pl.ds(32 + 16 * half, 16)], one_b, add_blocks
        )
        self.two_a = RingSum(
            net, along_y, lambda d, half: self.sum_a.at[up(y, d), pl.ds(16 * half, 16)], two_a, add_blocks
        )
        self.two_b = RingSum(
            net, along_z, lambda d, half: self.sum_b.at[up(z, d), pl.ds(16 * half, 16)], two_b, add_blocks
        )

    def start(self):
        c, y, z, x = self.me
        self.own = self.local.copy(self.grads.at[c], self.held)
        self.zero = self.net.send(self.grads.at[1 - c], self.other, at(1 - c, y, z, x))

    def send_filled(self, block):
        c, y, z, x = self.me
        self.own = None
        self.zero = self.net.send(block, self.other, at(1 - c, y, z, x))

    def start_summed(self):
        self.own, self.zero = self.local.copy(self.grads, self.held), None

    def first(self):
        if self.own is not None:
            self.own.wait()
        if self.zero is None:
            self.one_a.start()
            self.one_b.start()
            return
        self.zero.wait_recv()
        held, other = self.held, self.other

        def add(i, carry):
            for q in range(4):
                rows = pl.ds(q * 16, 16)
                held[i // 4, lax.rem(i, 4), rows, :] = (
                    held[i // 4, lax.rem(i, 4), rows, :].astype(F32)
                    + other[i // 4, lax.rem(i, 4), rows, :].astype(F32)
                ).astype(BF)
            return carry

        lax.fori_loop(0, 16, add, 0)
        self.one_a.start()
        self.one_b.start()

    def first_middle(self):
        self.one_a.middle()
        self.one_b.middle()

    def second(self):
        for one, two, total in ((self.one_a, self.two_a, self.sum_a), (self.one_b, self.two_b, self.sum_b)):
            one.arrive()
            for half in range(2):
                own, terms = one.mine(0, half), one.terms(half)

                def add(i, carry, half=half, own=own, terms=terms, total=total):
                    value = own[i].astype(F32)
                    for term in terms:
                        value += term[i].astype(F32)
                    total[i, pl.ds(16 * half, 16), :] = value.astype(BF)
                    return carry

                lax.fori_loop(0, 4, add, 0)
            two.start()

    def second_middle(self):
        self.two_a.middle()
        self.two_b.middle()

    def third(self):
        for first, two in ((0, self.two_a), (32, self.two_b)):
            two.arrive()
            for half in range(2):
                value = two.mine(0, half)[...].astype(F32)
                for term in two.terms(half):
                    value += term[...].astype(F32)
                self.out[pl.ds(first + 16 * half, 16), :] = value


def quarters_of(net, out, me):
    c, y, z, x = me

    def piece(d, half=None):
        return out.at[up(x, d)] if half is None else out.at[up(x, d), pl.ds(64 * half, 64)]

    return RingGather(net, lambda d: at(c, y, z, x + d), piece)


class SumX:
    def __init__(self, net, local, parts, held, spare, me):
        c, y, z, x = me
        self.local, self.parts, self.held, self.x, self.net, self.me = local, parts, held, x, net, me
        self.along = lambda d: at(c, y, z, x + d)
        self.ring = RingSum(
            net, self.along, lambda d, half: held.at[up(x, d), pl.ds(64 * half, 64)], spare, self.add
        )

    def add(self, total, term):
        def one(i, carry):
            rows = pl.ds(pl.multiple_of(i * 16, 16), 16)
            total[rows, :] = (total[rows, :].astype(F32) + term[rows, :].astype(F32)).astype(BF)
            return carry

        lax.fori_loop(0, 4, one, 0)

    def load(self):
        self.loads = [self.local.copy(self.parts.at[up(self.x, d)], self.held.at[up(self.x, d)]) for d in (2, 1, 3, 0)]

    def start(self):
        for copy in self.loads:
            copy.wait()
        self.ring.start()

    def start_held(self):
        self.ring.start()

    def middle(self):
        self.ring.middle()

    def totals(self, step):
        self.ring.arrive()
        for half in range(2):
            terms = self.ring.terms(half)

            def loop(i, carry, half=half, terms=terms):
                rows = pl.ds(pl.multiple_of(i * 32, 32), 32)
                own = pl.ds(pl.multiple_of(64 * half + i * 32, 32), 32)
                value = self.held[self.x, own, :].astype(F32)
                for term in terms:
                    value += term[rows, :].astype(F32)
                step(own, value)
                return carry

            lax.fori_loop(0, 2, loop, 0)

    def gather(self, block, out):
        x = self.x
        self.back = quarters_of(self.net, out, self.me)
        self.mine = self.local.copy(block, out.at[x])
        self.back.start(block)

    def gather_middle(self):
        self.back.from_back()
        self.back.from_ahead()

    def finish(self):
        self.mine.wait()
        self.back.arrive()


SUM_COPIES = RING_SUM + RING_GATHER
SUM_LOCALS = 5


def sum_scratch():
    return [pltpu.VMEM((4, 128, D), BF), pltpu.VMEM((6, 64, D), BF)]


def normed(values):
    centre = jnp.mean(values, axis=-1, keepdims=True)
    spread = values - centre
    inverse = lax.rsqrt(jnp.mean(spread * spread, axis=-1, keepdims=True) + EPSILON)
    return spread * inverse, inverse


def norm_pullback(upstream, norm, inverse, gain):
    scaled = upstream * gain
    first = jnp.mean(scaled, axis=-1, keepdims=True)
    second = jnp.mean(scaled * norm, axis=-1, keepdims=True)
    return inverse * (scaled - first - norm * second)


ANY = pl.BlockSpec(memory_space=pl.ANY)
IN_VMEM = pl.BlockSpec(memory_space=pltpu.VMEM)
IN_SMEM = pl.BlockSpec(memory_space=pltpu.SMEM)


def remote_call(body, name, cid, ins, outs, scratch, copies, locals_):
    return pl.pallas_call(
        body,
        name=name,
        in_specs=ins,
        out_specs=[spec for _, _, spec in outs],
        out_shape=[jax.ShapeDtypeStruct(shape, dtype) for shape, dtype, _ in outs],
        scratch_shapes=scratch
        + [
            pltpu.SemaphoreType.DMA((copies,)),
            pltpu.SemaphoreType.DMA((copies,)),
            pltpu.SemaphoreType.DMA((locals_,)),
        ],
        compiler_params=pltpu.CompilerParams(
            collective_id=cid, has_side_effects=True, vmem_limit_bytes=VMEM_LIMIT
        ),
    )


def assemble_vectors(weights, gains, bias, spots):
    for s in range(32):
        block = weights[s * 64 : s * 64 + 16, 2048:2176].astype(F32)
        gains[0:4, s * 64 : s * 64 + 64] = block[0:4, :64]
        spots[s : s + 1, :] = block[4:5, :]
    values = spots[...].astype(BF)
    head = lax.broadcasted_iota(jnp.int32, (32, 128), 0)
    held = lax.broadcasted_iota(jnp.int32, (32, 128), 1)
    shard = lax.broadcasted_iota(jnp.int32, (32, 64), 0)
    lane = lax.broadcasted_iota(jnp.int32, (32, 64), 1)
    total = jnp.zeros((32, 64), F32)
    for e in range(2):
        pick = jnp.where((held == 2 * head + e) & (head < 24), 1.0, 0.0).astype(BF)
        spread = jnp.where(lane == 2 * shard + e, 1.0, 0.0).astype(BF)
        total += jnp.dot(nt(pick, values).astype(BF), spread, preferred_element_type=F32)
    for n in range(24):
        bias[0:1, n * 64 : n * 64 + 64] = total[n : n + 1]


def front_forward(shard, tokens, group_place, base, steps):
    def kernel(
        src, x_ref, group_ref, base_ref, steps_ref, front, gains, low, out,
        weights, norm, blocks, bias, spots, turns, ss, rs, ls,
    ):
        me = here()
        c, y, z, x = me
        net, local = Net(ss, rs), Local(ls)
        greet(y_peers(*me) + z_peers(*me) + core_peer(*me))
        gather = Gather(net, local, src, flat_rows(weights), me)
        gather.start()
        for n in range(2):
            rows = slice(n * 128, n * 128 + 128)
            cosine, sine = turn_tables(base_ref, steps_ref, group_ref[(y * 4 + z) * 2 + n])
            turns[0, rows, :] = cosine
            turns[1, rows, :] = sine

        def centre(i, carry):
            rows = pl.ds(pl.multiple_of(i * 32, 32), 32)
            norm[rows, :] = normed(x_ref[rows, :].astype(F32))[0]
            return carry

        lax.fori_loop(0, 4, centre, 0)
        gather.near()
        lax.fori_loop(4, 8, centre, 0)
        gather.middle()
        lax.fori_loop(8, 16, centre, 0)
        for k in (3, 1, 2):
            gather.pass_on(k)
        gather.far()
        gather.finish()
        keep = local.copy(weights, front)
        assemble_vectors(weights, gains, bias, spots)

        def scale(i, carry):
            rows = pl.ds(pl.multiple_of(i * 32, 32), 32)
            low[rows, :] = (norm[rows, :] * gains[0:1, :] + gains[1:2, :]).astype(BF)
            return carry

        lax.fori_loop(0, 16, scale, 0)

        def project(t):
            columns = slice(t * 512, t * 512 + 512)
            for m in range(2):
                acc = jnp.dot(low[m * 256 : m * 256 + 256, :], weights[:, columns], preferred_element_type=F32)
                acc = acc + bias[:, columns]
                for h in range(4):
                    part = acc[:, h * 128 : h * 128 + 128]
                    if t < 2:
                        part = turn(part, turns[0], turns[1])
                    blocks[m, h, (t + 2) % 3] = part.astype(BF)

        along_y = lambda d: at(c, y + d, z, x)
        along_z = lambda d: at(c, y, z + d, x)
        kv = pl.ds(0, 2)

        def part(half):
            return kv if half is None else half

        rings = {}
        for k in range(4):
            rings[0, k] = RingGather(
                net, along_y, lambda d, half=None, k=k: out.at[0, up(y, d), up(z, k), part(half)]
            )
            rings[1, k] = RingGather(
                net, along_z, lambda d, half=None, k=k: out.at[1, up(y, k), up(z, d), part(half)]
            )
        project(1)
        project(2)
        first = {}
        for d in STEPS:
            first[0, d] = net.send(blocks.at[0, up(z, d), kv], out.at[0, y, z, kv], along_z(d))
            first[1, d] = net.send(blocks.at[1, up(y, d), kv], out.at[1, y, z, kv], along_y(d))
        rings[0, 0].start(blocks.at[0, z, kv])
        rings[1, 0].start(blocks.at[1, y, kv])
        project(0)
        last = []
        for d in STEPS:
            last.append(net.send(blocks.at[0, up(z, d), 2], out.at[0, y, z, 2], along_z(d)))
            last.append(net.send(blocks.at[1, up(y, d), 2], out.at[1, y, z, 2], along_y(d)))
        owns = [local.copy(blocks.at[0, z], out.at[0, y, z]), local.copy(blocks.at[1, y], out.at[1, y, z])]
        for d in STEPS:
            for m in range(2):
                first[m, d].wait_recv()
                ring = rings[m, 4 - d]
                ring.start(ring.out(0))
        for k in (0, 3, 1, 2):
            for m in range(2):
                rings[m, k].from_back()
                rings[m, k].from_ahead()
        for ring in rings.values():
            ring.arrive()
        for copy in last:
            copy.wait_recv()
        for copy in owns:
            copy.wait()
        keep.wait()
        net.finish()

    width = shard.shape[1]
    return remote_call(
        kernel,
        "front_forward",
        0,
        [ANY, IN_VMEM, IN_SMEM, IN_VMEM, IN_VMEM],
        [
            ((D, width), BF, ANY),
            ((4, D), F32, IN_VMEM),
            ((512, D), BF, IN_VMEM),
            ((2, 4, 4, 3, 256, 128), BF, ANY),
        ],
        [
            pltpu.VMEM((D, width), BF),
            pltpu.VMEM((512, D), F32),
            pltpu.VMEM((2, 4, 3, 256, 128), BF),
            pltpu.VMEM((1, 1536), F32),
            pltpu.VMEM((32, 128), F32),
            pltpu.VMEM((2, 256, 128), F32),
        ],
        GATHER_COPIES + 12 + 8 * RING_GATHER,
        4,
    )(shard, tokens, group_place, base, steps)


class Swap:
    def __init__(self, net, local, src, out, me):
        c, y, z, x = me
        self.owns = [local.copy(src.at[0, z], out.at[0, z]), local.copy(src.at[1, y], out.at[1, y])]
        self.copies = []
        for d in STEPS:
            self.copies.append(net.send(src.at[0, up(z, d)], out.at[0, z], at(c, y, z + d, x)))
            self.copies.append(net.send(src.at[1, up(y, d)], out.at[1, y], at(c, y + d, z, x)))

    def arrive(self):
        for copy in self.copies:
            copy.wait_recv()
        for copy in self.owns:
            copy.wait()


SWAP_COPIES, SWAP_LOCALS = 6, 2
TURNED = pl.ds(1536, 512)


def middle_forward(heads, front, inputs, gains, shard):
    width = shard.shape[1]

    def kernel(
        heads, front, inputs, gains, shard, attended, hidden, second, weights,
        swapped, out_w, held, spare, base, low, ss, rs, ls,
    ):
        me = here()
        c, y, z, x = me
        net, local = Net(ss, rs), Local(ls)
        sums = SumX(net, local, None, held, spare, me)
        load = local.copy(front.at[:, TURNED], out_w)
        residual = local.copy(inputs.at[x], base)
        greet(y_peers(*me) + z_peers(*me) + core_peer(*me) + x_peers(*me))
        swap = Swap(net, local, heads, swapped, me)
        gather = Gather(net, local, shard, flat_rows(weights), me)
        gather.start()
        load.wait()
        swap.arrive()
        for m in range(2):
            for h in range(4):
                attended[m * 256 : m * 256 + 256, h * 128 : h * 128 + 128] = swapped[m, h]
        for q in range(4):
            held[q] = nt(attended[q * 128 : q * 128 + 128, :], out_w[...]).astype(BF)
        sums.start_held()
        gather.near()
        sums.middle()
        gather.middle()
        gather.pass_on(3)
        residual.wait()

        def step(rows, total):
            value = base[rows, :].astype(F32) + total
            hidden[rows, :] = value
            norm, _ = normed(value)
            low[rows, :] = (norm * gains[2:3, :] + gains[3:4, :]).astype(BF)

        sums.totals(step)
        sums.gather(low, second)
        gather.pass_on(1)
        gather.pass_on(2)
        sums.gather_middle()
        gather.far()
        gather.finish()
        sums.finish()
        net.finish()

    return remote_call(
        kernel,
        "middle_forward",
        3,
        [ANY, ANY, ANY, IN_VMEM, ANY],
        [
            ((512, 512), BF, IN_VMEM),
            ((128, D), F32, IN_VMEM),
            ((4, 128, D), BF, ANY),
            ((D, width), BF, ANY),
        ],
        [pltpu.VMEM((2, 4, 256, 128), BF), pltpu.VMEM((D, 512), BF)]
        + sum_scratch()
        + [pltpu.VMEM((128, D), BF), pltpu.VMEM((128, D), BF)],
        SWAP_COPIES + GATHER_COPIES + SUM_COPIES,
        SWAP_LOCALS + SUM_LOCALS + 3,
    )(heads, front, inputs, gains, shard)


def other_half(c, k, size):
    core = 1 - c if k < 2 else c
    return pl.ds(pl.multiple_of(core * 1024 + (k % 2) * size, size), size)


def shard_block(k):
    return pl.ds((k % 2) * 2, 2)


def middle_backward(parts, cotangent, hidden, gains, attended, front, second_low, dup, mixed, branch, gate_grad):
    def kernel(
        parts, cotangent, hidden, gains, attended, front, second_low, dup, mixed, branch, gate_grad,
        dhidden, vectors, output_grad, upstream, out_block, gate_out, up_out, down_out,
        held, spare, low, hidden_low, out_w, blocks, lows, dys, extra, *rest,
    ):
        scratch, (ss, rs, ls) = rest[:-3], rest[-3:]
        me = here()
        c, y, z, x = me
        net, local = Net(ss, rs), Local(ls)
        sums = SumX(net, local, parts, held, spare, me)
        sums.load()
        loads = [local.copy(second_low, lows), local.copy(cotangent, dys)]
        load = local.copy(front.at[:, TURNED], out_w)
        greet(y_peers(*me) + z_peers(*me) + core_peer(*me) + x_peers(*me))
        gate, up_, down_ = [
            Scatter(net, local, grads, out, scratch[8 * k : 8 * k + 8], me)
            for k, (grads, out) in enumerate(((gate_grad, gate_out), (None, up_out), (None, down_out)))
        ]
        gate.start_summed()
        sums.start()
        gate.first()

        def multiply(left, right, k, to):
            value = tn(left[:, other_half(c, k, 512)], right[...]).astype(BF)
            to[shard_block(k)] = value.reshape(2, 4, 64, UNITS)

        loads[0].wait()
        for k in range(2):
            multiply(lows, dup, k, down_.held)
        up_.send_filled(down_.held)
        for k in range(2, 4):
            multiply(lows, dup, k, up_.held)
        gate.first_middle()
        sums.middle()
        loads[1].wait()
        for k in range(2):
            multiply(dys, mixed, k, extra)
        down_.send_filled(extra)
        up_.first()
        net.wait_sent(up_.zero)
        for k in range(2, 4):
            multiply(dys, mixed, k, down_.held)
        down_.first()
        up_.first_middle()
        vectors[...] = jnp.zeros_like(vectors)

        def step(rows, dsecond):
            norm, inverse = normed(hidden[rows, :])
            upper = dys[pl.ds(pl.multiple_of(x * 128 + rows.start, 32), 32), :].astype(F32)
            value = upper + norm_pullback(dsecond, norm, inverse, gains[2:3, :])
            dhidden[rows, :] = value
            low[rows, :] = value.astype(BF)
            vectors[0:1, :] += jnp.sum(dsecond * norm, axis=0, keepdims=True)
            vectors[1:2, :] += jnp.sum(dsecond, axis=0, keepdims=True)

        sums.totals(step)
        sums.ring.sent()
        sums.gather(low, hidden_low)
        gate.second()
        sums.gather_middle()
        late = SumX(net, local, branch, held, spare, me)
        late.load()
        late.start()
        down_.first_middle()
        up_.second()
        load.wait()
        sums.finish()
        for q in range(4):
            rows = slice((q % 2) * 128, (q % 2) * 128 + 128)
            result = jnp.dot(hidden_low[q], out_w[...], preferred_element_type=F32).astype(BF)
            for h in range(4):
                blocks[q // 2, h, rows, :] = result[:, h * 128 : h * 128 + 128]
        swap = Swap(net, local, blocks, upstream, me)
        late.middle()
        gate.second_middle()
        down_.second()
        whole = hidden_low[...].reshape(512, D)
        output_grad[...] = tn(whole, attended[...]).astype(BF)
        up_.second_middle()
        gate.third()
        down_.second_middle()

        def last(rows, total):
            out_block[rows, :] = (hidden[rows, :] + total).astype(BF)

        late.totals(last)
        up_.third()
        down_.third()
        swap.arrive()
        net.finish()

    scratch = sum_scratch() + [
        pltpu.VMEM((128, D), BF),
        pltpu.VMEM((4, 128, D), BF),
        pltpu.VMEM((D, 512), BF),
        pltpu.VMEM((2, 4, 256, 128), BF),
        pltpu.VMEM((512, D), BF),
        pltpu.VMEM((512, D), BF),
        pltpu.VMEM((4, 4, 64, UNITS), BF),
    ]
    return remote_call(
        kernel,
        "middle_backward",
        4,
        [ANY, ANY, IN_VMEM, IN_VMEM, IN_VMEM, ANY, ANY, IN_VMEM, IN_VMEM, ANY, ANY],
        [
            ((128, D), F32, IN_VMEM),
            ((2, D), F32, IN_VMEM),
            ((D, 512), BF, IN_VMEM),
            ((2, 4, 256, 128), BF, ANY),
            ((128, D), BF, IN_VMEM),
        ]
        + [((64, UNITS), F32, IN_VMEM)] * 3,
        scratch + scatter_scratch(UNITS) * 3,
        SUM_COPIES + RING_SUM + SCATTER_COPIES * 3 + SWAP_COPIES,
        SUM_LOCALS + 4 + SWAP_LOCALS + 3 + 1,
    )(parts, cotangent, hidden, gains, attended, front, second_low, dup, mixed, branch, gate_grad)


def collect_heads(dkv, dq, block):
    def kernel(dkv, dq, block, dproject, outputs, mine, got, summed, ss, rs, ls):
        me = here()
        c, y, z, x = me
        net, local = Net(ss, rs), Local(ls)
        order = (1, 3, 2, 0)
        loads = [local.copy(dkv.at[m], mine.at[m]) for m in range(2)]
        greet(y_peers(*me) + z_peers(*me) + x_peers(*me))
        kv = pl.ds(0, 2)
        along_y = lambda d: at(c, y + d, z, x)
        along_z = lambda d: at(c, y, z + d, x)

        def add(total, term):
            def one(i, carry):
                rows = pl.ds(pl.multiple_of(i * 64, 64), 64)
                total[rows, :] = (total[rows, :].astype(F32) + term[rows, :].astype(F32)).astype(BF)
                return carry

            lax.fori_loop(0, 4, one, 0)

        rings = {}
        for k in order:
            rings[0, k] = RingSum(
                net, along_y, lambda d, half, k=k: mine.at[0, up(y, d), up(z, k), half], got.at[0, k], add
            )
            rings[1, k] = RingSum(
                net, along_z, lambda d, half, k=k: mine.at[1, up(y, k), up(z, d), half], got.at[1, k], add
            )
        whole = quarters_of(net, outputs, me)
        own = local.copy(block, outputs.at[x])
        whole.start(block)
        for copy in loads:
            copy.wait()
        for ring in rings.values():
            ring.start()
        lates = [
            local.copy(dq.at[0, z], dproject.at[0, z, 2]),
            local.copy(dq.at[1, y], dproject.at[1, y, 2]),
        ]
        two = []
        for d in STEPS:
            two.append(net.send(dq.at[0, up(z, d)], dproject.at[0, z, 2], along_z(d)))
            two.append(net.send(dq.at[1, up(y, d)], dproject.at[1, y, 2], along_y(d)))
        for ring in rings.values():
            ring.middle()
        for k in order:
            for m, spot in ((0, z), (1, y)):
                ring = rings[m, k]
                ring.arrive()
                for half in range(2):
                    kept, terms = ring.mine(0, half), ring.terms(half)

                    def total(i, carry, m=m, k=k, half=half, kept=kept, terms=terms):
                        rows = pl.ds(pl.multiple_of(i * 64, 64), 64)
                        value = kept[rows, :].astype(F32)
                        for term in terms:
                            value += term[rows, :].astype(F32)
                        summed[m, k, half, rows, :] = value.astype(BF)
                        return carry

                    lax.fori_loop(0, 4, total, 0)
            if k:
                two.append(net.send(summed.at[0, k], dproject.at[0, z, kv], along_z(k)))
                two.append(net.send(summed.at[1, k], dproject.at[1, y, kv], along_y(k)))
            else:
                lates.append(local.copy(summed.at[0, 0], dproject.at[0, z, kv]))
                lates.append(local.copy(summed.at[1, 0], dproject.at[1, y, kv]))

        whole.from_back()
        whole.from_ahead()
        for copy in two:
            copy.wait_recv()
        for copy in lates:
            copy.wait()
        own.wait()
        whole.arrive()
        net.finish()

    return remote_call(
        kernel,
        "collect_heads",
        6,
        [ANY, ANY, IN_VMEM],
        [((2, 4, 3, 256, 128), BF, ANY), ((4, 128, D), BF, ANY)],
        [
            pltpu.VMEM((2, 4, 4, 2, 256, 128), BF),
            pltpu.VMEM((2, 4, 6, 256, 128), BF),
            pltpu.VMEM((2, 4, 2, 256, 128), BF),
        ],
        8 * RING_SUM + 6 + 6 + RING_GATHER,
        2 + 4 + 1,
    )(dkv, dq, block)


def last_backward(dproject, first_low, front, inputs, dhidden, gains, mixer_vectors, output_grad):
    def kernel(
        dproject, first_low, front, inputs, dhidden, gains, mixer_vectors, output_grad,
        input_grad, sums_out, project_out, output_out,
        wide, weights, lows, held, spare, base, low, extra, small, got, *rest,
    ):
        scratch, (ss, rs, ls) = rest[:-3], rest[-3:]
        me = here()
        c, y, z, x = me
        net, local = Net(ss, rs), Local(ls)
        load = local.copy(front.at[:, pl.ds(0, 1536)], weights)
        load_low = local.copy(first_low, lows)
        residual = local.copy(inputs.at[x], base)
        greet(y_peers(*me) + z_peers(*me) + core_peer(*me) + x_peers(*me))
        project = Scatter(net, local, None, project_out, scratch[:8], me)
        output = Scatter(net, local, output_grad, output_out, scratch[8:], me)
        output.start()
        sums = SumX(net, local, None, held, spare, me)
        for m in range(2):
            for t in range(3):
                for h in range(4):
                    to = t * 512 + h * 128
                    wide[m * 256 : m * 256 + 256, to : to + 128] = dproject[m, h, (t + 2) % 3]
        load.wait()

        def quarter(d):
            q = up(x, d)
            rows = wide[pl.ds(pl.multiple_of(q * 128, 128), 128), :]
            held[q] = nt(rows, weights[...]).astype(BF)

        quarter(2)
        sums.ring.start_far()
        quarter(1)
        quarter(3)
        sums.ring.start_near()

        def multiply(k, to):
            value = tn(lows[:, other_half(c, k, 512)], wide[...]).astype(BF)
            to[shard_block(k)] = value.reshape(2, 4, 64, 1536)

        load_low.wait()
        for k in range(2):
            multiply(k, extra)
        project.send_filled(extra)
        sums.middle()
        quarter(0)
        for k in range(2, 4):
            multiply(k, project.held)
        output.first()
        small[0, ...] = jnp.zeros_like(small[0])
        small[0, 2:4, :] = mixer_vectors[...]
        small[0, 4:5, 0:1536] = jnp.sum(wide[...].astype(F32), axis=0, keepdims=True)
        project.first()
        residual.wait()

        def step(rows, dfirst):
            norm, inverse = normed(base[rows, :].astype(F32))
            value = dhidden[rows, :] + norm_pullback(dfirst, norm, inverse, gains[0:1, :])
            low[rows, :] = value.astype(BF)
            small[0, 0:1, :] += jnp.sum(dfirst * norm, axis=0, keepdims=True)
            small[0, 1:2, :] += jnp.sum(dfirst, axis=0, keepdims=True)

        sums.totals(step)
        copies = [net.send(small.at[0], got.at[0, d - 1], at(c, y, z, x + d)) for d in STEPS]
        sums.gather(low, input_grad)
        output.first_middle()
        project.first_middle()
        for copy in copies:
            copy.wait_recv()
        small[1, ...] = small[0, ...]
        for n in range(3):
            small[1, 0:4, :] += got[0, n, 0:4, :]
        copies = [net.send(small.at[1], got.at[1, d - 1], at(c, y + d, z, x)) for d in STEPS]
        sums.gather_middle()
        output.second()
        project.second()
        for copy in copies:
            copy.wait_recv()
        small[2, ...] = small[1, ...] + got[1, 0] + got[1, 1] + got[1, 2]
        copies = [net.send(small.at[2], got.at[2, d - 1], at(c, y, z + d, x)) for d in STEPS]
        output.second_middle()
        project.second_middle()
        for copy in copies:
            copy.wait_recv()
        small[3, ...] = small[2, ...] + got[2, 0] + got[2, 1] + got[2, 2]
        copy = net.send(small.at[3], got.at[3, 0], at(1 - c, y, z, x))
        output.third()
        project.third()
        copy.wait_recv()
        sums_out[...] = small[3, ...] + got[3, 0]
        sums.finish()
        net.finish()

    scratch = (
        [pltpu.VMEM((512, 1536), BF), pltpu.VMEM((D, 1536), BF), pltpu.VMEM((512, D), BF)]
        + sum_scratch()
        + [
            pltpu.VMEM((128, D), BF),
            pltpu.VMEM((128, D), BF),
            pltpu.VMEM((4, 4, 64, 1536), BF),
            pltpu.VMEM((4, 8, D), F32),
            pltpu.VMEM((4, 3, 8, D), F32),
        ]
    )
    return remote_call(
        kernel,
        "last_backward",
        7,
        [IN_VMEM, ANY, ANY, ANY, IN_VMEM, IN_VMEM, IN_VMEM, ANY],
        [
            ((4, 128, D), BF, ANY),
            ((8, D), F32, IN_VMEM),
            ((64, 1536), F32, IN_VMEM),
            ((64, 512), F32, IN_VMEM),
        ],
        scratch + scatter_scratch(1536) + scatter_scratch(512),
        SUM_COPIES + 10 + SCATTER_COPIES * 2,
        SUM_LOCALS + 4,
    )(dproject, first_low, front, inputs, dhidden, gains, mixer_vectors, output_grad)


def turn(values, cosine, sine):
    lane = lax.broadcasted_iota(jnp.int32, values.shape, 1) & (HEAD_DIM - 1)
    swapped = jnp.where(lane < ROT // 2, -pltpu.roll(values, 120, 1), pltpu.roll(values, 8, 1))
    return values * cosine + swapped * sine


def turn_tables(base, steps, block):
    cosine, sine = base[0], base[1]
    far_cosine, far_sine = steps[0, pl.ds(block, 1), :], steps[1, pl.ds(block, 1), :]
    return far_cosine * cosine - far_sine * sine, far_sine * cosine + far_cosine * sine


def two_heads(block):
    lane = lax.broadcasted_iota(jnp.int32, (128, 128), 1)
    value = block.astype(F32)
    return jnp.concatenate(
        [jnp.where(lane < HEAD_DIM, value, 0.0), jnp.where(lane >= HEAD_DIM, value, 0.0)], axis=0
    )


def two_heads_t(block):
    feature = lax.broadcasted_iota(jnp.int32, (128, 128), 0)
    value = block.astype(F32).T
    return jnp.concatenate(
        [jnp.where(feature < HEAD_DIM, value, 0.0), jnp.where(feature >= HEAD_DIM, value, 0.0)], axis=1
    )


def one_block(stacked):
    feature = lax.broadcasted_iota(jnp.int32, (128, 128), 0)
    return jnp.where(feature < HEAD_DIM, stacked[:, :128], stacked[:, 128:]).T


def nt(left, right):
    return lax.dot_general(left, right, (((1,), (1,)), ((), ())), preferred_element_type=F32)


def plan_blocks(group_place, slots, places):
    _, y, z, _ = here()

    def one(j, carry):
        slots[group_place[j]] = j
        return carry

    lax.fori_loop(0, 32, one, 0)
    for b in range(8):
        places[b] = group_place[(y * 4 + b // 2) * 2 + b % 2]
        places[8 + b] = group_place[((b // 2) * 4 + z) * 2 + b % 2]


def row_of(m, i):
    _, y, z, _ = here()
    return jnp.where(m == 0, y * 4 + i, i * 4 + z)


def unit_of(places, m, n):
    pair, rest = n // 9, lax.rem(n, 9)
    ahead = places[m * 8 + pair * 2] // (TILE // 128) + 1
    late = rest >= ahead
    block = pair * 2 + jnp.where(late, 1, 0)
    tile = rest - jnp.where(late, ahead, 0)
    return block, tile, places[m * 8 + block] * 128 - tile * TILE


def lay_mask(steps, bars):
    row = lax.broadcasted_iota(jnp.int32, (1024, 128), 0) - 513
    lane = lax.broadcasted_iota(jnp.int32, (1024, 128), 1)
    steps[...] = jnp.where(jnp.minimum(row, 127) == lane, 1.0, 0.0).astype(BF)
    bar = lax.broadcasted_iota(jnp.int32, (128, 256), 0)
    query = lax.rem(lax.broadcasted_iota(jnp.int32, (128, 256), 1), 128)
    bars[...] = jnp.where(bar >= query, LOW, 0.0).astype(BF)


def with_mask(keys, steps, behind):
    first = 512 - jnp.minimum(behind, 512)
    return jnp.concatenate([keys, steps[pl.ds(pl.multiple_of(first, 128), TILE), :]], axis=1)


def tile_of(t):
    return pl.ds(pl.multiple_of(t * TILE, TILE), TILE)


def lay_blocks(slots, lay):
    def some(n, carry):
        for k in range(8):
            b = n * 8 + k
            slot = slots[b]
            rows = pl.ds(pl.multiple_of(lax.rem(slot, 2) * 128, 128), 128)
            lay(slot // 2, rows, pl.ds(pl.multiple_of(b * 128, 128), 128))
        return carry

    lax.fori_loop(0, 4, some, 0)


UNITS_EACH = 36


def attend(group_place, spread):
    def kernel(
        group_ref, k_ref, v_ref, q_ref, o_ref, full_ref, log_ref,
        slots, places, keys, values_t, queries, scores_0, scores_1, weights_0, weights_1, results, tops, steps, bars,
    ):
        scores, weights = (scores_0, scores_1), (weights_0, weights_1)
        m = pl.program_id(0)
        plan_blocks(group_ref, slots, places)

        def lay(slot, rows, to):
            keys[to, :] = k_ref[0, slot, 0, rows, :]
            values_t[:128, to] = v_ref[0, slot, 0, rows, :].T

        lay_blocks(slots, lay)
        for b in range(8):
            row = row_of(m, b // 2)
            block = q_ref[0, row, 0, (b % 2) * 128 : (b % 2) * 128 + 128, :]
            queries[b, :128] = (two_heads_t(block) * 0.125).astype(BF)
        lay_mask(steps, bars)
        for b in range(8):
            queries[b, 128:] = bars[...]
        values_t[128:, :] = jnp.ones((16, 4096), BF)

        def multiply(n, odd):
            block, tile, behind = unit_of(places, m, n)
            value = jnp.dot(
                with_mask(keys[tile_of(tile), :], steps, behind), queries[block], preferred_element_type=F32
            )
            scores[odd][...] = value
            return jnp.max(value, axis=0, keepdims=True) * LOG2E

        def soften(n, odd, top, most):
            block, tile, _ = unit_of(places, m, n)
            top = jnp.where(tile == 0, LOW, top)
            new_top = jnp.maximum(top, most)
            for r in range(0, TILE, ROWS):
                rows = slice(r, r + ROWS)
                weights[odd][rows, :] = jnp.exp2(scores[odd][rows, :] * LOG2E - new_top).astype(BF)
            tops[block, 0:1, :] = new_top
            return new_top, jnp.exp2(top - new_top)

        def gather(n, odd, shrink, acc):
            block, tile, _ = unit_of(places, m, n)
            acc = acc * shrink + jnp.dot(
                values_t[:, tile_of(tile)], weights[odd][...], preferred_element_type=F32
            )
            results[block] = acc
            return acc

        most = multiply(0, 0)
        after = multiply(1, 1)
        top, shrink = soften(0, 0, jnp.zeros((1, 256), F32), most)

        def step(k, carry):
            top, shrink, acc, most = carry
            for n, odd in [(AT_ONCE * k + 1 + j, 1 - j % 2) for j in range(AT_ONCE)]:
                after = multiply(n + 1, 1 - odd)
                acc = gather(n - 1, 1 - odd, shrink, acc)
                top, shrink = soften(n, odd, top, most)
                most = after
            return top, shrink, acc, most

        carry = (top, shrink, jnp.zeros((144, 256), F32), after)
        top, shrink, acc, most = lax.fori_loop(0, (UNITS_EACH - 2) // AT_ONCE, step, carry)
        last = UNITS_EACH - 1
        acc = gather(last - 1, 0, shrink, acc)
        _, shrink = soften(last, 1, top, most)
        gather(last, 1, shrink, acc)
        for b in range(8):
            rows = slice((b % 2) * 128, (b % 2) * 128 + 128)
            total = results[b, 128:129, :]
            result = one_block(results[b, :128, :] / total)
            full_ref[0, b // 2, rows, :] = result
            o_ref[0, b // 2, rows, :] = result.astype(BF)
            log_ref[0, b : b + 1, :] = tops[b, 0:1, :] + jnp.log2(total)

    grid_spec = pltpu.PrefetchScalarGridSpec(
        num_scalar_prefetch=1,
        grid=(2,),
        in_specs=[
            pl.BlockSpec((1, 16, 1, 256, 128), lambda m, g: (m, 0, 0, 0, 0)),
            pl.BlockSpec((1, 16, 1, 256, 128), lambda m, g: (m, 0, 1, 0, 0)),
            pl.BlockSpec((1, 16, 1, 256, 128), lambda m, g: (m, 0, 2, 0, 0)),
        ],
        out_specs=[
            pl.BlockSpec((1, 4, 256, 128), lambda m, g: (m, 0, 0, 0)),
            pl.BlockSpec((1, 4, 256, 128), lambda m, g: (m, 0, 0, 0)),
            pl.BlockSpec((1, 8, 256), lambda m, g: (m, 0, 0)),
        ],
        scratch_shapes=[
            pltpu.SMEM((32,), jnp.int32),
            pltpu.SMEM((16,), jnp.int32),
            pltpu.VMEM((4096, 128), BF),
            pltpu.VMEM((144, 4096), BF),
            pltpu.VMEM((8, 256, 256), BF),
            pltpu.VMEM((TILE, 256), F32),
            pltpu.VMEM((TILE, 256), F32),
            pltpu.VMEM((TILE, 256), BF),
            pltpu.VMEM((TILE, 256), BF),
            pltpu.VMEM((8, 144, 256), F32),
            pltpu.VMEM((8, 8, 256), F32),
            pltpu.VMEM((1024, 128), BF),
            pltpu.VMEM((128, 256), BF),
        ],
    )
    return pl.pallas_call(
        kernel,
        name="attend",
        grid_spec=grid_spec,
        out_shape=[
            jax.ShapeDtypeStruct((2, 4, 256, 128), BF),
            jax.ShapeDtypeStruct((2, 4, 256, 128), F32),
            jax.ShapeDtypeStruct((2, 8, 256), F32),
        ],
        compiler_params=pltpu.CompilerParams(vmem_limit_bytes=VMEM_LIMIT),
    )(group_place, spread, spread, spread)


def attend_back(group_place, spread, full, logs, upstream, base, steps):
    def kernel(
        group_ref, k_ref, v_ref, q_ref, full_ref, log_ref, up_ref, base_ref, steps_ref,
        dq_ref, dkv_ref,
        slots, places, keys, keys_t, values, dkeys, dvalues, queries, queries_t, grads, grads_t, delta,
        scores_0, scores_1, dprobs_0, dprobs_1, probs_0, probs_1, dscores_0, dscores_1, results, steps, bars,
    ):
        scores, dprobs = (scores_0, scores_1), (dprobs_0, dprobs_1)
        probs_low, dscores = (probs_0, probs_1), (dscores_0, dscores_1)
        m = pl.program_id(0)
        plan_blocks(group_ref, slots, places)

        def lay(slot, rows, to):
            block = k_ref[0, slot, 0, rows, :]
            keys[to, :] = block
            keys_t[:, to] = block.T
            values[to, :] = v_ref[0, slot, 0, rows, :]
            dkeys[to, :] = jnp.zeros((128, 128), F32)
            dvalues[to, :] = jnp.zeros((128, 128), F32)

        lay_blocks(slots, lay)
        for b in range(8):
            rows = slice((b % 2) * 128, (b % 2) * 128 + 128)
            block = q_ref[0, row_of(m, b // 2), 0, rows, :]
            queries[b] = (two_heads(block) * 0.125).astype(BF)
            queries_t[b, :128] = (two_heads_t(block) * 0.125).astype(BF)
            ups = up_ref[0, b // 2, rows, :]
            grads[b] = two_heads(ups).astype(BF)
            grads_t[b] = two_heads_t(ups).astype(BF)
            product = (ups.astype(F32) * full_ref[0, b // 2, rows, :]).T
            delta[b, 0:1, :128] = jnp.sum(product[:HEAD_DIM], axis=0, keepdims=True)
            delta[b, 0:1, 128:] = jnp.sum(product[HEAD_DIM:], axis=0, keepdims=True)
        lay_mask(steps, bars)
        for b in range(8):
            queries_t[b, 128:] = bars[...]

        def multiply(n, odd):
            block, tile, behind = unit_of(places, m, n)
            scores[odd][...] = jnp.dot(
                with_mask(keys[tile_of(tile), :], steps, behind), queries_t[block], preferred_element_type=F32
            )
            dprobs[odd][...] = jnp.dot(
                values[tile_of(tile), :], grads_t[block], preferred_element_type=F32
            )

        def soften(n, odd):
            block, _, _ = unit_of(places, m, n)
            logs, deltas = log_ref[0, pl.ds(block, 1), :], delta[block, 0:1, :]
            for r in range(0, TILE, ROWS):
                rows = slice(r, r + ROWS)
                value = jnp.exp2(scores[odd][rows, :] * LOG2E - logs)
                probs_low[odd][rows, :] = value.astype(BF)
                dscores[odd][rows, :] = (value * (dprobs[odd][rows, :] - deltas)).astype(BF)

        def gather(n, odd, acc):
            block, tile, _ = unit_of(places, m, n)
            span = tile_of(tile)
            dvalues[span, :] += jnp.dot(probs_low[odd][...], grads[block], preferred_element_type=F32)
            dkeys[span, :] += jnp.dot(dscores[odd][...], queries[block], preferred_element_type=F32)
            acc = jnp.where(tile == 0, 0.0, acc) + jnp.dot(
                keys_t[:, span], dscores[odd][...], preferred_element_type=F32
            )
            results[block] = acc
            return acc

        multiply(0, 0)
        multiply(1, 1)
        soften(0, 0)

        def step(k, acc):
            for n, odd in [(AT_ONCE * k + 1 + j, 1 - j % 2) for j in range(AT_ONCE)]:
                multiply(n + 1, 1 - odd)
                acc = gather(n - 1, 1 - odd, acc)
                soften(n, odd)
            return acc

        last = UNITS_EACH - 1
        acc = lax.fori_loop(0, (UNITS_EACH - 2) // AT_ONCE, step, jnp.zeros((128, 256), F32))
        acc = gather(last - 1, 0, acc)
        soften(last, 1)
        gather(last, 1, acc)

        def turned_back(values, place):
            cosine, sine = turn_tables(base_ref, steps_ref, place)
            return turn(values, cosine, -sine)

        for b in range(8):
            rows = slice((b % 2) * 128, (b % 2) * 128 + 128)
            dquery = one_block(results[b]) * 0.125
            dq_ref[0, b // 2, rows, :] = turned_back(dquery, places[m * 8 + b]).astype(BF)

        def flush(n, carry):
            for k in range(4):
                b = n * 4 + k
                slot = slots[b]
                rows = pl.ds(pl.multiple_of(lax.rem(slot, 2) * 128, 128), 128)
                to = pl.ds(pl.multiple_of(b * 128, 128), 128)
                dkv_ref[0, slot // 2, 0, rows, :] = turned_back(dkeys[to, :], b).astype(BF)
                dkv_ref[0, slot // 2, 1, rows, :] = dvalues[to, :].astype(BF)
            return carry

        lax.fori_loop(0, 8, flush, 0)

    grid_spec = pltpu.PrefetchScalarGridSpec(
        num_scalar_prefetch=1,
        grid=(2,),
        in_specs=[
            pl.BlockSpec((1, 16, 1, 256, 128), lambda m, g: (m, 0, 0, 0, 0)),
            pl.BlockSpec((1, 16, 1, 256, 128), lambda m, g: (m, 0, 1, 0, 0)),
            pl.BlockSpec((1, 16, 1, 256, 128), lambda m, g: (m, 0, 2, 0, 0)),
            pl.BlockSpec((1, 4, 256, 128), lambda m, g: (m, 0, 0, 0)),
            pl.BlockSpec((1, 8, 256), lambda m, g: (m, 0, 0)),
            pl.BlockSpec((1, 4, 256, 128), lambda m, g: (m, 0, 0, 0)),
            pl.BlockSpec((2, 128, 128), lambda m, g: (0, 0, 0)),
            pl.BlockSpec((2, 32, 128), lambda m, g: (0, 0, 0)),
        ],
        out_specs=[
            pl.BlockSpec((1, 4, 256, 128), lambda m, g: (m, 0, 0, 0)),
            pl.BlockSpec((1, 16, 2, 256, 128), lambda m, g: (m, 0, 0, 0, 0)),
        ],
        scratch_shapes=[
            pltpu.SMEM((32,), jnp.int32),
            pltpu.SMEM((16,), jnp.int32),
            pltpu.VMEM((4096, 128), BF),
            pltpu.VMEM((128, 4096), BF),
            pltpu.VMEM((4096, 128), BF),
            pltpu.VMEM((4096, 128), F32),
            pltpu.VMEM((4096, 128), F32),
            pltpu.VMEM((8, 256, 128), BF),
            pltpu.VMEM((8, 256, 256), BF),
            pltpu.VMEM((8, 256, 128), BF),
            pltpu.VMEM((8, 128, 256), BF),
            pltpu.VMEM((8, 8, 256), F32),
            pltpu.VMEM((TILE, 256), F32),
            pltpu.VMEM((TILE, 256), F32),
            pltpu.VMEM((TILE, 256), F32),
            pltpu.VMEM((TILE, 256), F32),
            pltpu.VMEM((TILE, 256), BF),
            pltpu.VMEM((TILE, 256), BF),
            pltpu.VMEM((TILE, 256), BF),
            pltpu.VMEM((TILE, 256), BF),
            pltpu.VMEM((8, 128, 256), F32),
            pltpu.VMEM((1024, 128), BF),
            pltpu.VMEM((128, 256), BF),
        ],
    )
    return pl.pallas_call(
        kernel,
        name="attend_back",
        grid_spec=grid_spec,
        out_shape=[
            jax.ShapeDtypeStruct((2, 4, 256, 128), BF),
            jax.ShapeDtypeStruct((2, 16, 2, 256, 128), BF),
        ],
        compiler_params=pltpu.CompilerParams(vmem_limit_bytes=VMEM_LIMIT),
    )(group_place, spread, spread, spread, full, logs, upstream, base, steps)


def tn(left, right):
    return lax.dot_general(left, right, (((0,), (0,)), ((), ())), preferred_element_type=F32)


def feed_forward(second_low, dy, weights):
    def kernel(
        low_hbm, dy_hbm, w_hbm, branch, dsecond, gate_half, dup, mixed,
        low, dys, gate_w, up_w, down_w, gate, up, dmixed, dgate, give, other, sems, ss, rs,
    ):
        me = here()
        c, y, z, x = me

        def load(n, src, dst):
            copy = pltpu.make_async_copy(src, dst, sems.at[n])
            copy.start()
            return copy

        def columns(k):
            return w_hbm.at[:, pl.ds(k * UNITS, UNITS)]

        loads = [
            load(0, low_hbm, low),
            load(1, columns(0), gate_w),
            load(2, columns(1), up_w),
            load(3, dy_hbm, dys),
            load(4, columns(2), down_w),
        ]
        greet(core_peer(*me))
        net = Net(ss, rs)
        loads[0].wait()
        loads[1].wait()
        gate[...] = jnp.dot(low[...], gate_w[...], preferred_element_type=F32)
        loads[2].wait()
        up[...] = jnp.dot(low[...], up_w[...], preferred_element_type=F32)
        loads[3].wait()
        loads[4].wait()
        dmixed[...] = jnp.dot(dys[...], down_w[...], preferred_element_type=F32)

        def step(i, carry):
            rows = pl.ds(pl.multiple_of(i * 16, 16), 16)
            g, u, d = gate[rows, :], up[rows, :], dmixed[rows, :]
            s = jax.nn.sigmoid(g)
            silu = g * s
            mixed[rows, :] = (silu * u).astype(BF)
            dgate[rows, :] = (d * u * s * (1.0 + g * (1.0 - s))).astype(BF)
            dup[rows, :] = (d * silu).astype(BF)
            return carry

        lax.fori_loop(0, 32, step, 0)
        for k in range(4):
            value = tn(low[:, other_half(c, k, 512)], dgate[...]).astype(BF)
            to = give if k < 2 else gate_half
            to[(k % 2) * 512 : (k % 2) * 512 + 512, :] = value
            if k == 1:
                copy = net.send(give, other, core_peer(*me)[0])
        dsecond[...] = (nt(dgate[...], gate_w[...]) + nt(dup[...], up_w[...])).astype(BF)
        branch[...] = nt(mixed[...], down_w[...]).astype(BF)
        copy.wait_recv()

        def add(i, carry):
            rows = pl.ds(pl.multiple_of(i * 32, 32), 32)
            gate_half[rows, :] = (gate_half[rows, :].astype(F32) + other[rows, :].astype(F32)).astype(BF)
            return carry

        lax.fori_loop(0, 32, add, 0)
        net.finish()

    return pl.pallas_call(
        kernel,
        name="feed_forward",
        in_specs=[ANY, ANY, ANY],
        out_specs=[IN_VMEM] * 5,
        out_shape=[jax.ShapeDtypeStruct((512, D), BF)] * 2
        + [jax.ShapeDtypeStruct((1024, UNITS), BF)]
        + [jax.ShapeDtypeStruct((512, UNITS), BF)] * 2,
        scratch_shapes=[pltpu.VMEM((512, D), BF)] * 2
        + [pltpu.VMEM((D, UNITS), BF)] * 3
        + [pltpu.VMEM((512, UNITS), F32)] * 3
        + [
            pltpu.VMEM((512, UNITS), BF),
            pltpu.VMEM((1024, UNITS), BF),
            pltpu.VMEM((1024, UNITS), BF),
            pltpu.SemaphoreType.DMA((5,)),
            pltpu.SemaphoreType.DMA((1,)),
            pltpu.SemaphoreType.DMA((1,)),
        ],
        compiler_params=pltpu.CompilerParams(
            collective_id=2, has_side_effects=True, vmem_limit_bytes=VMEM_LIMIT
        ),
    )(second_low, dy, weights)


def angle_tables():
    lane = np.arange(128) % HEAD_DIM
    power = 10000.0 ** (-2.0 * (lane % (ROT // 2)) / ROT)
    frequency = np.where(lane < ROT, power, 0.0)
    tables = []
    for places in (np.arange(128), np.arange(32) * 128):
        angles = places[:, None] * frequency[None, :]
        tables.append(jnp.asarray(np.stack([np.cos(angles), np.sin(angles)]).astype(np.float32)))
    return tables


def body(
    inputs,
    cotangent,
    group_place,
    attend_gain,
    attend_shift,
    project_weight,
    project_bias,
    output_weight,
    mixer_gain,
    mixer_shift,
    gate_weight,
    up_weight,
    down_weight,
):
    shard_index = lax.axis_index("dp") * 16 + lax.axis_index("ctx")
    base, steps = angle_tables()

    vectors = jnp.stack([attend_gain, attend_shift, mixer_gain, mixer_shift])
    vectors = jnp.concatenate(
        [
            jnp.pad(vectors, ((0, 0), (0, 64))),
            jnp.pad(project_bias.reshape(1, 48), ((0, 0), (0, 80))),
            jnp.zeros((59, 128), BF),
        ]
    )
    front_shard = jnp.concatenate(
        [project_weight.reshape(64, 1536), output_weight.T, vectors], axis=1
    )
    back_shard = jnp.concatenate([gate_weight, up_weight, down_weight.T], axis=1)

    tokens = inputs.reshape(512, D)
    quarters = inputs.reshape(4, 128, D)
    front, gains, first_low, spread = front_forward(front_shard, tokens, group_place, base, steps)
    spread = spread.reshape(2, 16, 3, 256, 128)
    attended_heads, attended_full, logs = attend(group_place, spread)
    attended_low, hidden, second_low, back = middle_forward(
        attended_heads, front, quarters, gains, back_shard
    )

    second_low = second_low.reshape(512, D)
    dy = cotangent.reshape(512, D)
    branch, second_part, gate_grad, dup, mixed = feed_forward(second_low, dy, back)
    dhidden, mixer_vectors, output_grad, upstream, out_block, gate_grad, up_grad, down_grad = middle_backward(
        second_part.reshape(4, 128, D),
        dy,
        hidden,
        gains,
        attended_low,
        front,
        second_low,
        dup,
        mixed,
        branch.reshape(4, 128, D),
        gate_grad.reshape(4, 4, 64, UNITS),
    )

    dq, dkv = attend_back(group_place, spread, attended_full, logs, upstream, base, steps)
    dproject, outputs = collect_heads(dkv.reshape(2, 4, 4, 2, 256, 128), dq, out_block)
    input_grad, small, project_grad, output_grad = last_backward(
        dproject, first_low, front, quarters, dhidden, gains, mixer_vectors, output_grad.reshape(2, 4, 4, 64, 512)
    )
    own = lax.dynamic_slice(small, (0, shard_index * 64), (4, 64))
    bias_grad = lax.dynamic_slice(
        small[4, :1536].reshape(3, 8, 64), (0, 0, shard_index * 2), (3, 8, 2)
    )
    shape = inputs.shape
    return (
        outputs.reshape(shape),
        input_grad.reshape(shape),
        own[0],
        own[1],
        project_grad.reshape(64, 3, 512),
        bias_grad,
        output_grad.T,
        own[2],
        own[3],
        gate_grad,
        up_grad,
        down_grad.T,
    )


def solution(mesh):
    weight = ("dp", "ctx")
    rows = P(None, "dp", "ctx", None)
    vector = P(weight)
    matrix = P(weight, "tensor")
    turned = P("tensor", weight)
    project = P(weight, None, "tensor")
    bias = P(None, "tensor", weight)
    params = (vector, vector, project, bias, turned, vector, vector, matrix, matrix, turned)
    return jax.shard_map(
        body,
        mesh=mesh,
        in_specs=(rows, rows, P()) + params,
        out_specs=(rows, rows) + params,
        check_vma=False,
    )
```

```python
import functools

import jax
import jax.numpy as jnp
import numpy as np
from jax import lax
from jax.experimental import pallas as pl
from jax.experimental.pallas import tpu as pltpu
from jax.sharding import PartitionSpec as P

MESH = pl.DeviceIdType.MESH
D = 2048
UNITS = 1408
HEAD_DIM = 64
ROT = 16
EPSILON = 1e-05
LOG2E = 1.4426950408889634
LOW = -1e30
TILE = 512
ROWS = 64
AT_ONCE = 34
VMEM_LIMIT = 58 * 2**20
STEPS = (1, 3, 2)
BF = jnp.bfloat16
F32 = jnp.float32


def here():
    ctx = lax.axis_index("ctx")
    return (lax.axis_index("dp"), ctx // 4, lax.rem(ctx, 4), lax.axis_index("tensor"))


def at(c, y, z, x):
    return (c, lax.rem(y, 4) * 4 + lax.rem(z, 4), lax.rem(x, 4))


def up(i, d):
    return lax.rem(i + d, 4)


def down(i, d):
    return lax.rem(i + 4 - d, 4)


class Net:
    def __init__(self, send_sems, recv_sems):
        self.send_sems, self.recv_sems = send_sems, recv_sems
        self.sent, self.gone = [], set()

    def send(self, src, dst, device):
        n = len(self.sent)
        copy = pltpu.make_async_remote_copy(
            src_ref=src,
            dst_ref=dst,
            send_sem=self.send_sems.at[n],
            recv_sem=self.recv_sems.at[n],
            device_id=device,
            device_id_type=MESH,
        )
        copy.start()
        self.sent.append(copy)
        return copy

    def finish(self):
        for n, copy in enumerate(self.sent):
            if n not in self.gone:
                copy.wait_send()

    def wait_sent(self, copy):
        copy.wait_send()
        self.gone.add([other is copy for other in self.sent].index(True))


class Local:
    def __init__(self, sems):
        self.sems, self.n = sems, 0

    def copy(self, src, dst):
        copy = pltpu.make_async_copy(src, dst, self.sems.at[self.n])
        copy.start()
        self.n += 1
        return copy


def greet(peers):
    barrier = pltpu.get_barrier_semaphore()
    for peer in peers:
        pl.semaphore_signal(barrier, inc=1, device_id=peer, device_id_type=MESH)
    pl.semaphore_wait(barrier, len(peers))


def y_peers(c, y, z, x):
    return [at(c, y + d, z, x) for d in (1, 2, 3)]


def z_peers(c, y, z, x):
    return [at(c, y, z + d, x) for d in (1, 2, 3)]


def x_peers(c, y, z, x):
    return [at(c, y, z, x + d) for d in (1, 2, 3)]


def core_peer(c, y, z, x):
    return [at(1 - c, y, z, x)]


class RingSum:
    def __init__(self, net, device, mine, spare, add):
        self.net, self.device, self.mine, self.spare, self.add = net, device, mine, spare, add

    def start(self):
        self.start_far()
        self.start_near()

    def start_far(self):
        send, mine, spare = self.net.send, self.mine, self.spare
        ahead, back = self.device(1), self.device(3)
        self.far_ahead = send(mine(2, 0), spare.at[0], ahead)
        self.far_back = send(mine(2, 1), spare.at[1], back)

    def start_near(self):
        send, mine, spare = self.net.send, self.mine, self.spare
        ahead, back = self.device(1), self.device(3)
        self.near = [send(mine(1, 1), spare.at[3], ahead), send(mine(3, 0), spare.at[2], back)]

    def middle(self):
        send, spare = self.net.send, self.spare
        self.far_ahead.wait_recv()
        self.add(spare.at[0], self.mine(1, 0))
        self.near.append(send(spare.at[0], spare.at[4], self.device(1)))
        self.far_back.wait_recv()
        self.add(spare.at[1], self.mine(3, 1))
        self.near.append(send(spare.at[1], spare.at[5], self.device(3)))

    def arrive(self):
        for copy in self.near:
            copy.wait_recv()

    def sent(self):
        for copy in [self.far_ahead, self.far_back] + self.near:
            self.net.wait_sent(copy)

    def terms(self, half):
        return [self.spare.at[4 if half == 0 else 3], self.spare.at[2 if half == 0 else 5]]


RING_SUM = 6


class RingGather:
    def __init__(self, net, device, out):
        self.net, self.device, self.out = net, device, out

    def start(self, block):
        self.ahead = self.net.send(block, self.out(0), self.device(1))
        self.back = self.net.send(block, self.out(0), self.device(3))

    def from_back(self):
        self.ahead.wait_recv()
        piece = self.out(3, 0)
        self.far_ahead = self.net.send(piece, piece, self.device(1))

    def from_ahead(self):
        self.back.wait_recv()
        piece = self.out(1, 1)
        self.far_back = self.net.send(piece, piece, self.device(3))

    def arrive(self):
        self.far_ahead.wait_recv()
        self.far_back.wait_recv()


RING_GATHER = 4


class Gather:
    def __init__(self, net, local, src, place, me):
        self.net, self.local, self.src, self.place, self.me = net, local, src, place, me
        self.core = []
        c, y, z, x = me
        along_y = lambda d: at(c, y + d, z, x)
        along_z = lambda d: at(c, y, z + d, x)

        def spot(far_y, far_z, first, half):
            if half is None:
                return place(c, up(y, far_y), up(z, far_z), first, 32)
            return place(c, up(y, far_y), up(z, far_z), first + 16 * half, 16)

        self.one = (
            RingGather(net, along_y, lambda d, half=None: spot(d, 0, 0, half)),
            RingGather(net, along_z, lambda d, half=None: spot(0, d, 32, half)),
        )
        self.two = {}
        for k in range(4):
            self.two[0, k] = RingGather(net, along_z, lambda d, half=None, k=k: spot(k, d, 0, half))
            self.two[1, k] = RingGather(net, along_y, lambda d, half=None, k=k: spot(d, k, 32, half))

    def hand_over(self, piece):
        c, y, z, x = self.me
        self.core.append(self.net.send(piece, piece, at(1 - c, y, z, x)))

    def start(self):
        c, y, z, x = self.me
        src, own = self.src, self.place(c, y, z, 0, 64)
        self.own = self.local.copy(src, own)
        halves = (src.at[pl.ds(0, 32)], src.at[pl.ds(32, 32)])
        for way in range(2):
            self.one[way].start(halves[way])
        for way in range(2):
            self.two[way, 0].start(halves[way])
        self.core.append(self.net.send(src, own, at(1 - c, y, z, x)))

    def near(self):
        for way in range(2):
            self.one[way].from_back()
            self.two[way, 3].start(self.one[way].out(3))
        for way in range(2):
            self.one[way].from_ahead()
            self.two[way, 1].start(self.one[way].out(1))
        for k in (3, 1):
            for way in range(2):
                self.hand_over(self.one[way].out(k))

    def middle(self):
        self.pass_on(0)
        for way in range(2):
            self.one[way].arrive()
            self.two[way, 2].start(self.one[way].out(2))
            self.hand_over(self.one[way].out(2))

    def pass_on(self, k):
        for way in range(2):
            self.two[way, k].from_back()
            self.two[way, k].from_ahead()
            self.hand_over(self.two[way, k].out(3))
            self.hand_over(self.two[way, k].out(1))

    def far(self):
        for k in (0, 3, 1, 2):
            for way in range(2):
                self.two[way, k].arrive()
                self.hand_over(self.two[way, k].out(2))

    def finish(self):
        for copy in self.core:
            copy.wait_recv()
        self.own.wait()


def flat_rows(ref):
    def place(c, y, z, first, count):
        return ref.at[pl.ds(pl.multiple_of(((c * 4 + y) * 4 + z) * 64 + first, 16), count)]

    return place


GATHER_COPIES = 10 * RING_GATHER + 31


def scatter_scratch(width):
    return [
        pltpu.VMEM((4, 4, 64, width), BF),
        pltpu.VMEM((4, 4, 64, width), BF),
        pltpu.VMEM((6, 4, 16, width), BF),
        pltpu.VMEM((6, 4, 16, width), BF),
        pltpu.VMEM((4, 32, width), BF),
        pltpu.VMEM((4, 32, width), BF),
        pltpu.VMEM((6, 16, width), BF),
        pltpu.VMEM((6, 16, width), BF),
    ]


SCATTER_COPIES = 1 + 4 * RING_SUM


def add_blocks(total, term):
    if len(total.shape) == 2:
        total[...] += term[...]
        return

    def one(i, carry):
        total[i] += term[i]
        return carry

    lax.fori_loop(0, total.shape[0], one, 0)


class Scatter:
    def __init__(self, net, local, grads, out, scratch, me):
        self.net, self.local, self.grads, self.out, self.me = net, local, grads, out, me
        (held, self.other, one_a, one_b, self.sum_a, self.sum_b, two_a, two_b) = scratch
        self.held = held
        c, y, z, x = me
        along_y = lambda d: at(c, y + d, z, x)
        along_z = lambda d: at(c, y, z + d, x)
        self.one_a = RingSum(
            net, along_z, lambda d, half: held.at[:, up(z, d), pl.ds(16 * half, 16)], one_a, add_blocks
        )
        self.one_b = RingSum(
            net, along_y, lambda d, half: held.at[up(y, d), :, pl.ds(32 + 16 * half, 16)], one_b, add_blocks
        )
        self.two_a = RingSum(
            net, along_y, lambda d, half: self.sum_a.at[up(y, d), pl.ds(16 * half, 16)], two_a, add_blocks
        )
        self.two_b = RingSum(
            net, along_z, lambda d, half: self.sum_b.at[up(z, d), pl.ds(16 * half, 16)], two_b, add_blocks
        )

    def start(self):
        c, y, z, x = self.me
        self.own = self.local.copy(self.grads.at[c], self.held)
        self.zero = self.net.send(self.grads.at[1 - c], self.other, at(1 - c, y, z, x))

    def send_filled(self, block):
        c, y, z, x = self.me
        self.own = None
        self.zero = self.net.send(block, self.other, at(1 - c, y, z, x))

    def first(self):
        if self.own is not None:
            self.own.wait()
        self.zero.wait_recv()
        held, other = self.held, self.other

        def add(i, carry):
            held[i // 4, lax.rem(i, 4)] += other[i // 4, lax.rem(i, 4)]
            return carry

        lax.fori_loop(0, 16, add, 0)
        self.one_a.start()
        self.one_b.start()

    def first_middle(self):
        self.one_a.middle()
        self.one_b.middle()

    def second(self):
        for one, two, total in ((self.one_a, self.two_a, self.sum_a), (self.one_b, self.two_b, self.sum_b)):
            one.arrive()
            for half in range(2):
                own, terms = one.mine(0, half), one.terms(half)

                def add(i, carry, half=half, own=own, terms=terms, total=total):
                    value = own[i].astype(F32)
                    for term in terms:
                        value += term[i].astype(F32)
                    total[i, pl.ds(16 * half, 16), :] = value.astype(BF)
                    return carry

                lax.fori_loop(0, 4, add, 0)
            two.start()

    def second_middle(self):
        self.two_a.middle()
        self.two_b.middle()

    def third(self):
        for first, two in ((0, self.two_a), (32, self.two_b)):
            two.arrive()
            for half in range(2):
                value = two.mine(0, half)[...].astype(F32)
                for term in two.terms(half):
                    value += term[...].astype(F32)
                self.out[pl.ds(first + 16 * half, 16), :] = value


def quarters_of(net, out, me):
    c, y, z, x = me

    def piece(d, half=None):
        return out.at[up(x, d)] if half is None else out.at[up(x, d), pl.ds(64 * half, 64)]

    return RingGather(net, lambda d: at(c, y, z, x + d), piece)


class SumX:
    def __init__(self, net, local, parts, held, spare, me):
        c, y, z, x = me
        self.local, self.parts, self.held, self.x, self.net, self.me = local, parts, held, x, net, me
        self.along = lambda d: at(c, y, z, x + d)
        self.ring = RingSum(
            net, self.along, lambda d, half: held.at[up(x, d), pl.ds(64 * half, 64)], spare, self.add
        )

    def add(self, total, term):
        def one(i, carry):
            rows = pl.ds(pl.multiple_of(i * 16, 16), 16)
            total[rows, :] += term[rows, :]
            return carry

        lax.fori_loop(0, 4, one, 0)

    def load(self):
        self.loads = [self.local.copy(self.parts.at[up(self.x, d)], self.held.at[up(self.x, d)]) for d in (2, 1, 3, 0)]

    def start(self):
        for copy in self.loads:
            copy.wait()
        self.ring.start()

    def start_held(self):
        self.ring.start()

    def middle(self):
        self.ring.middle()

    def totals(self, step):
        self.ring.arrive()
        for half in range(2):
            terms = self.ring.terms(half)

            def loop(i, carry, half=half, terms=terms):
                rows = pl.ds(pl.multiple_of(i * 32, 32), 32)
                own = pl.ds(pl.multiple_of(64 * half + i * 32, 32), 32)
                value = self.held[self.x, own, :].astype(F32)
                for term in terms:
                    value += term[rows, :].astype(F32)
                step(own, value)
                return carry

            lax.fori_loop(0, 2, loop, 0)

    def gather(self, block, out):
        x = self.x
        self.back = quarters_of(self.net, out, self.me)
        self.mine = self.local.copy(block, out.at[x])
        self.back.start(block)

    def gather_middle(self):
        self.back.from_back()
        self.back.from_ahead()

    def finish(self):
        self.mine.wait()
        self.back.arrive()


SUM_COPIES = RING_SUM + RING_GATHER
SUM_LOCALS = 5


def sum_scratch():
    return [pltpu.VMEM((4, 128, D), BF), pltpu.VMEM((6, 64, D), BF)]


def normed(values):
    centre = jnp.mean(values, axis=-1, keepdims=True)
    spread = values - centre
    inverse = lax.rsqrt(jnp.mean(spread * spread, axis=-1, keepdims=True) + EPSILON)
    return spread * inverse, inverse


def norm_pullback(upstream, norm, inverse, gain):
    scaled = upstream * gain
    first = jnp.mean(scaled, axis=-1, keepdims=True)
    second = jnp.mean(scaled * norm, axis=-1, keepdims=True)
    return inverse * (scaled - first - norm * second)


ANY = pl.BlockSpec(memory_space=pl.ANY)
IN_VMEM = pl.BlockSpec(memory_space=pltpu.VMEM)
IN_SMEM = pl.BlockSpec(memory_space=pltpu.SMEM)


def remote_call(body, name, cid, ins, outs, scratch, copies, locals_):
    return pl.pallas_call(
        body,
        name=name,
        in_specs=ins,
        out_specs=[spec for _, _, spec in outs],
        out_shape=[jax.ShapeDtypeStruct(shape, dtype) for shape, dtype, _ in outs],
        scratch_shapes=scratch
        + [
            pltpu.SemaphoreType.DMA((copies,)),
            pltpu.SemaphoreType.DMA((copies,)),
            pltpu.SemaphoreType.DMA((locals_,)),
        ],
        compiler_params=pltpu.CompilerParams(
            collective_id=cid, has_side_effects=True, vmem_limit_bytes=VMEM_LIMIT
        ),
    )


def assemble_vectors(weights, gains, bias, spots):
    for s in range(32):
        block = weights[s * 64 : s * 64 + 16, 2048:2176].astype(F32)
        gains[0:4, s * 64 : s * 64 + 64] = block[0:4, :64]
        spots[s : s + 1, :] = block[4:5, :]
    values = spots[...].astype(BF)
    head = lax.broadcasted_iota(jnp.int32, (32, 128), 0)
    held = lax.broadcasted_iota(jnp.int32, (32, 128), 1)
    shard = lax.broadcasted_iota(jnp.int32, (32, 64), 0)
    lane = lax.broadcasted_iota(jnp.int32, (32, 64), 1)
    total = jnp.zeros((32, 64), F32)
    for e in range(2):
        pick = jnp.where((held == 2 * head + e) & (head < 24), 1.0, 0.0).astype(BF)
        spread = jnp.where(lane == 2 * shard + e, 1.0, 0.0).astype(BF)
        total += jnp.dot(nt(pick, values).astype(BF), spread, preferred_element_type=F32)
    for n in range(24):
        bias[0:1, n * 64 : n * 64 + 64] = total[n : n + 1]


def front_forward(shard, tokens, group_place, base, steps):
    def kernel(
        src, x_ref, group_ref, base_ref, steps_ref, front, gains, low, out,
        weights, norm, blocks, bias, spots, turns, ss, rs, ls,
    ):
        me = here()
        c, y, z, x = me
        net, local = Net(ss, rs), Local(ls)
        greet(y_peers(*me) + z_peers(*me) + core_peer(*me))
        gather = Gather(net, local, src, flat_rows(weights), me)
        gather.start()
        for n in range(2):
            rows = slice(n * 128, n * 128 + 128)
            cosine, sine = turn_tables(base_ref, steps_ref, group_ref[(y * 4 + z) * 2 + n])
            turns[0, rows, :] = cosine
            turns[1, rows, :] = sine

        def centre(i, carry):
            rows = pl.ds(pl.multiple_of(i * 32, 32), 32)
            norm[rows, :] = normed(x_ref[rows, :].astype(F32))[0]
            return carry

        lax.fori_loop(0, 4, centre, 0)
        gather.near()
        lax.fori_loop(4, 8, centre, 0)
        gather.middle()
        lax.fori_loop(8, 16, centre, 0)
        for k in (3, 1, 2):
            gather.pass_on(k)
        gather.far()
        gather.finish()
        keep = local.copy(weights, front)
        assemble_vectors(weights, gains, bias, spots)

        def scale(i, carry):
            rows = pl.ds(pl.multiple_of(i * 32, 32), 32)
            low[rows, :] = (norm[rows, :] * gains[0:1, :] + gains[1:2, :]).astype(BF)
            return carry

        lax.fori_loop(0, 16, scale, 0)

        def project(t):
            columns = slice(t * 512, t * 512 + 512)
            for m in range(2):
                acc = jnp.dot(low[m * 256 : m * 256 + 256, :], weights[:, columns], preferred_element_type=F32)
                acc = acc + bias[:, columns]
                for h in range(4):
                    part = acc[:, h * 128 : h * 128 + 128]
                    if t < 2:
                        part = turn(part, turns[0], turns[1])
                    blocks[m, h, (t + 2) % 3] = part.astype(BF)

        along_y = lambda d: at(c, y + d, z, x)
        along_z = lambda d: at(c, y, z + d, x)
        kv = pl.ds(0, 2)

        def part(half):
            return kv if half is None else half

        rings = {}
        for k in range(4):
            rings[0, k] = RingGather(
                net, along_y, lambda d, half=None, k=k: out.at[0, up(y, d), up(z, k), part(half)]
            )
            rings[1, k] = RingGather(
                net, along_z, lambda d, half=None, k=k: out.at[1, up(y, k), up(z, d), part(half)]
            )
        project(1)
        project(2)
        first = {}
        for d in STEPS:
            first[0, d] = net.send(blocks.at[0, up(z, d), kv], out.at[0, y, z, kv], along_z(d))
            first[1, d] = net.send(blocks.at[1, up(y, d), kv], out.at[1, y, z, kv], along_y(d))
        rings[0, 0].start(blocks.at[0, z, kv])
        rings[1, 0].start(blocks.at[1, y, kv])
        project(0)
        last = []
        for d in STEPS:
            last.append(net.send(blocks.at[0, up(z, d), 2], out.at[0, y, z, 2], along_z(d)))
            last.append(net.send(blocks.at[1, up(y, d), 2], out.at[1, y, z, 2], along_y(d)))
        owns = [local.copy(blocks.at[0, z], out.at[0, y, z]), local.copy(blocks.at[1, y], out.at[1, y, z])]
        for d in STEPS:
            for m in range(2):
                first[m, d].wait_recv()
                ring = rings[m, 4 - d]
                ring.start(ring.out(0))
        for k in (0, 3, 1, 2):
            for m in range(2):
                rings[m, k].from_back()
                rings[m, k].from_ahead()
        for ring in rings.values():
            ring.arrive()
        for copy in last:
            copy.wait_recv()
        for copy in owns:
            copy.wait()
        keep.wait()
        net.finish()

    width = shard.shape[1]
    return remote_call(
        kernel,
        "front_forward",
        0,
        [ANY, IN_VMEM, IN_SMEM, IN_VMEM, IN_VMEM],
        [
            ((D, width), BF, ANY),
            ((4, D), F32, IN_VMEM),
            ((512, D), BF, IN_VMEM),
            ((2, 4, 4, 3, 256, 128), BF, ANY),
        ],
        [
            pltpu.VMEM((D, width), BF),
            pltpu.VMEM((512, D), F32),
            pltpu.VMEM((2, 4, 3, 256, 128), BF),
            pltpu.VMEM((1, 1536), F32),
            pltpu.VMEM((32, 128), F32),
            pltpu.VMEM((2, 256, 128), F32),
        ],
        GATHER_COPIES + 12 + 8 * RING_GATHER,
        4,
    )(shard, tokens, group_place, base, steps)


class Swap:
    def __init__(self, net, local, src, out, me):
        c, y, z, x = me
        self.owns = [local.copy(src.at[0, z], out.at[0, z]), local.copy(src.at[1, y], out.at[1, y])]
        self.copies = []
        for d in STEPS:
            self.copies.append(net.send(src.at[0, up(z, d)], out.at[0, z], at(c, y, z + d, x)))
            self.copies.append(net.send(src.at[1, up(y, d)], out.at[1, y], at(c, y + d, z, x)))

    def arrive(self):
        for copy in self.copies:
            copy.wait_recv()
        for copy in self.owns:
            copy.wait()


SWAP_COPIES, SWAP_LOCALS = 6, 2
TURNED = pl.ds(1536, 512)


def middle_forward(heads, front, inputs, gains, shard):
    width = shard.shape[1]

    def kernel(
        heads, front, inputs, gains, shard, attended, hidden, second, weights,
        swapped, out_w, held, spare, base, low, ss, rs, ls,
    ):
        me = here()
        c, y, z, x = me
        net, local = Net(ss, rs), Local(ls)
        sums = SumX(net, local, None, held, spare, me)
        load = local.copy(front.at[:, TURNED], out_w)
        residual = local.copy(inputs.at[x], base)
        greet(y_peers(*me) + z_peers(*me) + core_peer(*me) + x_peers(*me))
        swap = Swap(net, local, heads, swapped, me)
        gather = Gather(net, local, shard, flat_rows(weights), me)
        gather.start()
        load.wait()
        swap.arrive()
        for m in range(2):
            for h in range(4):
                attended[m * 256 : m * 256 + 256, h * 128 : h * 128 + 128] = swapped[m, h]
        for q in range(4):
            held[q] = nt(attended[q * 128 : q * 128 + 128, :], out_w[...]).astype(BF)
        sums.start_held()
        gather.near()
        sums.middle()
        gather.middle()
        gather.pass_on(3)
        residual.wait()

        def step(rows, total):
            value = base[rows, :].astype(F32) + total
            hidden[rows, :] = value
            norm, _ = normed(value)
            low[rows, :] = (norm * gains[2:3, :] + gains[3:4, :]).astype(BF)

        sums.totals(step)
        sums.gather(low, second)
        gather.pass_on(1)
        gather.pass_on(2)
        sums.gather_middle()
        gather.far()
        gather.finish()
        sums.finish()
        net.finish()

    return remote_call(
        kernel,
        "middle_forward",
        3,
        [ANY, ANY, ANY, IN_VMEM, ANY],
        [
            ((512, 512), BF, IN_VMEM),
            ((128, D), F32, IN_VMEM),
            ((4, 128, D), BF, ANY),
            ((D, width), BF, ANY),
        ],
        [pltpu.VMEM((2, 4, 256, 128), BF), pltpu.VMEM((D, 512), BF)]
        + sum_scratch()
        + [pltpu.VMEM((128, D), BF), pltpu.VMEM((128, D), BF)],
        SWAP_COPIES + GATHER_COPIES + SUM_COPIES,
        SWAP_LOCALS + SUM_LOCALS + 3,
    )(heads, front, inputs, gains, shard)


def other_half(c, k, size):
    core = 1 - c if k < 2 else c
    return pl.ds(pl.multiple_of(core * 1024 + (k % 2) * size, size), size)


def shard_block(k):
    return pl.ds((k % 2) * 2, 2)


def middle_backward(parts, cotangent, hidden, gains, attended, front, second_low, dup, mixed, branch, gate_grad):
    def kernel(
        parts, cotangent, hidden, gains, attended, front, second_low, dup, mixed, branch, gate_grad,
        dhidden, vectors, output_grad, upstream, out_block, gate_out, up_out, down_out,
        held, spare, low, hidden_low, out_w, blocks, lows, dys, extra, *rest,
    ):
        scratch, (ss, rs, ls) = rest[:-3], rest[-3:]
        me = here()
        c, y, z, x = me
        net, local = Net(ss, rs), Local(ls)
        sums = SumX(net, local, parts, held, spare, me)
        sums.load()
        loads = [local.copy(second_low, lows), local.copy(cotangent, dys)]
        load = local.copy(front.at[:, TURNED], out_w)
        greet(y_peers(*me) + z_peers(*me) + core_peer(*me) + x_peers(*me))
        gate, up_, down_ = [
            Scatter(net, local, grads, out, scratch[8 * k : 8 * k + 8], me)
            for k, (grads, out) in enumerate(((gate_grad, gate_out), (None, up_out), (None, down_out)))
        ]
        gate.start()
        sums.start()

        def multiply(left, right, k, to):
            value = tn(left[:, other_half(c, k, 512)], right[...]).astype(BF)
            to[shard_block(k)] = value.reshape(2, 4, 64, UNITS)

        loads[0].wait()
        for k in range(2):
            multiply(lows, dup, k, down_.held)
        up_.send_filled(down_.held)
        gate.first()
        sums.middle()
        for k in range(2, 4):
            multiply(lows, dup, k, up_.held)
        loads[1].wait()
        for k in range(2):
            multiply(dys, mixed, k, extra)
        down_.send_filled(extra)
        up_.first()
        net.wait_sent(up_.zero)
        gate.first_middle()
        vectors[...] = jnp.zeros_like(vectors)

        def step(rows, dsecond):
            norm, inverse = normed(hidden[rows, :])
            upper = dys[pl.ds(pl.multiple_of(x * 128 + rows.start, 32), 32), :].astype(F32)
            value = upper + norm_pullback(dsecond, norm, inverse, gains[2:3, :])
            dhidden[rows, :] = value
            low[rows, :] = value.astype(BF)
            vectors[0:1, :] += jnp.sum(dsecond * norm, axis=0, keepdims=True)
            vectors[1:2, :] += jnp.sum(dsecond, axis=0, keepdims=True)

        sums.totals(step)
        sums.ring.sent()
        sums.gather(low, hidden_low)
        for k in range(2, 4):
            multiply(dys, mixed, k, down_.held)
        down_.first()
        up_.first_middle()
        gate.second()
        sums.gather_middle()
        late = SumX(net, local, branch, held, spare, me)
        late.load()
        late.start()
        down_.first_middle()
        up_.second()
        load.wait()
        sums.finish()
        for q in range(4):
            rows = slice((q % 2) * 128, (q % 2) * 128 + 128)
            result = jnp.dot(hidden_low[q], out_w[...], preferred_element_type=F32).astype(BF)
            for h in range(4):
                blocks[q // 2, h, rows, :] = result[:, h * 128 : h * 128 + 128]
        swap = Swap(net, local, blocks, upstream, me)
        late.middle()
        gate.second_middle()
        down_.second()
        whole = hidden_low[...].reshape(512, D)
        output_grad[...] = tn(whole, attended[...]).astype(BF)
        up_.second_middle()
        gate.third()
        down_.second_middle()

        def last(rows, total):
            out_block[rows, :] = (hidden[rows, :] + total).astype(BF)

        late.totals(last)
        up_.third()
        down_.third()
        swap.arrive()
        net.finish()

    scratch = sum_scratch() + [
        pltpu.VMEM((128, D), BF),
        pltpu.VMEM((4, 128, D), BF),
        pltpu.VMEM((D, 512), BF),
        pltpu.VMEM((2, 4, 256, 128), BF),
        pltpu.VMEM((512, D), BF),
        pltpu.VMEM((512, D), BF),
        pltpu.VMEM((4, 4, 64, UNITS), BF),
    ]
    return remote_call(
        kernel,
        "middle_backward",
        4,
        [ANY, ANY, IN_VMEM, IN_VMEM, IN_VMEM, ANY, ANY, IN_VMEM, IN_VMEM, ANY, ANY],
        [
            ((128, D), F32, IN_VMEM),
            ((2, D), F32, IN_VMEM),
            ((D, 512), BF, IN_VMEM),
            ((2, 4, 256, 128), BF, ANY),
            ((128, D), BF, IN_VMEM),
        ]
        + [((64, UNITS), F32, IN_VMEM)] * 3,
        scratch + scatter_scratch(UNITS) * 3,
        SUM_COPIES + RING_SUM + SCATTER_COPIES * 3 + SWAP_COPIES,
        SUM_LOCALS + 4 + SWAP_LOCALS + 3 + 1,
    )(parts, cotangent, hidden, gains, attended, front, second_low, dup, mixed, branch, gate_grad)


def collect_heads(dkv, dq, block):
    def kernel(dkv, dq, block, dproject, outputs, mine, got, summed, ss, rs, ls):
        me = here()
        c, y, z, x = me
        net, local = Net(ss, rs), Local(ls)
        order = (1, 3, 2, 0)
        loads = [local.copy(dkv.at[m], mine.at[m]) for m in range(2)]
        greet(y_peers(*me) + z_peers(*me) + x_peers(*me))
        kv = pl.ds(0, 2)
        along_y = lambda d: at(c, y + d, z, x)
        along_z = lambda d: at(c, y, z + d, x)

        def add(total, term):
            def one(i, carry):
                rows = pl.ds(pl.multiple_of(i * 64, 64), 64)
                total[rows, :] += term[rows, :]
                return carry

            lax.fori_loop(0, 4, one, 0)

        rings = {}
        for k in order:
            rings[0, k] = RingSum(
                net, along_y, lambda d, half, k=k: mine.at[0, up(y, d), up(z, k), half], got.at[0, k], add
            )
            rings[1, k] = RingSum(
                net, along_z, lambda d, half, k=k: mine.at[1, up(y, k), up(z, d), half], got.at[1, k], add
            )
        whole = quarters_of(net, outputs, me)
        own = local.copy(block, outputs.at[x])
        whole.start(block)
        for copy in loads:
            copy.wait()
        for ring in rings.values():
            ring.start()
        lates = [
            local.copy(dq.at[0, z], dproject.at[0, z, 2]),
            local.copy(dq.at[1, y], dproject.at[1, y, 2]),
        ]
        two = []
        for d in STEPS:
            two.append(net.send(dq.at[0, up(z, d)], dproject.at[0, z, 2], along_z(d)))
            two.append(net.send(dq.at[1, up(y, d)], dproject.at[1, y, 2], along_y(d)))
        for ring in rings.values():
            ring.middle()
        for k in order:
            for m, spot in ((0, z), (1, y)):
                ring = rings[m, k]
                ring.arrive()
                for half in range(2):
                    kept, terms = ring.mine(0, half), ring.terms(half)

                    def total(i, carry, m=m, k=k, half=half, kept=kept, terms=terms):
                        rows = pl.ds(pl.multiple_of(i * 64, 64), 64)
                        value = kept[rows, :].astype(F32)
                        for term in terms:
                            value += term[rows, :].astype(F32)
                        summed[m, k, half, rows, :] = value.astype(BF)
                        return carry

                    lax.fori_loop(0, 4, total, 0)
            if k:
                two.append(net.send(summed.at[0, k], dproject.at[0, z, kv], along_z(k)))
                two.append(net.send(summed.at[1, k], dproject.at[1, y, kv], along_y(k)))
            else:
                lates.append(local.copy(summed.at[0, 0], dproject.at[0, z, kv]))
                lates.append(local.copy(summed.at[1, 0], dproject.at[1, y, kv]))

        whole.from_back()
        whole.from_ahead()
        for copy in two:
            copy.wait_recv()
        for copy in lates:
            copy.wait()
        own.wait()
        whole.arrive()
        net.finish()

    return remote_call(
        kernel,
        "collect_heads",
        6,
        [ANY, ANY, IN_VMEM],
        [((2, 4, 3, 256, 128), BF, ANY), ((4, 128, D), BF, ANY)],
        [
            pltpu.VMEM((2, 4, 4, 2, 256, 128), BF),
            pltpu.VMEM((2, 4, 6, 256, 128), BF),
            pltpu.VMEM((2, 4, 2, 256, 128), BF),
        ],
        8 * RING_SUM + 6 + 6 + RING_GATHER,
        2 + 4 + 1,
    )(dkv, dq, block)


def last_backward(dproject, first_low, front, inputs, dhidden, gains, mixer_vectors, output_grad):
    def kernel(
        dproject, first_low, front, inputs, dhidden, gains, mixer_vectors, output_grad,
        input_grad, sums_out, project_out, output_out,
        wide, weights, lows, held, spare, base, low, extra, small, got, *rest,
    ):
        scratch, (ss, rs, ls) = rest[:-3], rest[-3:]
        me = here()
        c, y, z, x = me
        net, local = Net(ss, rs), Local(ls)
        load = local.copy(front.at[:, pl.ds(0, 1536)], weights)
        load_low = local.copy(first_low, lows)
        residual = local.copy(inputs.at[x], base)
        greet(y_peers(*me) + z_peers(*me) + core_peer(*me) + x_peers(*me))
        project = Scatter(net, local, None, project_out, scratch[:8], me)
        output = Scatter(net, local, output_grad, output_out, scratch[8:], me)
        output.start()
        sums = SumX(net, local, None, held, spare, me)
        for m in range(2):
            for t in range(3):
                for h in range(4):
                    to = t * 512 + h * 128
                    wide[m * 256 : m * 256 + 256, to : to + 128] = dproject[m, h, (t + 2) % 3]
        load.wait()

        def quarter(d):
            q = up(x, d)
            rows = wide[pl.ds(pl.multiple_of(q * 128, 128), 128), :]
            held[q] = nt(rows, weights[...]).astype(BF)

        quarter(2)
        sums.ring.start_far()
        quarter(1)
        quarter(3)
        sums.ring.start_near()

        def multiply(k, to):
            value = tn(lows[:, other_half(c, k, 512)], wide[...]).astype(BF)
            to[shard_block(k)] = value.reshape(2, 4, 64, 1536)

        load_low.wait()
        for k in range(2):
            multiply(k, extra)
        project.send_filled(extra)
        sums.middle()
        quarter(0)
        for k in range(2, 4):
            multiply(k, project.held)
        output.first()
        small[0, ...] = jnp.zeros_like(small[0])
        small[0, 2:4, :] = mixer_vectors[...]
        small[0, 4:5, 0:1536] = jnp.sum(wide[...].astype(F32), axis=0, keepdims=True)
        project.first()
        residual.wait()

        def step(rows, dfirst):
            norm, inverse = normed(base[rows, :].astype(F32))
            value = dhidden[rows, :] + norm_pullback(dfirst, norm, inverse, gains[0:1, :])
            low[rows, :] = value.astype(BF)
            small[0, 0:1, :] += jnp.sum(dfirst * norm, axis=0, keepdims=True)
            small[0, 1:2, :] += jnp.sum(dfirst, axis=0, keepdims=True)

        sums.totals(step)
        copies = [net.send(small.at[0], got.at[0, d - 1], at(c, y, z, x + d)) for d in STEPS]
        sums.gather(low, input_grad)
        output.first_middle()
        project.first_middle()
        for copy in copies:
            copy.wait_recv()
        small[1, ...] = small[0, ...]
        for n in range(3):
            small[1, 0:4, :] += got[0, n, 0:4, :]
        copies = [net.send(small.at[1], got.at[1, d - 1], at(c, y + d, z, x)) for d in STEPS]
        sums.gather_middle()
        output.second()
        project.second()
        for copy in copies:
            copy.wait_recv()
        small[2, ...] = small[1, ...] + got[1, 0] + got[1, 1] + got[1, 2]
        copies = [net.send(small.at[2], got.at[2, d - 1], at(c, y, z + d, x)) for d in STEPS]
        output.second_middle()
        project.second_middle()
        for copy in copies:
            copy.wait_recv()
        small[3, ...] = small[2, ...] + got[2, 0] + got[2, 1] + got[2, 2]
        copy = net.send(small.at[3], got.at[3, 0], at(1 - c, y, z, x))
        output.third()
        project.third()
        copy.wait_recv()
        sums_out[...] = small[3, ...] + got[3, 0]
        sums.finish()
        net.finish()

    scratch = (
        [pltpu.VMEM((512, 1536), BF), pltpu.VMEM((D, 1536), BF), pltpu.VMEM((512, D), BF)]
        + sum_scratch()
        + [
            pltpu.VMEM((128, D), BF),
            pltpu.VMEM((128, D), BF),
            pltpu.VMEM((4, 4, 64, 1536), BF),
            pltpu.VMEM((4, 8, D), F32),
            pltpu.VMEM((4, 3, 8, D), F32),
        ]
    )
    return remote_call(
        kernel,
        "last_backward",
        7,
        [IN_VMEM, ANY, ANY, ANY, IN_VMEM, IN_VMEM, IN_VMEM, ANY],
        [
            ((4, 128, D), BF, ANY),
            ((8, D), F32, IN_VMEM),
            ((64, 1536), F32, IN_VMEM),
            ((64, 512), F32, IN_VMEM),
        ],
        scratch + scatter_scratch(1536) + scatter_scratch(512),
        SUM_COPIES + 10 + SCATTER_COPIES * 2,
        SUM_LOCALS + 4,
    )(dproject, first_low, front, inputs, dhidden, gains, mixer_vectors, output_grad)


def turn(values, cosine, sine):
    lane = lax.broadcasted_iota(jnp.int32, values.shape, 1) & (HEAD_DIM - 1)
    swapped = jnp.where(lane < ROT // 2, -pltpu.roll(values, 120, 1), pltpu.roll(values, 8, 1))
    return values * cosine + swapped * sine


def turn_tables(base, steps, block):
    cosine, sine = base[0], base[1]
    far_cosine, far_sine = steps[0, pl.ds(block, 1), :], steps[1, pl.ds(block, 1), :]
    return far_cosine * cosine - far_sine * sine, far_sine * cosine + far_cosine * sine


def two_heads(block):
    lane = lax.broadcasted_iota(jnp.int32, (128, 128), 1)
    value = block.astype(F32)
    return jnp.concatenate(
        [jnp.where(lane < HEAD_DIM, value, 0.0), jnp.where(lane >= HEAD_DIM, value, 0.0)], axis=0
    )


def two_heads_t(block):
    feature = lax.broadcasted_iota(jnp.int32, (128, 128), 0)
    value = block.astype(F32).T
    return jnp.concatenate(
        [jnp.where(feature < HEAD_DIM, value, 0.0), jnp.where(feature >= HEAD_DIM, value, 0.0)], axis=1
    )


def one_block(stacked):
    feature = lax.broadcasted_iota(jnp.int32, (128, 128), 0)
    return jnp.where(feature < HEAD_DIM, stacked[:, :128], stacked[:, 128:]).T


def nt(left, right):
    return lax.dot_general(left, right, (((1,), (1,)), ((), ())), preferred_element_type=F32)


def plan_blocks(group_place, slots, places):
    _, y, z, _ = here()

    def one(j, carry):
        slots[group_place[j]] = j
        return carry

    lax.fori_loop(0, 32, one, 0)
    for b in range(8):
        places[b] = group_place[(y * 4 + b // 2) * 2 + b % 2]
        places[8 + b] = group_place[((b // 2) * 4 + z) * 2 + b % 2]


def row_of(m, i):
    _, y, z, _ = here()
    return jnp.where(m == 0, y * 4 + i, i * 4 + z)


def unit_of(places, m, n):
    pair, rest = n // 9, lax.rem(n, 9)
    ahead = places[m * 8 + pair * 2] // (TILE // 128) + 1
    late = rest >= ahead
    block = pair * 2 + jnp.where(late, 1, 0)
    tile = rest - jnp.where(late, ahead, 0)
    return block, tile, places[m * 8 + block] * 128 - tile * TILE


def lay_mask(steps, bars):
    row = lax.broadcasted_iota(jnp.int32, (1024, 128), 0) - 513
    lane = lax.broadcasted_iota(jnp.int32, (1024, 128), 1)
    steps[...] = jnp.where(jnp.minimum(row, 127) == lane, 1.0, 0.0).astype(BF)
    bar = lax.broadcasted_iota(jnp.int32, (128, 256), 0)
    query = lax.rem(lax.broadcasted_iota(jnp.int32, (128, 256), 1), 128)
    bars[...] = jnp.where(bar >= query, LOW, 0.0).astype(BF)


def with_mask(keys, steps, behind):
    first = 512 - jnp.minimum(behind, 512)
    return jnp.concatenate([keys, steps[pl.ds(pl.multiple_of(first, 128), TILE), :]], axis=1)


def tile_of(t):
    return pl.ds(pl.multiple_of(t * TILE, TILE), TILE)


def lay_blocks(slots, lay):
    def some(n, carry):
        for k in range(8):
            b = n * 8 + k
            slot = slots[b]
            rows = pl.ds(pl.multiple_of(lax.rem(slot, 2) * 128, 128), 128)
            lay(slot // 2, rows, pl.ds(pl.multiple_of(b * 128, 128), 128))
        return carry

    lax.fori_loop(0, 4, some, 0)


UNITS_EACH = 36


def attend(group_place, spread):
    def kernel(
        group_ref, k_ref, v_ref, q_ref, o_ref, full_ref, log_ref,
        slots, places, keys, values_t, queries, scores_0, scores_1, weights_0, weights_1, results, tops, steps, bars,
    ):
        scores, weights = (scores_0, scores_1), (weights_0, weights_1)
        m = pl.program_id(0)
        plan_blocks(group_ref, slots, places)

        def lay(slot, rows, to):
            keys[to, :] = k_ref[0, slot, 0, rows, :]
            values_t[:128, to] = v_ref[0, slot, 0, rows, :].T

        lay_blocks(slots, lay)
        for b in range(8):
            row = row_of(m, b // 2)
            block = q_ref[0, row, 0, (b % 2) * 128 : (b % 2) * 128 + 128, :]
            queries[b, :128] = (two_heads_t(block) * 0.125).astype(BF)
        lay_mask(steps, bars)
        for b in range(8):
            queries[b, 128:] = bars[...]
        values_t[128:, :] = jnp.ones((16, 4096), BF)

        def multiply(n, odd):
            block, tile, behind = unit_of(places, m, n)
            value = jnp.dot(
                with_mask(keys[tile_of(tile), :], steps, behind), queries[block], preferred_element_type=F32
            )
            scores[odd][...] = value
            return jnp.max(value, axis=0, keepdims=True) * LOG2E

        def soften(n, odd, top, most):
            block, tile, _ = unit_of(places, m, n)
            top = jnp.where(tile == 0, LOW, top)
            new_top = jnp.maximum(top, most)
            for r in range(0, TILE, ROWS):
                rows = slice(r, r + ROWS)
                weights[odd][rows, :] = jnp.exp2(scores[odd][rows, :] * LOG2E - new_top).astype(BF)
            tops[block, 0:1, :] = new_top
            return new_top, jnp.exp2(top - new_top)

        def gather(n, odd, shrink, acc):
            block, tile, _ = unit_of(places, m, n)
            acc = acc * shrink + jnp.dot(
                values_t[:, tile_of(tile)], weights[odd][...], preferred_element_type=F32
            )
            results[block] = acc
            return acc

        most = multiply(0, 0)
        after = multiply(1, 1)
        top, shrink = soften(0, 0, jnp.zeros((1, 256), F32), most)

        def step(k, carry):
            top, shrink, acc, most = carry
            for n, odd in [(AT_ONCE * k + 1 + j, 1 - j % 2) for j in range(AT_ONCE)]:
                after = multiply(n + 1, 1 - odd)
                acc = gather(n - 1, 1 - odd, shrink, acc)
                top, shrink = soften(n, odd, top, most)
                most = after
            return top, shrink, acc, most

        carry = (top, shrink, jnp.zeros((144, 256), F32), after)
        top, shrink, acc, most = lax.fori_loop(0, (UNITS_EACH - 2) // AT_ONCE, step, carry)
        last = UNITS_EACH - 1
        acc = gather(last - 1, 0, shrink, acc)
        _, shrink = soften(last, 1, top, most)
        gather(last, 1, shrink, acc)
        for b in range(8):
            rows = slice((b % 2) * 128, (b % 2) * 128 + 128)
            total = results[b, 128:129, :]
            result = one_block(results[b, :128, :] / total)
            full_ref[0, b // 2, rows, :] = result
            o_ref[0, b // 2, rows, :] = result.astype(BF)
            log_ref[0, b : b + 1, :] = tops[b, 0:1, :] + jnp.log2(total)

    grid_spec = pltpu.PrefetchScalarGridSpec(
        num_scalar_prefetch=1,
        grid=(2,),
        in_specs=[
            pl.BlockSpec((1, 16, 1, 256, 128), lambda m, g: (m, 0, 0, 0, 0)),
            pl.BlockSpec((1, 16, 1, 256, 128), lambda m, g: (m, 0, 1, 0, 0)),
            pl.BlockSpec((1, 16, 1, 256, 128), lambda m, g: (m, 0, 2, 0, 0)),
        ],
        out_specs=[
            pl.BlockSpec((1, 4, 256, 128), lambda m, g: (m, 0, 0, 0)),
            pl.BlockSpec((1, 4, 256, 128), lambda m, g: (m, 0, 0, 0)),
            pl.BlockSpec((1, 8, 256), lambda m, g: (m, 0, 0)),
        ],
        scratch_shapes=[
            pltpu.SMEM((32,), jnp.int32),
            pltpu.SMEM((16,), jnp.int32),
            pltpu.VMEM((4096, 128), BF),
            pltpu.VMEM((144, 4096), BF),
            pltpu.VMEM((8, 256, 256), BF),
            pltpu.VMEM((TILE, 256), F32),
            pltpu.VMEM((TILE, 256), F32),
            pltpu.VMEM((TILE, 256), BF),
            pltpu.VMEM((TILE, 256), BF),
            pltpu.VMEM((8, 144, 256), F32),
            pltpu.VMEM((8, 8, 256), F32),
            pltpu.VMEM((1024, 128), BF),
            pltpu.VMEM((128, 256), BF),
        ],
    )
    return pl.pallas_call(
        kernel,
        name="attend",
        grid_spec=grid_spec,
        out_shape=[
            jax.ShapeDtypeStruct((2, 4, 256, 128), BF),
            jax.ShapeDtypeStruct((2, 4, 256, 128), F32),
            jax.ShapeDtypeStruct((2, 8, 256), F32),
        ],
        compiler_params=pltpu.CompilerParams(vmem_limit_bytes=VMEM_LIMIT),
    )(group_place, spread, spread, spread)


def attend_back(group_place, spread, full, logs, upstream, base, steps):
    def kernel(
        group_ref, k_ref, v_ref, q_ref, full_ref, log_ref, up_ref, base_ref, steps_ref,
        dq_ref, dkv_ref,
        slots, places, keys, keys_t, values, dkeys, dvalues, queries, queries_t, grads, grads_t, delta,
        scores_0, scores_1, dprobs_0, dprobs_1, probs_0, probs_1, dscores_0, dscores_1, results, steps, bars,
    ):
        scores, dprobs = (scores_0, scores_1), (dprobs_0, dprobs_1)
        probs_low, dscores = (probs_0, probs_1), (dscores_0, dscores_1)
        m = pl.program_id(0)
        plan_blocks(group_ref, slots, places)

        def lay(slot, rows, to):
            block = k_ref[0, slot, 0, rows, :]
            keys[to, :] = block
            keys_t[:, to] = block.T
            values[to, :] = v_ref[0, slot, 0, rows, :]
            dkeys[to, :] = jnp.zeros((128, 128), F32)
            dvalues[to, :] = jnp.zeros((128, 128), F32)

        lay_blocks(slots, lay)
        for b in range(8):
            rows = slice((b % 2) * 128, (b % 2) * 128 + 128)
            block = q_ref[0, row_of(m, b // 2), 0, rows, :]
            queries[b] = (two_heads(block) * 0.125).astype(BF)
            queries_t[b, :128] = (two_heads_t(block) * 0.125).astype(BF)
            ups = up_ref[0, b // 2, rows, :]
            grads[b] = two_heads(ups).astype(BF)
            grads_t[b] = two_heads_t(ups).astype(BF)
            product = (ups.astype(F32) * full_ref[0, b // 2, rows, :]).T
            delta[b, 0:1, :128] = jnp.sum(product[:HEAD_DIM], axis=0, keepdims=True)
            delta[b, 0:1, 128:] = jnp.sum(product[HEAD_DIM:], axis=0, keepdims=True)
        lay_mask(steps, bars)
        for b in range(8):
            queries_t[b, 128:] = bars[...]

        def multiply(n, odd):
            block, tile, behind = unit_of(places, m, n)
            scores[odd][...] = jnp.dot(
                with_mask(keys[tile_of(tile), :], steps, behind), queries_t[block], preferred_element_type=F32
            )
            dprobs[odd][...] = jnp.dot(
                values[tile_of(tile), :], grads_t[block], preferred_element_type=F32
            )

        def soften(n, odd):
            block, _, _ = unit_of(places, m, n)
            logs, deltas = log_ref[0, pl.ds(block, 1), :], delta[block, 0:1, :]
            for r in range(0, TILE, ROWS):
                rows = slice(r, r + ROWS)
                value = jnp.exp2(scores[odd][rows, :] * LOG2E - logs)
                probs_low[odd][rows, :] = value.astype(BF)
                dscores[odd][rows, :] = (value * (dprobs[odd][rows, :] - deltas)).astype(BF)

        def gather(n, odd, acc):
            block, tile, _ = unit_of(places, m, n)
            span = tile_of(tile)
            dvalues[span, :] += jnp.dot(probs_low[odd][...], grads[block], preferred_element_type=F32)
            dkeys[span, :] += jnp.dot(dscores[odd][...], queries[block], preferred_element_type=F32)
            acc = jnp.where(tile == 0, 0.0, acc) + jnp.dot(
                keys_t[:, span], dscores[odd][...], preferred_element_type=F32
            )
            results[block] = acc
            return acc

        multiply(0, 0)
        multiply(1, 1)
        soften(0, 0)

        def step(k, acc):
            for n, odd in [(AT_ONCE * k + 1 + j, 1 - j % 2) for j in range(AT_ONCE)]:
                multiply(n + 1, 1 - odd)
                acc = gather(n - 1, 1 - odd, acc)
                soften(n, odd)
            return acc

        last = UNITS_EACH - 1
        acc = lax.fori_loop(0, (UNITS_EACH - 2) // AT_ONCE, step, jnp.zeros((128, 256), F32))
        acc = gather(last - 1, 0, acc)
        soften(last, 1)
        gather(last, 1, acc)

        def turned_back(values, place):
            cosine, sine = turn_tables(base_ref, steps_ref, place)
            return turn(values, cosine, -sine)

        for b in range(8):
            rows = slice((b % 2) * 128, (b % 2) * 128 + 128)
            dquery = one_block(results[b]) * 0.125
            dq_ref[0, b // 2, rows, :] = turned_back(dquery, places[m * 8 + b]).astype(BF)

        def flush(n, carry):
            for k in range(4):
                b = n * 4 + k
                slot = slots[b]
                rows = pl.ds(pl.multiple_of(lax.rem(slot, 2) * 128, 128), 128)
                to = pl.ds(pl.multiple_of(b * 128, 128), 128)
                dkv_ref[0, slot // 2, 0, rows, :] = turned_back(dkeys[to, :], b).astype(BF)
                dkv_ref[0, slot // 2, 1, rows, :] = dvalues[to, :].astype(BF)
            return carry

        lax.fori_loop(0, 8, flush, 0)

    grid_spec = pltpu.PrefetchScalarGridSpec(
        num_scalar_prefetch=1,
        grid=(2,),
        in_specs=[
            pl.BlockSpec((1, 16, 1, 256, 128), lambda m, g: (m, 0, 0, 0, 0)),
            pl.BlockSpec((1, 16, 1, 256, 128), lambda m, g: (m, 0, 1, 0, 0)),
            pl.BlockSpec((1, 16, 1, 256, 128), lambda m, g: (m, 0, 2, 0, 0)),
            pl.BlockSpec((1, 4, 256, 128), lambda m, g: (m, 0, 0, 0)),
            pl.BlockSpec((1, 8, 256), lambda m, g: (m, 0, 0)),
            pl.BlockSpec((1, 4, 256, 128), lambda m, g: (m, 0, 0, 0)),
            pl.BlockSpec((2, 128, 128), lambda m, g: (0, 0, 0)),
            pl.BlockSpec((2, 32, 128), lambda m, g: (0, 0, 0)),
        ],
        out_specs=[
            pl.BlockSpec((1, 4, 256, 128), lambda m, g: (m, 0, 0, 0)),
            pl.BlockSpec((1, 16, 2, 256, 128), lambda m, g: (m, 0, 0, 0, 0)),
        ],
        scratch_shapes=[
            pltpu.SMEM((32,), jnp.int32),
            pltpu.SMEM((16,), jnp.int32),
            pltpu.VMEM((4096, 128), BF),
            pltpu.VMEM((128, 4096), BF),
            pltpu.VMEM((4096, 128), BF),
            pltpu.VMEM((4096, 128), F32),
            pltpu.VMEM((4096, 128), F32),
            pltpu.VMEM((8, 256, 128), BF),
            pltpu.VMEM((8, 256, 256), BF),
            pltpu.VMEM((8, 256, 128), BF),
            pltpu.VMEM((8, 128, 256), BF),
            pltpu.VMEM((8, 8, 256), F32),
            pltpu.VMEM((TILE, 256), F32),
            pltpu.VMEM((TILE, 256), F32),
            pltpu.VMEM((TILE, 256), F32),
            pltpu.VMEM((TILE, 256), F32),
            pltpu.VMEM((TILE, 256), BF),
            pltpu.VMEM((TILE, 256), BF),
            pltpu.VMEM((TILE, 256), BF),
            pltpu.VMEM((TILE, 256), BF),
            pltpu.VMEM((8, 128, 256), F32),
            pltpu.VMEM((1024, 128), BF),
            pltpu.VMEM((128, 256), BF),
        ],
    )
    return pl.pallas_call(
        kernel,
        name="attend_back",
        grid_spec=grid_spec,
        out_shape=[
            jax.ShapeDtypeStruct((2, 4, 256, 128), BF),
            jax.ShapeDtypeStruct((2, 16, 2, 256, 128), BF),
        ],
        compiler_params=pltpu.CompilerParams(vmem_limit_bytes=VMEM_LIMIT),
    )(group_place, spread, spread, spread, full, logs, upstream, base, steps)


def tn(left, right):
    return lax.dot_general(left, right, (((0,), (0,)), ((), ())), preferred_element_type=F32)


def feed_forward(second_low, dy, weights):
    def kernel(
        low_hbm, dy_hbm, w_hbm, branch, dsecond, gate_out, dup, mixed,
        low, dys, gate_w, up_w, down_w, gate, up, dmixed, dgate, chunks, sems, chunk_sems,
    ):
        def load(n, src, dst):
            copy = pltpu.make_async_copy(src, dst, sems.at[n])
            copy.start()
            return copy

        def columns(k):
            return w_hbm.at[:, pl.ds(k * UNITS, UNITS)]

        loads = [
            load(0, low_hbm, low),
            load(1, columns(0), gate_w),
            load(2, columns(1), up_w),
            load(3, dy_hbm, dys),
            load(4, columns(2), down_w),
        ]
        loads[0].wait()
        loads[1].wait()
        gate[...] = jnp.dot(low[...], gate_w[...], preferred_element_type=F32)
        loads[2].wait()
        up[...] = jnp.dot(low[...], up_w[...], preferred_element_type=F32)
        loads[3].wait()
        loads[4].wait()
        dmixed[...] = jnp.dot(dys[...], down_w[...], preferred_element_type=F32)

        def step(i, carry):
            rows = pl.ds(pl.multiple_of(i * 16, 16), 16)
            g, u, d = gate[rows, :], up[rows, :], dmixed[rows, :]
            s = jax.nn.sigmoid(g)
            silu = g * s
            mixed[rows, :] = (silu * u).astype(BF)
            dgate[rows, :] = (d * u * s * (1.0 + g * (1.0 - s))).astype(BF)
            dup[rows, :] = (d * silu).astype(BF)
            return carry

        lax.fori_loop(0, 32, step, 0)
        dsecond[...] = (nt(dgate[...], gate_w[...]) + nt(dup[...], up_w[...])).astype(BF)
        busy = {}
        for k in range(4):
            rows = pl.ds(k * 512, 512)
            slot = k % 2
            if slot in busy:
                busy[slot].wait()
            chunks[slot] = tn(low[:, rows], dgate[...]).astype(BF)
            busy[slot] = pltpu.make_async_copy(chunks.at[slot], gate_out.at[rows, :], chunk_sems.at[slot])
            busy[slot].start()
        branch[...] = nt(mixed[...], down_w[...]).astype(BF)
        busy[0].wait()
        busy[1].wait()

    return pl.pallas_call(
        kernel,
        name="feed_forward",
        in_specs=[ANY, ANY, ANY],
        out_specs=[IN_VMEM, IN_VMEM, ANY, IN_VMEM, IN_VMEM],
        out_shape=[jax.ShapeDtypeStruct((512, D), BF)] * 2
        + [jax.ShapeDtypeStruct((D, UNITS), BF)]
        + [jax.ShapeDtypeStruct((512, UNITS), BF)] * 2,
        scratch_shapes=[pltpu.VMEM((512, D), BF)] * 2
        + [pltpu.VMEM((D, UNITS), BF)] * 3
        + [pltpu.VMEM((512, UNITS), F32)] * 3
        + [
            pltpu.VMEM((512, UNITS), BF),
            pltpu.VMEM((2, 512, UNITS), BF),
            pltpu.SemaphoreType.DMA((5,)),
            pltpu.SemaphoreType.DMA((2,)),
        ],
        compiler_params=pltpu.CompilerParams(vmem_limit_bytes=VMEM_LIMIT),
    )(second_low, dy, weights)


def angle_tables():
    lane = np.arange(128) % HEAD_DIM
    power = 10000.0 ** (-2.0 * (lane % (ROT // 2)) / ROT)
    frequency = np.where(lane < ROT, power, 0.0)
    tables = []
    for places in (np.arange(128), np.arange(32) * 128):
        angles = places[:, None] * frequency[None, :]
        tables.append(jnp.asarray(np.stack([np.cos(angles), np.sin(angles)]).astype(np.float32)))
    return tables


def body(
    inputs,
    cotangent,
    group_place,
    attend_gain,
    attend_shift,
    project_weight,
    project_bias,
    output_weight,
    mixer_gain,
    mixer_shift,
    gate_weight,
    up_weight,
    down_weight,
):
    shard_index = lax.axis_index("dp") * 16 + lax.axis_index("ctx")
    base, steps = angle_tables()

    vectors = jnp.stack([attend_gain, attend_shift, mixer_gain, mixer_shift])
    vectors = jnp.concatenate(
        [
            jnp.pad(vectors, ((0, 0), (0, 64))),
            jnp.pad(project_bias.reshape(1, 48), ((0, 0), (0, 80))),
            jnp.zeros((59, 128), BF),
        ]
    )
    front_shard = jnp.concatenate(
        [project_weight.reshape(64, 1536), output_weight.T, vectors], axis=1
    )
    back_shard = jnp.concatenate([gate_weight, up_weight, down_weight.T], axis=1)

    tokens = inputs.reshape(512, D)
    quarters = inputs.reshape(4, 128, D)
    front, gains, first_low, spread = front_forward(front_shard, tokens, group_place, base, steps)
    spread = spread.reshape(2, 16, 3, 256, 128)
    attended_heads, attended_full, logs = attend(group_place, spread)
    attended_low, hidden, second_low, back = middle_forward(
        attended_heads, front, quarters, gains, back_shard
    )

    second_low = second_low.reshape(512, D)
    dy = cotangent.reshape(512, D)
    branch, second_part, gate_grad, dup, mixed = feed_forward(second_low, dy, back)
    dhidden, mixer_vectors, output_grad, upstream, out_block, gate_grad, up_grad, down_grad = middle_backward(
        second_part.reshape(4, 128, D),
        dy,
        hidden,
        gains,
        attended_low,
        front,
        second_low,
        dup,
        mixed,
        branch.reshape(4, 128, D),
        gate_grad.reshape(2, 4, 4, 64, UNITS),
    )

    dq, dkv = attend_back(group_place, spread, attended_full, logs, upstream, base, steps)
    dproject, outputs = collect_heads(dkv.reshape(2, 4, 4, 2, 256, 128), dq, out_block)
    input_grad, small, project_grad, output_grad = last_backward(
        dproject, first_low, front, quarters, dhidden, gains, mixer_vectors, output_grad.reshape(2, 4, 4, 64, 512)
    )
    own = lax.dynamic_slice(small, (0, shard_index * 64), (4, 64))
    bias_grad = lax.dynamic_slice(
        small[4, :1536].reshape(3, 8, 64), (0, 0, shard_index * 2), (3, 8, 2)
    )
    shape = inputs.shape
    return (
        outputs.reshape(shape),
        input_grad.reshape(shape),
        own[0],
        own[1],
        project_grad.reshape(64, 3, 512),
        bias_grad,
        output_grad.T,
        own[2],
        own[3],
        gate_grad,
        up_grad,
        down_grad.T,
    )


def solution(mesh):
    weight = ("dp", "ctx")
    rows = P(None, "dp", "ctx", None)
    vector = P(weight)
    matrix = P(weight, "tensor")
    turned = P("tensor", weight)
    project = P(weight, None, "tensor")
    bias = P(None, "tensor", weight)
    params = (vector, vector, project, bias, turned, vector, vector, matrix, matrix, turned)
    return jax.shard_map(
        body,
        mesh=mesh,
        in_specs=(rows, rows, P()) + params,
        out_specs=(rows, rows) + params,
        check_vma=False,
    )
```
